32 devices in a mesh: row: 4 (over y, x), col: 8 (over z, core).
Axes of the slice: x: 2, y: 2, z: 4, core: 2. Of those that a mesh axis runs over, the one named last changes fastest.
Arguments:
- image: bfloat16 [64, 512, 256], P('row', 'col'), may hold values from -7 to 7
- out_cotangent: bfloat16 [64, 512, 256], P('row', 'col'), may hold values from -6 to 6
- norm0_gain: bfloat16 [256], replicated, may hold values from 0.099609375 to 1.8984375
- w_expand: bfloat16 [256, 1024], replicated, may hold values from -0.375 to 0.375
- w_depth: bfloat16 [3, 3, 1024], replicated, may hold values from -2 to 2
- w_squeeze: bfloat16 [1024, 64], replicated, may hold values from -0.75 to 0.75
- w_excite: bfloat16 [64, 1024], replicated, may hold values from -3 to 3
- w_project: bfloat16 [1024, 256], replicated, may hold values from -0.1875 to 0.1875
- norm1_gain: bfloat16 [256], replicated, may hold values from 0.099609375 to 1.8984375
- w_qkv: bfloat16 [256, 768], replicated, may hold values from -0.375 to 0.375
- w_out: bfloat16 [256, 256], replicated, may hold values from -0.375 to 0.375
- attn_bias: float32 [8, 64, 64], replicated, may hold values from -2 to 250
Outputs:
- block_out: bfloat16 [64, 512, 256], P('row', 'col')
- grad_image: bfloat16 [64, 512, 256], P('row', 'col')
- grad_norm0: float32 [256], replicated
- grad_expand: float32 [256, 1024], replicated
- grad_depth: float32 [3, 3, 1024], replicated
- grad_squeeze: float32 [1024, 64], replicated
- grad_excite: float32 [64, 1024], replicated
- grad_project: float32 [1024, 256], replicated
- grad_norm1: float32 [256], replicated
- grad_qkv: float32 [256, 768], replicated
- grad_out_proj: float32 [256, 256], replicated
- grad_bias: float32 [8, 64, 64], replicated
The draws below stay inside these ranges and needn't reach their ends.
All inputs are finite; a program needn't handle non-finite values.
Results may differ from the reference program's by a relative error of at most 0.015.
Values may be sent and summed in bfloat16 or wider, within the bound.
No kernel may reach another device: no remote copies, remote signals or barrier semaphores. Data moves between devices by JAX's collectives and lax.ppermute only.
A program may use at most 128 MiB of HBM per device.

```python
import jax
import jax.numpy as jnp
from jax import lax

C = 256
HEADS = 8
E = 1024
SQ = 64
GRID = 8
HEIGHT = 64
WIDTH = 512


def draw_image(key, part):
    key = jax.random.fold_in(key, 11)
    noise_key, direction_key = jax.random.split(key)
    base = jnp.clip(jax.random.normal(noise_key, (HEIGHT, WIDTH, C), jnp.float32), -5.0, 5.0)
    slope = 1.5
    direction = jax.random.rademacher(direction_key, (C,), jnp.float32)
    row_frac = jnp.arange(HEIGHT, dtype=jnp.float32)[:, None] / HEIGHT
    col_frac = jnp.arange(WIDTH, dtype=jnp.float32)[None, :] / WIDTH
    ramp = 0.3 + slope * 0.5 * (row_frac + col_frac)
    return (base + ramp[:, :, None] * direction).astype(jnp.bfloat16)


def draw_attn_bias(key, part):
    key = jax.random.fold_in(key, 23)
    base_key = jax.random.fold_in(key, 0)
    members = GRID * GRID
    base = jax.random.uniform(base_key, (HEADS, members, members), jnp.float32, -2.0, 2.0)
    return base


def block_scale(rng, dims, cuts, least, high):
    factor_of = 1.0
    for axis_at, blocks in cuts:
        heights = jax.random.uniform(jax.random.fold_in(jax.random.fold_in(rng, 6), axis_at), (blocks,), jnp.float32, least / len(cuts), high / len(cuts))
        factor_of = factor_of * jnp.repeat(jnp.exp(heights), dims[axis_at] // blocks).reshape((-1,) + (1,) * (len(dims) - 1 - axis_at))
    return factor_of


def centred(key, extent, scale, most, pieces=(), kind=jnp.bfloat16):
    entries = scale * jax.random.normal(key, extent, jnp.float32)
    if pieces:
        entries = entries * block_scale(key, extent, pieces, -0.22, 0.18)
    return jnp.clip(entries, -most, most).astype(kind)


def setup_inputs(seed: int = 0) -> dict:
    key_of = jax.random.split(jax.random.key(seed), 13)
    return {
        "image": draw_image(jax.random.fold_in(key_of[12], 71), 0),
        "out_cotangent": centred(key_of[1], (HEIGHT, WIDTH, C), 1.0, 6.0, ((0, 4), (1, 8))),
        "norm0_gain": jnp.clip(1.0 + 0.18 * jax.random.normal(key_of[2], (C,), jnp.float32), 0.099609375, 1.8984375).astype(jnp.bfloat16),
        "w_expand": centred(key_of[3], (C, E), C ** -0.5, 0.375),
        "w_depth": centred(key_of[4], (3, 3, E), 9 ** -0.5, 2.0),
        "w_squeeze": centred(key_of[5], (E, SQ), (E // 16) ** -0.5, 0.75),
        "w_excite": centred(key_of[6], (SQ, E), (max(SQ // 16, 1)) ** -0.5, 3.0),
        "w_project": centred(key_of[7], (E, C), E ** -0.5, 0.1875),
        "norm1_gain": jnp.clip(1.0 + 0.18 * jax.random.normal(key_of[8], (C,), jnp.float32), 0.099609375, 1.8984375).astype(jnp.bfloat16),
        "w_qkv": centred(key_of[9], (C, 3 * C), C ** -0.5, 0.375),
        "w_out": centred(key_of[10], (C, C), C ** -0.5, 0.375),
        "attn_bias": draw_attn_bias(jax.random.fold_in(key_of[12], 71), 0),
    }


def norm_tokens(values, scale_gain):
    average = lax.optimization_barrier(jnp.mean(values, axis=-1, keepdims=True))
    centered = values - average
    variance = lax.optimization_barrier(jnp.mean(centered * centered, axis=-1, keepdims=True))
    return centered * lax.rsqrt(variance + 1e-05) * scale_gain

def matmul_last(left_side, right_side):
    flat_rows = left_side.reshape(-1, left_side.shape[-1])
    product = jnp.dot(flat_rows, right_side, preferred_element_type=jnp.float32)
    return product.reshape(left_side.shape[:-1] + (right_side.shape[-1],))

def smooth_gelu(values):
    return jax.nn.gelu(values, approximate=True)

def depthwise(padded, kernel, row_count, col_count):
    accumulated = jnp.zeros((row_count, col_count, padded.shape[-1]), jnp.float32)
    for shift_row in range(3):
        for shift_col in range(3):
            window = padded[shift_row:shift_row + row_count, shift_col:shift_col + col_count].astype(jnp.float32)
            accumulated = accumulated + window * kernel[shift_row, shift_col].astype(jnp.float32)
    return accumulated

def depthwise_back(padded_grad, kernel, row_count, col_count):
    accumulated = jnp.zeros((row_count, col_count, padded_grad.shape[-1]), jnp.float32)
    for shift_row in range(3):
        for shift_col in range(3):
            window = padded_grad[2 - shift_row:2 - shift_row + row_count, 2 - shift_col:2 - shift_col + col_count].astype(jnp.float32)
            accumulated = accumulated + window * kernel[shift_row, shift_col].astype(jnp.float32)
    return accumulated

def kernel_grad(padded, grad_pre, row_count, col_count):
    kernel_terms = []
    for shift_row in range(3):
        for shift_col in range(3):
            window = padded[shift_row:shift_row + row_count, shift_col:shift_col + col_count].astype(jnp.float32)
            kernel_terms.append(lax.optimization_barrier(jnp.sum(window * grad_pre.astype(jnp.float32), axis=(0, 1))))
    return jnp.stack(kernel_terms).reshape(3, 3, padded.shape[-1])

def excite_gate(pooled, squeeze_wide, excite_wide):
    hidden = jax.nn.silu(jnp.dot(pooled[None, :], squeeze_wide, precision=lax.Precision.HIGHEST))
    return jax.nn.sigmoid(jnp.dot(hidden, excite_wide, precision=lax.Precision.HIGHEST))[0]

def into_groups(values):
    row_count, col_count, channels = values.shape
    parted = values.reshape(GRID, row_count // GRID, GRID, col_count // GRID, channels).transpose(1, 3, 0, 2, 4)
    return parted.reshape(-1, GRID * GRID, channels)

def from_groups(values, row_count, col_count):
    channels = values.shape[-1]
    parted = values.reshape(row_count // GRID, col_count // GRID, GRID, GRID, channels).transpose(2, 0, 3, 1, 4)
    return parted.reshape(row_count, col_count, channels)

def attention_core(normed_groups, w_qkv, attn_bias):
    groups, members, channels = normed_groups.shape
    head_count = attn_bias.shape[0]
    head_dim = channels // head_count
    packed = matmul_last(normed_groups, w_qkv).astype(jnp.bfloat16).reshape(groups, members, 3, head_count, head_dim)
    queries = packed[:, :, 0]
    key_rows = packed[:, :, 1]
    values = packed[:, :, 2]
    scores = jnp.einsum('gihd,gjhd->ghij', queries.astype(jnp.float32), key_rows.astype(jnp.float32)) * head_dim ** (-0.5)
    scores = scores + attn_bias[None]
    row_max = lax.optimization_barrier(jnp.max(scores, axis=-1, keepdims=True))
    lifted = jnp.exp(scores - row_max)
    softmaxed = lifted / lax.optimization_barrier(jnp.sum(lifted, axis=-1, keepdims=True))
    weights_low = softmaxed.astype(jnp.bfloat16).astype(jnp.float32)
    attended = jnp.einsum('ghij,gjhd->gihd', weights_low, values.astype(jnp.float32)).astype(jnp.bfloat16)
    return (attended.reshape(groups, members, channels), queries, key_rows, values, softmaxed)

def attention_back(grad_att, queries, key_rows, values, softmaxed):
    groups, members, channels = grad_att.shape
    head_count = queries.shape[2]
    head_dim = channels // head_count
    grad_heads = grad_att.reshape(groups, members, head_count, head_dim).astype(jnp.float32)
    weights_low = softmaxed.astype(jnp.bfloat16).astype(jnp.float32)
    grad_values = jnp.einsum('ghij,gihd->gjhd', weights_low, grad_heads).astype(jnp.bfloat16)
    grad_probs = jnp.einsum('gihd,gjhd->ghij', grad_heads, values.astype(jnp.float32))
    grad_scores = softmaxed * (grad_probs - lax.optimization_barrier(jnp.sum(grad_probs * softmaxed, axis=-1, keepdims=True)))
    bias_part = lax.optimization_barrier(jnp.sum(grad_scores, axis=0))
    scaled = (grad_scores * head_dim ** (-0.5)).astype(jnp.bfloat16).astype(jnp.float32)
    grad_queries = jnp.einsum('ghij,gjhd->gihd', scaled, key_rows.astype(jnp.float32)).astype(jnp.bfloat16)
    grad_keys = jnp.einsum('ghij,gihd->gjhd', scaled, queries.astype(jnp.float32)).astype(jnp.bfloat16)
    stacked = jnp.stack([grad_queries, grad_keys, grad_values], axis=2)
    return (stacked.reshape(groups, members, 3 * channels), bias_part)

def reference(image, out_cotangent, norm0_gain, w_expand, w_depth, w_squeeze, w_excite, w_project, norm1_gain, w_qkv, w_out, attn_bias):
    row_count, col_count, channels = image.shape
    cells_total = row_count * col_count
    image_float = image.astype(jnp.float32)
    gain_first = norm0_gain.astype(jnp.float32)
    gain_second = norm1_gain.astype(jnp.float32)
    normed_first = norm_tokens(image_float, gain_first).astype(jnp.bfloat16)
    expanded = matmul_last(normed_first, w_expand)
    spread = smooth_gelu(expanded).astype(jnp.bfloat16)
    padded = jnp.pad(spread, ((1, 1), (1, 1), (0, 0)))
    depth_pre = depthwise(padded, w_depth, row_count, col_count)
    activated = smooth_gelu(depth_pre)
    pooled = lax.optimization_barrier(jnp.sum(activated, axis=(0, 1))) / cells_total
    squeeze_wide = w_squeeze.astype(jnp.float32)
    excite_wide = w_excite.astype(jnp.float32)
    channel_gate = excite_gate(pooled, squeeze_wide, excite_wide)
    gated_act = (activated * channel_gate).astype(jnp.bfloat16)
    mixed_map = (image_float + matmul_last(gated_act, w_project)).astype(jnp.bfloat16)
    mixed_float = mixed_map.astype(jnp.float32)
    normed_second = norm_tokens(mixed_float, gain_second).astype(jnp.bfloat16)
    grid_normed = into_groups(normed_second)
    group_total = grid_normed.shape[0]
    block_count = 8
    grid_blocks = grid_normed.reshape(block_count, group_total // block_count, GRID * GRID, channels)

    def forward_block(block_normed):
        return attention_core(block_normed, w_qkv, attn_bias)[0]
    attended_groups = lax.map(forward_block, grid_blocks).reshape(group_total, GRID * GRID, channels)
    attended_map = from_groups(attended_groups, row_count, col_count)
    block_out = (mixed_float + matmul_last(attended_map, w_out)).astype(jnp.bfloat16)
    grad_out_proj = jnp.dot(attended_map.reshape(-1, channels).T, out_cotangent.reshape(-1, channels), preferred_element_type=jnp.float32)
    grad_att = matmul_last(out_cotangent, w_out.T).astype(jnp.bfloat16)
    grad_blocks = into_groups(grad_att).reshape(block_count, group_total // block_count, GRID * GRID, channels)

    def backward_block(pair_blocks):
        block_normed, block_grad = pair_blocks
        attended_unused, queries, key_rows, values, softmaxed = attention_core(block_normed, w_qkv, attn_bias)
        return attention_back(block_grad, queries, key_rows, values, softmaxed)
    grad_packed, bias_parts = lax.map(backward_block, (grid_blocks, grad_blocks))
    grad_packed = grad_packed.reshape(group_total, GRID * GRID, 3 * channels)
    grad_bias = lax.optimization_barrier(jnp.sum(bias_parts, axis=0))
    grad_qkv = jnp.dot(grid_normed.reshape(-1, channels).T, grad_packed.reshape(-1, 3 * channels), preferred_element_type=jnp.float32)
    grad_normed_grid = matmul_last(grad_packed, w_qkv.T).astype(jnp.bfloat16)
    grad_normed = from_groups(grad_normed_grid, row_count, col_count)
    unused_second, norm_second_vjp = jax.vjp(norm_tokens, mixed_float, gain_second)
    grad_mixed_norm, grad_norm1 = norm_second_vjp(grad_normed.astype(jnp.float32))
    grad_mixed = out_cotangent.astype(jnp.float32) + grad_mixed_norm
    grad_mixed_b = grad_mixed.astype(jnp.bfloat16)
    grad_project = jnp.dot(gated_act.reshape(-1, gated_act.shape[-1]).T, grad_mixed_b.reshape(-1, channels), preferred_element_type=jnp.float32)
    grad_gated = matmul_last(grad_mixed_b, w_project.T)
    grad_gate = lax.optimization_barrier(jnp.sum(grad_gated * activated, axis=(0, 1)))
    unused_gate, gate_vjp = jax.vjp(excite_gate, pooled, squeeze_wide, excite_wide)
    grad_pooled, grad_squeeze, grad_excite = gate_vjp(grad_gate)
    grad_activated = grad_gated * channel_gate + grad_pooled / cells_total
    unused_act, gelu_depth_vjp = jax.vjp(smooth_gelu, depth_pre)
    grad_depth_pre = gelu_depth_vjp(grad_activated)[0].astype(jnp.bfloat16)
    grad_pad = jnp.pad(grad_depth_pre, ((1, 1), (1, 1), (0, 0)))
    grad_spread = depthwise_back(grad_pad, w_depth, row_count, col_count)
    grad_depth = kernel_grad(padded, grad_depth_pre, row_count, col_count)
    unused_spread, gelu_expand_vjp = jax.vjp(smooth_gelu, expanded)
    grad_expanded = gelu_expand_vjp(grad_spread)[0].astype(jnp.bfloat16)
    grad_expand = jnp.dot(normed_first.reshape(-1, channels).T, grad_expanded.reshape(-1, grad_expanded.shape[-1]), preferred_element_type=jnp.float32)
    grad_first = matmul_last(grad_expanded, w_expand.T)
    unused_first, norm_first_vjp = jax.vjp(norm_tokens, image_float, gain_first)
    grad_image_norm, grad_norm0 = norm_first_vjp(grad_first)
    grad_image = (grad_mixed + grad_image_norm).astype(jnp.bfloat16)
    return (block_out, grad_image, grad_norm0, grad_expand, grad_depth, grad_squeeze, grad_excite, grad_project, grad_norm1, grad_qkv, grad_out_proj, grad_bias)
```

```python
import jax
import jax.numpy as jnp
from jax import lax
from jax.sharding import PartitionSpec as P

GRID = 8
AXES = ("row", "col")


def sum_everywhere(vector):
    count = lax.axis_size("row") * lax.axis_size("col")
    sent = jnp.broadcast_to(vector[None], (count,) + vector.shape)
    return jnp.sum(lax.all_to_all(sent, AXES, split_axis=0, concat_axis=0, tiled=True), axis=0)


def sum_shares(matrix):
    count = lax.axis_size("row") * lax.axis_size("col")
    rows, columns = matrix.shape
    padded_rows = -(-rows // count) * count
    share = padded_rows // count
    low = matrix.astype(jnp.bfloat16)
    if padded_rows != rows:
        low = jnp.pad(low, ((0, padded_rows - rows), (0, 0)))
    arrived = lax.all_to_all(
        low.reshape(count, share, columns), AXES, split_axis=0, concat_axis=0, tiled=True
    )
    total = jnp.sum(arrived.astype(jnp.float32), axis=0).astype(jnp.bfloat16)
    sent = jnp.broadcast_to(total[None], (count, share, columns))
    whole = lax.all_to_all(sent, AXES, split_axis=0, concat_axis=0, tiled=True)
    return whole.reshape(padded_rows, columns)[:rows].astype(jnp.float32)


def with_halo(cells, sides, width):
    for axis, dim in sides:
        count = lax.axis_size(axis)
        ends = count - 1
        head = lax.slice_in_dim(cells, 0, width, axis=dim)
        tail = lax.slice_in_dim(cells, cells.shape[dim] - width, cells.shape[dim], axis=dim)
        cells = jnp.concatenate(
            [
                lax.ppermute(tail, axis, [(i, (i + 1) % count) for i in range(ends)]),
                cells,
                lax.ppermute(head, axis, [((i + 1) % count, i) for i in range(ends)]),
            ],
            axis=dim,
        )
    return cells


def norm_tokens(values, scale_gain):
    average = jnp.mean(values, axis=-1, keepdims=True)
    centered = values - average
    variance = jnp.mean(centered * centered, axis=-1, keepdims=True)
    return centered * lax.rsqrt(variance + 1e-05) * scale_gain


def matmul_last(left_side, right_side):
    flat_rows = left_side.reshape(-1, left_side.shape[-1])
    product = jnp.dot(flat_rows, right_side, preferred_element_type=jnp.float32)
    return product.reshape(left_side.shape[:-1] + (right_side.shape[-1],))


def smooth_gelu(values):
    return jax.nn.gelu(values, approximate=True)


def depthwise(padded, kernel, row_count, col_count):
    accumulated = jnp.zeros((row_count, col_count, padded.shape[-1]), jnp.float32)
    for shift_row in range(3):
        for shift_col in range(3):
            window = padded[
                shift_row : shift_row + row_count, shift_col : shift_col + col_count
            ].astype(jnp.float32)
            accumulated = accumulated + window * kernel[shift_row, shift_col].astype(jnp.float32)
    return accumulated


def depthwise_back(padded_grad, kernel, row_count, col_count):
    accumulated = jnp.zeros((row_count, col_count, padded_grad.shape[-1]), jnp.float32)
    for shift_row in range(3):
        for shift_col in range(3):
            window = padded_grad[
                2 - shift_row : 2 - shift_row + row_count, 2 - shift_col : 2 - shift_col + col_count
            ].astype(jnp.float32)
            accumulated = accumulated + window * kernel[shift_row, shift_col].astype(jnp.float32)
    return accumulated


def kernel_grad(padded, grad_pre, row_count, col_count):
    kernel_terms = []
    for shift_row in range(3):
        for shift_col in range(3):
            window = padded[
                shift_row : shift_row + row_count, shift_col : shift_col + col_count
            ].astype(jnp.float32)
            kernel_terms.append(jnp.sum(window * grad_pre.astype(jnp.float32), axis=(0, 1)))
    return jnp.stack(kernel_terms).reshape(3, 3, padded.shape[-1])


def excite_gate(pooled, squeeze_wide, excite_wide):
    hidden = jax.nn.silu(jnp.dot(pooled[None, :], squeeze_wide, precision=lax.Precision.HIGHEST))
    return jax.nn.sigmoid(jnp.dot(hidden, excite_wide, precision=lax.Precision.HIGHEST))[0]


def into_groups(values):
    row_count, col_count, channels = values.shape
    parted = values.reshape(GRID, row_count // GRID, GRID, col_count // GRID, channels).transpose(
        1, 3, 0, 2, 4
    )
    return parted.reshape(-1, GRID * GRID, channels)


def from_groups(values, row_count, col_count):
    channels = values.shape[-1]
    parted = values.reshape(row_count // GRID, col_count // GRID, GRID, GRID, channels).transpose(
        2, 0, 3, 1, 4
    )
    return parted.reshape(row_count, col_count, channels)


def flat_order_out(values):
    row_count, col_count, channels = values.shape
    row_devices = lax.axis_size("row")
    col_devices = lax.axis_size("col")
    ordered = values.reshape(
        row_count // row_devices, row_devices, col_count // col_devices, col_devices, channels
    )
    return ordered.transpose(1, 3, 0, 2, 4).reshape(
        row_devices * col_devices, row_count // row_devices, col_count // col_devices, channels
    )


def flat_order_in(arrived, row_count, col_count):
    channels = arrived.shape[-1]
    row_devices = lax.axis_size("row")
    col_devices = lax.axis_size("col")
    arrived = arrived.reshape(
        row_devices, col_devices, row_count // row_devices, col_count // col_devices, channels
    )
    return arrived.transpose(0, 2, 1, 3, 4).reshape(row_count, col_count, channels)


def flat_back_out(values):
    row_count, col_count, channels = values.shape
    row_devices = lax.axis_size("row")
    col_devices = lax.axis_size("col")
    ordered = values.reshape(
        row_devices, row_count // row_devices, col_devices, col_count // col_devices, channels
    )
    return ordered.transpose(0, 2, 1, 3, 4).reshape(
        row_devices * col_devices, row_count // row_devices, col_count // col_devices, channels
    )


def flat_back_in(arrived, row_count, col_count):
    channels = arrived.shape[-1]
    row_devices = lax.axis_size("row")
    col_devices = lax.axis_size("col")
    arrived = arrived.reshape(
        row_devices, col_devices, row_count // row_devices, col_count // col_devices, channels
    )
    return arrived.transpose(2, 0, 3, 1, 4).reshape(row_count, col_count, channels)


def to_grid(values):
    row_count, col_count, channels = values.shape
    arrived = lax.all_to_all(
        flat_order_out(values), ("row", "col"), split_axis=0, concat_axis=0, tiled=True
    )
    return flat_order_in(arrived, row_count, col_count)


def from_grid(values):
    row_count, col_count, channels = values.shape
    arrived = lax.all_to_all(
        flat_back_out(values), ("row", "col"), split_axis=0, concat_axis=0, tiled=True
    )
    return flat_back_in(arrived, row_count, col_count)


def attention_core(normed_groups, w_qkv, attn_bias):
    groups, members, channels = normed_groups.shape
    head_count = attn_bias.shape[0]
    head_dim = channels // head_count
    packed = (
        matmul_last(normed_groups, w_qkv)
        .astype(jnp.bfloat16)
        .reshape(groups, members, 3, head_count, head_dim)
    )
    queries = packed[:, :, 0]
    key_rows = packed[:, :, 1]
    values = packed[:, :, 2]
    scores = jnp.einsum(
        "gihd,gjhd->ghij", queries, key_rows, preferred_element_type=jnp.float32
    ) * head_dim ** (-0.5)
    scores = scores + attn_bias[None]
    row_max = jnp.max(scores, axis=-1, keepdims=True)
    lifted = jnp.exp(scores - row_max)
    softmaxed = lifted / jnp.sum(lifted, axis=-1, keepdims=True)
    attended = jnp.einsum(
        "ghij,gjhd->gihd",
        softmaxed.astype(jnp.bfloat16),
        values,
        preferred_element_type=jnp.float32,
    ).astype(jnp.bfloat16)
    return (attended.reshape(groups, members, channels), queries, key_rows, values, softmaxed)


def attention_back(grad_att, queries, key_rows, values, softmaxed):
    groups, members, channels = grad_att.shape
    head_count = queries.shape[2]
    head_dim = channels // head_count
    grad_heads = grad_att.reshape(groups, members, head_count, head_dim)
    grad_values = jnp.einsum(
        "ghij,gihd->gjhd",
        softmaxed.astype(jnp.bfloat16),
        grad_heads,
        preferred_element_type=jnp.float32,
    ).astype(jnp.bfloat16)
    grad_probs = jnp.einsum(
        "gihd,gjhd->ghij", grad_heads, values, preferred_element_type=jnp.float32
    )
    grad_scores = softmaxed * (grad_probs - jnp.sum(grad_probs * softmaxed, axis=-1, keepdims=True))
    bias_part = jnp.sum(grad_scores, axis=0)
    scaled = (grad_scores * head_dim ** (-0.5)).astype(jnp.bfloat16)
    grad_queries = jnp.einsum(
        "ghij,gjhd->gihd", scaled, key_rows, preferred_element_type=jnp.float32
    ).astype(jnp.bfloat16)
    grad_keys = jnp.einsum(
        "ghij,gihd->gjhd", scaled, queries, preferred_element_type=jnp.float32
    ).astype(jnp.bfloat16)
    stacked = jnp.stack([grad_queries, grad_keys, grad_values], axis=2)
    return (stacked.reshape(groups, members, 3 * channels), bias_part)


def on_device(
    image,
    out_cotangent,
    norm0_gain,
    w_expand,
    w_depth,
    w_squeeze,
    w_excite,
    w_project,
    norm1_gain,
    w_qkv,
    w_out,
    attn_bias,
):
    row_count, col_count, channels = image.shape
    cells_total = row_count * lax.axis_size("row") * col_count * lax.axis_size("col")
    image_float = image.astype(jnp.float32)
    gain_first = norm0_gain.astype(jnp.float32)
    gain_second = norm1_gain.astype(jnp.float32)
    normed_first = norm_tokens(image_float, gain_first).astype(jnp.bfloat16)
    expanded = matmul_last(normed_first, w_expand)
    spread = smooth_gelu(expanded).astype(jnp.bfloat16)
    padded = with_halo(spread, (("row", 0), ("col", 1)), 1)
    depth_pre = depthwise(padded, w_depth, row_count, col_count)
    activated = smooth_gelu(depth_pre)
    pooled = sum_everywhere(jnp.sum(activated, axis=(0, 1))) / cells_total
    squeeze_wide = w_squeeze.astype(jnp.float32)
    excite_wide = w_excite.astype(jnp.float32)
    channel_gate = excite_gate(pooled, squeeze_wide, excite_wide)
    gated_act = (activated * channel_gate).astype(jnp.bfloat16)
    mixed_map = (image_float + matmul_last(gated_act, w_project)).astype(jnp.bfloat16)
    mixed_float = mixed_map.astype(jnp.float32)
    normed_second = norm_tokens(mixed_float, gain_second).astype(jnp.bfloat16)
    grad_att = matmul_last(out_cotangent, w_out.T).astype(jnp.bfloat16)
    grid_normed = into_groups(to_grid(normed_second))
    attended_groups, queries, key_rows, values, softmaxed = attention_core(
        grid_normed, w_qkv, attn_bias
    )
    attended_map = from_grid(from_groups(attended_groups, row_count, col_count))
    grid_grad = into_groups(to_grid(grad_att))
    grad_packed, grad_bias = attention_back(grid_grad, queries, key_rows, values, softmaxed)
    grad_qkv = jnp.dot(
        grid_normed.reshape(-1, channels).T,
        grad_packed.reshape(-1, 3 * channels),
        preferred_element_type=jnp.float32,
    )
    grad_normed_grid = matmul_last(grad_packed, w_qkv.T).astype(jnp.bfloat16)
    grad_normed = from_grid(from_groups(grad_normed_grid, row_count, col_count))
    block_out = (mixed_float + matmul_last(attended_map, w_out)).astype(jnp.bfloat16)
    grad_out_proj = jnp.dot(
        attended_map.reshape(-1, channels).T,
        out_cotangent.reshape(-1, channels),
        preferred_element_type=jnp.float32,
    )
    unused_second, norm_second_vjp = jax.vjp(norm_tokens, mixed_float, gain_second)
    grad_mixed_norm, grad_norm1 = norm_second_vjp(grad_normed.astype(jnp.float32))
    grad_mixed = out_cotangent.astype(jnp.float32) + grad_mixed_norm
    grad_mixed_b = grad_mixed.astype(jnp.bfloat16)
    grad_project = jnp.dot(
        gated_act.reshape(-1, gated_act.shape[-1]).T,
        grad_mixed_b.reshape(-1, channels),
        preferred_element_type=jnp.float32,
    )
    grad_gated = matmul_last(grad_mixed_b, w_project.T)
    grad_gate = sum_everywhere(jnp.sum(grad_gated * activated, axis=(0, 1)))
    unused_gate, gate_vjp = jax.vjp(excite_gate, pooled, squeeze_wide, excite_wide)
    grad_pooled, grad_squeeze, grad_excite = gate_vjp(grad_gate)
    grad_activated = grad_gated * channel_gate + grad_pooled / cells_total
    unused_act, gelu_depth_vjp = jax.vjp(smooth_gelu, depth_pre)
    grad_depth_pre = gelu_depth_vjp(grad_activated)[0].astype(jnp.bfloat16)
    grad_pad = with_halo(grad_depth_pre, (("row", 0), ("col", 1)), 1)
    grad_spread = depthwise_back(grad_pad, w_depth, row_count, col_count)
    grad_depth = kernel_grad(padded, grad_depth_pre, row_count, col_count)
    unused_spread, gelu_expand_vjp = jax.vjp(smooth_gelu, expanded)
    grad_expanded = gelu_expand_vjp(grad_spread)[0].astype(jnp.bfloat16)
    grad_expand = jnp.dot(
        normed_first.reshape(-1, channels).T,
        grad_expanded.reshape(-1, grad_expanded.shape[-1]),
        preferred_element_type=jnp.float32,
    )
    grad_first = matmul_last(grad_expanded, w_expand.T)
    unused_first, norm_first_vjp = jax.vjp(norm_tokens, image_float, gain_first)
    grad_image_norm, grad_norm0 = norm_first_vjp(grad_first)
    grad_image = (grad_mixed + grad_image_norm).astype(jnp.bfloat16)
    early = sum_shares(
        jnp.concatenate(
            [
                grad_qkv.reshape(-1, 1024),
                grad_out_proj.reshape(-1, 1024),
                grad_bias.reshape(-1, 1024),
                grad_project.reshape(-1, 1024),
                jnp.pad(grad_norm1, (0, 1024 - channels))[None],
            ]
        )
    )
    late = sum_shares(
        jnp.concatenate(
            [
                grad_expand,
                grad_depth.reshape(9, -1),
                jnp.pad(grad_norm0, (0, 1024 - channels))[None],
            ]
        )
    )
    return (
        block_out,
        grad_image,
        late[265, :channels],
        late[:256],
        late[256:265].reshape(grad_depth.shape),
        grad_squeeze,
        grad_excite,
        early[288:544].reshape(grad_project.shape),
        early[544, :channels],
        early[:192].reshape(grad_qkv.shape),
        early[192:256].reshape(grad_out_proj.shape),
        early[256:288].reshape(grad_bias.shape),
    )


def solution(mesh):
    placed = (
        P("row", "col", None),
        P("row", "col", None),
        P(),
        P(),
        P(),
        P(),
        P(),
        P(),
        P(),
        P(),
        P(),
        P(),
    )
    return jax.shard_map(
        on_device,
        mesh=mesh,
        in_specs=placed,
        out_specs=(
            P("row", "col", None),
            P("row", "col", None),
            P(),
            P(),
            P(),
            P(),
            P(),
            P(),
            P(),
            P(),
            P(),
            P(),
        ),
        check_vma=False,
    )
```

```python
import functools
import math

import jax
import jax.numpy as jnp
from jax import lax
from jax.experimental import pallas as pl
from jax.experimental.pallas import tpu as pltpu
from jax.sharding import PartitionSpec as P

GRID = 8
AXES = ("row", "col")
BLOCK = 256
LANES = 128
SIDE = 16
GELU_A = math.sqrt(2.0 / math.pi)
GELU_B = GELU_A * 0.044715
F32 = jnp.float32
BF16 = jnp.bfloat16
PARAMS = pltpu.CompilerParams(vmem_limit_bytes=56 * 1024 * 1024)


def dot(left, right, contract=((1,), (0,))):
    return lax.dot_general(left, right, (contract, ((), ())), preferred_element_type=F32)


def dot_exact(vector, right, contract):
    tall = jnp.broadcast_to(vector, (8, vector.shape[1]))
    product = lax.dot_general(
        tall, right, (contract, ((), ())), precision=lax.Precision.HIGHEST, preferred_element_type=F32
    )
    return product[0:1]


def gelu_and_slope(x, with_slope=True):
    square = x * x
    t = jnp.tanh(x * (GELU_A + GELU_B * square))
    half = 0.5 + 0.5 * t
    value = x * half
    if not with_slope:
        return value, None
    slope = half + (value * (1.0 - t)) * (GELU_A + (3.0 * GELU_B) * square)
    return value, slope


def norm_rows(x):
    average = jnp.mean(x, axis=-1, keepdims=True)
    centered = x - average
    variance = jnp.mean(centered * centered, axis=-1, keepdims=True)
    rstd = lax.rsqrt(variance + 1e-05)
    return centered * rstd, rstd


def norm_rows_back(unit, rstd, gain, grad):
    unit_grad = grad * gain
    first = jnp.mean(unit_grad, axis=-1, keepdims=True)
    second = jnp.mean(unit_grad * unit, axis=-1, keepdims=True)
    return rstd * (unit_grad - first - unit * second)


def fold_rows(x):
    return jnp.sum(x.reshape(x.shape[0] // 8, 8, x.shape[1]), axis=0)


def expand_kernel(
    rows, cols,
    flags_ref, image_ref, up_ref, down_ref, strip_ref, gain_ref, w_exp_ref, w_dep_ref,
    normed_ref, spread_ref, spread_slope_ref, act_ref, act_slope_ref, pool_ref,
    halo_ref, expanded_ref, wide_ref,
):
    wide = cols + SIDE

    @pl.when(pl.program_id(0) == 0)
    def _():
        gain = gain_ref[...]

        def put(row, values, at, size):
            unit, _ = norm_rows(values.astype(F32))
            low = (unit * gain).astype(BF16)
            halo_ref[pl.ds(pl.multiple_of(row * wide + at, 16), size), :] = low
            return low

        for r in range(2):
            put(r, up_ref[r], 0, cols)
            put(rows + 2 + r, down_ref[r], 0, cols)

        @pl.loop(0, rows)
        def _(r):
            low = put(r + 2, image_ref[r], 0, cols)
            normed_ref[pl.ds(pl.multiple_of(r * cols, 16), cols), :] = low

        @pl.loop(0, rows + 4)
        def _(r):
            put(r, strip_ref[r], cols, SIDE)

    chunk = (rows + 4) * wide // 4

    @pl.loop(0, 4)
    def _(c):
        at = pl.ds(pl.multiple_of(c * chunk, 16), chunk)
        expanded_ref[at, :] = dot(halo_ref[at, :], w_exp_ref[...])

    def gelu_row(r, inner):
        for h in range(BLOCK // LANES):
            lanes = slice(h * LANES, (h + 1) * LANES)
            x = expanded_ref[pl.ds(pl.multiple_of(r * wide, 16), wide), lanes]
            value, slope = gelu_and_slope(x, inner)
            low = value.astype(BF16)
            wide_ref[r, :, lanes] = low.astype(F32)
            if inner:
                spread_ref[r - 2, :, lanes] = low[:cols]
                spread_slope_ref[r - 2, :, lanes] = slope[:cols].astype(BF16)

    for r in (0, 1, rows + 2, rows + 3):
        gelu_row(r, False)

    @pl.loop(0, rows)
    def _(r):
        gelu_row(r + 2, True)

    place = lax.broadcasted_iota(jnp.int32, (wide, LANES), 0)
    column_mask = jnp.where(
        place == wide - 1, flags_ref[2], jnp.where(place == cols, flags_ref[3], 1.0)
    ).astype(F32)

    def conv_row(i, inner, keep, pools):
        new_pools = []
        for h in range(BLOCK // LANES):
            lanes = slice(h * LANES, (h + 1) * LANES)
            x = [wide_ref[i + a, :, lanes] for a in range(3)]
            u = []
            for b in range(3):
                w = [w_dep_ref[a * 3 + b : a * 3 + b + 1, lanes] for a in range(3)]
                u.append(x[0] * w[0] + x[1] * w[1] + x[2] * w[2])
            pre = pltpu.roll(u[0], 1, 0) + u[1] + pltpu.roll(u[2], wide - 1, 0)
            value, slope = gelu_and_slope(pre)
            slope = slope * column_mask
            if keep is not None:
                slope = slope * keep
            act_slope_ref[i, :, lanes] = slope.astype(BF16)
            if inner:
                act_ref[i - 1, :, lanes] = value[:cols].astype(BF16)
                new_pools.append(pools[h] + fold_rows(value[:cols]))
        return tuple(new_pools)

    conv_row(0, False, flags_ref[0], None)
    conv_row(rows + 1, False, flags_ref[1], None)
    zero = jnp.zeros((8, LANES), F32)
    pools = lax.fori_loop(
        0, rows, lambda i, c: conv_row(i + 1, True, None, c), (zero,) * (BLOCK // LANES)
    )
    for h in range(BLOCK // LANES):
        pool_ref[:, h * LANES : (h + 1) * LANES] = jnp.sum(pools[h], axis=0, keepdims=True)


def whole(shape):
    return pl.BlockSpec(shape, lambda e: (0,) * len(shape))


def last_block(shape):
    lead = (0,) * (len(shape) - 1)
    return pl.BlockSpec(shape[:-1] + (BLOCK,), lambda e: lead + (e,))


def run_expand(flags, image, up, down, strip, gain, w_expand, w_depth9):
    rows, cols, channels = image.shape
    expanded = w_expand.shape[1]
    wide = cols + SIDE
    return pl.pallas_call(
        functools.partial(expand_kernel, rows, cols),
        grid=(expanded // BLOCK,),
        in_specs=[
            pl.BlockSpec(memory_space=pltpu.SMEM),
            whole(image.shape), whole(up.shape), whole(down.shape), whole(strip.shape),
            whole(gain.shape), last_block(w_expand.shape), last_block(w_depth9.shape),
        ],
        out_specs=[
            whole((rows * cols, channels)),
            last_block((rows, cols, expanded)), last_block((rows, cols, expanded)),
            last_block((rows, cols, expanded)), last_block((rows + 2, wide, expanded)),
            last_block((1, expanded)),
        ],
        out_shape=[
            jax.ShapeDtypeStruct((rows * cols, channels), BF16),
            jax.ShapeDtypeStruct((rows, cols, expanded), BF16),
            jax.ShapeDtypeStruct((rows, cols, expanded), BF16),
            jax.ShapeDtypeStruct((rows, cols, expanded), BF16),
            jax.ShapeDtypeStruct((rows + 2, wide, expanded), BF16),
            jax.ShapeDtypeStruct((1, expanded), F32),
        ],
        scratch_shapes=[
            pltpu.VMEM(((rows + 4) * wide, channels), BF16),
            pltpu.VMEM(((rows + 4) * wide, BLOCK), F32),
            pltpu.VMEM((rows + 4, wide, BLOCK), F32),
        ],
        compiler_params=PARAMS,
        name="expand",
    )(flags, image, up, down, strip, gain, w_expand, w_depth9)


def mix_kernel(
    cells_total, stride, bands,
    parts_ref, w_sq_ref, w_ex_ref, act_ref, image_ref, w_proj_ref, gain_ref,
    pooled_ref, hidden_ref, gate_ref, mixed_ref, send_ref,
):
    step = pl.program_id(0)

    @pl.when(step == 0)
    def _():
        pooled = jnp.sum(parts_ref[...], axis=0, keepdims=True) / cells_total
        hidden = dot_exact(pooled, w_sq_ref[...].astype(F32), ((1,), (0,)))
        silu = hidden * jax.nn.sigmoid(hidden)
        pooled_ref[...] = pooled
        hidden_ref[...] = hidden
        gate_ref[...] = jax.nn.sigmoid(dot_exact(silu, w_ex_ref[...].astype(F32), ((1,), (0,))))

    lines, cols, channels = image_ref.shape
    flat = act_ref[...].reshape(lines * cols, act_ref.shape[2])
    gated = (flat.astype(F32) * gate_ref[...]).astype(BF16)
    product = dot(gated, w_proj_ref[...])
    mixed = (image_ref[...].reshape(lines * cols, channels).astype(F32) + product).astype(BF16)
    mixed_ref[...] = mixed.reshape(lines, cols, channels)
    unit, _ = norm_rows(mixed.astype(F32))
    normed = (unit * gain_ref[...]).astype(BF16)
    for k in range(lines):
        line = step * lines + k
        for band in range(bands):
            start = k * cols + band * SIDE
            send_ref[lax.rem(line, stride) * bands + band, line // stride] = normed[
                start : start + SIDE
            ]


def run_mix(cells_total, stride, parts, w_squeeze, w_excite, act, image, w_project, gain):
    rows, cols, channels = image.shape
    expanded = act.shape[2]
    lines = 4
    bands = cols // SIDE
    block = lambda width: pl.BlockSpec((lines, cols, width), lambda r: (r, 0, 0))
    send = (stride * bands, rows // stride, SIDE, channels)
    return pl.pallas_call(
        functools.partial(mix_kernel, cells_total, stride, bands),
        grid=(rows // lines,),
        in_specs=[
            whole(parts.shape), whole(w_squeeze.shape), whole(w_excite.shape),
            block(expanded), block(channels), whole(w_project.shape), whole(gain.shape),
        ],
        out_specs=[
            whole((1, expanded)), whole((1, w_squeeze.shape[1])), whole((1, expanded)),
            block(channels), whole(send),
        ],
        out_shape=[
            jax.ShapeDtypeStruct((1, expanded), F32),
            jax.ShapeDtypeStruct((1, w_squeeze.shape[1]), F32),
            jax.ShapeDtypeStruct((1, expanded), F32),
            jax.ShapeDtypeStruct(image.shape, BF16),
            jax.ShapeDtypeStruct(send, BF16),
        ],
        compiler_params=PARAMS,
        name="mix",
    )(parts, w_squeeze, w_excite, act, image, w_project, gain)


def attention_kernel(
    members, heads,
    x_ref, cot_ref, w_qkv_ref, w_out_ref, bias_ref,
    att_ref, grad_ref, weights_ref,
    packed_ref, att_grad_ref, packed_grad_ref, bias_sum_ref,
):
    cells, channels = x_ref.shape
    dim = channels // heads
    per_half = LANES // dim
    scale = dim ** (-0.5)
    packed_ref[...] = dot(x_ref[...], w_qkv_ref[...]).astype(BF16)
    att_grad_ref[...] = dot(cot_ref[...], w_out_ref[...], ((1,), (1,))).astype(BF16)
    bias_sum_ref[...] = jnp.zeros(bias_sum_ref.shape, F32)
    tall = per_half * members
    head_mask = (
        lax.broadcasted_iota(jnp.int32, (tall, LANES), 0) // members
        == lax.broadcasted_iota(jnp.int32, (tall, LANES), 1) // dim
    )
    mask_low = head_mask.astype(F32).astype(BF16)
    mask_wide = head_mask.astype(F32)

    def spread_heads(v):
        return jnp.concatenate([v] * per_half, axis=0) * mask_low

    def collect_heads(v):
        picked = (v * mask_wide).reshape(per_half, members, LANES)
        return jnp.sum(picked, axis=0)

    def group(g, carry):
        at = pl.ds(pl.multiple_of(g * members, 16), members)
        for half in range(channels // LANES):
            lanes = slice(half * LANES, (half + 1) * LANES)
            take = lambda part: packed_ref[
                at, part * channels + half * LANES : part * channels + (half + 1) * LANES
            ]
            q, k, v = take(0), take(1), take(2)
            cot = att_grad_ref[at, lanes]
            q_tall = spread_heads(q)
            cot_tall = spread_heads(cot)
            scores = dot(q_tall, k, ((1,), (1,))) * scale + bias_ref[half]
            lifted = jnp.exp(scores - jnp.max(scores, axis=-1, keepdims=True))
            soft = lifted / jnp.sum(lifted, axis=-1, keepdims=True)
            soft_low = soft.astype(BF16)
            att_ref[at, lanes] = collect_heads(dot(soft_low, v)).astype(BF16)
            grad_probs = dot(cot_tall, v, ((1,), (1,)))
            grad_scores = soft * (
                grad_probs - jnp.sum(grad_probs * soft, axis=-1, keepdims=True)
            )
            bias_sum_ref[half] += grad_scores
            scaled = (grad_scores * scale).astype(BF16)
            grad_v = dot(soft_low, cot_tall, ((0,), (0,)))
            grad_q = collect_heads(dot(scaled, k))
            grad_k = dot(scaled, q_tall, ((0,), (0,)))
            for part, value in enumerate((grad_q, grad_k, grad_v)):
                packed_grad_ref[
                    at, part * channels + half * LANES : part * channels + (half + 1) * LANES
                ] = value.astype(BF16)
        return carry

    lax.fori_loop(0, cells // members, group, 0)
    grad_ref[...] = dot(packed_grad_ref[...], w_qkv_ref[...], ((1,), (1,))).astype(BF16)
    wide = 3 * channels
    weights_ref[:, :wide] = dot(x_ref[...], packed_grad_ref[...], ((0,), (0,))).astype(BF16)
    weights_ref[:, wide : wide + channels] = dot(att_ref[...], cot_ref[...], ((0,), (0,))).astype(BF16)
    weights_ref[:, wide + channels :] = jnp.concatenate(
        [bias_sum_ref[half] for half in range(channels // LANES)], axis=1
    ).astype(BF16)


def run_attention(x, cot, w_qkv, w_out, bias):
    cells, channels = x.shape
    heads, members, _ = bias.shape
    halves = channels // LANES
    bias_tall = bias.reshape(halves, heads // halves * members, members)
    width = 4 * channels + halves * members
    vmem = pl.BlockSpec(memory_space=pltpu.VMEM)
    return pl.pallas_call(
        functools.partial(attention_kernel, members, heads),
        in_specs=[vmem] * 5,
        out_specs=[vmem] * 3,
        out_shape=[
            jax.ShapeDtypeStruct((cells, channels), BF16),
            jax.ShapeDtypeStruct((cells, channels), BF16),
            jax.ShapeDtypeStruct((channels, width), BF16),
        ],
        scratch_shapes=[
            pltpu.VMEM((cells, 3 * channels), BF16),
            pltpu.VMEM((cells, channels), BF16),
            pltpu.VMEM((cells, 3 * channels), BF16),
            pltpu.VMEM(bias_tall.shape, F32),
        ],
        compiler_params=PARAMS,
        name="attention",
    )(x, cot, w_qkv, w_out, bias_tall)


def mixed_back_kernel(
    stride, bands,
    recv_ref, mixed_ref, cot_ref, gain_ref, act_ref, gate_ref, w_projt_ref,
    grad_ref, low_ref, norm_ref, project_ref, gate_grad_ref,
    turned_ref,
):
    rows, cols, channels = mixed_ref.shape

    @pl.when(pl.program_id(0) == 0)
    def _():
        gain = gain_ref[...]

        def one_row(i, total):
            a, p = lax.rem(i, stride), i // stride
            grad = jnp.concatenate(
                [recv_ref[a * bands + band, p] for band in range(bands)], axis=0
            ).astype(F32)
            unit, rstd = norm_rows(mixed_ref[i].astype(F32))
            back = cot_ref[i].astype(F32) + norm_rows_back(unit, rstd, gain, grad)
            grad_ref[i] = back
            low_ref[i] = back.astype(BF16)
            return total + fold_rows(grad * unit)

        total = lax.fori_loop(0, rows, one_row, jnp.zeros((8, channels), F32))
        norm_ref[...] = jnp.sum(total, axis=0, keepdims=True)
        turned_ref[...] = low_ref[...].reshape(rows * cols, channels).T

    flat = act_ref[...].reshape(rows * cols, BLOCK)
    product = dot(turned_ref[...], flat)
    gate_grad_ref[...] = jnp.sum(product * w_projt_ref[...].astype(F32), axis=0, keepdims=True)
    project_ref[...] = (product * gate_ref[...]).T.astype(BF16)


def run_mixed_back(stride, recv, mixed, cot, gain, act, gate, w_project_t):
    rows, cols, channels = mixed.shape
    expanded = act.shape[2]
    return pl.pallas_call(
        functools.partial(mixed_back_kernel, stride, cols // SIDE),
        grid=(expanded // BLOCK,),
        in_specs=[
            whole(recv.shape), whole(mixed.shape), whole(cot.shape), whole(gain.shape),
            last_block(act.shape), last_block(gate.shape), last_block(w_project_t.shape),
        ],
        out_specs=[
            whole(mixed.shape), whole(mixed.shape), whole((1, channels)),
            last_block((BLOCK, expanded)), last_block((1, expanded)),
        ],
        out_shape=[
            jax.ShapeDtypeStruct(mixed.shape, F32),
            jax.ShapeDtypeStruct(mixed.shape, BF16),
            jax.ShapeDtypeStruct((1, channels), F32),
            jax.ShapeDtypeStruct((BLOCK, expanded), BF16),
            jax.ShapeDtypeStruct((1, expanded), F32),
        ],
        scratch_shapes=[pltpu.VMEM((channels, rows * cols), BF16)],
        compiler_params=PARAMS,
        name="mixed_back",
    )(recv, mixed, cot, gain, act, gate, w_project_t)


def expand_back_kernel(
    cells_total,
    parts_ref, hidden_ref, gate_all_ref, w_sq_ref, w_ex_ref,
    low_ref, up_ref, down_ref, strip_ref, w_projt_ref, gate_ref, act_slope_ref,
    spread_slope_ref, spread_ref, w_dep_ref, normed_ref, w_exp_ref,
    expand_ref, depth_ref, first_ref, logit_ref, pre_ref,
    halo_ref, gated_ref, window_ref, expanded_ref, pool_ref, turned_ref,
):
    rows, cols, channels = low_ref.shape
    wide = cols + SIDE
    step = pl.program_id(0)

    @pl.when(step == 0)
    def _():
        gate = gate_all_ref[...]
        gate_grad = jnp.sum(parts_ref[...], axis=0, keepdims=True)
        logit = gate_grad * gate * (1.0 - gate)
        hidden = hidden_ref[...]
        sig = jax.nn.sigmoid(hidden)
        pre = dot_exact(logit, w_ex_ref[...].astype(F32), ((1,), (1,))) * (
            sig + hidden * sig * (1.0 - sig)
        )
        logit_ref[...] = logit
        pre_ref[...] = pre
        pooled = dot_exact(pre, w_sq_ref[...].astype(F32), ((1,), (1,))) / cells_total
        for e in range(pool_ref.shape[0]):
            pool_ref[e] = pooled[:, e * BLOCK : (e + 1) * BLOCK]
        halo_ref[pl.ds(0, cols), :] = up_ref[0]
        halo_ref[pl.ds((rows + 1) * wide, cols), :] = down_ref[0]

        @pl.loop(0, rows)
        def _(r):
            halo_ref[pl.ds(pl.multiple_of((r + 1) * wide, 16), cols), :] = low_ref[r]

        @pl.loop(0, rows + 2)
        def _(r):
            halo_ref[pl.ds(pl.multiple_of(r * wide + cols, 16), SIDE), :] = strip_ref[r]

        turned_ref[...] = normed_ref[...].T
        first_ref[...] = jnp.zeros(first_ref.shape, F32)

    chunk = (rows + 2) * wide // 3

    @pl.loop(0, 3)
    def _(c):
        at = pl.ds(pl.multiple_of(c * chunk, 16), chunk)
        gated_ref[at, :] = dot(halo_ref[at, :], w_projt_ref[...])

    @pl.loop(0, rows + 2)
    def _(i):
        for h in range(BLOCK // LANES):
            lanes = slice(h * LANES, (h + 1) * LANES)
            gated = gated_ref[pl.ds(pl.multiple_of(i * wide, 16), wide), lanes]
            pooled = pool_ref[step][:, lanes]
            grad = (gated * gate_ref[:, lanes] + pooled) * act_slope_ref[i, :, lanes].astype(F32)
            grad = grad.astype(BF16).astype(F32)
            window_ref[0, i, :, lanes] = pltpu.roll(grad, wide - 1, 0)[:cols]
            window_ref[1, i, :, lanes] = grad[:cols]
            window_ref[2, i, :, lanes] = pltpu.roll(grad, 1, 0)[:cols]

    for h in range(BLOCK // LANES):
        lanes = slice(h * LANES, (h + 1) * LANES)

        def back_row(i, sums):
            spread = spread_ref[i, :, lanes].astype(F32)
            total = jnp.zeros((cols, LANES), F32)
            new_sums = []
            for a in range(3):
                for b in range(3):
                    window = window_ref[b, i + 2 - a, :, lanes]
                    total = total + window * w_dep_ref[a * 3 + b : a * 3 + b + 1, lanes]
                    new_sums.append(sums[a * 3 + b] + fold_rows(window * spread))
            grad = total * spread_slope_ref[i, :, lanes].astype(F32)
            expanded_ref[pl.ds(pl.multiple_of(i * cols, 16), cols), lanes] = grad.astype(BF16)
            return tuple(new_sums)

        sums = lax.fori_loop(0, rows, back_row, (jnp.zeros((8, LANES), F32),) * 9)
        for t in range(9):
            depth_ref[t : t + 1, lanes] = jnp.sum(sums[t], axis=0, keepdims=True)

    grad_expanded = expanded_ref[...]
    expand_ref[...] = dot(turned_ref[...], grad_expanded).astype(BF16)
    first_ref[...] += dot(grad_expanded, w_exp_ref[...], ((1,), (1,)))


def run_expand_back(
    cells_total, parts, hidden, gate, w_squeeze, w_excite, low, up, down, strip,
    w_project_t, act_slope, spread_slope, spread, w_depth9, normed, w_expand,
):
    rows, cols, channels = low.shape
    expanded = w_expand.shape[1]
    wide = cols + SIDE
    return pl.pallas_call(
        functools.partial(expand_back_kernel, cells_total),
        grid=(expanded // BLOCK,),
        in_specs=[
            whole(parts.shape), whole(hidden.shape), whole(gate.shape),
            whole(w_squeeze.shape), whole(w_excite.shape),
            whole(low.shape), whole(up.shape), whole(down.shape), whole(strip.shape),
            last_block(w_project_t.shape), last_block(gate.shape), last_block(act_slope.shape),
            last_block(spread_slope.shape), last_block(spread.shape), last_block(w_depth9.shape),
            whole(normed.shape), last_block(w_expand.shape),
        ],
        out_specs=[
            last_block((channels, expanded)), last_block((9, expanded)),
            whole((rows * cols, channels)), whole((1, expanded)), whole(hidden.shape),
        ],
        out_shape=[
            jax.ShapeDtypeStruct((channels, expanded), BF16),
            jax.ShapeDtypeStruct((9, expanded), F32),
            jax.ShapeDtypeStruct((rows * cols, channels), F32),
            jax.ShapeDtypeStruct((1, expanded), F32),
            jax.ShapeDtypeStruct(hidden.shape, F32),
        ],
        scratch_shapes=[
            pltpu.VMEM(((rows + 2) * wide, channels), BF16),
            pltpu.VMEM(((rows + 2) * wide, BLOCK), F32),
            pltpu.VMEM((3, rows + 2, cols, BLOCK), F32),
            pltpu.VMEM((rows * cols, BLOCK), BF16),
            pltpu.VMEM((expanded // BLOCK, 1, BLOCK), F32),
            pltpu.VMEM((channels, rows * cols), BF16),
        ],
        compiler_params=PARAMS,
        name="expand_back",
    )(
        parts, hidden, gate, w_squeeze, w_excite, low, up, down, strip, w_project_t, gate,
        act_slope, spread_slope, spread, w_depth9, normed, w_expand,
    )


def image_back_kernel(image_ref, gain_ref, first_ref, mixed_ref, out_ref, norm_ref):
    @pl.when(pl.program_id(0) == 0)
    def _():
        norm_ref[...] = jnp.zeros(norm_ref.shape, F32)

    unit, rstd = norm_rows(image_ref[...].astype(F32))
    grad = first_ref[...]
    back = mixed_ref[...] + norm_rows_back(unit, rstd, gain_ref[...], grad)
    out_ref[...] = back.astype(BF16)
    norm_ref[...] += jnp.sum(grad * unit, axis=0, keepdims=True)


def run_image_back(image, gain, first, mixed):
    cells, channels = image.shape
    block = pl.BlockSpec((cells // 4, channels), lambda r: (r, 0))
    return pl.pallas_call(
        image_back_kernel,
        grid=(4,),
        in_specs=[block, whole(gain.shape), block, block],
        out_specs=[block, whole((1, channels))],
        out_shape=[
            jax.ShapeDtypeStruct((cells, channels), BF16),
            jax.ShapeDtypeStruct((1, channels), F32),
        ],
        compiler_params=PARAMS,
        name="image_back",
    )(image, gain, first, mixed)


def shift(cells, axis, step):
    count = lax.axis_size(axis)
    pairs = [(i, i + step) for i in range(count) if 0 <= i + step < count]
    return lax.ppermute(cells, axis, pairs)


def halo(cells, width):
    rows, cols, channels = cells.shape
    up = shift(cells[rows - width :], "row", 1)
    down = shift(cells[:width], "row", -1)
    first = jnp.concatenate([up[:, :width], cells[:, :width], down[:, :width]], axis=0)
    last = jnp.concatenate(
        [up[:, cols - width :], cells[:, cols - width :], down[:, cols - width :]], axis=0
    )
    left = shift(last, "col", 1)
    right = shift(first, "col", -1)
    gap = jnp.zeros((rows + 2 * width, SIDE - 2 * width, channels), cells.dtype)
    return up, down, jnp.concatenate([right, gap, left], axis=1)


def sum_everywhere(vector):
    count = lax.axis_size("row") * lax.axis_size("col")
    sent = jnp.broadcast_to(vector, (count, vector.shape[-1]))
    return lax.all_to_all(sent, AXES, split_axis=0, concat_axis=0, tiled=True)


def sum_shares(matrix):
    rows, columns = matrix.shape
    over_row = lax.axis_size("row")
    over_col = lax.axis_size("col")
    part = rows // over_row
    share = part // over_col
    arrived = lax.all_to_all(
        matrix.reshape(over_row, part, columns), "row", split_axis=0, concat_axis=0, tiled=True
    )
    total = jnp.sum(arrived.astype(F32), axis=0).astype(BF16)
    arrived = lax.all_to_all(
        total.reshape(over_col, share, columns), "col", split_axis=0, concat_axis=0, tiled=True
    )
    total = jnp.sum(arrived.astype(F32), axis=0).astype(BF16)
    sent = jnp.broadcast_to(total[None], (over_col, share, columns))
    gathered = lax.all_to_all(sent, "col", split_axis=0, concat_axis=0, tiled=True)
    sent = jnp.broadcast_to(gathered.reshape(1, part, columns), (over_row, part, columns))
    gathered = lax.all_to_all(sent, "row", split_axis=0, concat_axis=0, tiled=True)
    return gathered.reshape(rows, columns)


def swap_groups(blocks, parity):
    groups = None
    if parity > 1:
        over_row = lax.axis_size("row")
        over_col = lax.axis_size("col")
        groups = [
            [r * over_col + c for r in range(over_row) for c in range(k, over_col, parity)]
            for k in range(parity)
        ]
    return lax.all_to_all(
        blocks, AXES, split_axis=0, concat_axis=0, tiled=True, axis_index_groups=groups
    )


def on_device(
    image, out_cotangent, norm0_gain, w_expand, w_depth, w_squeeze, w_excite, w_project,
    norm1_gain, w_qkv, w_out, attn_bias,
):
    rows, cols, channels = image.shape
    over_row = lax.axis_size("row")
    over_col = lax.axis_size("col")
    cells_total = rows * over_row * cols * over_col
    stride = rows * over_row // GRID
    parity = cols and (cols * over_col // GRID) // cols
    lines = rows // stride
    bands = cols // SIDE
    members = GRID * GRID
    expanded = w_expand.shape[1]

    def into_members(arrived):
        parted = arrived.reshape(over_row, GRID, lines, SIDE, channels)
        return parted.transpose(3, 0, 2, 1, 4).reshape(SIDE * members, channels)

    def out_of_members(values):
        parted = values.reshape(SIDE, over_row, lines, GRID, channels)
        return parted.transpose(1, 3, 2, 0, 4).reshape(-1, lines, SIDE, channels)

    row, col = lax.axis_index("row"), lax.axis_index("col")
    flags = jnp.stack([row > 0, row < over_row - 1, col > 0, col < over_col - 1]).astype(F32)
    gain_first = norm0_gain.astype(F32)[None]
    gain_second = norm1_gain.astype(F32)[None]
    w_depth9 = w_depth.astype(F32).reshape(9, expanded)
    w_project_t = w_project.T

    up, down, strip = halo(image, 2)
    normed_first, spread, spread_slope, act, act_slope, pool = run_expand(
        flags, image, up, down, strip, gain_first, w_expand, w_depth9
    )
    cot_sent = (
        out_cotangent.reshape(lines, stride, bands, SIDE, channels)
        .transpose(1, 2, 0, 3, 4)
        .reshape(stride * bands, lines, SIDE, channels)
    )
    cot_members = into_members(swap_groups(cot_sent, parity))
    pooled, hidden, gate, mixed, normed_sent = run_mix(
        cells_total, stride, sum_everywhere(pool), w_squeeze, w_excite, act, image, w_project,
        gain_second,
    )
    normed_members = into_members(swap_groups(normed_sent, parity))
    attended, grad_normed, weights_early = run_attention(
        normed_members, cot_members, w_qkv, w_out, attn_bias
    )
    grad_normed_home = swap_groups(out_of_members(grad_normed), parity)
    attended_home = swap_groups(out_of_members(attended), parity)

    grad_mixed, grad_low, grad_norm1, weights_project, gate_grad = run_mixed_back(
        stride, grad_normed_home, mixed, out_cotangent, gain_second, act, gate, w_project_t
    )
    parts = sum_everywhere(gate_grad)
    up, down, strip = halo(grad_low, 1)
    grad_expand, grad_depth, grad_first, logit, pre = run_expand_back(
        cells_total, parts, hidden, gate, w_squeeze, w_excite, grad_low, up, down, strip,
        w_project_t, act_slope, spread_slope, spread, w_depth9, normed_first, w_expand,
    )
    grad_image, grad_norm0 = run_image_back(
        image.reshape(-1, channels), gain_first, grad_first, grad_mixed.reshape(-1, channels)
    )
    attended_map = (
        attended_home.reshape(stride, bands, lines, SIDE, channels)
        .transpose(2, 0, 1, 3, 4)
        .reshape(rows * cols, channels)
    )
    block_out = (mixed.reshape(-1, channels).astype(F32) + dot(attended_map, w_out)).astype(BF16)

    silu = jax.nn.silu(hidden)
    grad_squeeze = pooled.reshape(expanded, 1) * pre
    grad_excite = silu.reshape(-1, 1) * logit

    early = sum_shares(weights_early)
    middle = sum_shares(weights_project)
    small = jnp.concatenate([grad_depth.reshape(-1), grad_norm0[0], grad_norm1[0]])
    small = jnp.pad(small, (0, channels * LANES - small.shape[0])).reshape(channels, LANES)
    late = sum_shares(jnp.concatenate([grad_expand, small.astype(BF16)], axis=1)).astype(F32)
    early = early.astype(F32)
    heads = attn_bias.shape[0]
    halves = channels // LANES
    per_half = heads // halves
    grad_bias = (
        early[:, 4 * channels :]
        .reshape(per_half, members, halves, members)
        .transpose(2, 0, 1, 3)
        .reshape(attn_bias.shape)
    )
    grad_project = (
        middle.reshape(BLOCK, expanded // BLOCK, channels).transpose(1, 0, 2).astype(F32)
    )
    tail = late[:, expanded:].reshape(-1)
    return (
        block_out.reshape(image.shape),
        grad_image.reshape(image.shape),
        tail[9 * expanded : 9 * expanded + channels],
        late[:, :expanded],
        tail[: 9 * expanded].reshape(w_depth.shape),
        grad_squeeze,
        grad_excite,
        grad_project.reshape(w_project.shape),
        tail[9 * expanded + channels : 9 * expanded + 2 * channels],
        early[:, : 3 * channels],
        early[:, 3 * channels : 4 * channels],
        grad_bias,
    )


def solution(mesh):
    cells = P("row", "col", None)
    return jax.shard_map(
        on_device,
        mesh=mesh,
        in_specs=(cells, cells) + (P(),) * 10,
        out_specs=(cells, cells) + (P(),) * 10,
        check_vma=False,
    )
```

```python
import functools
import math

import jax
import jax.numpy as jnp
from jax import lax
from jax.experimental import pallas as pl
from jax.experimental.pallas import tpu as pltpu
from jax.sharding import PartitionSpec as P

GRID = 8
AXES = ("row", "col")
BLOCK = 256
LANES = 128
SIDE = 16
GELU_A = math.sqrt(2.0 / math.pi)
GELU_B = GELU_A * 0.044715
F32 = jnp.float32
BF16 = jnp.bfloat16
PARAMS = pltpu.CompilerParams(vmem_limit_bytes=56 * 1024 * 1024)


def estimate(us):
    return pl.CostEstimate(flops=int(us * 1.1e9), bytes_accessed=int(us * 3.6e6), transcendentals=0)


def dot(left, right, contract=((1,), (0,))):
    return lax.dot_general(left, right, (contract, ((), ())), preferred_element_type=F32)


def dot_exact(vector, right, contract):
    tall = jnp.broadcast_to(vector, (8, vector.shape[1]))
    product = lax.dot_general(
        tall, right, (contract, ((), ())), precision=lax.Precision.HIGHEST, preferred_element_type=F32
    )
    return product[0:1]


def gelu_and_slope(x, with_slope=True):
    square = x * x
    t = jnp.tanh(x * (GELU_A + GELU_B * square))
    half = 0.5 + 0.5 * t
    value = x * half
    if not with_slope:
        return value, None
    slope = half + (value * (1.0 - t)) * (GELU_A + (3.0 * GELU_B) * square)
    return value, slope


def norm_rows(x):
    average = jnp.mean(x, axis=-1, keepdims=True)
    centered = x - average
    variance = jnp.mean(centered * centered, axis=-1, keepdims=True)
    rstd = lax.rsqrt(variance + 1e-05)
    return centered * rstd, rstd


def norm_rows_back(unit, rstd, gain, grad):
    unit_grad = grad * gain
    first = jnp.mean(unit_grad, axis=-1, keepdims=True)
    second = jnp.mean(unit_grad * unit, axis=-1, keepdims=True)
    return rstd * (unit_grad - first - unit * second)


def fold_rows(x):
    return jnp.sum(x.reshape(x.shape[0] // 8, 8, x.shape[1]), axis=0)


def whole(shape):
    return pl.BlockSpec(shape, lambda e: (0,) * len(shape))


def last_block(shape):
    lead = (0,) * (len(shape) - 1)
    return pl.BlockSpec(shape[:-1] + (BLOCK,), lambda e: lead + (e,))


def expand_kernel(
    image_ref, gain_ref, w_exp_ref,
    normed_ref, turned_ref, spread_ref, slope_ref,
    expanded_ref,
):
    rows, cols, channels = image_ref.shape

    @pl.when(pl.program_id(0) == 0)
    def _():
        gain = gain_ref[...].astype(F32)

        @pl.loop(0, rows // 4)
        def _(c):
            flat = image_ref[pl.ds(c * 4, 4)].reshape(4 * cols, channels)
            unit, _ = norm_rows(flat.astype(F32))
            at = pl.ds(pl.multiple_of(c * 4 * cols, 16), 4 * cols)
            normed_ref[at, :] = (unit * gain).astype(BF16)

        turned_ref[...] = normed_ref[...].T

    expanded_ref[...] = dot(normed_ref[...], w_exp_ref[...])

    @pl.loop(0, rows)
    def _(r):
        for h in range(BLOCK // LANES):
            lanes = slice(h * LANES, (h + 1) * LANES)
            x = expanded_ref[pl.ds(pl.multiple_of(r * cols, 16), cols), lanes]
            value, slope = gelu_and_slope(x)
            spread_ref[r, :, lanes] = value.astype(BF16)
            slope_ref[r, :, lanes] = slope.astype(BF16)


def run_expand(image, gain, w_expand):
    rows, cols, channels = image.shape
    expanded = w_expand.shape[1]
    return pl.pallas_call(
        expand_kernel,
        grid=(expanded // BLOCK,),
        in_specs=[whole(image.shape), whole(gain.shape), last_block(w_expand.shape)],
        out_specs=[
            whole((rows * cols, channels)), whole((channels, rows * cols)),
            last_block((rows, cols, expanded)), last_block((rows, cols, expanded)),
        ],
        out_shape=[
            jax.ShapeDtypeStruct((rows * cols, channels), BF16),
            jax.ShapeDtypeStruct((channels, rows * cols), BF16),
            jax.ShapeDtypeStruct((rows, cols, expanded), BF16),
            jax.ShapeDtypeStruct((rows, cols, expanded), BF16),
        ],
        scratch_shapes=[pltpu.VMEM((rows * cols, BLOCK), F32)],
        compiler_params=PARAMS,
        cost_estimate=estimate(9),
        name="expand",
    )(image, gain, w_expand)


def depthwise_kernel(
    up_ref, down_ref, side_ref, gain_ref, w_exp_ref, w_dep_ref, spread_ref,
    ring_ref, act_ref, pool_ref,
    ring_normed_ref, ring_wide_ref,
):
    rows, cols, _ = spread_ref.shape
    channels = up_ref.shape[2]
    over = 4 * cols
    side = 8

    @pl.when(pl.program_id(0) == 0)
    def _():
        gain = gain_ref[...].astype(F32)

        def put(at, values):
            unit, _ = norm_rows(values.astype(F32))
            ring_normed_ref[at : at + values.shape[0], :] = (unit * gain).astype(BF16)

        put(0, up_ref[...].reshape(2 * cols, channels))
        put(2 * cols, down_ref[...].reshape(2 * cols, channels))
        put(over, side_ref[...])

    ring_wide_ref[...] = dot(ring_normed_ref[...], w_exp_ref[...])
    tile = 32

    @pl.loop(0, ring_wide_ref.shape[0] // tile)
    def _(t):
        at = pl.ds(pl.multiple_of(t * tile, tile), tile)
        value, _ = gelu_and_slope(ring_wide_ref[at, :], False)
        low = value.astype(BF16)
        ring_ref[at, :] = low
        ring_wide_ref[at, :] = low.astype(F32)

    for h in range(BLOCK // LANES):
        lanes = slice(h * LANES, (h + 1) * LANES)
        taps = w_dep_ref[:, :, lanes].astype(F32)
        w = [[taps[a, b : b + 1] for b in range(3)] for a in range(3)]

        def line(r, main):
            at = pl.multiple_of(over + (r + 2) * side, side)
            return jnp.concatenate([main, ring_wide_ref[pl.ds(at, side), lanes]], axis=0)

        def conv(i, x, total):
            u = [x[0] * w[0][b] + x[1] * w[1][b] + x[2] * w[2][b] for b in range(3)]
            wide = cols + side
            pre = pltpu.roll(u[0], 1, 0) + u[1] + pltpu.roll(u[2], wide - 1, 0)
            value, _ = gelu_and_slope(pre[:cols], False)
            act_ref[i, :, lanes] = value.astype(BF16)
            return total + fold_rows(value)

        def step(i, carry):
            first, second, total = carry
            third = line(i + 1, spread_ref[i + 1, :, lanes].astype(F32))
            return second, third, conv(i, (first, second, third), total)

        carry = (
            line(-1, ring_wide_ref[cols : 2 * cols, lanes]),
            line(0, spread_ref[0, :, lanes].astype(F32)),
            jnp.zeros((8, LANES), F32),
        )
        first, second, total = lax.fori_loop(0, rows - 1, step, carry)
        third = line(rows, ring_wide_ref[2 * cols : 3 * cols, lanes])
        total = conv(rows - 1, (first, second, third), total)
        total = jnp.sum(total, axis=0, keepdims=True)
        pool_ref[:, :, lanes] = jnp.broadcast_to(total[None], (pool_ref.shape[0], 1, LANES))


def run_depthwise(count, up, down, side, gain, w_expand, w_depth, spread):
    rows, cols, expanded = spread.shape
    channels = up.shape[2]
    ring = 4 * cols + 8 * (rows + 4)
    return pl.pallas_call(
        depthwise_kernel,
        grid=(expanded // BLOCK,),
        in_specs=[
            whole(up.shape), whole(down.shape), whole(side.shape), whole(gain.shape),
            last_block(w_expand.shape), last_block(w_depth.shape), last_block(spread.shape),
        ],
        out_specs=[
            last_block((ring, expanded)), last_block(spread.shape), last_block((count, 1, expanded)),
        ],
        out_shape=[
            jax.ShapeDtypeStruct((ring, expanded), BF16),
            jax.ShapeDtypeStruct(spread.shape, BF16),
            jax.ShapeDtypeStruct((count, 1, expanded), F32),
        ],
        scratch_shapes=[pltpu.VMEM((ring, channels), BF16), pltpu.VMEM((ring, BLOCK), F32)],
        compiler_params=PARAMS,
        cost_estimate=estimate(9),
        name="depthwise",
    )(up, down, side, gain, w_expand, w_depth, spread)


def slope_kernel(flags_ref, ring_ref, w_dep_ref, spread_ref, main_ref, side_out_ref, wide_ref):
    rows, cols, _ = spread_ref.shape
    over = 4 * cols
    side = 8
    wide = cols + side

    for k, r in enumerate((0, 1, rows + 2, rows + 3)):
        wide_ref[r, :cols, :] = ring_ref[k * cols : (k + 1) * cols, :].astype(F32)
    sides = ring_ref[over:, :].astype(F32)
    for r in range(rows + 4):
        wide_ref[r, cols:, :] = sides[r * side : (r + 1) * side]

    @pl.loop(0, rows)
    def _(r):
        wide_ref[r + 2, :cols, :] = spread_ref[r].astype(F32)

    place = lax.broadcasted_iota(jnp.int32, (side, LANES), 0)
    side_mask = jnp.where(
        place == side - 1, flags_ref[2], jnp.where(place == 0, flags_ref[3], 1.0)
    ).astype(F32)

    @pl.loop(0, rows + 2)
    def _(i):
        keep = jnp.where(i == 0, flags_ref[0], jnp.where(i == rows + 1, flags_ref[1], 1.0))
        for h in range(BLOCK // LANES):
            lanes = slice(h * LANES, (h + 1) * LANES)
            taps = w_dep_ref[:, :, lanes].astype(F32)
            x = [wide_ref[i + a, :, lanes] for a in range(3)]
            u = [sum(x[a] * taps[a, b : b + 1] for a in range(3)) for b in range(3)]
            pre = pltpu.roll(u[0], 1, 0) + u[1] + pltpu.roll(u[2], wide - 1, 0)
            _, slope = gelu_and_slope(pre)
            slope = slope * keep
            main_ref[i, :, lanes] = slope[:cols].astype(BF16)
            side_out_ref[i, :, lanes] = slope[cols:] * side_mask


def run_slope(flags, ring, w_depth, spread):
    rows, cols, expanded = spread.shape
    return pl.pallas_call(
        slope_kernel,
        grid=(expanded // BLOCK,),
        in_specs=[
            pl.BlockSpec(memory_space=pltpu.SMEM),
            last_block(ring.shape), last_block(w_depth.shape), last_block(spread.shape),
        ],
        out_specs=[last_block((rows + 2, cols, expanded)), last_block((rows + 2, 8, expanded))],
        out_shape=[
            jax.ShapeDtypeStruct((rows + 2, cols, expanded), BF16),
            jax.ShapeDtypeStruct((rows + 2, 8, expanded), F32),
        ],
        scratch_shapes=[pltpu.VMEM((rows + 4, cols + 8, BLOCK), F32)],
        compiler_params=PARAMS,
        cost_estimate=estimate(13),
        name="slope",
    )(flags, ring, w_depth, spread)


def mix_kernel(
    cells_total, stride, bands,
    parts_ref, w_sq_ref, w_ex_ref, act_ref, image_ref, w_proj_ref, gain_ref, after_ref,
    pooled_ref, hidden_ref, gate_ref, mixed_ref, send_ref,
):
    step = pl.program_id(0)

    @pl.when(step == 0)
    def _():
        pooled = jnp.sum(parts_ref[...], axis=0) / cells_total
        hidden = dot_exact(pooled, w_sq_ref[...].astype(F32), ((1,), (0,)))
        silu = hidden * jax.nn.sigmoid(hidden)
        pooled_ref[...] = pooled
        hidden_ref[...] = hidden
        gate_ref[...] = jax.nn.sigmoid(dot_exact(silu, w_ex_ref[...].astype(F32), ((1,), (0,))))

    lines, cols, channels = image_ref.shape
    flat = act_ref[...].reshape(lines * cols, act_ref.shape[2])
    gated = (flat.astype(F32) * gate_ref[...]).astype(BF16)
    product = dot(gated, w_proj_ref[...])
    mixed = (image_ref[...].reshape(lines * cols, channels).astype(F32) + product).astype(BF16)
    mixed_ref[...] = mixed.reshape(lines, cols, channels)
    unit, _ = norm_rows(mixed.astype(F32))
    normed = (unit * gain_ref[...].astype(F32)).astype(BF16)
    for k in range(lines):
        line = step * lines + k
        for band in range(bands):
            start = k * cols + band * SIDE
            send_ref[lax.rem(line, stride) * bands + band, line // stride] = normed[
                start : start + SIDE
            ]


def run_mix(cells_total, stride, parts, w_squeeze, w_excite, act, image, w_project, gain, after):
    rows, cols, channels = image.shape
    expanded = act.shape[2]
    lines = 4
    bands = cols // SIDE
    block = lambda width: pl.BlockSpec((lines, cols, width), lambda r: (r, 0, 0))
    send = (stride * bands, rows // stride, SIDE, channels)
    return pl.pallas_call(
        functools.partial(mix_kernel, cells_total, stride, bands),
        grid=(rows // lines,),
        in_specs=[
            whole(parts.shape), whole(w_squeeze.shape), whole(w_excite.shape),
            block(expanded), block(channels), whole(w_project.shape), whole(gain.shape),
            pl.BlockSpec(memory_space=pl.ANY),
        ],
        out_specs=[
            whole((1, expanded)), whole((1, w_squeeze.shape[1])), whole((1, expanded)),
            block(channels), whole(send),
        ],
        out_shape=[
            jax.ShapeDtypeStruct((1, expanded), F32),
            jax.ShapeDtypeStruct((1, w_squeeze.shape[1]), F32),
            jax.ShapeDtypeStruct((1, expanded), F32),
            jax.ShapeDtypeStruct(image.shape, BF16),
            jax.ShapeDtypeStruct(send, BF16),
        ],
        compiler_params=PARAMS,
        cost_estimate=estimate(5),
        name="mix",
    )(parts, w_squeeze, w_excite, act, image, w_project, gain, after)


def attention_kernel(
    members, heads,
    x_ref, cot_ref, w_qkv_ref, w_out_ref, bias_ref,
    att_ref, grad_ref, packed_grad_ref, bias_out_ref,
    packed_ref, att_grad_ref, bias_sum_ref,
):
    cells, channels = x_ref.shape
    dim = channels // heads
    per_half = LANES // dim
    halves = channels // LANES
    scale = dim ** (-0.5)
    packed_ref[...] = dot(x_ref[...], w_qkv_ref[...]).astype(BF16)
    att_grad_ref[...] = dot(cot_ref[...], w_out_ref[...], ((1,), (1,))).astype(BF16)
    bias_sum_ref[...] = jnp.zeros(bias_sum_ref.shape, F32)
    tall = per_half * members
    mask = (
        lax.broadcasted_iota(jnp.int32, (tall, LANES), 0) // members
        == lax.broadcasted_iota(jnp.int32, (tall, LANES), 1) // dim
    ).astype(F32).astype(BF16)
    owner = lax.broadcasted_iota(jnp.int32, (members, 2 * LANES), 1) % LANES // dim
    zero = jnp.zeros((members, LANES), BF16)

    def by_head(pair):
        return jnp.concatenate(
            [jnp.concatenate([v] * per_half, axis=0) * mask for v in pair], axis=1
        )

    def diagonal(pair):
        return jnp.concatenate(
            [
                jnp.concatenate([pair[0], zero], axis=1),
                jnp.concatenate([zero, pair[1]], axis=1),
            ],
            axis=0,
        )

    def collect(v):
        parts = [v[h * members : (h + 1) * members] for h in range(per_half)]
        picked = parts[-1]
        for h in range(per_half - 1):
            picked = jnp.where(owner == h, parts[h], picked)
        return [picked[:, :LANES], picked[:, LANES:]]

    def blocks(v):
        return [v[:members, :LANES], v[members:, LANES:]]

    def over_members(v, reduce):
        parted = v.reshape(per_half, members, 2 * members)
        small = reduce(parted, axis=1, keepdims=True)
        return jnp.broadcast_to(small, parted.shape).reshape(v.shape)

    def pair_step(g, carry):
        at = [pl.ds(pl.multiple_of((2 * g + k) * members, 16), members) for k in range(2)]
        for half in range(halves):
            def lanes(part):
                start = part * channels + half * LANES
                return slice(start, start + LANES)

            q, k, v = ([packed_ref[at[n], lanes(part)] for n in range(2)] for part in range(3))
            cot = [att_grad_ref[at[n], lanes(0)] for n in range(2)]
            q_diag, cot_diag = diagonal(q), diagonal(cot)
            k_tall, v_tall = by_head(k), by_head(v)
            scores = dot(k_tall, q_diag, ((1,), (1,))) * scale + bias_ref[half]
            grad_probs = dot(v_tall, cot_diag, ((1,), (1,)))
            lifted = jnp.exp(scores - over_members(scores, jnp.max))
            soft = lifted * (1.0 / over_members(lifted, jnp.sum))
            soft_low = soft.astype(BF16)
            grad_scores = soft * (grad_probs - over_members(grad_probs * soft, jnp.sum))
            bias_sum_ref[half] += grad_scores
            scaled = (grad_scores * scale).astype(BF16)
            attended = blocks(dot(soft_low, v_tall, ((0,), (0,))))
            grad_q = blocks(dot(scaled, k_tall, ((0,), (0,))))
            grad_v = collect(dot(soft_low, cot_diag))
            grad_k = collect(dot(scaled, q_diag))
            for n in range(2):
                att_ref[at[n], lanes(0)] = attended[n].astype(BF16)
                for part, value in enumerate((grad_q, grad_k, grad_v)):
                    packed_grad_ref[at[n], lanes(part)] = value[n].astype(BF16)
        return carry

    lax.fori_loop(0, cells // members // 2, pair_step, 0)
    grad_ref[...] = dot(packed_grad_ref[...], w_qkv_ref[...], ((1,), (1,))).astype(BF16)
    for half in range(halves):
        both = bias_sum_ref[half]
        bias_out_ref[half] = both[:, :members] + both[:, members:]


def run_attention(x, cot, w_qkv, w_out, bias_tall, heads):
    cells, channels = x.shape
    halves, tall, members2 = bias_tall.shape
    members = members2 // 2
    vmem = pl.BlockSpec(memory_space=pltpu.VMEM)
    return pl.pallas_call(
        functools.partial(attention_kernel, members, heads),
        in_specs=[vmem] * 5,
        out_specs=[vmem] * 4,
        out_shape=[
            jax.ShapeDtypeStruct((cells, channels), BF16),
            jax.ShapeDtypeStruct((cells, channels), BF16),
            jax.ShapeDtypeStruct((cells, 3 * channels), BF16),
            jax.ShapeDtypeStruct((halves, tall, members), F32),
        ],
        scratch_shapes=[
            pltpu.VMEM((cells, 3 * channels), BF16),
            pltpu.VMEM((cells, channels), BF16),
            pltpu.VMEM(bias_tall.shape, F32),
        ],
        compiler_params=PARAMS,
        cost_estimate=estimate(14),
        name="attention",
    )(x, cot, w_qkv, w_out, bias_tall)


def attention_weights_kernel(x_ref, packed_grad_ref, att_ref, cot_ref, qkv_ref, out_ref):
    qkv_ref[...] = dot(x_ref[...], packed_grad_ref[...], ((0,), (0,)))
    out_ref[...] = dot(att_ref[...], cot_ref[...], ((0,), (0,)))


def run_attention_weights(x, packed_grad, att, cot):
    channels = x.shape[1]
    vmem = pl.BlockSpec(memory_space=pltpu.VMEM)
    return pl.pallas_call(
        attention_weights_kernel,
        in_specs=[vmem] * 4,
        out_specs=[vmem] * 2,
        out_shape=[
            jax.ShapeDtypeStruct((channels, packed_grad.shape[1]), F32),
            jax.ShapeDtypeStruct((channels, channels), F32),
        ],
        compiler_params=PARAMS,
        cost_estimate=estimate(5),
        name="attention_weights",
    )(x, packed_grad, att, cot)


def mixed_back_kernel(
    stride, bands,
    recv_ref, mixed_ref, cot_ref, gain_ref, act_ref, gate_ref, w_projt_ref,
    grad_ref, low_ref, norm_ref, project_ref, gate_grad_ref,
    turned_ref,
):
    rows, cols, channels = mixed_ref.shape

    @pl.when(pl.program_id(0) == 0)
    def _():
        gain = gain_ref[...].astype(F32)
        lines = 4

        def some_rows(c, total):
            pieces = []
            for k in range(lines):
                i = c * lines + k
                a, p = lax.rem(i, stride), i // stride
                pieces += [recv_ref[a * bands + band, p] for band in range(bands)]
            grad = jnp.concatenate(pieces, axis=0).astype(F32)
            at = pl.ds(c * lines, lines)
            flat = lambda ref: ref[at].reshape(lines * cols, channels).astype(F32)
            unit, rstd = norm_rows(flat(mixed_ref))
            back = flat(cot_ref) + norm_rows_back(unit, rstd, gain, grad)
            grad_ref[at] = back.reshape(lines, cols, channels)
            low_ref[at] = back.astype(BF16).reshape(lines, cols, channels)
            return total + fold_rows(grad * unit)

        total = lax.fori_loop(0, rows // lines, some_rows, jnp.zeros((8, channels), F32))
        norm_ref[...] = jnp.sum(total, axis=0, keepdims=True)
        turned_ref[...] = low_ref[...].reshape(rows * cols, channels).T

    flat = act_ref[...].reshape(rows * cols, BLOCK)
    product = dot(turned_ref[...], flat)
    total = jnp.sum(product * w_projt_ref[...].astype(F32), axis=0, keepdims=True)
    gate_grad_ref[...] = jnp.broadcast_to(total[None], gate_grad_ref.shape)
    project_ref[...] = (product * gate_ref[...]).T


def run_mixed_back(count, stride, recv, mixed, cot, gain, act, gate, w_project_t):
    rows, cols, channels = mixed.shape
    expanded = act.shape[2]
    return pl.pallas_call(
        functools.partial(mixed_back_kernel, stride, cols // SIDE),
        grid=(expanded // BLOCK,),
        in_specs=[
            whole(recv.shape), whole(mixed.shape), whole(cot.shape), whole(gain.shape),
            last_block(act.shape), last_block(gate.shape), last_block(w_project_t.shape),
        ],
        out_specs=[
            whole(mixed.shape), whole(mixed.shape), whole((1, channels)),
            pl.BlockSpec((BLOCK, channels), lambda e: (e, 0)), last_block((count, 1, expanded)),
        ],
        out_shape=[
            jax.ShapeDtypeStruct(mixed.shape, F32),
            jax.ShapeDtypeStruct(mixed.shape, BF16),
            jax.ShapeDtypeStruct((1, channels), F32),
            jax.ShapeDtypeStruct((expanded, channels), F32),
            jax.ShapeDtypeStruct((count, 1, expanded), F32),
        ],
        scratch_shapes=[pltpu.VMEM((channels, rows * cols), BF16)],
        compiler_params=PARAMS,
        cost_estimate=estimate(7),
        name="mixed_back",
    )(recv, mixed, cot, gain, act, gate, w_project_t)


def expand_back_kernel(
    cells_total,
    parts_ref, hidden_ref, gate_all_ref, w_sq_ref, w_ex_ref,
    low_ref, up_ref, down_ref, side_ref, w_projt_ref, gate_ref, slope_ref, side_slope_ref,
    spread_slope_ref, spread_ref, w_dep_ref, turned_ref, w_exp_ref, gain_ref, norm1_ref,
    weights_ref, first_ref, logit_ref, pre_ref,
    main_ref, side_grad_ref, window_ref, expanded_ref, pool_ref, tail_ref, norm_ref,
):
    rows, cols, channels = low_ref.shape
    side = 8
    wide = cols + side
    step = pl.program_id(0)
    steps = pl.num_programs(0)

    @pl.when(step == 0)
    def _():
        gate = gate_all_ref[...]
        gate_grad = jnp.sum(parts_ref[...], axis=0)
        logit = gate_grad * gate * (1.0 - gate)
        hidden = hidden_ref[...]
        sig = jax.nn.sigmoid(hidden)
        pre = dot_exact(logit, w_ex_ref[...].astype(F32), ((1,), (1,))) * (
            sig + hidden * sig * (1.0 - sig)
        )
        logit_ref[...] = logit
        pre_ref[...] = pre
        pooled = dot_exact(pre, w_sq_ref[...].astype(F32), ((1,), (1,))) / cells_total
        for e in range(pool_ref.shape[0]):
            pool_ref[e] = pooled[:, e * BLOCK : (e + 1) * BLOCK]
        first_ref[...] = jnp.zeros(first_ref.shape, F32)
        tail_ref[...] = jnp.zeros(tail_ref.shape, F32)
        norm_ref[...] = jnp.zeros(norm_ref.shape, F32)

    w_projt = w_projt_ref[...]
    main_ref[pl.ds(0, cols), :] = dot(up_ref[0], w_projt)
    main_ref[pl.ds(cols, rows * cols), :] = dot(
        low_ref[...].reshape(rows * cols, channels), w_projt
    )
    main_ref[pl.ds((rows + 1) * cols, cols), :] = dot(down_ref[0], w_projt)
    side_grad_ref[...] = dot(side_ref[...], w_projt)

    @pl.loop(0, rows + 2)
    def _(i):
        for h in range(BLOCK // LANES):
            lanes = slice(h * LANES, (h + 1) * LANES)
            gate = gate_ref[:, lanes]
            pooled = pool_ref[step][:, lanes]
            gated = main_ref[pl.ds(pl.multiple_of(i * cols, 16), cols), lanes]
            main = (gated * gate + pooled) * slope_ref[i, :, lanes].astype(F32)
            gated = side_grad_ref[pl.ds(pl.multiple_of(i * side, side), side), lanes]
            edge = (gated * gate + pooled) * side_slope_ref[i, :, lanes]
            grad = jnp.concatenate([main, edge], axis=0)
            grad = grad.astype(BF16).astype(F32)
            window_ref[0, i, :, lanes] = pltpu.roll(grad, wide - 1, 0)[:cols]
            window_ref[1, i, :, lanes] = grad[:cols]
            window_ref[2, i, :, lanes] = pltpu.roll(grad, 1, 0)[:cols]

    for h in range(BLOCK // LANES):
        lanes = slice(h * LANES, (h + 1) * LANES)
        taps = w_dep_ref[:, :, lanes].astype(F32)

        def back_row(i, sums):
            spread = spread_ref[i, :, lanes].astype(F32)
            total = jnp.zeros((cols, LANES), F32)
            new_sums = []
            for a in range(3):
                for b in range(3):
                    window = window_ref[b, i + 2 - a, :, lanes]
                    total = total + window * taps[a, b : b + 1]
                    new_sums.append(sums[a * 3 + b] + fold_rows(window * spread))
            grad = total * spread_slope_ref[i, :, lanes].astype(F32)
            expanded_ref[pl.ds(pl.multiple_of(i * cols, 16), cols), lanes] = grad.astype(BF16)
            return tuple(new_sums)

        sums = lax.fori_loop(0, rows, back_row, (jnp.zeros((8, LANES), F32),) * 9)
        for t in range(9):
            row = t * (steps * BLOCK // LANES) + step * (BLOCK // LANES) + h
            tail_ref[pl.ds(row, 1), :] = jnp.sum(sums[t], axis=0, keepdims=True)

    grad_expanded = expanded_ref[...]
    w_exp = w_exp_ref[...]
    weights = dot(turned_ref[...], grad_expanded)
    weights_ref[:, pl.ds(pl.multiple_of(step * BLOCK, BLOCK), BLOCK)] = weights.astype(BF16)
    norm_ref[...] += jnp.sum(weights * w_exp.astype(F32), axis=1, keepdims=True)
    first_ref[...] += dot(grad_expanded, w_exp, ((1,), (1,)))

    @pl.when(step == steps - 1)
    def _():
        norm = norm_ref[...].T[0:1] / gain_ref[...].astype(F32)
        start = 9 * steps * (BLOCK // LANES)
        for k in range(channels // LANES):
            piece = slice(k * LANES, (k + 1) * LANES)
            tail_ref[start + k : start + k + 1, :] = norm[:, piece]
            at = start + channels // LANES + k
            tail_ref[at : at + 1, :] = norm1_ref[:, piece]
        weights_ref[:, steps * BLOCK :] = tail_ref[...].astype(BF16)


def run_expand_back(
    cells_total, parts, hidden, gate, w_squeeze, w_excite, low, up, down, side,
    w_project_t, slope, side_slope, spread_slope, spread, w_depth, turned, w_expand, gain, norm1,
):
    rows, cols, channels = low.shape
    expanded = w_expand.shape[1]
    steps = expanded // BLOCK
    return pl.pallas_call(
        functools.partial(expand_back_kernel, cells_total),
        grid=(steps,),
        in_specs=[
            whole(parts.shape), whole(hidden.shape), whole(gate.shape),
            whole(w_squeeze.shape), whole(w_excite.shape),
            whole(low.shape), whole(up.shape), whole(down.shape), whole(side.shape),
            last_block(w_project_t.shape), last_block(gate.shape), last_block(slope.shape),
            last_block(side_slope.shape), last_block(spread_slope.shape), last_block(spread.shape),
            last_block(w_depth.shape), whole(turned.shape), last_block(w_expand.shape),
            whole(gain.shape), whole(norm1.shape),
        ],
        out_specs=[
            whole((channels, expanded + LANES)), whole((rows * cols, channels)),
            whole((1, expanded)), whole(hidden.shape),
        ],
        out_shape=[
            jax.ShapeDtypeStruct((channels, expanded + LANES), BF16),
            jax.ShapeDtypeStruct((rows * cols, channels), F32),
            jax.ShapeDtypeStruct((1, expanded), F32),
            jax.ShapeDtypeStruct(hidden.shape, F32),
        ],
        scratch_shapes=[
            pltpu.VMEM(((rows + 2) * cols, BLOCK), F32),
            pltpu.VMEM(((rows + 2) * 8, BLOCK), F32),
            pltpu.VMEM((3, rows + 2, cols, BLOCK), F32),
            pltpu.VMEM((rows * cols, BLOCK), BF16),
            pltpu.VMEM((steps, 1, BLOCK), F32),
            pltpu.VMEM((channels, LANES), F32),
            pltpu.VMEM((channels, LANES), F32),
        ],
        compiler_params=PARAMS,
        cost_estimate=estimate(14),
        name="expand_back",
    )(
        parts, hidden, gate, w_squeeze, w_excite, low, up, down, side, w_project_t, gate,
        slope, side_slope, spread_slope, spread, w_depth, turned, w_expand, gain, norm1,
    )


def image_back_kernel(image_ref, gain_ref, first_ref, mixed_ref, out_ref):
    unit, rstd = norm_rows(image_ref[...].astype(F32))
    grad = first_ref[...]
    back = mixed_ref[...] + norm_rows_back(unit, rstd, gain_ref[...].astype(F32), grad)
    out_ref[...] = back.astype(BF16)


def run_image_back(image, gain, first, mixed):
    cells, channels = image.shape
    block = pl.BlockSpec((cells // 4, channels), lambda r: (r, 0))
    return pl.pallas_call(
        image_back_kernel,
        grid=(4,),
        in_specs=[block, whole(gain.shape), block, block],
        out_specs=block,
        out_shape=jax.ShapeDtypeStruct((cells, channels), BF16),
        compiler_params=PARAMS,
        cost_estimate=estimate(4),
        name="image_back",
    )(image, gain, first, mixed)


def shift(cells, axis, step):
    count = lax.axis_size(axis)
    pairs = [(i, i + step) for i in range(count) if 0 <= i + step < count]
    return lax.ppermute(cells, axis, pairs)


def halo(cells, width):
    rows, cols, channels = cells.shape
    up = shift(cells[rows - width :], "row", 1)
    down = shift(cells[:width], "row", -1)
    first = jnp.concatenate([up[:, :width], cells[:, :width], down[:, :width]], axis=0)
    last = jnp.concatenate(
        [up[:, cols - width :], cells[:, cols - width :], down[:, cols - width :]], axis=0
    )
    left = shift(last, "col", 1)
    right = shift(first, "col", -1)
    gap = jnp.zeros((rows + 2 * width, 8 - 2 * width, channels), cells.dtype)
    side = jnp.concatenate([right, gap, left], axis=1)
    return up, down, side.reshape(-1, channels)


def hand_around(blocks):
    return lax.all_to_all(blocks, AXES, split_axis=0, concat_axis=0, tiled=True)


def sum_shares(matrix):
    rows, columns = matrix.shape
    count = lax.axis_size("row") * lax.axis_size("col")
    share = rows // count
    arrived = hand_around(matrix.reshape(count, share, columns))
    total = jnp.sum(arrived.astype(F32), axis=0).astype(BF16)
    sent = jnp.broadcast_to(total[None], (count, share, columns))
    return hand_around(sent).reshape(rows, columns)


def swap_groups(blocks, parity):
    groups = None
    if parity > 1:
        over_row = lax.axis_size("row")
        over_col = lax.axis_size("col")
        groups = [
            [r * over_col + c for r in range(over_row) for c in range(k, over_col, parity)]
            for k in range(parity)
        ]
    return lax.all_to_all(
        blocks, AXES, split_axis=0, concat_axis=0, tiled=True, axis_index_groups=groups
    )


def on_device(
    image, out_cotangent, norm0_gain, w_expand, w_depth, w_squeeze, w_excite, w_project,
    norm1_gain, w_qkv, w_out, attn_bias,
):
    rows, cols, channels = image.shape
    over_row = lax.axis_size("row")
    over_col = lax.axis_size("col")
    count = over_row * over_col
    cells_total = rows * cols * count
    stride = rows * over_row // GRID
    parity = over_col // GRID
    lines = rows // stride
    bands = cols // SIDE
    members = GRID * GRID
    expanded = w_expand.shape[1]

    def into_members(arrived):
        parted = arrived.reshape(over_row, GRID, lines, SIDE, channels)
        return parted.transpose(3, 0, 2, 1, 4).reshape(SIDE * members, channels)

    def out_of_members(values):
        parted = values.reshape(SIDE, over_row, lines, GRID, channels)
        return parted.transpose(1, 3, 2, 0, 4).reshape(-1, lines, SIDE, channels)

    row, col = lax.axis_index("row"), lax.axis_index("col")
    flags = jnp.stack([row > 0, row < over_row - 1, col > 0, col < over_col - 1]).astype(F32)
    gain_first = norm0_gain.reshape(1, channels)
    gain_second = norm1_gain.reshape(1, channels)
    w_project_t = w_project.T
    heads = attn_bias.shape[0]
    halves = channels // LANES
    bias_tall = attn_bias.transpose(0, 2, 1).reshape(halves, heads // halves * members, members)
    bias_tall = jnp.concatenate([bias_tall, bias_tall], axis=2)

    up, down, side = halo(image, 2)
    normed_first, turned_first, spread, spread_slope = run_expand(image, gain_first, w_expand)
    cot_sent = (
        out_cotangent.reshape(lines, stride, bands, SIDE, channels)
        .transpose(1, 2, 0, 3, 4)
        .reshape(stride * bands, lines, SIDE, channels)
    )
    cot_members = into_members(swap_groups(cot_sent, parity))
    ring, act, pool = run_depthwise(count, up, down, side, gain_first, w_expand, w_depth, spread)
    pooled, hidden, gate, mixed, normed_sent = run_mix(
        cells_total, stride, hand_around(pool), w_squeeze, w_excite, act, image, w_project,
        gain_second, cot_members,
    )
    slope, side_slope = run_slope(flags, ring, w_depth, spread)
    normed_members = into_members(swap_groups(normed_sent, parity))
    normed_members, slope = lax.optimization_barrier((normed_members, slope))
    attended, grad_normed, packed_grad, grad_bias = run_attention(
        normed_members, cot_members, w_qkv, w_out, bias_tall, heads
    )
    grad_normed_home = swap_groups(out_of_members(grad_normed), parity)
    grad_qkv, grad_out_proj = run_attention_weights(
        normed_members, packed_grad, attended, cot_members
    )
    grad_normed_home, grad_qkv = lax.optimization_barrier((grad_normed_home, grad_qkv))
    grad_mixed, grad_low, grad_norm1, grad_project, gate_grad = run_mixed_back(
        count, stride, grad_normed_home, mixed, out_cotangent, gain_second, act, gate, w_project_t
    )
    parts = hand_around(gate_grad)
    attended, parts = lax.optimization_barrier((attended, parts))
    attended_home = swap_groups(out_of_members(attended), parity)
    up, down, side = halo(grad_low, 1)
    late, grad_first, logit, pre = run_expand_back(
        cells_total, parts, hidden, gate, w_squeeze, w_excite, grad_low, up, down, side,
        w_project_t, slope, side_slope, spread_slope, spread, w_depth, turned_first, w_expand,
        gain_first, grad_norm1,
    )
    late = sum_shares(late).astype(F32)
    grad_image = run_image_back(
        image.reshape(-1, channels), gain_first, grad_first, grad_mixed.reshape(-1, channels)
    )
    attended_map = (
        attended_home.reshape(stride, bands, lines, SIDE, channels)
        .transpose(2, 0, 1, 3, 4)
        .reshape(rows * cols, channels)
    )
    block_out = (mixed.reshape(-1, channels).astype(F32) + dot(attended_map, w_out)).astype(BF16)

    silu = jax.nn.silu(hidden)
    grad_squeeze = pooled.reshape(expanded, 1) * pre
    grad_excite = silu.reshape(-1, 1) * logit

    grad_qkv, grad_out_proj, grad_bias = lax.psum((grad_qkv, grad_out_proj, grad_bias), AXES)
    grad_project = lax.psum(grad_project, AXES)
    grad_bias = grad_bias.reshape(heads, members, members).transpose(0, 2, 1)
    tail = late[:, expanded:].reshape(-1)
    return (
        block_out.reshape(image.shape),
        grad_image.reshape(image.shape),
        tail[9 * expanded : 9 * expanded + channels],
        late[:, :expanded],
        tail[: 9 * expanded].reshape(w_depth.shape),
        grad_squeeze,
        grad_excite,
        grad_project,
        tail[9 * expanded + channels : 9 * expanded + 2 * channels],
        grad_qkv,
        grad_out_proj,
        grad_bias,
    )


def solution(mesh):
    cells = P("row", "col", None)
    return jax.shard_map(
        on_device,
        mesh=mesh,
        in_specs=(cells, cells) + (P(),) * 10,
        out_specs=(cells, cells) + (P(),) * 10,
        check_vma=False,
    )
```

```python
import functools
import math

import jax
import jax.numpy as jnp
from jax import lax
from jax.experimental import pallas as pl
from jax.experimental.pallas import tpu as pltpu
from jax.sharding import PartitionSpec as P

GRID = 8
AXES = ("row", "col")
BLOCK = 256
LANES = 128
SIDE = 16
GELU_A = math.sqrt(2.0 / math.pi)
GELU_B = GELU_A * 0.044715
F32 = jnp.float32
BF16 = jnp.bfloat16
PARAMS = pltpu.CompilerParams(vmem_limit_bytes=56 * 1024 * 1024)


def estimate(us):
    return pl.CostEstimate(flops=int(us * 1.1e9), bytes_accessed=int(us * 3.6e6), transcendentals=0)


def dot(left, right, contract=((1,), (0,))):
    return lax.dot_general(left, right, (contract, ((), ())), preferred_element_type=F32)


def dot_exact(vector, right, contract):
    tall = jnp.broadcast_to(vector, (8, vector.shape[1]))
    product = lax.dot_general(
        tall, right, (contract, ((), ())), precision=lax.Precision.HIGHEST, preferred_element_type=F32
    )
    return product[0:1]


def gelu_and_slope(x, with_slope=True):
    square = x * x
    t = jnp.tanh(x * (GELU_A + GELU_B * square))
    half = 0.5 + 0.5 * t
    value = x * half
    if not with_slope:
        return value, None
    slope = half + (value * (1.0 - t)) * (GELU_A + (3.0 * GELU_B) * square)
    return value, slope


def norm_rows(x):
    average = jnp.mean(x, axis=-1, keepdims=True)
    centered = x - average
    variance = jnp.mean(centered * centered, axis=-1, keepdims=True)
    rstd = lax.rsqrt(variance + 1e-05)
    return centered * rstd, rstd


def norm_rows_back(unit, rstd, gain, grad):
    unit_grad = grad * gain
    first = jnp.mean(unit_grad, axis=-1, keepdims=True)
    second = jnp.mean(unit_grad * unit, axis=-1, keepdims=True)
    return rstd * (unit_grad - first - unit * second)


def fold_rows(x):
    return jnp.sum(x.reshape(x.shape[0] // 8, 8, x.shape[1]), axis=0)


def whole(shape):
    return pl.BlockSpec(shape, lambda e: (0,) * len(shape))


def last_block(shape):
    lead = (0,) * (len(shape) - 1)
    return pl.BlockSpec(shape[:-1] + (BLOCK,), lambda e: lead + (e,))


def expand_kernel(
    image_ref, gain_ref, w_exp_ref,
    normed_ref, turned_ref, spread_ref, slope_ref,
    expanded_ref,
):
    rows, cols, channels = image_ref.shape

    @pl.when(pl.program_id(0) == 0)
    def _():
        gain = gain_ref[...].astype(F32)

        @pl.loop(0, rows // 4)
        def _(c):
            flat = image_ref[pl.ds(c * 4, 4)].reshape(4 * cols, channels)
            unit, _ = norm_rows(flat.astype(F32))
            at = pl.ds(pl.multiple_of(c * 4 * cols, 16), 4 * cols)
            normed_ref[at, :] = (unit * gain).astype(BF16)

        turned_ref[...] = normed_ref[...].T

    expanded_ref[...] = dot(normed_ref[...], w_exp_ref[...])

    @pl.loop(0, rows)
    def _(r):
        for h in range(BLOCK // LANES):
            lanes = slice(h * LANES, (h + 1) * LANES)
            x = expanded_ref[pl.ds(pl.multiple_of(r * cols, 16), cols), lanes]
            value, slope = gelu_and_slope(x)
            spread_ref[r, :, lanes] = value.astype(BF16)
            slope_ref[r, :, lanes] = slope.astype(BF16)


def run_expand(image, gain, w_expand):
    rows, cols, channels = image.shape
    expanded = w_expand.shape[1]
    return pl.pallas_call(
        expand_kernel,
        grid=(expanded // BLOCK,),
        in_specs=[whole(image.shape), whole(gain.shape), last_block(w_expand.shape)],
        out_specs=[
            whole((rows * cols, channels)), whole((channels, rows * cols)),
            last_block((rows, cols, expanded)), last_block((rows, cols, expanded)),
        ],
        out_shape=[
            jax.ShapeDtypeStruct((rows * cols, channels), BF16),
            jax.ShapeDtypeStruct((channels, rows * cols), BF16),
            jax.ShapeDtypeStruct((rows, cols, expanded), BF16),
            jax.ShapeDtypeStruct((rows, cols, expanded), BF16),
        ],
        scratch_shapes=[pltpu.VMEM((rows * cols, BLOCK), F32)],
        compiler_params=PARAMS,
        cost_estimate=estimate(9),
        name="expand",
    )(image, gain, w_expand)


def depthwise_kernel(
    up_ref, down_ref, side_ref, gain_ref, w_exp_ref, w_dep_ref, spread_ref,
    ring_ref, act_ref, pool_ref,
    ring_normed_ref, ring_wide_ref,
):
    rows, cols, _ = spread_ref.shape
    channels = up_ref.shape[2]
    over = 4 * cols
    side = 8

    @pl.when(pl.program_id(0) == 0)
    def _():
        gain = gain_ref[...].astype(F32)

        def put(at, values):
            unit, _ = norm_rows(values.astype(F32))
            ring_normed_ref[at : at + values.shape[0], :] = (unit * gain).astype(BF16)

        put(0, up_ref[...].reshape(2 * cols, channels))
        put(2 * cols, down_ref[...].reshape(2 * cols, channels))
        put(over, side_ref[...])

    ring_wide_ref[...] = dot(ring_normed_ref[...], w_exp_ref[...])
    tile = 32

    @pl.loop(0, ring_wide_ref.shape[0] // tile)
    def _(t):
        at = pl.ds(pl.multiple_of(t * tile, tile), tile)
        value, _ = gelu_and_slope(ring_wide_ref[at, :], False)
        low = value.astype(BF16)
        ring_ref[at, :] = low
        ring_wide_ref[at, :] = low.astype(F32)

    for h in range(BLOCK // LANES):
        lanes = slice(h * LANES, (h + 1) * LANES)
        taps = w_dep_ref[:, :, lanes].astype(F32)
        w = [[taps[a, b : b + 1] for b in range(3)] for a in range(3)]

        def line(r, main):
            at = pl.multiple_of(over + (r + 2) * side, side)
            return jnp.concatenate([main, ring_wide_ref[pl.ds(at, side), lanes]], axis=0)

        def conv(i, x, total):
            u = [x[0] * w[0][b] + x[1] * w[1][b] + x[2] * w[2][b] for b in range(3)]
            wide = cols + side
            pre = pltpu.roll(u[0], 1, 0) + u[1] + pltpu.roll(u[2], wide - 1, 0)
            value, _ = gelu_and_slope(pre[:cols], False)
            act_ref[i, :, lanes] = value.astype(BF16)
            return total + fold_rows(value)

        def step(i, carry):
            first, second, total = carry
            third = line(i + 1, spread_ref[i + 1, :, lanes].astype(F32))
            return second, third, conv(i, (first, second, third), total)

        carry = (
            line(-1, ring_wide_ref[cols : 2 * cols, lanes]),
            line(0, spread_ref[0, :, lanes].astype(F32)),
            jnp.zeros((8, LANES), F32),
        )
        first, second, total = lax.fori_loop(0, rows - 1, step, carry)
        third = line(rows, ring_wide_ref[2 * cols : 3 * cols, lanes])
        total = conv(rows - 1, (first, second, third), total)
        total = jnp.sum(total, axis=0, keepdims=True)
        pool_ref[:, :, lanes] = jnp.broadcast_to(total[None], (pool_ref.shape[0], 1, LANES))


def run_depthwise(count, up, down, side, gain, w_expand, w_depth, spread):
    rows, cols, expanded = spread.shape
    channels = up.shape[2]
    ring = 4 * cols + 8 * (rows + 4)
    return pl.pallas_call(
        depthwise_kernel,
        grid=(expanded // BLOCK,),
        in_specs=[
            whole(up.shape), whole(down.shape), whole(side.shape), whole(gain.shape),
            last_block(w_expand.shape), last_block(w_depth.shape), last_block(spread.shape),
        ],
        out_specs=[
            last_block((ring, expanded)), last_block(spread.shape), last_block((count, 1, expanded)),
        ],
        out_shape=[
            jax.ShapeDtypeStruct((ring, expanded), BF16),
            jax.ShapeDtypeStruct(spread.shape, BF16),
            jax.ShapeDtypeStruct((count, 1, expanded), F32),
        ],
        scratch_shapes=[pltpu.VMEM((ring, channels), BF16), pltpu.VMEM((ring, BLOCK), F32)],
        compiler_params=PARAMS,
        cost_estimate=estimate(9),
        name="depthwise",
    )(up, down, side, gain, w_expand, w_depth, spread)


def slope_kernel(flags_ref, ring_ref, w_dep_ref, spread_ref, main_ref, side_out_ref, wide_ref):
    rows, cols, _ = spread_ref.shape
    over = 4 * cols
    side = 8
    wide = cols + side

    for k, r in enumerate((0, 1, rows + 2, rows + 3)):
        wide_ref[r, :cols, :] = ring_ref[k * cols : (k + 1) * cols, :].astype(F32)
    sides = ring_ref[over:, :].astype(F32)
    for r in range(rows + 4):
        wide_ref[r, cols:, :] = sides[r * side : (r + 1) * side]

    @pl.loop(0, rows)
    def _(r):
        wide_ref[r + 2, :cols, :] = spread_ref[r].astype(F32)

    place = lax.broadcasted_iota(jnp.int32, (side, LANES), 0)
    side_mask = jnp.where(
        place == side - 1, flags_ref[2], jnp.where(place == 0, flags_ref[3], 1.0)
    ).astype(F32)

    @pl.loop(0, rows + 2)
    def _(i):
        keep = jnp.where(i == 0, flags_ref[0], jnp.where(i == rows + 1, flags_ref[1], 1.0))
        for h in range(BLOCK // LANES):
            lanes = slice(h * LANES, (h + 1) * LANES)
            taps = w_dep_ref[:, :, lanes].astype(F32)
            x = [wide_ref[i + a, :, lanes] for a in range(3)]
            u = [sum(x[a] * taps[a, b : b + 1] for a in range(3)) for b in range(3)]
            pre = pltpu.roll(u[0], 1, 0) + u[1] + pltpu.roll(u[2], wide - 1, 0)
            _, slope = gelu_and_slope(pre)
            slope = slope * keep
            main_ref[i, :, lanes] = slope[:cols].astype(BF16)
            side_out_ref[i, :, lanes] = slope[cols:] * side_mask


def run_slope(flags, ring, w_depth, spread):
    rows, cols, expanded = spread.shape
    return pl.pallas_call(
        slope_kernel,
        grid=(expanded // BLOCK,),
        in_specs=[
            pl.BlockSpec(memory_space=pltpu.SMEM),
            last_block(ring.shape), last_block(w_depth.shape), last_block(spread.shape),
        ],
        out_specs=[last_block((rows + 2, cols, expanded)), last_block((rows + 2, 8, expanded))],
        out_shape=[
            jax.ShapeDtypeStruct((rows + 2, cols, expanded), BF16),
            jax.ShapeDtypeStruct((rows + 2, 8, expanded), F32),
        ],
        scratch_shapes=[pltpu.VMEM((rows + 4, cols + 8, BLOCK), F32)],
        compiler_params=PARAMS,
        cost_estimate=estimate(13),
        name="slope",
    )(flags, ring, w_depth, spread)


def mix_kernel(
    cells_total, stride, bands,
    parts_ref, w_sq_ref, w_ex_ref, act_ref, image_ref, w_proj_ref, gain_ref, after_ref,
    pooled_ref, hidden_ref, gate_ref, mixed_ref, send_ref,
):
    step = pl.program_id(0)

    @pl.when(step == 0)
    def _():
        pooled = jnp.sum(parts_ref[...], axis=0) / cells_total
        hidden = dot_exact(pooled, w_sq_ref[...].astype(F32), ((1,), (0,)))
        silu = hidden * jax.nn.sigmoid(hidden)
        pooled_ref[...] = pooled
        hidden_ref[...] = hidden
        gate_ref[...] = jax.nn.sigmoid(dot_exact(silu, w_ex_ref[...].astype(F32), ((1,), (0,))))

    lines, cols, channels = image_ref.shape
    flat = act_ref[...].reshape(lines * cols, act_ref.shape[2])
    gated = (flat.astype(F32) * gate_ref[...]).astype(BF16)
    product = dot(gated, w_proj_ref[...])
    mixed = (image_ref[...].reshape(lines * cols, channels).astype(F32) + product).astype(BF16)
    mixed_ref[...] = mixed.reshape(lines, cols, channels)
    unit, _ = norm_rows(mixed.astype(F32))
    normed = (unit * gain_ref[...].astype(F32)).astype(BF16)
    for k in range(lines):
        line = step * lines + k
        for band in range(bands):
            start = k * cols + band * SIDE
            send_ref[lax.rem(line, stride) * bands + band, line // stride] = normed[
                start : start + SIDE
            ]


def run_mix(cells_total, stride, parts, w_squeeze, w_excite, act, image, w_project, gain, after):
    rows, cols, channels = image.shape
    expanded = act.shape[2]
    lines = 4
    bands = cols // SIDE
    block = lambda width: pl.BlockSpec((lines, cols, width), lambda r: (r, 0, 0))
    send = (stride * bands, rows // stride, SIDE, channels)
    return pl.pallas_call(
        functools.partial(mix_kernel, cells_total, stride, bands),
        grid=(rows // lines,),
        in_specs=[
            whole(parts.shape), whole(w_squeeze.shape), whole(w_excite.shape),
            block(expanded), block(channels), whole(w_project.shape), whole(gain.shape),
            pl.BlockSpec(memory_space=pl.ANY),
        ],
        out_specs=[
            whole((1, expanded)), whole((1, w_squeeze.shape[1])), whole((1, expanded)),
            block(channels), whole(send),
        ],
        out_shape=[
            jax.ShapeDtypeStruct((1, expanded), F32),
            jax.ShapeDtypeStruct((1, w_squeeze.shape[1]), F32),
            jax.ShapeDtypeStruct((1, expanded), F32),
            jax.ShapeDtypeStruct(image.shape, BF16),
            jax.ShapeDtypeStruct(send, BF16),
        ],
        compiler_params=PARAMS,
        cost_estimate=estimate(5),
        name="mix",
    )(parts, w_squeeze, w_excite, act, image, w_project, gain, after)


def attention_kernel(
    members, heads, lines,
    arrived_ref, cot_ref, w_qkv_ref, w_out_ref, bias_ref,
    x_ref, att_ref, grad_ref, packed_grad_ref, bias_out_ref,
    order_ref, packed_ref, att_grad_ref, bias_sum_ref,
):
    cells, channels = x_ref.shape
    groups = cells // members

    def places():
        for g in range(groups):
            for m in range(0, members, GRID):
                line, row = (m // GRID) % lines, m // GRID // lines
                start = (row * GRID * lines + line) * groups + g
                yield g * members + m, pl.ds(start, GRID, stride=lines * groups)

    for half in range(channels // LANES):
        lanes = slice(half * LANES, (half + 1) * LANES)
        order_ref[half] = arrived_ref[:, lanes].astype(F32)
        for g in range(groups):
            pieces = [order_ref[half, at, :] for k, at in places() if k // members == g]
            at = slice(g * members, (g + 1) * members)
            x_ref[at, lanes] = jnp.concatenate(pieces, axis=0).astype(BF16)
    dim = channels // heads
    per_half = LANES // dim
    halves = channels // LANES
    scale = dim ** (-0.5)
    packed_ref[...] = dot(x_ref[...], w_qkv_ref[...]).astype(BF16)
    att_grad_ref[...] = dot(cot_ref[...], w_out_ref[...], ((1,), (1,))).astype(BF16)
    bias_sum_ref[...] = jnp.zeros(bias_sum_ref.shape, F32)
    tall = per_half * members
    mask = (
        lax.broadcasted_iota(jnp.int32, (tall, LANES), 0) // members
        == lax.broadcasted_iota(jnp.int32, (tall, LANES), 1) // dim
    ).astype(F32).astype(BF16)
    owner = lax.broadcasted_iota(jnp.int32, (members, 2 * LANES), 1) % LANES // dim
    zero = jnp.zeros((members, LANES), BF16)

    def by_head(pair):
        return jnp.concatenate(
            [jnp.concatenate([v] * per_half, axis=0) * mask for v in pair], axis=1
        )

    def diagonal(pair):
        return jnp.concatenate(
            [
                jnp.concatenate([pair[0], zero], axis=1),
                jnp.concatenate([zero, pair[1]], axis=1),
            ],
            axis=0,
        )

    def collect(v):
        parts = [v[h * members : (h + 1) * members] for h in range(per_half)]
        picked = parts[-1]
        for h in range(per_half - 1):
            picked = jnp.where(owner == h, parts[h], picked)
        return [picked[:, :LANES], picked[:, LANES:]]

    def blocks(v):
        return [v[:members, :LANES], v[members:, LANES:]]

    def over_members(v, reduce):
        parted = v.reshape(per_half, members, 2 * members)
        small = reduce(parted, axis=1, keepdims=True)
        return jnp.broadcast_to(small, parted.shape).reshape(v.shape)

    def pair_step(g, carry):
        at = [pl.ds(pl.multiple_of((2 * g + k) * members, 16), members) for k in range(2)]
        for half in range(halves):
            def lanes(part):
                start = part * channels + half * LANES
                return slice(start, start + LANES)

            q, k, v = ([packed_ref[at[n], lanes(part)] for n in range(2)] for part in range(3))
            cot = [att_grad_ref[at[n], lanes(0)] for n in range(2)]
            q_diag, cot_diag = diagonal(q), diagonal(cot)
            k_tall, v_tall = by_head(k), by_head(v)
            scores = dot(k_tall, q_diag, ((1,), (1,))) * scale + bias_ref[half]
            grad_probs = dot(v_tall, cot_diag, ((1,), (1,)))
            lifted = jnp.exp(scores - over_members(scores, jnp.max))
            soft = lifted * (1.0 / over_members(lifted, jnp.sum))
            soft_low = soft.astype(BF16)
            grad_scores = soft * (grad_probs - over_members(grad_probs * soft, jnp.sum))
            bias_sum_ref[half] += grad_scores
            scaled = (grad_scores * scale).astype(BF16)
            attended = blocks(dot(soft_low, v_tall, ((0,), (0,))))
            grad_q = blocks(dot(scaled, k_tall, ((0,), (0,))))
            grad_v = collect(dot(soft_low, cot_diag))
            grad_k = collect(dot(scaled, q_diag))
            for n in range(2):
                att_ref[at[n], lanes(0)] = attended[n].astype(BF16)
                for part, value in enumerate((grad_q, grad_k, grad_v)):
                    packed_grad_ref[at[n], lanes(part)] = value[n].astype(BF16)
        return carry

    lax.fori_loop(0, cells // members // 2, pair_step, 0)
    grad = dot(packed_grad_ref[...], w_qkv_ref[...], ((1,), (1,)))
    for half in range(halves):
        lanes = slice(half * LANES, (half + 1) * LANES)
        for k, at in places():
            order_ref[half, at, :] = grad[k : k + GRID, lanes]
        grad_ref[:, lanes] = order_ref[half].astype(BF16)
    for half in range(halves):
        both = bias_sum_ref[half]
        bias_out_ref[half] = both[:, :members] + both[:, members:]


def run_attention(arrived, cot, w_qkv, w_out, bias_tall, heads, lines):
    cells, channels = cot.shape
    halves, tall, members2 = bias_tall.shape
    members = members2 // 2
    vmem = pl.BlockSpec(memory_space=pltpu.VMEM)
    return pl.pallas_call(
        functools.partial(attention_kernel, members, heads, lines),
        in_specs=[vmem] * 5,
        out_specs=[vmem] * 5,
        out_shape=[
            jax.ShapeDtypeStruct((cells, channels), BF16),
            jax.ShapeDtypeStruct((cells, channels), BF16),
            jax.ShapeDtypeStruct((cells, channels), BF16),
            jax.ShapeDtypeStruct((cells, 3 * channels), BF16),
            jax.ShapeDtypeStruct((halves, tall, members), F32),
        ],
        scratch_shapes=[
            pltpu.VMEM((channels // LANES, cells, LANES), F32),
            pltpu.VMEM((cells, 3 * channels), BF16),
            pltpu.VMEM((cells, channels), BF16),
            pltpu.VMEM(bias_tall.shape, F32),
        ],
        compiler_params=PARAMS,
        cost_estimate=estimate(14),
        name="attention",
    )(arrived.reshape(cells, channels), cot, w_qkv, w_out, bias_tall)


def attention_weights_kernel(x_ref, packed_grad_ref, att_ref, cot_ref, bias_ref, out_ref):
    channels = x_ref.shape[1]
    wide = 3 * channels
    out_ref[:, :wide] = dot(x_ref[...], packed_grad_ref[...], ((0,), (0,))).astype(BF16)
    out_ref[:, wide : wide + channels] = dot(att_ref[...], cot_ref[...], ((0,), (0,))).astype(BF16)
    bias = jnp.concatenate([bias_ref[half] for half in range(bias_ref.shape[0])], axis=1)
    out_ref[:, wide + channels :] = bias.astype(BF16)


def run_attention_weights(x, packed_grad, att, cot, bias):
    channels = x.shape[1]
    vmem = pl.BlockSpec(memory_space=pltpu.VMEM)
    width = 4 * channels + bias.shape[0] * bias.shape[2]
    return pl.pallas_call(
        attention_weights_kernel,
        in_specs=[vmem] * 5,
        out_specs=vmem,
        out_shape=jax.ShapeDtypeStruct((channels, width), BF16),
        compiler_params=PARAMS,
        cost_estimate=estimate(5),
        name="attention_weights",
    )(x, packed_grad, att, cot, bias)


def mixed_back_kernel(
    stride, bands,
    recv_ref, mixed_ref, cot_ref, gain_ref, act_ref, gate_ref, w_projt_ref,
    grad_ref, low_ref, norm_ref, project_ref, gate_grad_ref,
    turned_ref, total_ref,
):
    rows, cols, channels = mixed_ref.shape

    @pl.when(pl.program_id(0) == 0)
    def _():
        gain = gain_ref[...].astype(F32)
        lines = 4

        def some_rows(c, total):
            pieces = []
            for k in range(lines):
                i = c * lines + k
                a, p = lax.rem(i, stride), i // stride
                pieces += [recv_ref[a * bands + band, p] for band in range(bands)]
            grad = jnp.concatenate(pieces, axis=0).astype(F32)
            at = pl.ds(c * lines, lines)
            flat = lambda ref: ref[at].reshape(lines * cols, channels).astype(F32)
            unit, rstd = norm_rows(flat(mixed_ref))
            back = flat(cot_ref) + norm_rows_back(unit, rstd, gain, grad)
            grad_ref[at] = back.reshape(lines, cols, channels)
            low_ref[at] = back.astype(BF16).reshape(lines, cols, channels)
            return total + fold_rows(grad * unit)

        total = lax.fori_loop(0, rows // lines, some_rows, jnp.zeros((8, channels), F32))
        norm_ref[...] = jnp.sum(total, axis=0, keepdims=True)
        turned_ref[...] = low_ref[...].reshape(rows * cols, channels).T

    flat = act_ref[...].reshape(rows * cols, BLOCK)
    product = dot(turned_ref[...], flat)
    total = jnp.sum(product * w_projt_ref[...].astype(F32), axis=0, keepdims=True)
    step, steps = pl.program_id(0), pl.num_programs(0)
    total_ref[step] = total
    project_ref[...] = (product * gate_ref[...]).T.astype(BF16)

    @pl.when(step == steps - 1)
    def _():
        sums = [total_ref[e] for e in range(total_ref.shape[0])]
        high = [v.astype(BF16).astype(F32) for v in sums]
        terms = jnp.concatenate(high + [v - w for v, w in zip(sums, high)], axis=0)
        gate_grad_ref[...] = jnp.broadcast_to(terms.astype(BF16)[None], gate_grad_ref.shape)


def run_mixed_back(count, stride, recv, mixed, cot, gain, act, gate, w_project_t):
    rows, cols, channels = mixed.shape
    expanded = act.shape[2]
    return pl.pallas_call(
        functools.partial(mixed_back_kernel, stride, cols // SIDE),
        grid=(expanded // BLOCK,),
        in_specs=[
            whole(recv.shape), whole(mixed.shape), whole(cot.shape), whole(gain.shape),
            last_block(act.shape), last_block(gate.shape), last_block(w_project_t.shape),
        ],
        out_specs=[
            whole(mixed.shape), whole(mixed.shape), whole((1, channels)),
            last_block((BLOCK, expanded)), whole((count, 2 * expanded // BLOCK, BLOCK)),
        ],
        out_shape=[
            jax.ShapeDtypeStruct(mixed.shape, F32),
            jax.ShapeDtypeStruct(mixed.shape, BF16),
            jax.ShapeDtypeStruct((1, channels), F32),
            jax.ShapeDtypeStruct((BLOCK, expanded), BF16),
            jax.ShapeDtypeStruct((count, 2 * expanded // BLOCK, BLOCK), BF16),
        ],
        scratch_shapes=[
            pltpu.VMEM((channels, rows * cols), BF16),
            pltpu.VMEM((expanded // BLOCK, 1, BLOCK), F32),
        ],
        compiler_params=PARAMS,
        cost_estimate=estimate(7),
        name="mixed_back",
    )(recv, mixed, cot, gain, act, gate, w_project_t)


def expand_back_kernel(
    cells_total,
    parts_ref, hidden_ref, gate_all_ref, w_sq_ref, w_ex_ref,
    low_ref, up_ref, down_ref, side_ref, w_projt_ref, gate_ref, slope_ref, side_slope_ref,
    spread_slope_ref, spread_ref, w_dep_ref, turned_ref, w_exp_ref, gain_ref, norm1_ref,
    weights_ref, first_ref, logit_ref, pre_ref,
    main_ref, side_grad_ref, window_ref, expanded_ref, pool_ref, tail_ref, norm_ref,
):
    rows, cols, channels = low_ref.shape
    side = 8
    wide = cols + side
    step = pl.program_id(0)
    steps = pl.num_programs(0)

    @pl.when(step == 0)
    def _():
        gate = gate_all_ref[...]
        len_e = pool_ref.shape[0]
        terms = jnp.sum(parts_ref[...].astype(F32), axis=0)
        gate_grad = jnp.concatenate(
            [terms[e : e + 1] + terms[len_e + e : len_e + e + 1] for e in range(len_e)],
            axis=1,
        )
        logit = gate_grad * gate * (1.0 - gate)
        hidden = hidden_ref[...]
        sig = jax.nn.sigmoid(hidden)
        pre = dot_exact(logit, w_ex_ref[...].astype(F32), ((1,), (1,))) * (
            sig + hidden * sig * (1.0 - sig)
        )
        logit_ref[...] = logit
        pre_ref[...] = pre
        pooled = dot_exact(pre, w_sq_ref[...].astype(F32), ((1,), (1,))) / cells_total
        for e in range(pool_ref.shape[0]):
            pool_ref[e] = pooled[:, e * BLOCK : (e + 1) * BLOCK]
        first_ref[...] = jnp.zeros(first_ref.shape, F32)
        tail_ref[...] = jnp.zeros(tail_ref.shape, F32)
        norm_ref[...] = jnp.zeros(norm_ref.shape, F32)

    w_projt = w_projt_ref[...]
    main_ref[pl.ds(0, cols), :] = dot(up_ref[0], w_projt)
    main_ref[pl.ds(cols, rows * cols), :] = dot(
        low_ref[...].reshape(rows * cols, channels), w_projt
    )
    main_ref[pl.ds((rows + 1) * cols, cols), :] = dot(down_ref[0], w_projt)
    side_grad_ref[...] = dot(side_ref[...], w_projt)

    @pl.loop(0, rows + 2)
    def _(i):
        for h in range(BLOCK // LANES):
            lanes = slice(h * LANES, (h + 1) * LANES)
            gate = gate_ref[:, lanes]
            pooled = pool_ref[step][:, lanes]
            gated = main_ref[pl.ds(pl.multiple_of(i * cols, 16), cols), lanes]
            main = (gated * gate + pooled) * slope_ref[i, :, lanes].astype(F32)
            gated = side_grad_ref[pl.ds(pl.multiple_of(i * side, side), side), lanes]
            edge = (gated * gate + pooled) * side_slope_ref[i, :, lanes]
            grad = jnp.concatenate([main, edge], axis=0)
            grad = grad.astype(BF16).astype(F32)
            window_ref[0, i, :, lanes] = pltpu.roll(grad, wide - 1, 0)[:cols]
            window_ref[1, i, :, lanes] = grad[:cols]
            window_ref[2, i, :, lanes] = pltpu.roll(grad, 1, 0)[:cols]

    for h in range(BLOCK // LANES):
        lanes = slice(h * LANES, (h + 1) * LANES)
        taps = w_dep_ref[:, :, lanes].astype(F32)

        def back_row(i, sums):
            spread = spread_ref[i, :, lanes].astype(F32)
            total = jnp.zeros((cols, LANES), F32)
            new_sums = []
            for a in range(3):
                for b in range(3):
                    window = window_ref[b, i + 2 - a, :, lanes]
                    total = total + window * taps[a, b : b + 1]
                    new_sums.append(sums[a * 3 + b] + fold_rows(window * spread))
            grad = total * spread_slope_ref[i, :, lanes].astype(F32)
            expanded_ref[pl.ds(pl.multiple_of(i * cols, 16), cols), lanes] = grad.astype(BF16)
            return tuple(new_sums)

        sums = lax.fori_loop(0, rows, back_row, (jnp.zeros((8, LANES), F32),) * 9)
        for t in range(9):
            row = t * (steps * BLOCK // LANES) + step * (BLOCK // LANES) + h
            tail_ref[pl.ds(row, 1), :] = jnp.sum(sums[t], axis=0, keepdims=True)

    grad_expanded = expanded_ref[...]
    w_exp = w_exp_ref[...]
    weights = dot(turned_ref[...], grad_expanded)
    weights_ref[:, pl.ds(pl.multiple_of(step * BLOCK, BLOCK), BLOCK)] = weights.astype(BF16)
    norm_ref[...] += jnp.sum(weights * w_exp.astype(F32), axis=1, keepdims=True)
    first_ref[...] += dot(grad_expanded, w_exp, ((1,), (1,)))

    @pl.when(step == steps - 1)
    def _():
        norm = norm_ref[...].T[0:1] / gain_ref[...].astype(F32)
        start = 9 * steps * (BLOCK // LANES)
        for k in range(channels // LANES):
            piece = slice(k * LANES, (k + 1) * LANES)
            tail_ref[start + k : start + k + 1, :] = norm[:, piece]
            at = start + channels // LANES + k
            tail_ref[at : at + 1, :] = norm1_ref[:, piece]
        weights_ref[:, steps * BLOCK :] = tail_ref[...].astype(BF16)


def run_expand_back(
    cells_total, parts, hidden, gate, w_squeeze, w_excite, low, up, down, side,
    w_project_t, slope, side_slope, spread_slope, spread, w_depth, turned, w_expand, gain, norm1,
):
    rows, cols, channels = low.shape
    expanded = w_expand.shape[1]
    steps = expanded // BLOCK
    return pl.pallas_call(
        functools.partial(expand_back_kernel, cells_total),
        grid=(steps,),
        in_specs=[
            pl.BlockSpec(
                (parts.shape[0], 2 * steps, BLOCK), lambda e: (0, parts.shape[1] // (2 * steps) - 1, 0)
            ),
            whole(hidden.shape), whole(gate.shape),
            whole(w_squeeze.shape), whole(w_excite.shape),
            whole(low.shape), whole(up.shape), whole(down.shape), whole(side.shape),
            last_block(w_project_t.shape), last_block(gate.shape), last_block(slope.shape),
            last_block(side_slope.shape), last_block(spread_slope.shape), last_block(spread.shape),
            last_block(w_depth.shape), whole(turned.shape), last_block(w_expand.shape),
            whole(gain.shape), whole(norm1.shape),
        ],
        out_specs=[
            whole((channels, expanded + LANES)), whole((rows * cols, channels)),
            whole((1, expanded)), whole(hidden.shape),
        ],
        out_shape=[
            jax.ShapeDtypeStruct((channels, expanded + LANES), BF16),
            jax.ShapeDtypeStruct((rows * cols, channels), F32),
            jax.ShapeDtypeStruct((1, expanded), F32),
            jax.ShapeDtypeStruct(hidden.shape, F32),
        ],
        scratch_shapes=[
            pltpu.VMEM(((rows + 2) * cols, BLOCK), F32),
            pltpu.VMEM(((rows + 2) * 8, BLOCK), F32),
            pltpu.VMEM((3, rows + 2, cols, BLOCK), F32),
            pltpu.VMEM((rows * cols, BLOCK), BF16),
            pltpu.VMEM((steps, 1, BLOCK), F32),
            pltpu.VMEM((channels, LANES), F32),
            pltpu.VMEM((channels, LANES), F32),
        ],
        compiler_params=PARAMS,
        cost_estimate=estimate(14),
        name="expand_back",
    )(
        parts, hidden, gate, w_squeeze, w_excite, low, up, down, side, w_project_t, gate,
        slope, side_slope, spread_slope, spread, w_depth, turned, w_expand, gain, norm1,
    )


def image_back_kernel(image_ref, gain_ref, first_ref, mixed_ref, out_ref):
    unit, rstd = norm_rows(image_ref[...].astype(F32))
    grad = first_ref[...]
    back = mixed_ref[...] + norm_rows_back(unit, rstd, gain_ref[...].astype(F32), grad)
    out_ref[...] = back.astype(BF16)


def run_image_back(image, gain, first, mixed):
    cells, channels = image.shape
    block = pl.BlockSpec((cells // 4, channels), lambda r: (r, 0))
    return pl.pallas_call(
        image_back_kernel,
        grid=(4,),
        in_specs=[block, whole(gain.shape), block, block],
        out_specs=block,
        out_shape=jax.ShapeDtypeStruct((cells, channels), BF16),
        compiler_params=PARAMS,
        cost_estimate=estimate(4),
        name="image_back",
    )(image, gain, first, mixed)


def shift(cells, axis, step):
    count = lax.axis_size(axis)
    pairs = [(i, i + step) for i in range(count) if 0 <= i + step < count]
    return lax.ppermute(cells, axis, pairs)


def halo_rows(cells, width):
    up = shift(cells[cells.shape[0] - width :], "row", 1)
    down = shift(cells[:width], "row", -1)
    return up, down


def halo_sides(cells, up, down, width):
    rows, cols, channels = cells.shape
    first = jnp.concatenate([up[:, :width], cells[:, :width], down[:, :width]], axis=0)
    last = jnp.concatenate(
        [up[:, cols - width :], cells[:, cols - width :], down[:, cols - width :]], axis=0
    )
    left = shift(last, "col", 1)
    right = shift(first, "col", -1)
    gap = jnp.zeros((rows + 2 * width, 8 - 2 * width, channels), cells.dtype)
    side = jnp.concatenate([right, gap, left], axis=1)
    return side.reshape(-1, channels)


def hand_around(blocks):
    return lax.all_to_all(blocks, AXES, split_axis=0, concat_axis=0, tiled=True)


def sum_shares(matrix):
    rows, columns = matrix.shape
    count = lax.axis_size("row") * lax.axis_size("col")
    share = rows // count
    arrived = hand_around(matrix.reshape(count, share, columns))
    total = jnp.sum(arrived.astype(F32), axis=0).astype(BF16)
    sent = jnp.broadcast_to(total[None], (count, share, columns))
    return hand_around(sent).reshape(rows, columns)


def cube_steps():
    steps = [("col", 1)]
    for axis in ("row", "col"):
        step = 1 if axis == "row" else 2
        while step < lax.axis_size(axis):
            steps.append((axis, step))
            step *= 2
    return steps


def sum_by_halves(matrix):
    width = matrix.shape[1]

    def swap(v, axis, step):
        return lax.ppermute(v, axis, [(i, i ^ step) for i in range(lax.axis_size(axis))])

    steps = cube_steps()
    for axis, step in steps:
        bit = lax.axis_index(axis) // step % 2
        halves = matrix.reshape(2, matrix.shape[0] // 2, width)
        sent = lax.dynamic_index_in_dim(halves, 1 - bit, 0, False)
        kept = lax.dynamic_index_in_dim(halves, bit, 0, False)
        matrix = (kept.astype(F32) + swap(sent, axis, step).astype(F32)).astype(BF16)
    for axis, step in reversed(steps):
        bit = lax.axis_index(axis) // step % 2
        other = swap(matrix, axis, step)
        matrix = jnp.where(
            bit == 0,
            jnp.concatenate([matrix, other], axis=0),
            jnp.concatenate([other, matrix], axis=0),
        )
    return matrix


def swap_groups(blocks, parity):
    groups = None
    if parity > 1:
        over_row = lax.axis_size("row")
        over_col = lax.axis_size("col")
        groups = [
            [r * over_col + c for r in range(over_row) for c in range(k, over_col, parity)]
            for k in range(parity)
        ]
    return lax.all_to_all(
        blocks, AXES, split_axis=0, concat_axis=0, tiled=True, axis_index_groups=groups
    )


def on_device(
    image, out_cotangent, norm0_gain, w_expand, w_depth, w_squeeze, w_excite, w_project,
    norm1_gain, w_qkv, w_out, attn_bias,
):
    rows, cols, channels = image.shape
    over_row = lax.axis_size("row")
    over_col = lax.axis_size("col")
    count = over_row * over_col
    cells_total = rows * cols * count
    stride = rows * over_row // GRID
    parity = over_col // GRID
    lines = rows // stride
    bands = cols // SIDE
    members = GRID * GRID
    expanded = w_expand.shape[1]

    def into_members(arrived):
        parted = arrived.reshape(over_row, GRID, lines, SIDE, channels)
        return parted.transpose(3, 0, 2, 1, 4).reshape(SIDE * members, channels)

    def out_of_members(values):
        parted = values.reshape(SIDE, over_row, lines, GRID, channels)
        return parted.transpose(1, 3, 2, 0, 4).reshape(-1, lines, SIDE, channels)

    row, col = lax.axis_index("row"), lax.axis_index("col")
    flags = jnp.stack([row > 0, row < over_row - 1, col > 0, col < over_col - 1]).astype(F32)
    gain_first = norm0_gain.reshape(1, channels)
    gain_second = norm1_gain.reshape(1, channels)
    w_project_t = w_project.T
    heads = attn_bias.shape[0]
    halves = channels // LANES
    bias_tall = attn_bias.transpose(0, 2, 1).reshape(halves, heads // halves * members, members)
    bias_tall = jnp.concatenate([bias_tall, bias_tall], axis=2)

    up, down = halo_rows(image, 2)
    normed_first, turned_first, spread, spread_slope = run_expand(image, gain_first, w_expand)
    up, down, out_cotangent, spread = lax.optimization_barrier((up, down, out_cotangent, spread))
    side = halo_sides(image, up, down, 2)
    cot_sent = (
        out_cotangent.reshape(lines, stride, bands, SIDE, channels)
        .transpose(1, 2, 0, 3, 4)
        .reshape(stride * bands, lines, SIDE, channels)
    )
    cot_members = into_members(swap_groups(cot_sent, parity))
    ring, act, pool = run_depthwise(count, up, down, side, gain_first, w_expand, w_depth, spread)
    pooled, hidden, gate, mixed, normed_sent = run_mix(
        cells_total, stride, hand_around(pool), w_squeeze, w_excite, act, image, w_project,
        gain_second, cot_members,
    )
    slope, side_slope = run_slope(flags, ring, w_depth, spread)
    normed_arrived = swap_groups(normed_sent, parity)
    normed_arrived, slope = lax.optimization_barrier((normed_arrived, slope))
    normed_members, attended, grad_normed, packed_grad, grad_bias = run_attention(
        normed_arrived, cot_members, w_qkv, w_out, bias_tall, heads, lines
    )
    grad_normed_home = swap_groups(grad_normed.reshape(normed_sent.shape), parity)
    weights = run_attention_weights(normed_members, packed_grad, attended, cot_members, grad_bias)
    grad_normed_home, weights = lax.optimization_barrier((grad_normed_home, weights))
    grad_mixed, grad_low, grad_norm1, grad_project, gate_grad = run_mixed_back(
        count, stride, grad_normed_home, mixed, out_cotangent, gain_second, act, gate, w_project_t
    )
    attended_sent = out_of_members(attended)
    if parity == 1:
        both = hand_around(
            jnp.concatenate([attended_sent.reshape(count, -1, channels), gate_grad], axis=1)
        )
        parts = both
        attended_home = both[:, : lines * SIDE].reshape(attended_sent.shape)
    else:
        parts = hand_around(gate_grad)
        attended_home = swap_groups(attended_sent, parity)
    up, down = halo_rows(grad_low, 1)
    side = halo_sides(grad_low, up, down, 1)
    late, grad_first, logit, pre = run_expand_back(
        cells_total, parts, hidden, gate, w_squeeze, w_excite, grad_low, up, down, side,
        w_project_t, slope, side_slope, spread_slope, spread, w_depth, turned_first, w_expand,
        gain_first, grad_norm1,
    )
    weights = sum_by_halves(jnp.concatenate([weights, grad_project], axis=1)).astype(F32)
    late = sum_shares(late).astype(F32)
    grad_image = run_image_back(
        image.reshape(-1, channels), gain_first, grad_first, grad_mixed.reshape(-1, channels)
    )
    attended_map = (
        attended_home.reshape(stride, bands, lines, SIDE, channels)
        .transpose(2, 0, 1, 3, 4)
        .reshape(rows * cols, channels)
    )
    block_out = (mixed.reshape(-1, channels).astype(F32) + dot(attended_map, w_out)).astype(BF16)

    silu = jax.nn.silu(hidden)
    grad_squeeze = pooled.reshape(expanded, 1) * pre
    grad_excite = silu.reshape(-1, 1) * logit

    ends = 4 * channels + halves * members
    grad_bias = (
        weights[:, 4 * channels : ends]
        .reshape(heads // halves, members, halves, members)
        .transpose(2, 0, 3, 1)
        .reshape(attn_bias.shape)
    )
    grad_project = (
        weights[:, ends:].reshape(BLOCK, expanded // BLOCK, channels).transpose(1, 0, 2)
    ).reshape(w_project.shape)
    tail = late[:, expanded:].reshape(-1)
    return (
        block_out.reshape(image.shape),
        grad_image.reshape(image.shape),
        tail[9 * expanded : 9 * expanded + channels],
        late[:, :expanded],
        tail[: 9 * expanded].reshape(w_depth.shape),
        grad_squeeze,
        grad_excite,
        grad_project,
        tail[9 * expanded + channels : 9 * expanded + 2 * channels],
        weights[:, : 3 * channels],
        weights[:, 3 * channels : 4 * channels],
        grad_bias,
    )


def solution(mesh):
    cells = P("row", "col", None)
    return jax.shard_map(
        on_device,
        mesh=mesh,
        in_specs=(cells, cells) + (P(),) * 10,
        out_specs=(cells, cells) + (P(),) * 10,
        check_vma=False,
    )
```

```python
import functools
import math

import jax
import jax.numpy as jnp
from jax import lax
from jax.experimental import pallas as pl
from jax.experimental.pallas import tpu as pltpu
from jax.sharding import PartitionSpec as P

GRID = 8
AXES = ("row", "col")
BLOCK = 256
LANES = 128
SIDE = 16
GELU_A = math.sqrt(2.0 / math.pi)
GELU_B = GELU_A * 0.044715
F32 = jnp.float32
BF16 = jnp.bfloat16
PARAMS = pltpu.CompilerParams(vmem_limit_bytes=56 * 1024 * 1024)


def estimate(us):
    return pl.CostEstimate(flops=int(us * 1.1e9), bytes_accessed=int(us * 3.6e6), transcendentals=0)


def dot(left, right, contract=((1,), (0,))):
    return lax.dot_general(left, right, (contract, ((), ())), preferred_element_type=F32)


def dot_exact(vector, right, contract):
    tall = jnp.broadcast_to(vector, (8, vector.shape[1]))
    product = lax.dot_general(
        tall, right, (contract, ((), ())), precision=lax.Precision.HIGHEST, preferred_element_type=F32
    )
    return product[0:1]


def gelu_and_slope(x, with_slope=True):
    square = x * x
    t = jnp.tanh(x * (GELU_A + GELU_B * square))
    half = 0.5 + 0.5 * t
    value = x * half
    if not with_slope:
        return value, None
    slope = half + (value * (1.0 - t)) * (GELU_A + (3.0 * GELU_B) * square)
    return value, slope


def norm_rows(x):
    average = jnp.mean(x, axis=-1, keepdims=True)
    centered = x - average
    variance = jnp.mean(centered * centered, axis=-1, keepdims=True)
    rstd = lax.rsqrt(variance + 1e-05)
    return centered * rstd, rstd


def norm_rows_back(unit, rstd, gain, grad):
    unit_grad = grad * gain
    first = jnp.mean(unit_grad, axis=-1, keepdims=True)
    second = jnp.mean(unit_grad * unit, axis=-1, keepdims=True)
    return rstd * (unit_grad - first - unit * second)


def fold_rows(x):
    return jnp.sum(x.reshape(x.shape[0] // 8, 8, x.shape[1]), axis=0)


def whole(shape):
    return pl.BlockSpec(shape, lambda e: (0,) * len(shape))


def last_block(shape):
    lead = (0,) * (len(shape) - 1)
    return pl.BlockSpec(shape[:-1] + (BLOCK,), lambda e: lead + (e,))


def expand_kernel(
    image_ref, gain_ref, w_exp_ref,
    normed_ref, turned_ref, spread_ref, slope_ref,
    expanded_ref,
):
    rows, cols, channels = image_ref.shape

    @pl.when(pl.program_id(0) == 0)
    def _():
        gain = gain_ref[...].astype(F32)

        @pl.loop(0, rows // 4)
        def _(c):
            flat = image_ref[pl.ds(c * 4, 4)].reshape(4 * cols, channels)
            unit, _ = norm_rows(flat.astype(F32))
            at = pl.ds(pl.multiple_of(c * 4 * cols, 16), 4 * cols)
            normed_ref[at, :] = (unit * gain).astype(BF16)

        turned_ref[...] = normed_ref[...].T

    expanded_ref[...] = dot(normed_ref[...], w_exp_ref[...])

    @pl.loop(0, rows, unroll=4)
    def _(r):
        for h in range(BLOCK // LANES):
            lanes = slice(h * LANES, (h + 1) * LANES)
            x = expanded_ref[pl.ds(pl.multiple_of(r * cols, 16), cols), lanes]
            value, slope = gelu_and_slope(x)
            spread_ref[r, :, lanes] = value.astype(BF16)
            slope_ref[r, :, lanes] = slope.astype(BF16)


def run_expand(image, gain, w_expand):
    rows, cols, channels = image.shape
    expanded = w_expand.shape[1]
    return pl.pallas_call(
        expand_kernel,
        grid=(expanded // BLOCK,),
        in_specs=[whole(image.shape), whole(gain.shape), last_block(w_expand.shape)],
        out_specs=[
            whole((rows * cols, channels)), whole((channels, rows * cols)),
            last_block((rows, cols, expanded)), last_block((rows, cols, expanded)),
        ],
        out_shape=[
            jax.ShapeDtypeStruct((rows * cols, channels), BF16),
            jax.ShapeDtypeStruct((channels, rows * cols), BF16),
            jax.ShapeDtypeStruct((rows, cols, expanded), BF16),
            jax.ShapeDtypeStruct((rows, cols, expanded), BF16),
        ],
        scratch_shapes=[pltpu.VMEM((rows * cols, BLOCK), F32)],
        compiler_params=PARAMS,
        cost_estimate=estimate(9),
        name="expand",
    )(image, gain, w_expand)


def depthwise_kernel(
    up_ref, down_ref, side_ref, gain_ref, w_exp_ref, w_dep_ref, spread_ref,
    ring_ref, act_ref, pool_ref,
    ring_normed_ref, ring_wide_ref,
):
    rows, cols, _ = spread_ref.shape
    channels = up_ref.shape[2]
    over = 4 * cols
    side = 8

    @pl.when(pl.program_id(0) == 0)
    def _():
        gain = gain_ref[...].astype(F32)

        def put(at, values):
            unit, _ = norm_rows(values.astype(F32))
            ring_normed_ref[at : at + values.shape[0], :] = (unit * gain).astype(BF16)

        put(0, up_ref[...].reshape(2 * cols, channels))
        put(2 * cols, down_ref[...].reshape(2 * cols, channels))
        put(over, side_ref[...])

    ring_wide_ref[...] = dot(ring_normed_ref[...], w_exp_ref[...])
    tile = 32

    @pl.loop(0, ring_wide_ref.shape[0] // tile, unroll=True)
    def _(t):
        at = pl.ds(pl.multiple_of(t * tile, tile), tile)
        value, _ = gelu_and_slope(ring_wide_ref[at, :], False)
        low = value.astype(BF16)
        ring_ref[at, :] = low
        ring_wide_ref[at, :] = low.astype(F32)

    for h in range(BLOCK // LANES):
        lanes = slice(h * LANES, (h + 1) * LANES)
        taps = w_dep_ref[:, :, lanes].astype(F32)
        w = [[taps[a, b : b + 1] for b in range(3)] for a in range(3)]

        def line(r, main):
            at = pl.multiple_of(over + (r + 2) * side, side)
            return jnp.concatenate([main, ring_wide_ref[pl.ds(at, side), lanes]], axis=0)

        def conv(i, x, total):
            u = [x[0] * w[0][b] + x[1] * w[1][b] + x[2] * w[2][b] for b in range(3)]
            wide = cols + side
            pre = pltpu.roll(u[0], 1, 0) + u[1] + pltpu.roll(u[2], wide - 1, 0)
            value, _ = gelu_and_slope(pre[:cols], False)
            act_ref[i, :, lanes] = value.astype(BF16)
            return total + fold_rows(value)

        def step(i, carry):
            first, second, total = carry
            third = line(i + 1, spread_ref[i + 1, :, lanes].astype(F32))
            return second, third, conv(i, (first, second, third), total)

        carry = (
            line(-1, ring_wide_ref[cols : 2 * cols, lanes]),
            line(0, spread_ref[0, :, lanes].astype(F32)),
            jnp.zeros((8, LANES), F32),
        )
        first, second, total = lax.fori_loop(0, rows - 1, step, carry, unroll=5)
        third = line(rows, ring_wide_ref[2 * cols : 3 * cols, lanes])
        total = conv(rows - 1, (first, second, third), total)
        total = jnp.sum(total, axis=0, keepdims=True)
        pool_ref[:, :, lanes] = jnp.broadcast_to(total[None], (pool_ref.shape[0], 1, LANES))


def run_depthwise(count, up, down, side, gain, w_expand, w_depth, spread):
    rows, cols, expanded = spread.shape
    channels = up.shape[2]
    ring = 4 * cols + 8 * (rows + 4)
    return pl.pallas_call(
        depthwise_kernel,
        grid=(expanded // BLOCK,),
        in_specs=[
            whole(up.shape), whole(down.shape), whole(side.shape), whole(gain.shape),
            last_block(w_expand.shape), last_block(w_depth.shape), last_block(spread.shape),
        ],
        out_specs=[
            last_block((ring, expanded)), last_block(spread.shape), last_block((count, 1, expanded)),
        ],
        out_shape=[
            jax.ShapeDtypeStruct((ring, expanded), BF16),
            jax.ShapeDtypeStruct(spread.shape, BF16),
            jax.ShapeDtypeStruct((count, 1, expanded), F32),
        ],
        scratch_shapes=[pltpu.VMEM((ring, channels), BF16), pltpu.VMEM((ring, BLOCK), F32)],
        compiler_params=PARAMS,
        cost_estimate=estimate(9),
        name="depthwise",
    )(up, down, side, gain, w_expand, w_depth, spread)


def slope_kernel(flags_ref, ring_ref, w_dep_ref, spread_ref, main_ref, side_out_ref, wide_ref):
    rows, cols, _ = spread_ref.shape
    over = 4 * cols
    side = 8
    wide = cols + side

    for k, r in enumerate((0, 1, rows + 2, rows + 3)):
        wide_ref[r, :cols, :] = ring_ref[k * cols : (k + 1) * cols, :].astype(F32)
    sides = ring_ref[over:, :].astype(F32)
    for r in range(rows + 4):
        wide_ref[r, cols:, :] = sides[r * side : (r + 1) * side]

    @pl.loop(0, rows)
    def _(r):
        wide_ref[r + 2, :cols, :] = spread_ref[r].astype(F32)

    place = lax.broadcasted_iota(jnp.int32, (side, LANES), 0)
    side_mask = jnp.where(
        place == side - 1, flags_ref[2], jnp.where(place == 0, flags_ref[3], 1.0)
    ).astype(F32)

    @pl.loop(0, rows + 2)
    def _(i):
        keep = jnp.where(i == 0, flags_ref[0], jnp.where(i == rows + 1, flags_ref[1], 1.0))
        for h in range(BLOCK // LANES):
            lanes = slice(h * LANES, (h + 1) * LANES)
            taps = w_dep_ref[:, :, lanes].astype(F32)
            x = [wide_ref[i + a, :, lanes] for a in range(3)]
            u = [sum(x[a] * taps[a, b : b + 1] for a in range(3)) for b in range(3)]
            pre = pltpu.roll(u[0], 1, 0) + u[1] + pltpu.roll(u[2], wide - 1, 0)
            _, slope = gelu_and_slope(pre)
            slope = slope * keep
            main_ref[i, :, lanes] = slope[:cols].astype(BF16)
            side_out_ref[i, :, lanes] = slope[cols:] * side_mask


def run_slope(flags, ring, w_depth, spread):
    rows, cols, expanded = spread.shape
    return pl.pallas_call(
        slope_kernel,
        grid=(expanded // BLOCK,),
        in_specs=[
            pl.BlockSpec(memory_space=pltpu.SMEM),
            last_block(ring.shape), last_block(w_depth.shape), last_block(spread.shape),
        ],
        out_specs=[last_block((rows + 2, cols, expanded)), last_block((rows + 2, 8, expanded))],
        out_shape=[
            jax.ShapeDtypeStruct((rows + 2, cols, expanded), BF16),
            jax.ShapeDtypeStruct((rows + 2, 8, expanded), F32),
        ],
        scratch_shapes=[pltpu.VMEM((rows + 4, cols + 8, BLOCK), F32)],
        compiler_params=PARAMS,
        cost_estimate=estimate(13),
        name="slope",
    )(flags, ring, w_depth, spread)


def mix_kernel(
    cells_total, stride, bands,
    parts_ref, w_sq_ref, w_ex_ref, act_ref, image_ref, w_proj_ref, gain_ref, after_ref,
    pooled_ref, hidden_ref, gate_ref, mixed_ref, send_ref,
):
    step = pl.program_id(0)

    @pl.when(step == 0)
    def _():
        pooled = jnp.sum(parts_ref[...], axis=0) / cells_total
        hidden = dot_exact(pooled, w_sq_ref[...].astype(F32), ((1,), (0,)))
        silu = hidden * jax.nn.sigmoid(hidden)
        pooled_ref[...] = pooled
        hidden_ref[...] = hidden
        gate_ref[...] = jax.nn.sigmoid(dot_exact(silu, w_ex_ref[...].astype(F32), ((1,), (0,))))

    lines, cols, channels = image_ref.shape
    flat = act_ref[...].reshape(lines * cols, act_ref.shape[2])
    gated = (flat.astype(F32) * gate_ref[...]).astype(BF16)
    product = dot(gated, w_proj_ref[...])
    mixed = (image_ref[...].reshape(lines * cols, channels).astype(F32) + product).astype(BF16)
    mixed_ref[...] = mixed.reshape(lines, cols, channels)
    unit, _ = norm_rows(mixed.astype(F32))
    normed = (unit * gain_ref[...].astype(F32)).astype(BF16)
    for k in range(lines):
        line = step * lines + k
        for band in range(bands):
            start = k * cols + band * SIDE
            send_ref[lax.rem(line, stride) * bands + band, line // stride] = normed[
                start : start + SIDE
            ]


def run_mix(cells_total, stride, parts, w_squeeze, w_excite, act, image, w_project, gain, after):
    rows, cols, channels = image.shape
    expanded = act.shape[2]
    lines = 4
    bands = cols // SIDE
    block = lambda width: pl.BlockSpec((lines, cols, width), lambda r: (r, 0, 0))
    send = (stride * bands, rows // stride, SIDE, channels)
    return pl.pallas_call(
        functools.partial(mix_kernel, cells_total, stride, bands),
        grid=(rows // lines,),
        in_specs=[
            whole(parts.shape), whole(w_squeeze.shape), whole(w_excite.shape),
            block(expanded), block(channels), whole(w_project.shape), whole(gain.shape),
            pl.BlockSpec(memory_space=pl.ANY),
        ],
        out_specs=[
            whole((1, expanded)), whole((1, w_squeeze.shape[1])), whole((1, expanded)),
            block(channels), whole(send),
        ],
        out_shape=[
            jax.ShapeDtypeStruct((1, expanded), F32),
            jax.ShapeDtypeStruct((1, w_squeeze.shape[1]), F32),
            jax.ShapeDtypeStruct((1, expanded), F32),
            jax.ShapeDtypeStruct(image.shape, BF16),
            jax.ShapeDtypeStruct(send, BF16),
        ],
        compiler_params=PARAMS,
        cost_estimate=estimate(5),
        name="mix",
    )(parts, w_squeeze, w_excite, act, image, w_project, gain, after)


def attention_kernel(
    members, heads, lines,
    arrived_ref, cot_ref, w_qkv_ref, w_out_ref, bias_ref,
    x_ref, att_ref, grad_ref, packed_grad_ref, bias_out_ref,
    order_ref, packed_ref, att_grad_ref, bias_sum_ref,
):
    cells, channels = x_ref.shape
    groups = cells // members

    def places():
        for g in range(groups):
            for m in range(0, members, GRID):
                line, row = (m // GRID) % lines, m // GRID // lines
                start = (row * GRID * lines + line) * groups + g
                yield g * members + m, pl.ds(start, GRID, stride=lines * groups)

    for half in range(channels // LANES):
        lanes = slice(half * LANES, (half + 1) * LANES)
        order_ref[half] = arrived_ref[:, lanes].astype(F32)
        for g in range(groups):
            pieces = [order_ref[half, at, :] for k, at in places() if k // members == g]
            at = slice(g * members, (g + 1) * members)
            x_ref[at, lanes] = jnp.concatenate(pieces, axis=0).astype(BF16)
    dim = channels // heads
    per_half = LANES // dim
    halves = channels // LANES
    scale = dim ** (-0.5)
    packed_ref[...] = dot(x_ref[...], w_qkv_ref[...]).astype(BF16)
    att_grad_ref[...] = dot(cot_ref[...], w_out_ref[...], ((1,), (1,))).astype(BF16)
    bias_sum_ref[...] = jnp.zeros(bias_sum_ref.shape, F32)
    tall = per_half * members
    mask = (
        lax.broadcasted_iota(jnp.int32, (tall, LANES), 0) // members
        == lax.broadcasted_iota(jnp.int32, (tall, LANES), 1) // dim
    ).astype(F32).astype(BF16)
    owner = lax.broadcasted_iota(jnp.int32, (members, 2 * LANES), 1) % LANES // dim
    zero = jnp.zeros((members, LANES), BF16)

    def by_head(pair):
        return jnp.concatenate(
            [jnp.concatenate([v] * per_half, axis=0) * mask for v in pair], axis=1
        )

    def diagonal(pair):
        return jnp.concatenate(
            [
                jnp.concatenate([pair[0], zero], axis=1),
                jnp.concatenate([zero, pair[1]], axis=1),
            ],
            axis=0,
        )

    def collect(v):
        parts = [v[h * members : (h + 1) * members] for h in range(per_half)]
        picked = parts[-1]
        for h in range(per_half - 1):
            picked = jnp.where(owner == h, parts[h], picked)
        return [picked[:, :LANES], picked[:, LANES:]]

    def blocks(v):
        return [v[:members, :LANES], v[members:, LANES:]]

    def over_members(v, reduce):
        parted = v.reshape(per_half, members, 2 * members)
        small = reduce(parted, axis=1, keepdims=True)
        return jnp.broadcast_to(small, parted.shape).reshape(v.shape)

    def pair_step(g, carry):
        at = [pl.ds(pl.multiple_of((2 * g + k) * members, 16), members) for k in range(2)]
        for half in range(halves):
            def lanes(part):
                start = part * channels + half * LANES
                return slice(start, start + LANES)

            q, k, v = ([packed_ref[at[n], lanes(part)] for n in range(2)] for part in range(3))
            cot = [att_grad_ref[at[n], lanes(0)] for n in range(2)]
            q_diag, cot_diag = diagonal(q), diagonal(cot)
            k_tall, v_tall = by_head(k), by_head(v)
            scores = dot(k_tall, q_diag, ((1,), (1,))) * scale + bias_ref[half]
            grad_probs = dot(v_tall, cot_diag, ((1,), (1,)))
            lifted = jnp.exp(scores - over_members(scores, jnp.max))
            soft = lifted * (1.0 / over_members(lifted, jnp.sum))
            soft_low = soft.astype(BF16)
            grad_scores = soft * (grad_probs - over_members(grad_probs * soft, jnp.sum))
            bias_sum_ref[half] += grad_scores
            scaled = (grad_scores * scale).astype(BF16)
            attended = blocks(dot(soft_low, v_tall, ((0,), (0,))))
            grad_q = blocks(dot(scaled, k_tall, ((0,), (0,))))
            grad_v = collect(dot(soft_low, cot_diag))
            grad_k = collect(dot(scaled, q_diag))
            for n in range(2):
                att_ref[at[n], lanes(0)] = attended[n].astype(BF16)
                for part, value in enumerate((grad_q, grad_k, grad_v)):
                    packed_grad_ref[at[n], lanes(part)] = value[n].astype(BF16)
        return carry

    lax.fori_loop(0, cells // members // 2, pair_step, 0, unroll=2)
    grad = dot(packed_grad_ref[...], w_qkv_ref[...], ((1,), (1,)))
    for half in range(halves):
        lanes = slice(half * LANES, (half + 1) * LANES)
        for k, at in places():
            order_ref[half, at, :] = grad[k : k + GRID, lanes]
        grad_ref[:, lanes] = order_ref[half].astype(BF16)
    for half in range(halves):
        both = bias_sum_ref[half]
        bias_out_ref[half] = both[:, :members] + both[:, members:]


def run_attention(arrived, cot, w_qkv, w_out, bias_tall, heads, lines):
    cells, channels = cot.shape
    halves, tall, members2 = bias_tall.shape
    members = members2 // 2
    vmem = pl.BlockSpec(memory_space=pltpu.VMEM)
    return pl.pallas_call(
        functools.partial(attention_kernel, members, heads, lines),
        in_specs=[vmem] * 5,
        out_specs=[vmem] * 5,
        out_shape=[
            jax.ShapeDtypeStruct((cells, channels), BF16),
            jax.ShapeDtypeStruct((cells, channels), BF16),
            jax.ShapeDtypeStruct((cells, channels), BF16),
            jax.ShapeDtypeStruct((cells, 3 * channels), BF16),
            jax.ShapeDtypeStruct((halves, tall, members), F32),
        ],
        scratch_shapes=[
            pltpu.VMEM((channels // LANES, cells, LANES), F32),
            pltpu.VMEM((cells, 3 * channels), BF16),
            pltpu.VMEM((cells, channels), BF16),
            pltpu.VMEM(bias_tall.shape, F32),
        ],
        compiler_params=PARAMS,
        cost_estimate=estimate(14),
        name="attention",
    )(arrived.reshape(cells, channels), cot, w_qkv, w_out, bias_tall)


def attention_weights_kernel(x_ref, packed_grad_ref, att_ref, cot_ref, bias_ref, out_ref):
    channels = x_ref.shape[1]
    wide = 3 * channels
    out_ref[:, :wide] = dot(x_ref[...], packed_grad_ref[...], ((0,), (0,))).astype(BF16)
    out_ref[:, wide : wide + channels] = dot(att_ref[...], cot_ref[...], ((0,), (0,))).astype(BF16)
    bias = jnp.concatenate([bias_ref[half] for half in range(bias_ref.shape[0])], axis=1)
    out_ref[:, wide + channels :] = bias.astype(BF16)


def run_attention_weights(x, packed_grad, att, cot, bias):
    channels = x.shape[1]
    vmem = pl.BlockSpec(memory_space=pltpu.VMEM)
    width = 4 * channels + bias.shape[0] * bias.shape[2]
    return pl.pallas_call(
        attention_weights_kernel,
        in_specs=[vmem] * 5,
        out_specs=vmem,
        out_shape=jax.ShapeDtypeStruct((channels, width), BF16),
        compiler_params=PARAMS,
        cost_estimate=estimate(5),
        name="attention_weights",
    )(x, packed_grad, att, cot, bias)


def mixed_back_kernel(
    stride, bands,
    recv_ref, mixed_ref, cot_ref, gain_ref, act_ref, gate_ref, w_projt_ref,
    grad_ref, low_ref, norm_ref, project_ref, gate_grad_ref,
    turned_ref, total_ref,
):
    rows, cols, channels = mixed_ref.shape

    @pl.when(pl.program_id(0) == 0)
    def _():
        gain = gain_ref[...].astype(F32)
        lines = 4

        def some_rows(c, total):
            pieces = []
            for k in range(lines):
                i = c * lines + k
                a, p = lax.rem(i, stride), i // stride
                pieces += [recv_ref[a * bands + band, p] for band in range(bands)]
            grad = jnp.concatenate(pieces, axis=0).astype(F32)
            at = pl.ds(c * lines, lines)
            flat = lambda ref: ref[at].reshape(lines * cols, channels).astype(F32)
            unit, rstd = norm_rows(flat(mixed_ref))
            back = flat(cot_ref) + norm_rows_back(unit, rstd, gain, grad)
            grad_ref[at] = back.reshape(lines, cols, channels)
            low_ref[at] = back.astype(BF16).reshape(lines, cols, channels)
            return total + fold_rows(grad * unit)

        total = lax.fori_loop(
            0, rows // lines, some_rows, jnp.zeros((8, channels), F32), unroll=2
        )
        norm_ref[...] = jnp.sum(total, axis=0, keepdims=True)
        turned_ref[...] = low_ref[...].reshape(rows * cols, channels).T

    flat = act_ref[...].reshape(rows * cols, BLOCK)
    product = dot(turned_ref[...], flat)
    total = jnp.sum(product * w_projt_ref[...].astype(F32), axis=0, keepdims=True)
    step, steps = pl.program_id(0), pl.num_programs(0)
    total_ref[step] = total
    project_ref[...] = (product * gate_ref[...]).T.astype(BF16)

    @pl.when(step == steps - 1)
    def _():
        sums = [total_ref[e] for e in range(total_ref.shape[0])]
        high = [v.astype(BF16).astype(F32) for v in sums]
        terms = jnp.concatenate(high + [v - w for v, w in zip(sums, high)], axis=0)
        gate_grad_ref[...] = jnp.broadcast_to(terms.astype(BF16)[None], gate_grad_ref.shape)


def run_mixed_back(count, stride, recv, mixed, cot, gain, act, gate, w_project_t):
    rows, cols, channels = mixed.shape
    expanded = act.shape[2]
    return pl.pallas_call(
        functools.partial(mixed_back_kernel, stride, cols // SIDE),
        grid=(expanded // BLOCK,),
        in_specs=[
            whole(recv.shape), whole(mixed.shape), whole(cot.shape), whole(gain.shape),
            last_block(act.shape), last_block(gate.shape), last_block(w_project_t.shape),
        ],
        out_specs=[
            whole(mixed.shape), whole(mixed.shape), whole((1, channels)),
            last_block((BLOCK, expanded)), whole((count, 2 * expanded // BLOCK, BLOCK)),
        ],
        out_shape=[
            jax.ShapeDtypeStruct(mixed.shape, F32),
            jax.ShapeDtypeStruct(mixed.shape, BF16),
            jax.ShapeDtypeStruct((1, channels), F32),
            jax.ShapeDtypeStruct((BLOCK, expanded), BF16),
            jax.ShapeDtypeStruct((count, 2 * expanded // BLOCK, BLOCK), BF16),
        ],
        scratch_shapes=[
            pltpu.VMEM((channels, rows * cols), BF16),
            pltpu.VMEM((expanded // BLOCK, 1, BLOCK), F32),
        ],
        compiler_params=PARAMS,
        cost_estimate=estimate(7),
        name="mixed_back",
    )(recv, mixed, cot, gain, act, gate, w_project_t)


def expand_back_kernel(
    cells_total,
    parts_ref, hidden_ref, gate_all_ref, w_sq_ref, w_ex_ref,
    low_ref, up_ref, down_ref, side_ref, w_projt_ref, gate_ref, slope_ref, side_slope_ref,
    spread_slope_ref, spread_ref, w_dep_ref, turned_ref, w_exp_ref, gain_ref, norm1_ref,
    weights_ref, first_ref, logit_ref, pre_ref,
    main_ref, side_grad_ref, window_ref, expanded_ref, pool_ref, tail_ref, norm_ref,
):
    rows, cols, channels = low_ref.shape
    side = 8
    wide = cols + side
    step = pl.program_id(0)
    steps = pl.num_programs(0)

    @pl.when(step == 0)
    def _():
        gate = gate_all_ref[...]
        len_e = pool_ref.shape[0]
        terms = jnp.sum(parts_ref[...].astype(F32), axis=0)
        gate_grad = jnp.concatenate(
            [terms[e : e + 1] + terms[len_e + e : len_e + e + 1] for e in range(len_e)],
            axis=1,
        )
        logit = gate_grad * gate * (1.0 - gate)
        hidden = hidden_ref[...]
        sig = jax.nn.sigmoid(hidden)
        pre = dot_exact(logit, w_ex_ref[...].astype(F32), ((1,), (1,))) * (
            sig + hidden * sig * (1.0 - sig)
        )
        logit_ref[...] = logit
        pre_ref[...] = pre
        pooled = dot_exact(pre, w_sq_ref[...].astype(F32), ((1,), (1,))) / cells_total
        for e in range(pool_ref.shape[0]):
            pool_ref[e] = pooled[:, e * BLOCK : (e + 1) * BLOCK]
        first_ref[...] = jnp.zeros(first_ref.shape, F32)
        tail_ref[...] = jnp.zeros(tail_ref.shape, F32)
        norm_ref[...] = jnp.zeros(norm_ref.shape, F32)

    w_projt = w_projt_ref[...]
    main_ref[pl.ds(0, cols), :] = dot(up_ref[0], w_projt)
    main_ref[pl.ds(cols, rows * cols), :] = dot(
        low_ref[...].reshape(rows * cols, channels), w_projt
    )
    main_ref[pl.ds((rows + 1) * cols, cols), :] = dot(down_ref[0], w_projt)
    side_grad_ref[...] = dot(side_ref[...], w_projt)

    @pl.loop(0, rows + 2, unroll=3)
    def _(i):
        for h in range(BLOCK // LANES):
            lanes = slice(h * LANES, (h + 1) * LANES)
            gate = gate_ref[:, lanes]
            pooled = pool_ref[step][:, lanes]
            gated = main_ref[pl.ds(pl.multiple_of(i * cols, 16), cols), lanes]
            main = (gated * gate + pooled) * slope_ref[i, :, lanes].astype(F32)
            gated = side_grad_ref[pl.ds(pl.multiple_of(i * side, side), side), lanes]
            edge = (gated * gate + pooled) * side_slope_ref[i, :, lanes]
            grad = jnp.concatenate([main, edge], axis=0)
            grad = grad.astype(BF16).astype(F32)
            window_ref[0, i, :, lanes] = pltpu.roll(grad, wide - 1, 0)[:cols]
            window_ref[1, i, :, lanes] = grad[:cols]
            window_ref[2, i, :, lanes] = pltpu.roll(grad, 1, 0)[:cols]

    for h in range(BLOCK // LANES):
        lanes = slice(h * LANES, (h + 1) * LANES)
        taps = w_dep_ref[:, :, lanes].astype(F32)

        def back_row(i, sums):
            spread = spread_ref[i, :, lanes].astype(F32)
            total = jnp.zeros((cols, LANES), F32)
            new_sums = []
            for a in range(3):
                for b in range(3):
                    window = window_ref[b, i + 2 - a, :, lanes]
                    total = total + window * taps[a, b : b + 1]
                    new_sums.append(sums[a * 3 + b] + fold_rows(window * spread))
            grad = total * spread_slope_ref[i, :, lanes].astype(F32)
            expanded_ref[pl.ds(pl.multiple_of(i * cols, 16), cols), lanes] = grad.astype(BF16)
            return tuple(new_sums)

        sums = lax.fori_loop(0, rows, back_row, (jnp.zeros((8, LANES), F32),) * 9, unroll=2)
        for t in range(9):
            row = t * (steps * BLOCK // LANES) + step * (BLOCK // LANES) + h
            tail_ref[pl.ds(row, 1), :] = jnp.sum(sums[t], axis=0, keepdims=True)

    grad_expanded = expanded_ref[...]
    w_exp = w_exp_ref[...]
    weights = dot(turned_ref[...], grad_expanded)
    weights_ref[:, pl.ds(pl.multiple_of(step * BLOCK, BLOCK), BLOCK)] = weights.astype(BF16)
    norm_ref[...] += jnp.sum(weights * w_exp.astype(F32), axis=1, keepdims=True)
    first_ref[...] += dot(grad_expanded, w_exp, ((1,), (1,)))

    @pl.when(step == steps - 1)
    def _():
        norm = norm_ref[...].T[0:1] / gain_ref[...].astype(F32)
        start = 9 * steps * (BLOCK // LANES)
        for k in range(channels // LANES):
            piece = slice(k * LANES, (k + 1) * LANES)
            tail_ref[start + k : start + k + 1, :] = norm[:, piece]
            at = start + channels // LANES + k
            tail_ref[at : at + 1, :] = norm1_ref[:, piece]
        weights_ref[:, steps * BLOCK :] = tail_ref[...].astype(BF16)


def run_expand_back(
    cells_total, parts, hidden, gate, w_squeeze, w_excite, low, up, down, side,
    w_project_t, slope, side_slope, spread_slope, spread, w_depth, turned, w_expand, gain, norm1,
):
    rows, cols, channels = low.shape
    expanded = w_expand.shape[1]
    steps = expanded // BLOCK
    return pl.pallas_call(
        functools.partial(expand_back_kernel, cells_total),
        grid=(steps,),
        in_specs=[
            pl.BlockSpec(
                (parts.shape[0], 2 * steps, BLOCK), lambda e: (0, parts.shape[1] // (2 * steps) - 1, 0)
            ),
            whole(hidden.shape), whole(gate.shape),
            whole(w_squeeze.shape), whole(w_excite.shape),
            whole(low.shape), whole(up.shape), whole(down.shape), whole(side.shape),
            last_block(w_project_t.shape), last_block(gate.shape), last_block(slope.shape),
            last_block(side_slope.shape), last_block(spread_slope.shape), last_block(spread.shape),
            last_block(w_depth.shape), whole(turned.shape), last_block(w_expand.shape),
            whole(gain.shape), whole(norm1.shape),
        ],
        out_specs=[
            whole((channels, expanded + LANES)), whole((rows * cols, channels)),
            whole((1, expanded)), whole(hidden.shape),
        ],
        out_shape=[
            jax.ShapeDtypeStruct((channels, expanded + LANES), BF16),
            jax.ShapeDtypeStruct((rows * cols, channels), F32),
            jax.ShapeDtypeStruct((1, expanded), F32),
            jax.ShapeDtypeStruct(hidden.shape, F32),
        ],
        scratch_shapes=[
            pltpu.VMEM(((rows + 2) * cols, BLOCK), F32),
            pltpu.VMEM(((rows + 2) * 8, BLOCK), F32),
            pltpu.VMEM((3, rows + 2, cols, BLOCK), F32),
            pltpu.VMEM((rows * cols, BLOCK), BF16),
            pltpu.VMEM((steps, 1, BLOCK), F32),
            pltpu.VMEM((channels, LANES), F32),
            pltpu.VMEM((channels, LANES), F32),
        ],
        compiler_params=PARAMS,
        cost_estimate=estimate(14),
        name="expand_back",
    )(
        parts, hidden, gate, w_squeeze, w_excite, low, up, down, side, w_project_t, gate,
        slope, side_slope, spread_slope, spread, w_depth, turned, w_expand, gain, norm1,
    )


def image_back_kernel(image_ref, gain_ref, first_ref, mixed_ref, out_ref):
    unit, rstd = norm_rows(image_ref[...].astype(F32))
    grad = first_ref[...]
    back = mixed_ref[...] + norm_rows_back(unit, rstd, gain_ref[...].astype(F32), grad)
    out_ref[...] = back.astype(BF16)


def run_image_back(image, gain, first, mixed):
    cells, channels = image.shape
    block = pl.BlockSpec((cells // 4, channels), lambda r: (r, 0))
    return pl.pallas_call(
        image_back_kernel,
        grid=(4,),
        in_specs=[block, whole(gain.shape), block, block],
        out_specs=block,
        out_shape=jax.ShapeDtypeStruct((cells, channels), BF16),
        compiler_params=PARAMS,
        cost_estimate=estimate(4),
        name="image_back",
    )(image, gain, first, mixed)


def shift(cells, axis, step):
    count = lax.axis_size(axis)
    pairs = [(i, i + step) for i in range(count) if 0 <= i + step < count]
    return lax.ppermute(cells, axis, pairs)


def halo_rows(cells, width):
    up = shift(cells[cells.shape[0] - width :], "row", 1)
    down = shift(cells[:width], "row", -1)
    return up, down


def halo_sides(cells, up, down, width):
    rows, cols, channels = cells.shape
    first = jnp.concatenate([up[:, :width], cells[:, :width], down[:, :width]], axis=0)
    last = jnp.concatenate(
        [up[:, cols - width :], cells[:, cols - width :], down[:, cols - width :]], axis=0
    )
    left = shift(last, "col", 1)
    right = shift(first, "col", -1)
    gap = jnp.zeros((rows + 2 * width, 8 - 2 * width, channels), cells.dtype)
    side = jnp.concatenate([right, gap, left], axis=1)
    return side.reshape(-1, channels)


def hand_around(blocks):
    return lax.all_to_all(blocks, AXES, split_axis=0, concat_axis=0, tiled=True)


def sum_shares(matrix):
    rows, columns = matrix.shape
    count = lax.axis_size("row") * lax.axis_size("col")
    share = rows // count
    arrived = hand_around(matrix.reshape(count, share, columns))
    total = jnp.sum(arrived.astype(F32), axis=0).astype(BF16)
    sent = jnp.broadcast_to(total[None], (count, share, columns))
    return hand_around(sent).reshape(rows, columns)


def cube_steps():
    steps = [("col", 1)]
    for axis in ("row", "col"):
        step = 1 if axis == "row" else 2
        while step < lax.axis_size(axis):
            steps.append((axis, step))
            step *= 2
    return steps


def sum_by_halves(matrix, after):
    width = matrix.shape[1]

    def swap(v, axis, step):
        return lax.ppermute(v, axis, [(i, i ^ step) for i in range(lax.axis_size(axis))])

    steps = cube_steps()
    for k, (axis, step) in enumerate(steps):
        if k in after:
            matrix, _ = lax.optimization_barrier((matrix, after[k]))
        bit = lax.axis_index(axis) // step % 2
        halves = matrix.reshape(2, matrix.shape[0] // 2, width)
        sent = lax.dynamic_index_in_dim(halves, 1 - bit, 0, False)
        kept = lax.dynamic_index_in_dim(halves, bit, 0, False)
        matrix = (kept.astype(F32) + swap(sent, axis, step).astype(F32)).astype(BF16)
    for axis, step in reversed(steps):
        bit = lax.axis_index(axis) // step % 2
        other = swap(matrix, axis, step)
        matrix = jnp.where(
            bit == 0,
            jnp.concatenate([matrix, other], axis=0),
            jnp.concatenate([other, matrix], axis=0),
        )
    return matrix


def swap_groups(blocks, parity):
    groups = None
    if parity > 1:
        over_row = lax.axis_size("row")
        over_col = lax.axis_size("col")
        groups = [
            [r * over_col + c for r in range(over_row) for c in range(k, over_col, parity)]
            for k in range(parity)
        ]
    return lax.all_to_all(
        blocks, AXES, split_axis=0, concat_axis=0, tiled=True, axis_index_groups=groups
    )


def on_device(
    image, out_cotangent, norm0_gain, w_expand, w_depth, w_squeeze, w_excite, w_project,
    norm1_gain, w_qkv, w_out, attn_bias,
):
    rows, cols, channels = image.shape
    over_row = lax.axis_size("row")
    over_col = lax.axis_size("col")
    count = over_row * over_col
    cells_total = rows * cols * count
    stride = rows * over_row // GRID
    parity = over_col // GRID
    lines = rows // stride
    bands = cols // SIDE
    members = GRID * GRID
    expanded = w_expand.shape[1]

    def into_members(arrived):
        parted = arrived.reshape(over_row, GRID, lines, SIDE, channels)
        return parted.transpose(3, 0, 2, 1, 4).reshape(SIDE * members, channels)

    def out_of_members(values):
        parted = values.reshape(SIDE, over_row, lines, GRID, channels)
        return parted.transpose(1, 3, 2, 0, 4).reshape(-1, lines, SIDE, channels)

    row, col = lax.axis_index("row"), lax.axis_index("col")
    flags = jnp.stack([row > 0, row < over_row - 1, col > 0, col < over_col - 1]).astype(F32)
    gain_first = norm0_gain.reshape(1, channels)
    gain_second = norm1_gain.reshape(1, channels)
    w_project_t = w_project.T
    heads = attn_bias.shape[0]
    halves = channels // LANES
    bias_tall = attn_bias.transpose(0, 2, 1).reshape(halves, heads // halves * members, members)
    bias_tall = jnp.concatenate([bias_tall, bias_tall], axis=2)

    up, down = halo_rows(image, 2)
    normed_first, turned_first, spread, spread_slope = run_expand(image, gain_first, w_expand)
    up, down, spread = lax.optimization_barrier((up, down, spread))
    side = halo_sides(image, up, down, 2)
    cot_sent = (
        out_cotangent.reshape(lines, stride, bands, SIDE, channels)
        .transpose(1, 2, 0, 3, 4)
        .reshape(stride * bands, lines, SIDE, channels)
    )
    cot_members = into_members(swap_groups(cot_sent, parity))
    ring, act, pool = run_depthwise(count, up, down, side, gain_first, w_expand, w_depth, spread)
    pooled, hidden, gate, mixed, normed_sent = run_mix(
        cells_total, stride, hand_around(pool), w_squeeze, w_excite, act, image, w_project,
        gain_second, cot_members,
    )
    slope, side_slope = run_slope(flags, ring, w_depth, spread)
    normed_arrived = swap_groups(normed_sent, parity)
    normed_arrived, slope = lax.optimization_barrier((normed_arrived, slope))
    normed_members, attended, grad_normed, packed_grad, grad_bias = run_attention(
        normed_arrived, cot_members, w_qkv, w_out, bias_tall, heads, lines
    )
    grad_normed_home = swap_groups(grad_normed.reshape(normed_sent.shape), parity)
    weights = run_attention_weights(normed_members, packed_grad, attended, cot_members, grad_bias)
    grad_normed_home, weights = lax.optimization_barrier((grad_normed_home, weights))
    grad_mixed, grad_low, grad_norm1, grad_project, gate_grad = run_mixed_back(
        count, stride, grad_normed_home, mixed, out_cotangent, gain_second, act, gate, w_project_t
    )
    attended_sent = out_of_members(attended)
    if parity == 1:
        both = hand_around(
            jnp.concatenate([attended_sent.reshape(count, -1, channels), gate_grad], axis=1)
        )
        parts = both
        attended_home = both[:, : lines * SIDE].reshape(attended_sent.shape)
    else:
        parts = hand_around(gate_grad)
        attended_home = swap_groups(attended_sent, parity)
    up, down = halo_rows(grad_low, 1)
    side = halo_sides(grad_low, up, down, 1)
    late, grad_first, logit, pre = run_expand_back(
        cells_total, parts, hidden, gate, w_squeeze, w_excite, grad_low, up, down, side,
        w_project_t, slope, side_slope, spread_slope, spread, w_depth, turned_first, w_expand,
        gain_first, grad_norm1,
    )
    weights = sum_by_halves(
        jnp.concatenate([weights, grad_project], axis=1), {0: up, 2: late}
    ).astype(F32)
    late = sum_shares(late).astype(F32)
    grad_image = run_image_back(
        image.reshape(-1, channels), gain_first, grad_first, grad_mixed.reshape(-1, channels)
    )
    attended_map = (
        attended_home.reshape(stride, bands, lines, SIDE, channels)
        .transpose(2, 0, 1, 3, 4)
        .reshape(rows * cols, channels)
    )
    block_out = (mixed.reshape(-1, channels).astype(F32) + dot(attended_map, w_out)).astype(BF16)

    silu = jax.nn.silu(hidden)
    grad_squeeze = pooled.reshape(expanded, 1) * pre
    grad_excite = silu.reshape(-1, 1) * logit

    ends = 4 * channels + halves * members
    grad_bias = (
        weights[:, 4 * channels : ends]
        .reshape(heads // halves, members, halves, members)
        .transpose(2, 0, 3, 1)
        .reshape(attn_bias.shape)
    )
    grad_project = (
        weights[:, ends:].reshape(BLOCK, expanded // BLOCK, channels).transpose(1, 0, 2)
    ).reshape(w_project.shape)
    tail = late[:, expanded:].reshape(-1)
    return (
        block_out.reshape(image.shape),
        grad_image.reshape(image.shape),
        tail[9 * expanded : 9 * expanded + channels],
        late[:, :expanded],
        tail[: 9 * expanded].reshape(w_depth.shape),
        grad_squeeze,
        grad_excite,
        grad_project,
        tail[9 * expanded + channels : 9 * expanded + 2 * channels],
        weights[:, : 3 * channels],
        weights[:, 3 * channels : 4 * channels],
        grad_bias,
    )


def solution(mesh):
    cells = P("row", "col", None)
    return jax.shard_map(
        on_device,
        mesh=mesh,
        in_specs=(cells, cells) + (P(),) * 10,
        out_specs=(cells, cells) + (P(),) * 10,
        check_vma=False,
    )
```

```python
import functools
import math

import jax
import jax.numpy as jnp
from jax import lax
from jax.experimental import pallas as pl
from jax.experimental.pallas import tpu as pltpu
from jax.sharding import PartitionSpec as P

GRID = 8
AXES = ("row", "col")
BLOCK = 256
LANES = 128
SIDE = 16
GELU_A = math.sqrt(2.0 / math.pi)
GELU_B = GELU_A * 0.044715
F32 = jnp.float32
BF16 = jnp.bfloat16
PARAMS = pltpu.CompilerParams(vmem_limit_bytes=56 * 1024 * 1024)


def estimate(us):
    return pl.CostEstimate(flops=int(us * 1.1e9), bytes_accessed=int(us * 3.6e6), transcendentals=0)


def dot(left, right, contract=((1,), (0,))):
    return lax.dot_general(left, right, (contract, ((), ())), preferred_element_type=F32)


def dot_exact(vector, right, contract):
    tall = jnp.broadcast_to(vector, (8, vector.shape[1]))
    product = lax.dot_general(
        tall, right, (contract, ((), ())), precision=lax.Precision.HIGHEST, preferred_element_type=F32
    )
    return product[0:1]


def gelu_and_slope(x, with_slope=True):
    square = x * x
    t = jnp.tanh(x * (GELU_A + GELU_B * square))
    half = 0.5 + 0.5 * t
    value = x * half
    if not with_slope:
        return value, None
    slope = half + (value * (1.0 - t)) * (GELU_A + (3.0 * GELU_B) * square)
    return value, slope


def norm_rows(x):
    average = jnp.mean(x, axis=-1, keepdims=True)
    centered = x - average
    variance = jnp.mean(centered * centered, axis=-1, keepdims=True)
    rstd = lax.rsqrt(variance + 1e-05)
    return centered * rstd, rstd


def norm_rows_back(unit, rstd, gain, grad):
    unit_grad = grad * gain
    first = jnp.mean(unit_grad, axis=-1, keepdims=True)
    second = jnp.mean(unit_grad * unit, axis=-1, keepdims=True)
    return rstd * (unit_grad - first - unit * second)


def fold_rows(x):
    return jnp.sum(x.reshape(x.shape[0] // 8, 8, x.shape[1]), axis=0)


def whole(shape):
    return pl.BlockSpec(shape, lambda e: (0,) * len(shape))


def last_block(shape):
    lead = (0,) * (len(shape) - 1)
    return pl.BlockSpec(shape[:-1] + (BLOCK,), lambda e: lead + (e,))


def expand_kernel(
    image_ref, gain_ref, w_exp_ref,
    normed_ref, turned_ref, spread_ref, slope_ref,
    expanded_ref,
):
    rows, cols, channels = image_ref.shape

    @pl.when(pl.program_id(0) == 0)
    def _():
        gain = gain_ref[...].astype(F32)

        @pl.loop(0, rows // 4)
        def _(c):
            flat = image_ref[pl.ds(c * 4, 4)].reshape(4 * cols, channels)
            unit, _ = norm_rows(flat.astype(F32))
            at = pl.ds(pl.multiple_of(c * 4 * cols, 16), 4 * cols)
            normed_ref[at, :] = (unit * gain).astype(BF16)

        turned_ref[...] = normed_ref[...].T

    expanded_ref[...] = dot(normed_ref[...], w_exp_ref[...])

    @pl.loop(0, rows, unroll=4)
    def _(r):
        for h in range(BLOCK // LANES):
            lanes = slice(h * LANES, (h + 1) * LANES)
            x = expanded_ref[pl.ds(pl.multiple_of(r * cols, 16), cols), lanes]
            value, slope = gelu_and_slope(x)
            spread_ref[r, :, lanes] = value.astype(BF16)
            slope_ref[r, :, lanes] = slope.astype(BF16)


def run_expand(image, gain, w_expand):
    rows, cols, channels = image.shape
    expanded = w_expand.shape[1]
    return pl.pallas_call(
        expand_kernel,
        grid=(expanded // BLOCK,),
        in_specs=[whole(image.shape), whole(gain.shape), last_block(w_expand.shape)],
        out_specs=[
            whole((rows * cols, channels)), whole((channels, rows * cols)),
            last_block((rows, cols, expanded)), last_block((rows, cols, expanded)),
        ],
        out_shape=[
            jax.ShapeDtypeStruct((rows * cols, channels), BF16),
            jax.ShapeDtypeStruct((channels, rows * cols), BF16),
            jax.ShapeDtypeStruct((rows, cols, expanded), BF16),
            jax.ShapeDtypeStruct((rows, cols, expanded), BF16),
        ],
        scratch_shapes=[pltpu.VMEM((rows * cols, BLOCK), F32)],
        compiler_params=PARAMS,
        cost_estimate=estimate(14),
        name="expand",
    )(image, gain, w_expand)


def depthwise_kernel(
    up_ref, down_ref, side_ref, gain_ref, w_exp_ref, w_dep_ref, spread_ref,
    ring_ref, act_ref, pool_ref,
    ring_normed_ref, ring_wide_ref,
):
    rows, cols, _ = spread_ref.shape
    channels = up_ref.shape[2]
    over = 4 * cols
    side = 8

    @pl.when(pl.program_id(0) == 0)
    def _():
        gain = gain_ref[...].astype(F32)

        def put(at, values):
            unit, _ = norm_rows(values.astype(F32))
            ring_normed_ref[at : at + values.shape[0], :] = (unit * gain).astype(BF16)

        put(0, up_ref[...].reshape(2 * cols, channels))
        put(2 * cols, down_ref[...].reshape(2 * cols, channels))
        put(over, side_ref[...])

    ring_wide_ref[...] = dot(ring_normed_ref[...], w_exp_ref[...])
    tile = 32

    @pl.loop(0, ring_wide_ref.shape[0] // tile, unroll=True)
    def _(t):
        at = pl.ds(pl.multiple_of(t * tile, tile), tile)
        value, _ = gelu_and_slope(ring_wide_ref[at, :], False)
        low = value.astype(BF16)
        ring_ref[at, :] = low
        ring_wide_ref[at, :] = low.astype(F32)

    for h in range(BLOCK // LANES):
        lanes = slice(h * LANES, (h + 1) * LANES)
        taps = w_dep_ref[:, :, lanes].astype(F32)
        w = [[taps[a, b : b + 1] for b in range(3)] for a in range(3)]

        def line(r, main):
            at = pl.multiple_of(over + (r + 2) * side, side)
            return jnp.concatenate([main, ring_wide_ref[pl.ds(at, side), lanes]], axis=0)

        def conv(i, x, total):
            u = [x[0] * w[0][b] + x[1] * w[1][b] + x[2] * w[2][b] for b in range(3)]
            wide = cols + side
            pre = pltpu.roll(u[0], 1, 0) + u[1] + pltpu.roll(u[2], wide - 1, 0)
            value, _ = gelu_and_slope(pre[:cols], False)
            act_ref[i, :, lanes] = value.astype(BF16)
            return total + fold_rows(value)

        def step(i, carry):
            first, second, total = carry
            third = line(i + 1, spread_ref[i + 1, :, lanes].astype(F32))
            return second, third, conv(i, (first, second, third), total)

        carry = (
            line(-1, ring_wide_ref[cols : 2 * cols, lanes]),
            line(0, spread_ref[0, :, lanes].astype(F32)),
            jnp.zeros((8, LANES), F32),
        )
        first, second, total = lax.fori_loop(0, rows - 1, step, carry, unroll=5)
        third = line(rows, ring_wide_ref[2 * cols : 3 * cols, lanes])
        total = conv(rows - 1, (first, second, third), total)
        total = jnp.sum(total, axis=0, keepdims=True)
        pool_ref[:, :, lanes] = jnp.broadcast_to(total[None], (pool_ref.shape[0], 1, LANES))


def run_depthwise(count, up, down, side, gain, w_expand, w_depth, spread):
    rows, cols, expanded = spread.shape
    channels = up.shape[2]
    ring = 4 * cols + 8 * (rows + 4)
    return pl.pallas_call(
        depthwise_kernel,
        grid=(expanded // BLOCK,),
        in_specs=[
            whole(up.shape), whole(down.shape), whole(side.shape), whole(gain.shape),
            last_block(w_expand.shape), last_block(w_depth.shape), last_block(spread.shape),
        ],
        out_specs=[
            last_block((ring, expanded)), last_block(spread.shape), last_block((count, 1, expanded)),
        ],
        out_shape=[
            jax.ShapeDtypeStruct((ring, expanded), BF16),
            jax.ShapeDtypeStruct(spread.shape, BF16),
            jax.ShapeDtypeStruct((count, 1, expanded), F32),
        ],
        scratch_shapes=[pltpu.VMEM((ring, channels), BF16), pltpu.VMEM((ring, BLOCK), F32)],
        compiler_params=PARAMS,
        cost_estimate=estimate(1),
        name="depthwise",
    )(up, down, side, gain, w_expand, w_depth, spread)


def slope_kernel(flags_ref, ring_ref, w_dep_ref, spread_ref, main_ref, side_out_ref, wide_ref):
    rows, cols, _ = spread_ref.shape
    over = 4 * cols
    side = 8
    wide = cols + side

    for k, r in enumerate((0, 1, rows + 2, rows + 3)):
        wide_ref[r, :cols, :] = ring_ref[k * cols : (k + 1) * cols, :].astype(F32)
    sides = ring_ref[over:, :].astype(F32)
    for r in range(rows + 4):
        wide_ref[r, cols:, :] = sides[r * side : (r + 1) * side]

    @pl.loop(0, rows)
    def _(r):
        wide_ref[r + 2, :cols, :] = spread_ref[r].astype(F32)

    place = lax.broadcasted_iota(jnp.int32, (side, LANES), 0)
    side_mask = jnp.where(
        place == side - 1, flags_ref[2], jnp.where(place == 0, flags_ref[3], 1.0)
    ).astype(F32)

    @pl.loop(0, rows + 2)
    def _(i):
        keep = jnp.where(i == 0, flags_ref[0], jnp.where(i == rows + 1, flags_ref[1], 1.0))
        for h in range(BLOCK // LANES):
            lanes = slice(h * LANES, (h + 1) * LANES)
            taps = w_dep_ref[:, :, lanes].astype(F32)
            x = [wide_ref[i + a, :, lanes] for a in range(3)]
            u = [sum(x[a] * taps[a, b : b + 1] for a in range(3)) for b in range(3)]
            pre = pltpu.roll(u[0], 1, 0) + u[1] + pltpu.roll(u[2], wide - 1, 0)
            _, slope = gelu_and_slope(pre)
            slope = slope * keep
            main_ref[i, :, lanes] = slope[:cols].astype(BF16)
            side_out_ref[i, :, lanes] = slope[cols:] * side_mask


def run_slope(flags, ring, w_depth, spread):
    rows, cols, expanded = spread.shape
    return pl.pallas_call(
        slope_kernel,
        grid=(expanded // BLOCK,),
        in_specs=[
            pl.BlockSpec(memory_space=pltpu.SMEM),
            last_block(ring.shape), last_block(w_depth.shape), last_block(spread.shape),
        ],
        out_specs=[last_block((rows + 2, cols, expanded)), last_block((rows + 2, 8, expanded))],
        out_shape=[
            jax.ShapeDtypeStruct((rows + 2, cols, expanded), BF16),
            jax.ShapeDtypeStruct((rows + 2, 8, expanded), F32),
        ],
        scratch_shapes=[pltpu.VMEM((rows + 4, cols + 8, BLOCK), F32)],
        compiler_params=PARAMS,
        cost_estimate=estimate(13),
        name="slope",
    )(flags, ring, w_depth, spread)


def mix_kernel(
    cells_total, stride, bands,
    parts_ref, w_sq_ref, w_ex_ref, act_ref, image_ref, w_proj_ref, gain_ref, after_ref,
    pooled_ref, hidden_ref, gate_ref, mixed_ref, send_ref,
):
    step = pl.program_id(0)

    @pl.when(step == 0)
    def _():
        pooled = jnp.sum(parts_ref[...], axis=0) / cells_total
        hidden = dot_exact(pooled, w_sq_ref[...].astype(F32), ((1,), (0,)))
        silu = hidden * jax.nn.sigmoid(hidden)
        pooled_ref[...] = pooled
        hidden_ref[...] = hidden
        gate_ref[...] = jax.nn.sigmoid(dot_exact(silu, w_ex_ref[...].astype(F32), ((1,), (0,))))

    lines, cols, channels = image_ref.shape
    flat = act_ref[...].reshape(lines * cols, act_ref.shape[2])
    gated = (flat.astype(F32) * gate_ref[...]).astype(BF16)
    product = dot(gated, w_proj_ref[...])
    mixed = (image_ref[...].reshape(lines * cols, channels).astype(F32) + product).astype(BF16)
    mixed_ref[...] = mixed.reshape(lines, cols, channels)
    unit, _ = norm_rows(mixed.astype(F32))
    normed = (unit * gain_ref[...].astype(F32)).astype(BF16)
    for k in range(lines):
        line = step * lines + k
        for band in range(bands):
            start = k * cols + band * SIDE
            send_ref[lax.rem(line, stride) * bands + band, line // stride] = normed[
                start : start + SIDE
            ]


def run_mix(cells_total, stride, parts, w_squeeze, w_excite, act, image, w_project, gain, after):
    rows, cols, channels = image.shape
    expanded = act.shape[2]
    lines = 4
    bands = cols // SIDE
    block = lambda width: pl.BlockSpec((lines, cols, width), lambda r: (r, 0, 0))
    send = (stride * bands, rows // stride, SIDE, channels)
    return pl.pallas_call(
        functools.partial(mix_kernel, cells_total, stride, bands),
        grid=(rows // lines,),
        in_specs=[
            whole(parts.shape), whole(w_squeeze.shape), whole(w_excite.shape),
            block(expanded), block(channels), whole(w_project.shape), whole(gain.shape),
            pl.BlockSpec(memory_space=pl.ANY),
        ],
        out_specs=[
            whole((1, expanded)), whole((1, w_squeeze.shape[1])), whole((1, expanded)),
            block(channels), whole(send),
        ],
        out_shape=[
            jax.ShapeDtypeStruct((1, expanded), F32),
            jax.ShapeDtypeStruct((1, w_squeeze.shape[1]), F32),
            jax.ShapeDtypeStruct((1, expanded), F32),
            jax.ShapeDtypeStruct(image.shape, BF16),
            jax.ShapeDtypeStruct(send, BF16),
        ],
        compiler_params=PARAMS,
        cost_estimate=estimate(5),
        name="mix",
    )(parts, w_squeeze, w_excite, act, image, w_project, gain, after)


def attention_kernel(
    members, heads, lines,
    arrived_ref, cot_ref, w_qkv_ref, w_out_ref, bias_ref,
    x_ref, att_ref, grad_ref, packed_grad_ref, bias_out_ref,
    order_ref, packed_ref, att_grad_ref, bias_sum_ref,
):
    cells, channels = x_ref.shape
    groups = cells // members

    def places():
        for g in range(groups):
            for m in range(0, members, GRID):
                line, row = (m // GRID) % lines, m // GRID // lines
                start = (row * GRID * lines + line) * groups + g
                yield g * members + m, pl.ds(start, GRID, stride=lines * groups)

    for half in range(channels // LANES):
        lanes = slice(half * LANES, (half + 1) * LANES)
        order_ref[half] = arrived_ref[:, lanes].astype(F32)
        for g in range(groups):
            pieces = [order_ref[half, at, :] for k, at in places() if k // members == g]
            at = slice(g * members, (g + 1) * members)
            x_ref[at, lanes] = jnp.concatenate(pieces, axis=0).astype(BF16)
    dim = channels // heads
    per_half = LANES // dim
    halves = channels // LANES
    scale = dim ** (-0.5)
    packed_ref[...] = dot(x_ref[...], w_qkv_ref[...]).astype(BF16)
    att_grad_ref[...] = dot(cot_ref[...], w_out_ref[...], ((1,), (1,))).astype(BF16)
    bias_sum_ref[...] = jnp.zeros(bias_sum_ref.shape, F32)
    tall = per_half * members
    mask = (
        lax.broadcasted_iota(jnp.int32, (tall, LANES), 0) // members
        == lax.broadcasted_iota(jnp.int32, (tall, LANES), 1) // dim
    ).astype(F32).astype(BF16)
    owner = lax.broadcasted_iota(jnp.int32, (members, 2 * LANES), 1) % LANES // dim
    zero = jnp.zeros((members, LANES), BF16)

    def by_head(pair):
        return jnp.concatenate(
            [jnp.concatenate([v] * per_half, axis=0) * mask for v in pair], axis=1
        )

    def diagonal(pair):
        return jnp.concatenate(
            [
                jnp.concatenate([pair[0], zero], axis=1),
                jnp.concatenate([zero, pair[1]], axis=1),
            ],
            axis=0,
        )

    def collect(v):
        parts = [v[h * members : (h + 1) * members] for h in range(per_half)]
        picked = parts[-1]
        for h in range(per_half - 1):
            picked = jnp.where(owner == h, parts[h], picked)
        return [picked[:, :LANES], picked[:, LANES:]]

    def blocks(v):
        return [v[:members, :LANES], v[members:, LANES:]]

    def over_members(v, reduce):
        parted = v.reshape(per_half, members, 2 * members)
        small = reduce(parted, axis=1, keepdims=True)
        return jnp.broadcast_to(small, parted.shape).reshape(v.shape)

    def pair_step(g, carry):
        at = [pl.ds(pl.multiple_of((2 * g + k) * members, 16), members) for k in range(2)]
        for half in range(halves):
            def lanes(part):
                start = part * channels + half * LANES
                return slice(start, start + LANES)

            q, k, v = ([packed_ref[at[n], lanes(part)] for n in range(2)] for part in range(3))
            cot = [att_grad_ref[at[n], lanes(0)] for n in range(2)]
            q_diag, cot_diag = diagonal(q), diagonal(cot)
            k_tall, v_tall = by_head(k), by_head(v)
            scores = dot(k_tall, q_diag, ((1,), (1,))) * scale + bias_ref[half]
            grad_probs = dot(v_tall, cot_diag, ((1,), (1,)))
            lifted = jnp.exp(scores - over_members(scores, jnp.max))
            soft = lifted * (1.0 / over_members(lifted, jnp.sum))
            soft_low = soft.astype(BF16)
            grad_scores = soft * (grad_probs - over_members(grad_probs * soft, jnp.sum))
            bias_sum_ref[half] += grad_scores
            scaled = (grad_scores * scale).astype(BF16)
            attended = blocks(dot(soft_low, v_tall, ((0,), (0,))))
            grad_q = blocks(dot(scaled, k_tall, ((0,), (0,))))
            grad_v = collect(dot(soft_low, cot_diag))
            grad_k = collect(dot(scaled, q_diag))
            for n in range(2):
                att_ref[at[n], lanes(0)] = attended[n].astype(BF16)
                for part, value in enumerate((grad_q, grad_k, grad_v)):
                    packed_grad_ref[at[n], lanes(part)] = value[n].astype(BF16)
        return carry

    lax.fori_loop(0, cells // members // 2, pair_step, 0, unroll=2)
    grad = dot(packed_grad_ref[...], w_qkv_ref[...], ((1,), (1,)))
    for half in range(halves):
        lanes = slice(half * LANES, (half + 1) * LANES)
        for k, at in places():
            order_ref[half, at, :] = grad[k : k + GRID, lanes]
        grad_ref[:, lanes] = order_ref[half].astype(BF16)
    for half in range(halves):
        both = bias_sum_ref[half]
        bias_out_ref[half] = both[:, :members] + both[:, members:]


def run_attention(arrived, cot, w_qkv, w_out, bias_tall, heads, lines):
    cells, channels = cot.shape
    halves, tall, members2 = bias_tall.shape
    members = members2 // 2
    vmem = pl.BlockSpec(memory_space=pltpu.VMEM)
    return pl.pallas_call(
        functools.partial(attention_kernel, members, heads, lines),
        in_specs=[vmem] * 5,
        out_specs=[vmem] * 5,
        out_shape=[
            jax.ShapeDtypeStruct((cells, channels), BF16),
            jax.ShapeDtypeStruct((cells, channels), BF16),
            jax.ShapeDtypeStruct((cells, channels), BF16),
            jax.ShapeDtypeStruct((cells, 3 * channels), BF16),
            jax.ShapeDtypeStruct((halves, tall, members), F32),
        ],
        scratch_shapes=[
            pltpu.VMEM((channels // LANES, cells, LANES), F32),
            pltpu.VMEM((cells, 3 * channels), BF16),
            pltpu.VMEM((cells, channels), BF16),
            pltpu.VMEM(bias_tall.shape, F32),
        ],
        compiler_params=PARAMS,
        cost_estimate=estimate(14),
        name="attention",
    )(arrived.reshape(cells, channels), cot, w_qkv, w_out, bias_tall)


def attention_weights_kernel(x_ref, packed_grad_ref, att_ref, cot_ref, bias_ref, out_ref):
    channels = x_ref.shape[1]
    wide = 3 * channels
    out_ref[:, :wide] = dot(x_ref[...], packed_grad_ref[...], ((0,), (0,))).astype(BF16)
    out_ref[:, wide : wide + channels] = dot(att_ref[...], cot_ref[...], ((0,), (0,))).astype(BF16)
    bias = jnp.concatenate([bias_ref[half] for half in range(bias_ref.shape[0])], axis=1)
    out_ref[:, wide + channels :] = bias.astype(BF16)


def run_attention_weights(x, packed_grad, att, cot, bias):
    channels = x.shape[1]
    vmem = pl.BlockSpec(memory_space=pltpu.VMEM)
    width = 4 * channels + bias.shape[0] * bias.shape[2]
    return pl.pallas_call(
        attention_weights_kernel,
        in_specs=[vmem] * 5,
        out_specs=vmem,
        out_shape=jax.ShapeDtypeStruct((channels, width), BF16),
        compiler_params=PARAMS,
        cost_estimate=estimate(5),
        name="attention_weights",
    )(x, packed_grad, att, cot, bias)


def mixed_back_kernel(
    stride, bands,
    recv_ref, mixed_ref, cot_ref, gain_ref, act_ref, gate_ref, w_projt_ref,
    grad_ref, low_ref, norm_ref, project_ref, gate_grad_ref,
    turned_ref, total_ref,
):
    rows, cols, channels = mixed_ref.shape

    @pl.when(pl.program_id(0) == 0)
    def _():
        gain = gain_ref[...].astype(F32)
        lines = 4

        def some_rows(c, total):
            pieces = []
            for k in range(lines):
                i = c * lines + k
                a, p = lax.rem(i, stride), i // stride
                pieces += [recv_ref[a * bands + band, p] for band in range(bands)]
            grad = jnp.concatenate(pieces, axis=0).astype(F32)
            at = pl.ds(c * lines, lines)
            flat = lambda ref: ref[at].reshape(lines * cols, channels).astype(F32)
            unit, rstd = norm_rows(flat(mixed_ref))
            back = flat(cot_ref) + norm_rows_back(unit, rstd, gain, grad)
            grad_ref[at] = back.reshape(lines, cols, channels)
            low_ref[at] = back.astype(BF16).reshape(lines, cols, channels)
            return total + fold_rows(grad * unit)

        total = lax.fori_loop(
            0, rows // lines, some_rows, jnp.zeros((8, channels), F32), unroll=2
        )
        norm_ref[...] = jnp.sum(total, axis=0, keepdims=True)
        turned_ref[...] = low_ref[...].reshape(rows * cols, channels).T

    flat = act_ref[...].reshape(rows * cols, BLOCK)
    product = dot(turned_ref[...], flat)
    total = jnp.sum(product * w_projt_ref[...].astype(F32), axis=0, keepdims=True)
    step, steps = pl.program_id(0), pl.num_programs(0)
    total_ref[step] = total
    project_ref[...] = (product * gate_ref[...]).T.astype(BF16)

    @pl.when(step == steps - 1)
    def _():
        sums = [total_ref[e] for e in range(total_ref.shape[0])]
        high = [v.astype(BF16).astype(F32) for v in sums]
        terms = jnp.concatenate(high + [v - w for v, w in zip(sums, high)], axis=0)
        gate_grad_ref[...] = jnp.broadcast_to(terms.astype(BF16)[None], gate_grad_ref.shape)


def run_mixed_back(count, stride, recv, mixed, cot, gain, act, gate, w_project_t):
    rows, cols, channels = mixed.shape
    expanded = act.shape[2]
    return pl.pallas_call(
        functools.partial(mixed_back_kernel, stride, cols // SIDE),
        grid=(expanded // BLOCK,),
        in_specs=[
            whole(recv.shape), whole(mixed.shape), whole(cot.shape), whole(gain.shape),
            last_block(act.shape), last_block(gate.shape), last_block(w_project_t.shape),
        ],
        out_specs=[
            whole(mixed.shape), whole(mixed.shape), whole((1, channels)),
            last_block((BLOCK, expanded)), whole((count, 2 * expanded // BLOCK, BLOCK)),
        ],
        out_shape=[
            jax.ShapeDtypeStruct(mixed.shape, F32),
            jax.ShapeDtypeStruct(mixed.shape, BF16),
            jax.ShapeDtypeStruct((1, channels), F32),
            jax.ShapeDtypeStruct((BLOCK, expanded), BF16),
            jax.ShapeDtypeStruct((count, 2 * expanded // BLOCK, BLOCK), BF16),
        ],
        scratch_shapes=[
            pltpu.VMEM((channels, rows * cols), BF16),
            pltpu.VMEM((expanded // BLOCK, 1, BLOCK), F32),
        ],
        compiler_params=PARAMS,
        cost_estimate=estimate(7),
        name="mixed_back",
    )(recv, mixed, cot, gain, act, gate, w_project_t)


def expand_back_kernel(
    cells_total,
    parts_ref, hidden_ref, gate_all_ref, w_sq_ref, w_ex_ref,
    low_ref, up_ref, down_ref, side_ref, w_projt_ref, gate_ref, slope_ref, side_slope_ref,
    spread_slope_ref, spread_ref, w_dep_ref, turned_ref, w_exp_ref, gain_ref, norm1_ref,
    weights_ref, first_ref, logit_ref, pre_ref,
    main_ref, side_grad_ref, window_ref, expanded_ref, pool_ref, tail_ref, norm_ref,
):
    rows, cols, channels = low_ref.shape
    side = 8
    wide = cols + side
    step = pl.program_id(0)
    steps = pl.num_programs(0)

    @pl.when(step == 0)
    def _():
        gate = gate_all_ref[...]
        len_e = pool_ref.shape[0]
        terms = jnp.sum(parts_ref[...].astype(F32), axis=0)
        gate_grad = jnp.concatenate(
            [terms[e : e + 1] + terms[len_e + e : len_e + e + 1] for e in range(len_e)],
            axis=1,
        )
        logit = gate_grad * gate * (1.0 - gate)
        hidden = hidden_ref[...]
        sig = jax.nn.sigmoid(hidden)
        pre = dot_exact(logit, w_ex_ref[...].astype(F32), ((1,), (1,))) * (
            sig + hidden * sig * (1.0 - sig)
        )
        logit_ref[...] = logit
        pre_ref[...] = pre
        pooled = dot_exact(pre, w_sq_ref[...].astype(F32), ((1,), (1,))) / cells_total
        for e in range(pool_ref.shape[0]):
            pool_ref[e] = pooled[:, e * BLOCK : (e + 1) * BLOCK]
        first_ref[...] = jnp.zeros(first_ref.shape, F32)
        tail_ref[...] = jnp.zeros(tail_ref.shape, F32)
        norm_ref[...] = jnp.zeros(norm_ref.shape, F32)

    w_projt = w_projt_ref[...]
    main_ref[pl.ds(0, cols), :] = dot(up_ref[0], w_projt)
    main_ref[pl.ds(cols, rows * cols), :] = dot(
        low_ref[...].reshape(rows * cols, channels), w_projt
    )
    main_ref[pl.ds((rows + 1) * cols, cols), :] = dot(down_ref[0], w_projt)
    side_grad_ref[...] = dot(side_ref[...], w_projt)

    @pl.loop(0, rows + 2, unroll=3)
    def _(i):
        for h in range(BLOCK // LANES):
            lanes = slice(h * LANES, (h + 1) * LANES)
            gate = gate_ref[:, lanes]
            pooled = pool_ref[step][:, lanes]
            gated = main_ref[pl.ds(pl.multiple_of(i * cols, 16), cols), lanes]
            main = (gated * gate + pooled) * slope_ref[i, :, lanes].astype(F32)
            gated = side_grad_ref[pl.ds(pl.multiple_of(i * side, side), side), lanes]
            edge = (gated * gate + pooled) * side_slope_ref[i, :, lanes]
            grad = jnp.concatenate([main, edge], axis=0)
            grad = grad.astype(BF16).astype(F32)
            window_ref[0, i, :, lanes] = pltpu.roll(grad, wide - 1, 0)[:cols]
            window_ref[1, i, :, lanes] = grad[:cols]
            window_ref[2, i, :, lanes] = pltpu.roll(grad, 1, 0)[:cols]

    for h in range(BLOCK // LANES):
        lanes = slice(h * LANES, (h + 1) * LANES)
        taps = w_dep_ref[:, :, lanes].astype(F32)

        def back_row(i, sums):
            spread = spread_ref[i, :, lanes].astype(F32)
            total = jnp.zeros((cols, LANES), F32)
            new_sums = []
            for a in range(3):
                for b in range(3):
                    window = window_ref[b, i + 2 - a, :, lanes]
                    total = total + window * taps[a, b : b + 1]
                    new_sums.append(sums[a * 3 + b] + fold_rows(window * spread))
            grad = total * spread_slope_ref[i, :, lanes].astype(F32)
            expanded_ref[pl.ds(pl.multiple_of(i * cols, 16), cols), lanes] = grad.astype(BF16)
            return tuple(new_sums)

        sums = lax.fori_loop(0, rows, back_row, (jnp.zeros((8, LANES), F32),) * 9, unroll=2)
        for t in range(9):
            row = t * (steps * BLOCK // LANES) + step * (BLOCK // LANES) + h
            tail_ref[pl.ds(row, 1), :] = jnp.sum(sums[t], axis=0, keepdims=True)

    grad_expanded = expanded_ref[...]
    w_exp = w_exp_ref[...]
    weights = dot(turned_ref[...], grad_expanded)
    weights_ref[:, pl.ds(pl.multiple_of(step * BLOCK, BLOCK), BLOCK)] = weights.astype(BF16)
    norm_ref[...] += jnp.sum(weights * w_exp.astype(F32), axis=1, keepdims=True)
    first_ref[...] += dot(grad_expanded, w_exp, ((1,), (1,)))

    @pl.when(step == steps - 1)
    def _():
        norm = norm_ref[...].T[0:1] / gain_ref[...].astype(F32)
        start = 9 * steps * (BLOCK // LANES)
        for k in range(channels // LANES):
            piece = slice(k * LANES, (k + 1) * LANES)
            tail_ref[start + k : start + k + 1, :] = norm[:, piece]
            at = start + channels // LANES + k
            tail_ref[at : at + 1, :] = norm1_ref[:, piece]
        weights_ref[:, steps * BLOCK :] = tail_ref[...].astype(BF16)


def run_expand_back(
    cells_total, parts, hidden, gate, w_squeeze, w_excite, low, up, down, side,
    w_project_t, slope, side_slope, spread_slope, spread, w_depth, turned, w_expand, gain, norm1,
):
    rows, cols, channels = low.shape
    expanded = w_expand.shape[1]
    steps = expanded // BLOCK
    return pl.pallas_call(
        functools.partial(expand_back_kernel, cells_total),
        grid=(steps,),
        in_specs=[
            pl.BlockSpec(
                (parts.shape[0], 2 * steps, BLOCK), lambda e: (0, parts.shape[1] // (2 * steps) - 1, 0)
            ),
            whole(hidden.shape), whole(gate.shape),
            whole(w_squeeze.shape), whole(w_excite.shape),
            whole(low.shape), whole(up.shape), whole(down.shape), whole(side.shape),
            last_block(w_project_t.shape), last_block(gate.shape), last_block(slope.shape),
            last_block(side_slope.shape), last_block(spread_slope.shape), last_block(spread.shape),
            last_block(w_depth.shape), whole(turned.shape), last_block(w_expand.shape),
            whole(gain.shape), whole(norm1.shape),
        ],
        out_specs=[
            whole((channels, expanded + LANES)), whole((rows * cols, channels)),
            whole((1, expanded)), whole(hidden.shape),
        ],
        out_shape=[
            jax.ShapeDtypeStruct((channels, expanded + LANES), BF16),
            jax.ShapeDtypeStruct((rows * cols, channels), F32),
            jax.ShapeDtypeStruct((1, expanded), F32),
            jax.ShapeDtypeStruct(hidden.shape, F32),
        ],
        scratch_shapes=[
            pltpu.VMEM(((rows + 2) * cols, BLOCK), F32),
            pltpu.VMEM(((rows + 2) * 8, BLOCK), F32),
            pltpu.VMEM((3, rows + 2, cols, BLOCK), F32),
            pltpu.VMEM((rows * cols, BLOCK), BF16),
            pltpu.VMEM((steps, 1, BLOCK), F32),
            pltpu.VMEM((channels, LANES), F32),
            pltpu.VMEM((channels, LANES), F32),
        ],
        compiler_params=PARAMS,
        cost_estimate=estimate(14),
        name="expand_back",
    )(
        parts, hidden, gate, w_squeeze, w_excite, low, up, down, side, w_project_t, gate,
        slope, side_slope, spread_slope, spread, w_depth, turned, w_expand, gain, norm1,
    )


def image_back_kernel(image_ref, gain_ref, first_ref, mixed_ref, out_ref):
    unit, rstd = norm_rows(image_ref[...].astype(F32))
    grad = first_ref[...]
    back = mixed_ref[...] + norm_rows_back(unit, rstd, gain_ref[...].astype(F32), grad)
    out_ref[...] = back.astype(BF16)


def run_image_back(image, gain, first, mixed):
    cells, channels = image.shape
    block = pl.BlockSpec((cells // 4, channels), lambda r: (r, 0))
    return pl.pallas_call(
        image_back_kernel,
        grid=(4,),
        in_specs=[block, whole(gain.shape), block, block],
        out_specs=block,
        out_shape=jax.ShapeDtypeStruct((cells, channels), BF16),
        compiler_params=PARAMS,
        cost_estimate=estimate(4),
        name="image_back",
    )(image, gain, first, mixed)


def shift(cells, axis, step):
    count = lax.axis_size(axis)
    pairs = [(i, i + step) for i in range(count) if 0 <= i + step < count]
    return lax.ppermute(cells, axis, pairs)


def halo_rows(cells, width):
    up = shift(cells[cells.shape[0] - width :], "row", 1)
    down = shift(cells[:width], "row", -1)
    return up, down


def halo_sides(cells, up, down, width):
    rows, cols, channels = cells.shape
    first = jnp.concatenate([up[:, :width], cells[:, :width], down[:, :width]], axis=0)
    last = jnp.concatenate(
        [up[:, cols - width :], cells[:, cols - width :], down[:, cols - width :]], axis=0
    )
    left = shift(last, "col", 1)
    right = shift(first, "col", -1)
    gap = jnp.zeros((rows + 2 * width, 8 - 2 * width, channels), cells.dtype)
    side = jnp.concatenate([right, gap, left], axis=1)
    return side.reshape(-1, channels)


def hand_around(blocks):
    return lax.all_to_all(blocks, AXES, split_axis=0, concat_axis=0, tiled=True)


def sum_shares(matrix):
    rows, columns = matrix.shape
    count = lax.axis_size("row") * lax.axis_size("col")
    share = rows // count
    arrived = hand_around(matrix.reshape(count, share, columns))
    total = jnp.sum(arrived.astype(F32), axis=0).astype(BF16)
    sent = jnp.broadcast_to(total[None], (count, share, columns))
    return hand_around(sent).reshape(rows, columns)


def cube_steps():
    steps = [("col", 1)]
    for axis in ("row", "col"):
        step = 1 if axis == "row" else 2
        while step < lax.axis_size(axis):
            steps.append((axis, step))
            step *= 2
    return steps


def swap_pairs(v, axis, step):
    return lax.ppermute(v, axis, [(i, i ^ step) for i in range(lax.axis_size(axis))])


def sum_half(matrix, axis, step):
    bit = lax.axis_index(axis) // step % 2
    halves = matrix.reshape(2, matrix.shape[0] // 2, matrix.shape[1])
    sent = lax.dynamic_index_in_dim(halves, 1 - bit, 0, False)
    kept = lax.dynamic_index_in_dim(halves, bit, 0, False)
    return (kept.astype(F32) + swap_pairs(sent, axis, step).astype(F32)).astype(BF16)


def join_halves(matrix, axis, step):
    bit = lax.axis_index(axis) // step % 2
    other = swap_pairs(matrix, axis, step)
    return jnp.where(
        bit == 0,
        jnp.concatenate([matrix, other], axis=0),
        jnp.concatenate([other, matrix], axis=0),
    )


def swap_groups(blocks, parity):
    groups = None
    if parity > 1:
        over_row = lax.axis_size("row")
        over_col = lax.axis_size("col")
        groups = [
            [r * over_col + c for r in range(over_row) for c in range(k, over_col, parity)]
            for k in range(parity)
        ]
    return lax.all_to_all(
        blocks, AXES, split_axis=0, concat_axis=0, tiled=True, axis_index_groups=groups
    )


def on_device(
    image, out_cotangent, norm0_gain, w_expand, w_depth, w_squeeze, w_excite, w_project,
    norm1_gain, w_qkv, w_out, attn_bias,
):
    rows, cols, channels = image.shape
    over_row = lax.axis_size("row")
    over_col = lax.axis_size("col")
    count = over_row * over_col
    cells_total = rows * cols * count
    stride = rows * over_row // GRID
    parity = over_col // GRID
    lines = rows // stride
    bands = cols // SIDE
    members = GRID * GRID
    expanded = w_expand.shape[1]

    def into_members(arrived):
        parted = arrived.reshape(over_row, GRID, lines, SIDE, channels)
        return parted.transpose(3, 0, 2, 1, 4).reshape(SIDE * members, channels)

    def out_of_members(values):
        parted = values.reshape(SIDE, over_row, lines, GRID, channels)
        return parted.transpose(1, 3, 2, 0, 4).reshape(-1, lines, SIDE, channels)

    row, col = lax.axis_index("row"), lax.axis_index("col")
    flags = jnp.stack([row > 0, row < over_row - 1, col > 0, col < over_col - 1]).astype(F32)
    gain_first = norm0_gain.reshape(1, channels)
    gain_second = norm1_gain.reshape(1, channels)
    w_project_t = w_project.T
    heads = attn_bias.shape[0]
    halves = channels // LANES
    bias_tall = attn_bias.transpose(0, 2, 1).reshape(halves, heads // halves * members, members)
    bias_tall = jnp.concatenate([bias_tall, bias_tall], axis=2)

    up, down = halo_rows(image, 2)
    normed_first, turned_first, spread, spread_slope = run_expand(image, gain_first, w_expand)
    up, down, spread = lax.optimization_barrier((up, down, spread))
    side = halo_sides(image, up, down, 2)
    cot_sent = (
        out_cotangent.reshape(lines, stride, bands, SIDE, channels)
        .transpose(1, 2, 0, 3, 4)
        .reshape(stride * bands, lines, SIDE, channels)
    )
    cot_members = into_members(swap_groups(cot_sent, parity))
    ring, act, pool = run_depthwise(count, up, down, side, gain_first, w_expand, w_depth, spread)
    pooled, hidden, gate, mixed, normed_sent = run_mix(
        cells_total, stride, hand_around(pool), w_squeeze, w_excite, act, image, w_project,
        gain_second, cot_members,
    )
    slope, side_slope = run_slope(flags, ring, w_depth, spread)
    normed_arrived = swap_groups(normed_sent, parity)
    normed_arrived, slope = lax.optimization_barrier((normed_arrived, slope))
    normed_members, attended, grad_normed, packed_grad, grad_bias = run_attention(
        normed_arrived, cot_members, w_qkv, w_out, bias_tall, heads, lines
    )
    grad_normed_home = swap_groups(grad_normed.reshape(normed_sent.shape), parity)
    weights = run_attention_weights(normed_members, packed_grad, attended, cot_members, grad_bias)
    steps = cube_steps()
    for axis, step in steps[:2]:
        weights = sum_half(weights, axis, step)
    grad_normed_home, weights = lax.optimization_barrier((grad_normed_home, weights))
    grad_mixed, grad_low, grad_norm1, grad_project, gate_grad = run_mixed_back(
        count, stride, grad_normed_home, mixed, out_cotangent, gain_second, act, gate, w_project_t
    )
    attended_sent = out_of_members(attended)
    if parity == 1:
        both = hand_around(
            jnp.concatenate([attended_sent.reshape(count, -1, channels), gate_grad], axis=1)
        )
        parts = both
        attended_home = both[:, : lines * SIDE].reshape(attended_sent.shape)
    else:
        parts = hand_around(gate_grad)
        attended_home = swap_groups(attended_sent, parity)
    up, down = halo_rows(grad_low, 1)
    side = halo_sides(grad_low, up, down, 1)
    grad_project, _ = lax.optimization_barrier((grad_project, up))
    for axis, step in steps[:2]:
        grad_project = sum_half(grad_project, axis, step)
    weights = jnp.concatenate([weights, grad_project], axis=1)
    for axis, step in steps[2:-1]:
        weights = sum_half(weights, axis, step)
    late, grad_first, logit, pre = run_expand_back(
        cells_total, parts, hidden, gate, w_squeeze, w_excite, grad_low, up, down, side,
        w_project_t, slope, side_slope, spread_slope, spread, w_depth, turned_first, w_expand,
        gain_first, grad_norm1,
    )
    weights, _ = lax.optimization_barrier((weights, late))
    weights = sum_half(weights, *steps[-1])
    for axis, step in reversed(steps):
        weights = join_halves(weights, axis, step)
    weights = weights.astype(F32)
    late = sum_shares(late).astype(F32)
    grad_image = run_image_back(
        image.reshape(-1, channels), gain_first, grad_first, grad_mixed.reshape(-1, channels)
    )
    attended_map = (
        attended_home.reshape(stride, bands, lines, SIDE, channels)
        .transpose(2, 0, 1, 3, 4)
        .reshape(rows * cols, channels)
    )
    block_out = (mixed.reshape(-1, channels).astype(F32) + dot(attended_map, w_out)).astype(BF16)

    silu = jax.nn.silu(hidden)
    grad_squeeze = pooled.reshape(expanded, 1) * pre
    grad_excite = silu.reshape(-1, 1) * logit

    ends = 4 * channels + halves * members
    grad_bias = (
        weights[:, 4 * channels : ends]
        .reshape(heads // halves, members, halves, members)
        .transpose(2, 0, 3, 1)
        .reshape(attn_bias.shape)
    )
    grad_project = (
        weights[:, ends:].reshape(BLOCK, expanded // BLOCK, channels).transpose(1, 0, 2)
    ).reshape(w_project.shape)
    tail = late[:, expanded:].reshape(-1)
    return (
        block_out.reshape(image.shape),
        grad_image.reshape(image.shape),
        tail[9 * expanded : 9 * expanded + channels],
        late[:, :expanded],
        tail[: 9 * expanded].reshape(w_depth.shape),
        grad_squeeze,
        grad_excite,
        grad_project,
        tail[9 * expanded + channels : 9 * expanded + 2 * channels],
        weights[:, : 3 * channels],
        weights[:, 3 * channels : 4 * channels],
        grad_bias,
    )


def solution(mesh):
    cells = P("row", "col", None)
    return jax.shard_map(
        on_device,
        mesh=mesh,
        in_specs=(cells, cells) + (P(),) * 10,
        out_specs=(cells, cells) + (P(),) * 10,
        check_vma=False,
    )
```

```python
import functools
import math

import jax
import jax.numpy as jnp
from jax import lax
from jax.experimental import pallas as pl
from jax.experimental.pallas import tpu as pltpu
from jax.sharding import PartitionSpec as P

GRID = 8
AXES = ("row", "col")
BLOCK = 256
LANES = 128
SIDE = 16
GELU_A = math.sqrt(2.0 / math.pi)
GELU_B = GELU_A * 0.044715
F32 = jnp.float32
BF16 = jnp.bfloat16
PARAMS = pltpu.CompilerParams(vmem_limit_bytes=56 * 1024 * 1024)


def estimate(us):
    return pl.CostEstimate(flops=int(us * 1.1e9), bytes_accessed=int(us * 3.6e6), transcendentals=0)


def dot(left, right, contract=((1,), (0,))):
    return lax.dot_general(left, right, (contract, ((), ())), preferred_element_type=F32)


def dot_exact(vector, right, contract):
    tall = jnp.broadcast_to(vector, (8, vector.shape[1]))
    product = lax.dot_general(
        tall, right, (contract, ((), ())), precision=lax.Precision.HIGHEST, preferred_element_type=F32
    )
    return product[0:1]


def gelu_and_slope(x, with_slope=True):
    square = x * x
    t = jnp.tanh(x * (GELU_A + GELU_B * square))
    half = 0.5 + 0.5 * t
    value = x * half
    if not with_slope:
        return value, None
    slope = half + (value * (1.0 - t)) * (GELU_A + (3.0 * GELU_B) * square)
    return value, slope


def norm_rows(x):
    average = jnp.mean(x, axis=-1, keepdims=True)
    centered = x - average
    variance = jnp.mean(centered * centered, axis=-1, keepdims=True)
    rstd = lax.rsqrt(variance + 1e-05)
    return centered * rstd, rstd


def norm_rows_back(unit, rstd, gain, grad):
    unit_grad = grad * gain
    first = jnp.mean(unit_grad, axis=-1, keepdims=True)
    second = jnp.mean(unit_grad * unit, axis=-1, keepdims=True)
    return rstd * (unit_grad - first - unit * second)


def fold_rows(x):
    return jnp.sum(x.reshape(x.shape[0] // 8, 8, x.shape[1]), axis=0)


def whole(shape):
    return pl.BlockSpec(shape, lambda e: (0,) * len(shape))


def last_block(shape):
    lead = (0,) * (len(shape) - 1)
    return pl.BlockSpec(shape[:-1] + (BLOCK,), lambda e: lead + (e,))


def expand_kernel(
    image_ref, gain_ref, w_exp_ref,
    normed_ref, turned_ref, spread_ref, slope_ref,
    expanded_ref,
):
    rows, cols, channels = image_ref.shape

    @pl.when(pl.program_id(0) == 0)
    def _():
        gain = gain_ref[...].astype(F32)

        @pl.loop(0, rows // 4)
        def _(c):
            flat = image_ref[pl.ds(c * 4, 4)].reshape(4 * cols, channels)
            unit, _ = norm_rows(flat.astype(F32))
            at = pl.ds(pl.multiple_of(c * 4 * cols, 16), 4 * cols)
            normed_ref[at, :] = (unit * gain).astype(BF16)

        turned_ref[...] = normed_ref[...].T

    expanded_ref[...] = dot(normed_ref[...], w_exp_ref[...])

    @pl.loop(0, rows, unroll=4)
    def _(r):
        for h in range(BLOCK // LANES):
            lanes = slice(h * LANES, (h + 1) * LANES)
            x = expanded_ref[pl.ds(pl.multiple_of(r * cols, 16), cols), lanes]
            value, slope = gelu_and_slope(x)
            spread_ref[r, :, lanes] = value.astype(BF16)
            slope_ref[r, :, lanes] = slope.astype(BF16)


def run_expand(image, gain, w_expand):
    rows, cols, channels = image.shape
    expanded = w_expand.shape[1]
    return pl.pallas_call(
        expand_kernel,
        grid=(expanded // BLOCK,),
        in_specs=[whole(image.shape), whole(gain.shape), last_block(w_expand.shape)],
        out_specs=[
            whole((rows * cols, channels)), whole((channels, rows * cols)),
            last_block((rows, cols, expanded)), last_block((rows, cols, expanded)),
        ],
        out_shape=[
            jax.ShapeDtypeStruct((rows * cols, channels), BF16),
            jax.ShapeDtypeStruct((channels, rows * cols), BF16),
            jax.ShapeDtypeStruct((rows, cols, expanded), BF16),
            jax.ShapeDtypeStruct((rows, cols, expanded), BF16),
        ],
        scratch_shapes=[pltpu.VMEM((rows * cols, BLOCK), F32)],
        compiler_params=PARAMS,
        cost_estimate=estimate(14),
        name="expand",
    )(image, gain, w_expand)


def depthwise_kernel(
    up_ref, down_ref, side_ref, gain_ref, w_exp_ref, w_dep_ref, spread_ref,
    ring_ref, act_ref, pool_ref,
    ring_normed_ref, ring_wide_ref,
):
    rows, cols, _ = spread_ref.shape
    channels = up_ref.shape[2]
    over = 4 * cols
    side = 8

    @pl.when(pl.program_id(0) == 0)
    def _():
        gain = gain_ref[...].astype(F32)

        def put(at, values):
            unit, _ = norm_rows(values.astype(F32))
            ring_normed_ref[at : at + values.shape[0], :] = (unit * gain).astype(BF16)

        put(0, up_ref[...].reshape(2 * cols, channels))
        put(2 * cols, down_ref[...].reshape(2 * cols, channels))
        put(over, side_ref[...])

    ring_wide_ref[...] = dot(ring_normed_ref[...], w_exp_ref[...])
    tile = 32

    @pl.loop(0, ring_wide_ref.shape[0] // tile, unroll=True)
    def _(t):
        at = pl.ds(pl.multiple_of(t * tile, tile), tile)
        value, _ = gelu_and_slope(ring_wide_ref[at, :], False)
        low = value.astype(BF16)
        ring_ref[at, :] = low
        ring_wide_ref[at, :] = low.astype(F32)

    for h in range(BLOCK // LANES):
        lanes = slice(h * LANES, (h + 1) * LANES)
        taps = w_dep_ref[:, :, lanes].astype(F32)
        w = [[taps[a, b : b + 1] for b in range(3)] for a in range(3)]

        def line(r, main):
            at = pl.multiple_of(over + (r + 2) * side, side)
            return jnp.concatenate([main, ring_wide_ref[pl.ds(at, side), lanes]], axis=0)

        def conv(i, x, total):
            u = [x[0] * w[0][b] + x[1] * w[1][b] + x[2] * w[2][b] for b in range(3)]
            wide = cols + side
            pre = pltpu.roll(u[0], 1, 0) + u[1] + pltpu.roll(u[2], wide - 1, 0)
            value, _ = gelu_and_slope(pre[:cols], False)
            act_ref[i, :, lanes] = value.astype(BF16)
            return total + fold_rows(value)

        def step(i, carry):
            first, second, total = carry
            third = line(i + 1, spread_ref[i + 1, :, lanes].astype(F32))
            return second, third, conv(i, (first, second, third), total)

        carry = (
            line(-1, ring_wide_ref[cols : 2 * cols, lanes]),
            line(0, spread_ref[0, :, lanes].astype(F32)),
            jnp.zeros((8, LANES), F32),
        )
        first, second, total = lax.fori_loop(0, rows - 1, step, carry, unroll=5)
        third = line(rows, ring_wide_ref[2 * cols : 3 * cols, lanes])
        total = conv(rows - 1, (first, second, third), total)
        total = jnp.sum(total, axis=0, keepdims=True)
        pool_ref[:, :, lanes] = jnp.broadcast_to(total[None], (pool_ref.shape[0], 1, LANES))


def run_depthwise(count, up, down, side, gain, w_expand, w_depth, spread):
    rows, cols, expanded = spread.shape
    channels = up.shape[2]
    ring = 4 * cols + 8 * (rows + 4)
    return pl.pallas_call(
        depthwise_kernel,
        grid=(expanded // BLOCK,),
        in_specs=[
            whole(up.shape), whole(down.shape), whole(side.shape), whole(gain.shape),
            last_block(w_expand.shape), last_block(w_depth.shape), last_block(spread.shape),
        ],
        out_specs=[
            last_block((ring, expanded)), last_block(spread.shape), last_block((count, 1, expanded)),
        ],
        out_shape=[
            jax.ShapeDtypeStruct((ring, expanded), BF16),
            jax.ShapeDtypeStruct(spread.shape, BF16),
            jax.ShapeDtypeStruct((count, 1, expanded), F32),
        ],
        scratch_shapes=[pltpu.VMEM((ring, channels), BF16), pltpu.VMEM((ring, BLOCK), F32)],
        compiler_params=PARAMS,
        cost_estimate=estimate(1),
        name="depthwise",
    )(up, down, side, gain, w_expand, w_depth, spread)


def slope_kernel(flags_ref, ring_ref, w_dep_ref, spread_ref, main_ref, side_out_ref, wide_ref):
    rows, cols, _ = spread_ref.shape
    over = 4 * cols
    side = 8
    wide = cols + side

    for k, r in enumerate((0, 1, rows + 2, rows + 3)):
        wide_ref[r, :cols, :] = ring_ref[k * cols : (k + 1) * cols, :].astype(F32)
    sides = ring_ref[over:, :].astype(F32)
    for r in range(rows + 4):
        wide_ref[r, cols:, :] = sides[r * side : (r + 1) * side]

    @pl.loop(0, rows)
    def _(r):
        wide_ref[r + 2, :cols, :] = spread_ref[r].astype(F32)

    place = lax.broadcasted_iota(jnp.int32, (side, LANES), 0)
    side_mask = jnp.where(
        place == side - 1, flags_ref[2], jnp.where(place == 0, flags_ref[3], 1.0)
    ).astype(F32)

    @pl.loop(0, rows + 2)
    def _(i):
        keep = jnp.where(i == 0, flags_ref[0], jnp.where(i == rows + 1, flags_ref[1], 1.0))
        for h in range(BLOCK // LANES):
            lanes = slice(h * LANES, (h + 1) * LANES)
            taps = w_dep_ref[:, :, lanes].astype(F32)
            x = [wide_ref[i + a, :, lanes] for a in range(3)]
            u = [sum(x[a] * taps[a, b : b + 1] for a in range(3)) for b in range(3)]
            pre = pltpu.roll(u[0], 1, 0) + u[1] + pltpu.roll(u[2], wide - 1, 0)
            _, slope = gelu_and_slope(pre)
            slope = slope * keep
            main_ref[i, :, lanes] = slope[:cols].astype(BF16)
            side_out_ref[i, :, lanes] = slope[cols:] * side_mask


def run_slope(flags, ring, w_depth, spread):
    rows, cols, expanded = spread.shape
    return pl.pallas_call(
        slope_kernel,
        grid=(expanded // BLOCK,),
        in_specs=[
            pl.BlockSpec(memory_space=pltpu.SMEM),
            last_block(ring.shape), last_block(w_depth.shape), last_block(spread.shape),
        ],
        out_specs=[last_block((rows + 2, cols, expanded)), last_block((rows + 2, 8, expanded))],
        out_shape=[
            jax.ShapeDtypeStruct((rows + 2, cols, expanded), BF16),
            jax.ShapeDtypeStruct((rows + 2, 8, expanded), F32),
        ],
        scratch_shapes=[pltpu.VMEM((rows + 4, cols + 8, BLOCK), F32)],
        compiler_params=PARAMS,
        cost_estimate=estimate(13),
        name="slope",
    )(flags, ring, w_depth, spread)


def mix_kernel(
    cells_total, stride, bands,
    parts_ref, w_sq_ref, w_ex_ref, act_ref, image_ref, w_proj_ref, gain_ref, after_ref,
    pooled_ref, hidden_ref, gate_ref, mixed_ref, send_ref,
):
    step = pl.program_id(0)

    @pl.when(step == 0)
    def _():
        pooled = jnp.sum(parts_ref[...], axis=0) / cells_total
        hidden = dot_exact(pooled, w_sq_ref[...].astype(F32), ((1,), (0,)))
        silu = hidden * jax.nn.sigmoid(hidden)
        pooled_ref[...] = pooled
        hidden_ref[...] = hidden
        gate_ref[...] = jax.nn.sigmoid(dot_exact(silu, w_ex_ref[...].astype(F32), ((1,), (0,))))

    lines, cols, channels = image_ref.shape
    flat = act_ref[...].reshape(lines * cols, act_ref.shape[2])
    gated = (flat.astype(F32) * gate_ref[...]).astype(BF16)
    product = dot(gated, w_proj_ref[...])
    mixed = (image_ref[...].reshape(lines * cols, channels).astype(F32) + product).astype(BF16)
    mixed_ref[...] = mixed.reshape(lines, cols, channels)
    unit, _ = norm_rows(mixed.astype(F32))
    normed = (unit * gain_ref[...].astype(F32)).astype(BF16)
    for k in range(lines):
        line = step * lines + k
        for band in range(bands):
            start = k * cols + band * SIDE
            send_ref[lax.rem(line, stride) * bands + band, line // stride] = normed[
                start : start + SIDE
            ]


def run_mix(cells_total, stride, parts, w_squeeze, w_excite, act, image, w_project, gain, after):
    rows, cols, channels = image.shape
    expanded = act.shape[2]
    lines = 4
    bands = cols // SIDE
    block = lambda width: pl.BlockSpec((lines, cols, width), lambda r: (r, 0, 0))
    send = (stride * bands, rows // stride, SIDE, channels)
    return pl.pallas_call(
        functools.partial(mix_kernel, cells_total, stride, bands),
        grid=(rows // lines,),
        in_specs=[
            whole(parts.shape), whole(w_squeeze.shape), whole(w_excite.shape),
            block(expanded), block(channels), whole(w_project.shape), whole(gain.shape),
            pl.BlockSpec(memory_space=pl.ANY),
        ],
        out_specs=[
            whole((1, expanded)), whole((1, w_squeeze.shape[1])), whole((1, expanded)),
            block(channels), whole(send),
        ],
        out_shape=[
            jax.ShapeDtypeStruct((1, expanded), F32),
            jax.ShapeDtypeStruct((1, w_squeeze.shape[1]), F32),
            jax.ShapeDtypeStruct((1, expanded), F32),
            jax.ShapeDtypeStruct(image.shape, BF16),
            jax.ShapeDtypeStruct(send, BF16),
        ],
        compiler_params=PARAMS,
        cost_estimate=estimate(5),
        name="mix",
    )(parts, w_squeeze, w_excite, act, image, w_project, gain, after)


def attention_kernel(
    members, heads, lines,
    arrived_ref, cot_ref, w_qkv_ref, w_out_ref, bias_ref,
    x_ref, att_ref, grad_ref, packed_grad_ref, bias_out_ref,
    order_ref, packed_ref, att_grad_ref, bias_sum_ref,
):
    cells, channels = x_ref.shape
    groups = cells // members

    def places():
        for g in range(groups):
            for m in range(0, members, GRID):
                line, row = (m // GRID) % lines, m // GRID // lines
                start = (row * GRID * lines + line) * groups + g
                yield g * members + m, pl.ds(start, GRID, stride=lines * groups)

    for half in range(channels // LANES):
        lanes = slice(half * LANES, (half + 1) * LANES)
        order_ref[half] = arrived_ref[:, lanes].astype(F32)
        for g in range(groups):
            pieces = [order_ref[half, at, :] for k, at in places() if k // members == g]
            at = slice(g * members, (g + 1) * members)
            x_ref[at, lanes] = jnp.concatenate(pieces, axis=0).astype(BF16)
    dim = channels // heads
    per_half = LANES // dim
    halves = channels // LANES
    scale = dim ** (-0.5)
    packed_ref[...] = dot(x_ref[...], w_qkv_ref[...]).astype(BF16)
    att_grad_ref[...] = dot(cot_ref[...], w_out_ref[...], ((1,), (1,))).astype(BF16)
    bias_sum_ref[...] = jnp.zeros(bias_sum_ref.shape, F32)
    tall = per_half * members
    mask = (
        lax.broadcasted_iota(jnp.int32, (tall, LANES), 0) // members
        == lax.broadcasted_iota(jnp.int32, (tall, LANES), 1) // dim
    ).astype(F32).astype(BF16)
    owner = lax.broadcasted_iota(jnp.int32, (members, 2 * LANES), 1) % LANES // dim
    zero = jnp.zeros((members, LANES), BF16)

    def by_head(pair):
        return jnp.concatenate(
            [jnp.concatenate([v] * per_half, axis=0) * mask for v in pair], axis=1
        )

    def diagonal(pair):
        return jnp.concatenate(
            [
                jnp.concatenate([pair[0], zero], axis=1),
                jnp.concatenate([zero, pair[1]], axis=1),
            ],
            axis=0,
        )

    def collect(v):
        parts = [v[h * members : (h + 1) * members] for h in range(per_half)]
        picked = parts[-1]
        for h in range(per_half - 1):
            picked = jnp.where(owner == h, parts[h], picked)
        return [picked[:, :LANES], picked[:, LANES:]]

    def blocks(v):
        return [v[:members, :LANES], v[members:, LANES:]]

    def over_members(v, reduce):
        parted = v.reshape(per_half, members, 2 * members)
        small = reduce(parted, axis=1, keepdims=True)
        return jnp.broadcast_to(small, parted.shape).reshape(v.shape)

    def pair_step(g, carry):
        at = [pl.ds(pl.multiple_of((2 * g + k) * members, 16), members) for k in range(2)]
        for half in range(halves):
            def lanes(part):
                start = part * channels + half * LANES
                return slice(start, start + LANES)

            q, k, v = ([packed_ref[at[n], lanes(part)] for n in range(2)] for part in range(3))
            cot = [att_grad_ref[at[n], lanes(0)] for n in range(2)]
            q_diag, cot_diag = diagonal(q), diagonal(cot)
            k_tall, v_tall = by_head(k), by_head(v)
            scores = dot(k_tall, q_diag, ((1,), (1,))) * scale + bias_ref[half]
            grad_probs = dot(v_tall, cot_diag, ((1,), (1,)))
            lifted = jnp.exp(scores - over_members(scores, jnp.max))
            soft = lifted * (1.0 / over_members(lifted, jnp.sum))
            soft_low = soft.astype(BF16)
            grad_scores = soft * (grad_probs - over_members(grad_probs * soft, jnp.sum))
            bias_sum_ref[half] += grad_scores
            scaled = (grad_scores * scale).astype(BF16)
            attended = blocks(dot(soft_low, v_tall, ((0,), (0,))))
            grad_q = blocks(dot(scaled, k_tall, ((0,), (0,))))
            grad_v = collect(dot(soft_low, cot_diag))
            grad_k = collect(dot(scaled, q_diag))
            for n in range(2):
                att_ref[at[n], lanes(0)] = attended[n].astype(BF16)
                for part, value in enumerate((grad_q, grad_k, grad_v)):
                    packed_grad_ref[at[n], lanes(part)] = value[n].astype(BF16)
        return carry

    lax.fori_loop(0, cells // members // 2, pair_step, 0, unroll=2)
    grad = dot(packed_grad_ref[...], w_qkv_ref[...], ((1,), (1,)))
    for half in range(halves):
        lanes = slice(half * LANES, (half + 1) * LANES)
        for k, at in places():
            order_ref[half, at, :] = grad[k : k + GRID, lanes]
        grad_ref[:, lanes] = order_ref[half].astype(BF16)
    for half in range(halves):
        both = bias_sum_ref[half]
        bias_out_ref[half] = both[:, :members] + both[:, members:]


def run_attention(arrived, cot, w_qkv, w_out, bias_tall, heads, lines):
    cells, channels = cot.shape
    halves, tall, members2 = bias_tall.shape
    members = members2 // 2
    vmem = pl.BlockSpec(memory_space=pltpu.VMEM)
    return pl.pallas_call(
        functools.partial(attention_kernel, members, heads, lines),
        in_specs=[vmem] * 5,
        out_specs=[vmem] * 5,
        out_shape=[
            jax.ShapeDtypeStruct((cells, channels), BF16),
            jax.ShapeDtypeStruct((cells, channels), BF16),
            jax.ShapeDtypeStruct((cells, channels), BF16),
            jax.ShapeDtypeStruct((cells, 3 * channels), BF16),
            jax.ShapeDtypeStruct((halves, tall, members), F32),
        ],
        scratch_shapes=[
            pltpu.VMEM((channels // LANES, cells, LANES), F32),
            pltpu.VMEM((cells, 3 * channels), BF16),
            pltpu.VMEM((cells, channels), BF16),
            pltpu.VMEM(bias_tall.shape, F32),
        ],
        compiler_params=PARAMS,
        cost_estimate=estimate(14),
        name="attention",
    )(arrived.reshape(cells, channels), cot, w_qkv, w_out, bias_tall)


def attention_weights_kernel(x_ref, packed_grad_ref, att_ref, cot_ref, bias_ref, out_ref):
    channels = x_ref.shape[1]
    wide = 3 * channels
    out_ref[:, :wide] = dot(x_ref[...], packed_grad_ref[...], ((0,), (0,))).astype(BF16)
    out_ref[:, wide : wide + channels] = dot(att_ref[...], cot_ref[...], ((0,), (0,))).astype(BF16)
    bias = jnp.concatenate([bias_ref[half] for half in range(bias_ref.shape[0])], axis=1)
    out_ref[:, wide + channels :] = bias.astype(BF16)


def run_attention_weights(x, packed_grad, att, cot, bias):
    channels = x.shape[1]
    vmem = pl.BlockSpec(memory_space=pltpu.VMEM)
    width = 4 * channels + bias.shape[0] * bias.shape[2]
    return pl.pallas_call(
        attention_weights_kernel,
        in_specs=[vmem] * 5,
        out_specs=vmem,
        out_shape=jax.ShapeDtypeStruct((channels, width), BF16),
        compiler_params=PARAMS,
        cost_estimate=estimate(5),
        name="attention_weights",
    )(x, packed_grad, att, cot, bias)


def mixed_back_kernel(
    stride, bands,
    recv_ref, mixed_ref, cot_ref, gain_ref, act_ref, gate_ref, w_projt_ref,
    grad_ref, low_ref, norm_ref, project_ref, gate_grad_ref,
    turned_ref, total_ref,
):
    rows, cols, channels = mixed_ref.shape

    @pl.when(pl.program_id(0) == 0)
    def _():
        gain = gain_ref[...].astype(F32)
        lines = 4

        def some_rows(c, total):
            pieces = []
            for k in range(lines):
                i = c * lines + k
                a, p = lax.rem(i, stride), i // stride
                pieces += [recv_ref[a * bands + band, p] for band in range(bands)]
            grad = jnp.concatenate(pieces, axis=0).astype(F32)
            at = pl.ds(c * lines, lines)
            flat = lambda ref: ref[at].reshape(lines * cols, channels).astype(F32)
            unit, rstd = norm_rows(flat(mixed_ref))
            back = flat(cot_ref) + norm_rows_back(unit, rstd, gain, grad)
            grad_ref[at] = back.reshape(lines, cols, channels)
            low_ref[at] = back.astype(BF16).reshape(lines, cols, channels)
            return total + fold_rows(grad * unit)

        total = lax.fori_loop(
            0, rows // lines, some_rows, jnp.zeros((8, channels), F32), unroll=2
        )
        norm_ref[...] = jnp.sum(total, axis=0, keepdims=True)
        turned_ref[...] = low_ref[...].reshape(rows * cols, channels).T

    flat = act_ref[...].reshape(rows * cols, BLOCK)
    product = dot(turned_ref[...], flat)
    total = jnp.sum(product * w_projt_ref[...].astype(F32), axis=0, keepdims=True)
    step, steps = pl.program_id(0), pl.num_programs(0)
    total_ref[step] = total
    project_ref[...] = (product * gate_ref[...]).T.astype(BF16)

    @pl.when(step == steps - 1)
    def _():
        sums = [total_ref[e] for e in range(total_ref.shape[0])]
        high = [v.astype(BF16).astype(F32) for v in sums]
        terms = jnp.concatenate(high + [v - w for v, w in zip(sums, high)], axis=0)
        gate_grad_ref[...] = jnp.broadcast_to(terms.astype(BF16)[None], gate_grad_ref.shape)


def run_mixed_back(count, stride, recv, mixed, cot, gain, act, gate, w_project_t):
    rows, cols, channels = mixed.shape
    expanded = act.shape[2]
    return pl.pallas_call(
        functools.partial(mixed_back_kernel, stride, cols // SIDE),
        grid=(expanded // BLOCK,),
        in_specs=[
            whole(recv.shape), whole(mixed.shape), whole(cot.shape), whole(gain.shape),
            last_block(act.shape), last_block(gate.shape), last_block(w_project_t.shape),
        ],
        out_specs=[
            whole(mixed.shape), whole(mixed.shape), whole((1, channels)),
            last_block((BLOCK, expanded)), whole((count, 2 * expanded // BLOCK, BLOCK)),
        ],
        out_shape=[
            jax.ShapeDtypeStruct(mixed.shape, F32),
            jax.ShapeDtypeStruct(mixed.shape, BF16),
            jax.ShapeDtypeStruct((1, channels), F32),
            jax.ShapeDtypeStruct((BLOCK, expanded), BF16),
            jax.ShapeDtypeStruct((count, 2 * expanded // BLOCK, BLOCK), BF16),
        ],
        scratch_shapes=[
            pltpu.VMEM((channels, rows * cols), BF16),
            pltpu.VMEM((expanded // BLOCK, 1, BLOCK), F32),
        ],
        compiler_params=PARAMS,
        cost_estimate=estimate(7),
        name="mixed_back",
    )(recv, mixed, cot, gain, act, gate, w_project_t)


def gate_back_kernel(
    cells_total, parts_ref, hidden_ref, gate_ref, w_sq_ref, w_ex_ref, logit_ref, pre_ref, pool_ref
):
    gate = gate_ref[...]
    terms = jnp.sum(parts_ref[...].astype(F32), axis=0)
    blocks = terms.shape[0] // 2
    gate_grad = jnp.concatenate(
        [terms[e : e + 1] + terms[blocks + e : blocks + e + 1] for e in range(blocks)], axis=1
    )
    logit = gate_grad * gate * (1.0 - gate)
    hidden = hidden_ref[...]
    sig = jax.nn.sigmoid(hidden)
    pre = dot_exact(logit, w_ex_ref[...].astype(F32), ((1,), (1,))) * (
        sig + hidden * sig * (1.0 - sig)
    )
    logit_ref[...] = logit
    pre_ref[...] = pre
    pool_ref[...] = dot_exact(pre, w_sq_ref[...].astype(F32), ((1,), (1,))) / cells_total


def run_gate_back(cells_total, parts, hidden, gate, w_squeeze, w_excite):
    expanded = gate.shape[1]
    terms = 2 * expanded // BLOCK
    return pl.pallas_call(
        functools.partial(gate_back_kernel, cells_total),
        grid=(1,),
        in_specs=[
            pl.BlockSpec(
                (parts.shape[0], terms, BLOCK), lambda e: (0, parts.shape[1] // terms - 1, 0)
            ),
            whole(hidden.shape), whole(gate.shape), whole(w_squeeze.shape), whole(w_excite.shape),
        ],
        out_specs=[whole(gate.shape), whole(hidden.shape), whole(gate.shape)],
        out_shape=[
            jax.ShapeDtypeStruct(gate.shape, F32),
            jax.ShapeDtypeStruct(hidden.shape, F32),
            jax.ShapeDtypeStruct(gate.shape, F32),
        ],
        compiler_params=PARAMS,
        cost_estimate=estimate(60),
        name="gate_back",
    )(parts, hidden, gate, w_squeeze, w_excite)


def unpack_kernel(late_ref, expand_ref, depth_ref, norm0_ref, norm1_ref):
    channels, expanded = expand_ref.shape
    expand_ref[...] = late_ref[:, :expanded].astype(F32)
    tail = late_ref[:, expanded:].astype(F32)
    pieces = expanded // LANES
    for t in range(9):
        for k in range(pieces):
            row = t * pieces + k
            lanes = slice(k * LANES, (k + 1) * LANES)
            depth_ref[t // 3, t % 3 : t % 3 + 1, lanes] = tail[row : row + 1]
    start = 9 * pieces
    half = channels // LANES
    for k in range(half):
        lanes = slice(k * LANES, (k + 1) * LANES)
        norm0_ref[:, lanes] = tail[start + k : start + k + 1]
        norm1_ref[:, lanes] = tail[start + half + k : start + half + k + 1]


def run_unpack(late, expanded):
    channels = late.shape[0]
    vmem = pl.BlockSpec(memory_space=pltpu.VMEM)
    return pl.pallas_call(
        unpack_kernel,
        in_specs=[vmem],
        out_specs=[vmem] * 4,
        out_shape=[
            jax.ShapeDtypeStruct((channels, expanded), F32),
            jax.ShapeDtypeStruct((3, 3, expanded), F32),
            jax.ShapeDtypeStruct((1, channels), F32),
            jax.ShapeDtypeStruct((1, channels), F32),
        ],
        compiler_params=PARAMS,
        cost_estimate=estimate(100),
        name="unpack",
    )(late)


def expand_back_kernel(
    pool_ref, low_ref, up_ref, down_ref, side_ref, w_projt_ref, gate_ref, slope_ref, side_slope_ref,
    spread_slope_ref, spread_ref, w_dep_ref, turned_ref, w_exp_ref, gain_ref, norm1_ref,
    weights_ref, first_ref,
    main_ref, side_grad_ref, window_ref, expanded_ref, tail_ref, norm_ref,
):
    rows, cols, channels = low_ref.shape
    side = 8
    wide = cols + side
    step = pl.program_id(0)
    steps = pl.num_programs(0)

    @pl.when(step == 0)
    def _():
        first_ref[...] = jnp.zeros(first_ref.shape, F32)
        tail_ref[...] = jnp.zeros(tail_ref.shape, F32)
        norm_ref[...] = jnp.zeros(norm_ref.shape, F32)

    w_projt = w_projt_ref[...]
    main_ref[pl.ds(0, cols), :] = dot(up_ref[0], w_projt)
    main_ref[pl.ds(cols, rows * cols), :] = dot(
        low_ref[...].reshape(rows * cols, channels), w_projt
    )
    main_ref[pl.ds((rows + 1) * cols, cols), :] = dot(down_ref[0], w_projt)
    side_grad_ref[...] = dot(side_ref[...], w_projt)

    @pl.loop(0, rows + 2, unroll=3)
    def _(i):
        for h in range(BLOCK // LANES):
            lanes = slice(h * LANES, (h + 1) * LANES)
            gate = gate_ref[:, lanes]
            pooled = pool_ref[:, lanes]
            gated = main_ref[pl.ds(pl.multiple_of(i * cols, 16), cols), lanes]
            main = (gated * gate + pooled) * slope_ref[i, :, lanes].astype(F32)
            gated = side_grad_ref[pl.ds(pl.multiple_of(i * side, side), side), lanes]
            edge = (gated * gate + pooled) * side_slope_ref[i, :, lanes]
            grad = jnp.concatenate([main, edge], axis=0)
            window_ref[0, i, :, lanes] = pltpu.roll(grad, wide - 1, 0)[:cols]
            window_ref[1, i, :, lanes] = grad[:cols]
            window_ref[2, i, :, lanes] = pltpu.roll(grad, 1, 0)[:cols]

    for h in range(BLOCK // LANES):
        lanes = slice(h * LANES, (h + 1) * LANES)
        taps = w_dep_ref[:, :, lanes].astype(F32)

        def back_row(i, sums):
            spread = spread_ref[i, :, lanes].astype(F32)
            total = jnp.zeros((cols, LANES), F32)
            new_sums = []
            for a in range(3):
                for b in range(3):
                    window = window_ref[b, i + 2 - a, :, lanes]
                    total = total + window * taps[a, b : b + 1]
                    new_sums.append(sums[a * 3 + b] + fold_rows(window * spread))
            grad = total * spread_slope_ref[i, :, lanes].astype(F32)
            expanded_ref[pl.ds(pl.multiple_of(i * cols, 16), cols), lanes] = grad.astype(BF16)
            return tuple(new_sums)

        sums = lax.fori_loop(0, rows, back_row, (jnp.zeros((8, LANES), F32),) * 9, unroll=2)
        for t in range(9):
            row = t * (steps * BLOCK // LANES) + step * (BLOCK // LANES) + h
            tail_ref[pl.ds(row, 1), :] = jnp.sum(sums[t], axis=0, keepdims=True)

    grad_expanded = expanded_ref[...]
    w_exp = w_exp_ref[...]
    weights = dot(turned_ref[...], grad_expanded)
    weights_ref[:, pl.ds(pl.multiple_of(step * BLOCK, BLOCK), BLOCK)] = weights.astype(BF16)
    norm_ref[...] += jnp.sum(weights * w_exp.astype(F32), axis=1, keepdims=True)
    first_ref[...] += dot(grad_expanded, w_exp, ((1,), (1,)))

    @pl.when(step == steps - 1)
    def _():
        norm = norm_ref[...].T[0:1] / gain_ref[...].astype(F32)
        start = 9 * steps * (BLOCK // LANES)
        for k in range(channels // LANES):
            piece = slice(k * LANES, (k + 1) * LANES)
            tail_ref[start + k : start + k + 1, :] = norm[:, piece]
            at = start + channels // LANES + k
            tail_ref[at : at + 1, :] = norm1_ref[:, piece]
        weights_ref[:, steps * BLOCK :] = tail_ref[...].astype(BF16)


def run_expand_back(
    pool, gate, low, up, down, side,
    w_project_t, slope, side_slope, spread_slope, spread, w_depth, turned, w_expand, gain, norm1,
):
    rows, cols, channels = low.shape
    expanded = w_expand.shape[1]
    steps = expanded // BLOCK
    return pl.pallas_call(
        expand_back_kernel,
        grid=(steps,),
        in_specs=[
            last_block(pool.shape),
            whole(low.shape), whole(up.shape), whole(down.shape), whole(side.shape),
            last_block(w_project_t.shape), last_block(gate.shape), last_block(slope.shape),
            last_block(side_slope.shape), last_block(spread_slope.shape), last_block(spread.shape),
            last_block(w_depth.shape), whole(turned.shape), last_block(w_expand.shape),
            whole(gain.shape), whole(norm1.shape),
        ],
        out_specs=[
            whole((channels, expanded + LANES)), whole((rows * cols, channels)),
        ],
        out_shape=[
            jax.ShapeDtypeStruct((channels, expanded + LANES), BF16),
            jax.ShapeDtypeStruct((rows * cols, channels), F32),
        ],
        scratch_shapes=[
            pltpu.VMEM(((rows + 2) * cols, BLOCK), F32),
            pltpu.VMEM(((rows + 2) * 8, BLOCK), F32),
            pltpu.VMEM((3, rows + 2, cols, BLOCK), F32),
            pltpu.VMEM((rows * cols, BLOCK), BF16),
            pltpu.VMEM((channels, LANES), F32),
            pltpu.VMEM((channels, LANES), F32),
        ],
        compiler_params=PARAMS,
        cost_estimate=estimate(14),
        name="expand_back",
    )(
        pool, low, up, down, side, w_project_t, gate,
        slope, side_slope, spread_slope, spread, w_depth, turned, w_expand, gain, norm1,
    )


def image_back_kernel(image_ref, gain_ref, first_ref, mixed_ref, out_ref):
    unit, rstd = norm_rows(image_ref[...].astype(F32))
    grad = first_ref[...]
    back = mixed_ref[...] + norm_rows_back(unit, rstd, gain_ref[...].astype(F32), grad)
    out_ref[...] = back.astype(BF16)


def run_image_back(image, gain, first, mixed):
    cells, channels = image.shape
    block = pl.BlockSpec((cells // 4, channels), lambda r: (r, 0))
    return pl.pallas_call(
        image_back_kernel,
        grid=(4,),
        in_specs=[block, whole(gain.shape), block, block],
        out_specs=block,
        out_shape=jax.ShapeDtypeStruct((cells, channels), BF16),
        compiler_params=PARAMS,
        cost_estimate=estimate(4),
        name="image_back",
    )(image, gain, first, mixed)


def shift(cells, axis, step):
    count = lax.axis_size(axis)
    pairs = [(i, i + step) for i in range(count) if 0 <= i + step < count]
    return lax.ppermute(cells, axis, pairs)


def halo_rows(cells, width):
    up = shift(cells[cells.shape[0] - width :], "row", 1)
    down = shift(cells[:width], "row", -1)
    return up, down


def halo_sides(cells, up, down, width):
    rows, cols, channels = cells.shape
    first = jnp.concatenate([up[:, :width], cells[:, :width], down[:, :width]], axis=0)
    last = jnp.concatenate(
        [up[:, cols - width :], cells[:, cols - width :], down[:, cols - width :]], axis=0
    )
    left = shift(last, "col", 1)
    right = shift(first, "col", -1)
    gap = jnp.zeros((rows + 2 * width, 8 - 2 * width, channels), cells.dtype)
    side = jnp.concatenate([right, gap, left], axis=1)
    return side.reshape(-1, channels)


def hand_around(blocks):
    return lax.all_to_all(blocks, AXES, split_axis=0, concat_axis=0, tiled=True)


def sum_shares(matrix):
    rows, columns = matrix.shape
    count = lax.axis_size("row") * lax.axis_size("col")
    share = rows // count
    arrived = hand_around(matrix.reshape(count, share, columns))
    total = jnp.sum(arrived.astype(F32), axis=0).astype(BF16)
    sent = jnp.broadcast_to(total[None], (count, share, columns))
    return hand_around(sent).reshape(rows, columns)


def cube_steps():
    steps = [("col", 1)]
    for axis in ("row", "col"):
        step = 1 if axis == "row" else 2
        while step < lax.axis_size(axis):
            steps.append((axis, step))
            step *= 2
    return steps


def swap_pairs(v, axis, step):
    return lax.ppermute(v, axis, [(i, i ^ step) for i in range(lax.axis_size(axis))])


def sum_half(matrix, axis, step):
    bit = lax.axis_index(axis) // step % 2
    halves = matrix.reshape(2, matrix.shape[0] // 2, matrix.shape[1])
    sent = lax.dynamic_index_in_dim(halves, 1 - bit, 0, False)
    kept = lax.dynamic_index_in_dim(halves, bit, 0, False)
    return (kept.astype(F32) + swap_pairs(sent, axis, step).astype(F32)).astype(BF16)


def join_halves(matrix, axis, step):
    bit = lax.axis_index(axis) // step % 2
    other = swap_pairs(matrix, axis, step)
    return jnp.where(
        bit == 0,
        jnp.concatenate([matrix, other], axis=0),
        jnp.concatenate([other, matrix], axis=0),
    )


def swap_groups(blocks, parity):
    groups = None
    if parity > 1:
        over_row = lax.axis_size("row")
        over_col = lax.axis_size("col")
        groups = [
            [r * over_col + c for r in range(over_row) for c in range(k, over_col, parity)]
            for k in range(parity)
        ]
    return lax.all_to_all(
        blocks, AXES, split_axis=0, concat_axis=0, tiled=True, axis_index_groups=groups
    )


def on_device(
    image, out_cotangent, norm0_gain, w_expand, w_depth, w_squeeze, w_excite, w_project,
    norm1_gain, w_qkv, w_out, attn_bias,
):
    rows, cols, channels = image.shape
    over_row = lax.axis_size("row")
    over_col = lax.axis_size("col")
    count = over_row * over_col
    cells_total = rows * cols * count
    stride = rows * over_row // GRID
    parity = over_col // GRID
    lines = rows // stride
    bands = cols // SIDE
    members = GRID * GRID
    expanded = w_expand.shape[1]

    def into_members(arrived):
        parted = arrived.reshape(over_row, GRID, lines, SIDE, channels)
        return parted.transpose(3, 0, 2, 1, 4).reshape(SIDE * members, channels)

    def out_of_members(values):
        parted = values.reshape(SIDE, over_row, lines, GRID, channels)
        return parted.transpose(1, 3, 2, 0, 4).reshape(-1, lines, SIDE, channels)

    row, col = lax.axis_index("row"), lax.axis_index("col")
    flags = jnp.stack([row > 0, row < over_row - 1, col > 0, col < over_col - 1]).astype(F32)
    gain_first = norm0_gain.reshape(1, channels)
    gain_second = norm1_gain.reshape(1, channels)
    w_project_t = w_project.T
    heads = attn_bias.shape[0]
    halves = channels // LANES
    bias_tall = attn_bias.transpose(0, 2, 1).reshape(halves, heads // halves * members, members)
    bias_tall = jnp.concatenate([bias_tall, bias_tall], axis=2)

    up, down = halo_rows(image, 2)
    normed_first, turned_first, spread, spread_slope = run_expand(image, gain_first, w_expand)
    up, down, spread = lax.optimization_barrier((up, down, spread))
    side = halo_sides(image, up, down, 2)
    cot_sent = (
        out_cotangent.reshape(lines, stride, bands, SIDE, channels)
        .transpose(1, 2, 0, 3, 4)
        .reshape(stride * bands, lines, SIDE, channels)
    )
    cot_members = into_members(swap_groups(cot_sent, parity))
    ring, act, pool = run_depthwise(count, up, down, side, gain_first, w_expand, w_depth, spread)
    pooled, hidden, gate, mixed, normed_sent = run_mix(
        cells_total, stride, hand_around(pool), w_squeeze, w_excite, act, image, w_project,
        gain_second, cot_members,
    )
    slope, side_slope = run_slope(flags, ring, w_depth, spread)
    normed_arrived = swap_groups(normed_sent, parity)
    normed_arrived, slope = lax.optimization_barrier((normed_arrived, slope))
    normed_members, attended, grad_normed, packed_grad, grad_bias = run_attention(
        normed_arrived, cot_members, w_qkv, w_out, bias_tall, heads, lines
    )
    grad_normed_home = swap_groups(grad_normed.reshape(normed_sent.shape), parity)
    weights = run_attention_weights(normed_members, packed_grad, attended, cot_members, grad_bias)
    steps = cube_steps()
    for axis, step in steps[:2]:
        weights = sum_half(weights, axis, step)
    grad_normed_home, weights = lax.optimization_barrier((grad_normed_home, weights))
    grad_mixed, grad_low, grad_norm1, grad_project, gate_grad = run_mixed_back(
        count, stride, grad_normed_home, mixed, out_cotangent, gain_second, act, gate, w_project_t
    )
    attended_sent = out_of_members(attended)
    if parity == 1:
        both = hand_around(
            jnp.concatenate([attended_sent.reshape(count, -1, channels), gate_grad], axis=1)
        )
        parts = both
        attended_home = both[:, : lines * SIDE].reshape(attended_sent.shape)
    else:
        parts = hand_around(gate_grad)
        attended_home = swap_groups(attended_sent, parity)
    up, down = halo_rows(grad_low, 1)
    side = halo_sides(grad_low, up, down, 1)
    grad_project, _ = lax.optimization_barrier((grad_project, up))
    for axis, step in steps[:2]:
        grad_project = sum_half(grad_project, axis, step)
    weights = jnp.concatenate([weights, grad_project], axis=1)
    for axis, step in steps[2:-1]:
        weights = sum_half(weights, axis, step)
    logit, pre, pool_grad = run_gate_back(cells_total, parts, hidden, gate, w_squeeze, w_excite)
    late, grad_first = run_expand_back(
        pool_grad, gate, grad_low, up, down, side,
        w_project_t, slope, side_slope, spread_slope, spread, w_depth, turned_first, w_expand,
        gain_first, grad_norm1,
    )
    weights, _ = lax.optimization_barrier((weights, late))
    weights = sum_half(weights, *steps[-1])
    for axis, step in reversed(steps):
        weights = join_halves(weights, axis, step)
    weights = weights.astype(F32)
    grad_expand, grad_depth, grad_norm0, grad_norm1 = run_unpack(sum_shares(late), expanded)
    grad_image = run_image_back(
        image.reshape(-1, channels), gain_first, grad_first, grad_mixed.reshape(-1, channels)
    )
    attended_map = (
        attended_home.reshape(stride, bands, lines, SIDE, channels)
        .transpose(2, 0, 1, 3, 4)
        .reshape(rows * cols, channels)
    )
    block_out = (mixed.reshape(-1, channels).astype(F32) + dot(attended_map, w_out)).astype(BF16)

    silu = jax.nn.silu(hidden)
    grad_squeeze = pooled.reshape(expanded, 1) * pre
    grad_excite = silu.reshape(-1, 1) * logit

    ends = 4 * channels + halves * members
    grad_bias = (
        weights[:, 4 * channels : ends]
        .reshape(heads // halves, members, halves, members)
        .transpose(2, 0, 3, 1)
        .reshape(attn_bias.shape)
    )
    grad_project = (
        weights[:, ends:].reshape(BLOCK, expanded // BLOCK, channels).transpose(1, 0, 2)
    ).reshape(w_project.shape)
    return (
        block_out.reshape(image.shape),
        grad_image.reshape(image.shape),
        grad_norm0[0],
        grad_expand,
        grad_depth,
        grad_squeeze,
        grad_excite,
        grad_project,
        grad_norm1[0],
        weights[:, : 3 * channels],
        weights[:, 3 * channels : 4 * channels],
        grad_bias,
    )


def solution(mesh):
    cells = P("row", "col", None)
    return jax.shard_map(
        on_device,
        mesh=mesh,
        in_specs=(cells, cells) + (P(),) * 10,
        out_specs=(cells, cells) + (P(),) * 10,
        check_vma=False,
    )
```

```python
import functools
import math

import jax
import jax.numpy as jnp
from jax import lax
from jax.experimental import pallas as pl
from jax.experimental.pallas import tpu as pltpu
from jax.sharding import PartitionSpec as P

GRID = 8
AXES = ("row", "col")
BLOCK = 256
LANES = 128
SIDE = 16
GELU_A = math.sqrt(2.0 / math.pi)
GELU_B = GELU_A * 0.044715
F32 = jnp.float32
BF16 = jnp.bfloat16
PARAMS = pltpu.CompilerParams(vmem_limit_bytes=56 * 1024 * 1024)


def estimate(us):
    return pl.CostEstimate(flops=int(us * 1.1e9), bytes_accessed=int(us * 3.6e6), transcendentals=0)


def dot(left, right, contract=((1,), (0,))):
    return lax.dot_general(left, right, (contract, ((), ())), preferred_element_type=F32)


def dot_exact(vector, right, contract):
    tall = jnp.broadcast_to(vector, (8, vector.shape[1]))
    product = lax.dot_general(
        tall, right, (contract, ((), ())), precision=lax.Precision.HIGHEST, preferred_element_type=F32
    )
    return product[0:1]


def gelu_and_slope(x, with_slope=True):
    square = x * x
    t = jnp.tanh(x * (GELU_A + GELU_B * square))
    half = 0.5 + 0.5 * t
    value = x * half
    if not with_slope:
        return value, None
    slope = half + (value * (1.0 - t)) * (GELU_A + (3.0 * GELU_B) * square)
    return value, slope


def norm_rows(x):
    average = jnp.mean(x, axis=-1, keepdims=True)
    centered = x - average
    variance = jnp.mean(centered * centered, axis=-1, keepdims=True)
    rstd = lax.rsqrt(variance + 1e-05)
    return centered * rstd, rstd


def norm_rows_back(unit, rstd, gain, grad):
    unit_grad = grad * gain
    first = jnp.mean(unit_grad, axis=-1, keepdims=True)
    second = jnp.mean(unit_grad * unit, axis=-1, keepdims=True)
    return rstd * (unit_grad - first - unit * second)


def fold_rows(x):
    return jnp.sum(x.reshape(x.shape[0] // 8, 8, x.shape[1]), axis=0)


def whole(shape):
    return pl.BlockSpec(shape, lambda e: (0,) * len(shape))


def last_block(shape):
    lead = (0,) * (len(shape) - 1)
    return pl.BlockSpec(shape[:-1] + (BLOCK,), lambda e: lead + (e,))


def expand_kernel(
    image_ref, gain_ref, w_exp_ref,
    normed_ref, turned_ref, spread_ref, slope_ref,
    expanded_ref,
):
    rows, cols, channels = image_ref.shape

    @pl.when(pl.program_id(0) == 0)
    def _():
        gain = gain_ref[...].astype(F32)

        @pl.loop(0, rows // 4)
        def _(c):
            flat = image_ref[pl.ds(c * 4, 4)].reshape(4 * cols, channels)
            unit, _ = norm_rows(flat.astype(F32))
            at = pl.ds(pl.multiple_of(c * 4 * cols, 16), 4 * cols)
            normed_ref[at, :] = (unit * gain).astype(BF16)

        turned_ref[...] = normed_ref[...].T

    expanded_ref[...] = dot(normed_ref[...], w_exp_ref[...])

    @pl.loop(0, rows, unroll=4)
    def _(r):
        for h in range(BLOCK // LANES):
            lanes = slice(h * LANES, (h + 1) * LANES)
            x = expanded_ref[pl.ds(pl.multiple_of(r * cols, 16), cols), lanes]
            value, slope = gelu_and_slope(x)
            spread_ref[r, :, lanes] = value.astype(BF16)
            slope_ref[r, :, lanes] = slope.astype(BF16)


def run_expand(image, gain, w_expand):
    rows, cols, channels = image.shape
    expanded = w_expand.shape[1]
    return pl.pallas_call(
        expand_kernel,
        grid=(expanded // BLOCK,),
        in_specs=[whole(image.shape), whole(gain.shape), last_block(w_expand.shape)],
        out_specs=[
            whole((rows * cols, channels)), whole((channels, rows * cols)),
            last_block((rows, cols, expanded)), last_block((rows, cols, expanded)),
        ],
        out_shape=[
            jax.ShapeDtypeStruct((rows * cols, channels), BF16),
            jax.ShapeDtypeStruct((channels, rows * cols), BF16),
            jax.ShapeDtypeStruct((rows, cols, expanded), BF16),
            jax.ShapeDtypeStruct((rows, cols, expanded), BF16),
        ],
        scratch_shapes=[pltpu.VMEM((rows * cols, BLOCK), F32)],
        compiler_params=PARAMS,
        cost_estimate=estimate(14),
        name="expand",
    )(image, gain, w_expand)


def depthwise_kernel(
    up_ref, down_ref, side_ref, gain_ref, w_exp_ref, w_dep_ref, spread_ref,
    ring_ref, act_ref, pool_ref,
    ring_normed_ref, ring_wide_ref,
):
    rows, cols, _ = spread_ref.shape
    channels = up_ref.shape[2]
    over = 4 * cols
    side = 8

    @pl.when(pl.program_id(0) == 0)
    def _():
        gain = gain_ref[...].astype(F32)

        def put(at, values):
            unit, _ = norm_rows(values.astype(F32))
            ring_normed_ref[at : at + values.shape[0], :] = (unit * gain).astype(BF16)

        put(0, up_ref[...].reshape(2 * cols, channels))
        put(2 * cols, down_ref[...].reshape(2 * cols, channels))
        put(over, side_ref[...])

    ring_wide_ref[...] = dot(ring_normed_ref[...], w_exp_ref[...])
    tile = 32

    @pl.loop(0, ring_wide_ref.shape[0] // tile, unroll=True)
    def _(t):
        at = pl.ds(pl.multiple_of(t * tile, tile), tile)
        value, _ = gelu_and_slope(ring_wide_ref[at, :], False)
        low = value.astype(BF16)
        ring_ref[at, :] = low
        ring_wide_ref[at, :] = low.astype(F32)

    for h in range(BLOCK // LANES):
        lanes = slice(h * LANES, (h + 1) * LANES)
        taps = w_dep_ref[:, :, lanes].astype(F32)
        w = [[taps[a, b : b + 1] for b in range(3)] for a in range(3)]

        def line(r, main):
            at = pl.multiple_of(over + (r + 2) * side, side)
            return jnp.concatenate([main, ring_wide_ref[pl.ds(at, side), lanes]], axis=0)

        def conv(i, x, total):
            u = [x[0] * w[0][b] + x[1] * w[1][b] + x[2] * w[2][b] for b in range(3)]
            wide = cols + side
            pre = pltpu.roll(u[0], 1, 0) + u[1] + pltpu.roll(u[2], wide - 1, 0)
            value, _ = gelu_and_slope(pre[:cols], False)
            act_ref[i, :, lanes] = value.astype(BF16)
            return total + fold_rows(value)

        def step(i, carry):
            first, second, total = carry
            third = line(i + 1, spread_ref[i + 1, :, lanes].astype(F32))
            return second, third, conv(i, (first, second, third), total)

        carry = (
            line(-1, ring_wide_ref[cols : 2 * cols, lanes]),
            line(0, spread_ref[0, :, lanes].astype(F32)),
            jnp.zeros((8, LANES), F32),
        )
        first, second, total = lax.fori_loop(0, rows - 1, step, carry, unroll=5)
        third = line(rows, ring_wide_ref[2 * cols : 3 * cols, lanes])
        total = conv(rows - 1, (first, second, third), total)
        total = jnp.sum(total, axis=0, keepdims=True)
        pool_ref[:, :, lanes] = jnp.broadcast_to(total[None], (pool_ref.shape[0], 1, LANES))


def run_depthwise(count, up, down, side, gain, w_expand, w_depth, spread):
    rows, cols, expanded = spread.shape
    channels = up.shape[2]
    ring = 4 * cols + 8 * (rows + 4)
    return pl.pallas_call(
        depthwise_kernel,
        grid=(expanded // BLOCK,),
        in_specs=[
            whole(up.shape), whole(down.shape), whole(side.shape), whole(gain.shape),
            last_block(w_expand.shape), last_block(w_depth.shape), last_block(spread.shape),
        ],
        out_specs=[
            last_block((ring, expanded)), last_block(spread.shape), last_block((count, 1, expanded)),
        ],
        out_shape=[
            jax.ShapeDtypeStruct((ring, expanded), BF16),
            jax.ShapeDtypeStruct(spread.shape, BF16),
            jax.ShapeDtypeStruct((count, 1, expanded), F32),
        ],
        scratch_shapes=[pltpu.VMEM((ring, channels), BF16), pltpu.VMEM((ring, BLOCK), F32)],
        compiler_params=PARAMS,
        cost_estimate=estimate(1),
        name="depthwise",
    )(up, down, side, gain, w_expand, w_depth, spread)


def slope_kernel(flags_ref, ring_ref, w_dep_ref, spread_ref, main_ref, side_out_ref, wide_ref):
    rows, cols, _ = spread_ref.shape
    over = 4 * cols
    side = 8
    wide = cols + side

    for k, r in enumerate((0, 1, rows + 2, rows + 3)):
        wide_ref[r, :cols, :] = ring_ref[k * cols : (k + 1) * cols, :].astype(F32)
    sides = ring_ref[over:, :].astype(F32)
    for r in range(rows + 4):
        wide_ref[r, cols:, :] = sides[r * side : (r + 1) * side]

    @pl.loop(0, rows)
    def _(r):
        wide_ref[r + 2, :cols, :] = spread_ref[r].astype(F32)

    place = lax.broadcasted_iota(jnp.int32, (side, LANES), 0)
    side_mask = jnp.where(
        place == side - 1, flags_ref[2], jnp.where(place == 0, flags_ref[3], 1.0)
    ).astype(F32)

    @pl.loop(0, rows + 2)
    def _(i):
        keep = jnp.where(i == 0, flags_ref[0], jnp.where(i == rows + 1, flags_ref[1], 1.0))
        for h in range(BLOCK // LANES):
            lanes = slice(h * LANES, (h + 1) * LANES)
            taps = w_dep_ref[:, :, lanes].astype(F32)
            x = [wide_ref[i + a, :, lanes] for a in range(3)]
            u = [sum(x[a] * taps[a, b : b + 1] for a in range(3)) for b in range(3)]
            pre = pltpu.roll(u[0], 1, 0) + u[1] + pltpu.roll(u[2], wide - 1, 0)
            _, slope = gelu_and_slope(pre)
            slope = slope * keep
            main_ref[i, :, lanes] = slope[:cols].astype(BF16)
            side_out_ref[i, :, lanes] = slope[cols:] * side_mask


def run_slope(flags, ring, w_depth, spread):
    rows, cols, expanded = spread.shape
    return pl.pallas_call(
        slope_kernel,
        grid=(expanded // BLOCK,),
        in_specs=[
            pl.BlockSpec(memory_space=pltpu.SMEM),
            last_block(ring.shape), last_block(w_depth.shape), last_block(spread.shape),
        ],
        out_specs=[last_block((rows + 2, cols, expanded)), last_block((rows + 2, 8, expanded))],
        out_shape=[
            jax.ShapeDtypeStruct((rows + 2, cols, expanded), BF16),
            jax.ShapeDtypeStruct((rows + 2, 8, expanded), F32),
        ],
        scratch_shapes=[pltpu.VMEM((rows + 4, cols + 8, BLOCK), F32)],
        compiler_params=PARAMS,
        cost_estimate=estimate(13),
        name="slope",
    )(flags, ring, w_depth, spread)


def mix_kernel(
    cells_total, stride, bands,
    parts_ref, w_sq_ref, w_ex_ref, act_ref, image_ref, w_proj_ref, gain_ref, after_ref,
    pooled_ref, hidden_ref, gate_ref, mixed_ref, send_ref,
):
    step = pl.program_id(0)

    @pl.when(step == 0)
    def _():
        pooled = jnp.sum(parts_ref[...], axis=0) / cells_total
        hidden = dot_exact(pooled, w_sq_ref[...].astype(F32), ((1,), (0,)))
        silu = hidden * jax.nn.sigmoid(hidden)
        pooled_ref[...] = pooled
        hidden_ref[...] = hidden
        gate_ref[...] = jax.nn.sigmoid(dot_exact(silu, w_ex_ref[...].astype(F32), ((1,), (0,))))

    lines, cols, channels = image_ref.shape
    flat = act_ref[...].reshape(lines * cols, act_ref.shape[2])
    gated = (flat.astype(F32) * gate_ref[...]).astype(BF16)
    product = dot(gated, w_proj_ref[...])
    mixed = (image_ref[...].reshape(lines * cols, channels).astype(F32) + product).astype(BF16)
    mixed_ref[...] = mixed.reshape(lines, cols, channels)
    unit, _ = norm_rows(mixed.astype(F32))
    normed = (unit * gain_ref[...].astype(F32)).astype(BF16)
    for k in range(lines):
        line = step * lines + k
        for band in range(bands):
            start = k * cols + band * SIDE
            send_ref[lax.rem(line, stride) * bands + band, line // stride] = normed[
                start : start + SIDE
            ]


def run_mix(cells_total, stride, parts, w_squeeze, w_excite, act, image, w_project, gain, after):
    rows, cols, channels = image.shape
    expanded = act.shape[2]
    lines = 4
    bands = cols // SIDE
    block = lambda width: pl.BlockSpec((lines, cols, width), lambda r: (r, 0, 0))
    send = (stride * bands, rows // stride, SIDE, channels)
    return pl.pallas_call(
        functools.partial(mix_kernel, cells_total, stride, bands),
        grid=(rows // lines,),
        in_specs=[
            whole(parts.shape), whole(w_squeeze.shape), whole(w_excite.shape),
            block(expanded), block(channels), whole(w_project.shape), whole(gain.shape),
            pl.BlockSpec(memory_space=pl.ANY),
        ],
        out_specs=[
            whole((1, expanded)), whole((1, w_squeeze.shape[1])), whole((1, expanded)),
            block(channels), whole(send),
        ],
        out_shape=[
            jax.ShapeDtypeStruct((1, expanded), F32),
            jax.ShapeDtypeStruct((1, w_squeeze.shape[1]), F32),
            jax.ShapeDtypeStruct((1, expanded), F32),
            jax.ShapeDtypeStruct(image.shape, BF16),
            jax.ShapeDtypeStruct(send, BF16),
        ],
        compiler_params=PARAMS,
        cost_estimate=estimate(5),
        name="mix",
    )(parts, w_squeeze, w_excite, act, image, w_project, gain, after)


def attention_kernel(
    members, heads, lines,
    arrived_ref, cot_ref, w_qkv_ref, w_out_ref, bias_ref,
    x_ref, att_ref, grad_ref, packed_grad_ref, bias_out_ref,
    order_ref, packed_ref, att_grad_ref, bias_sum_ref,
):
    cells, channels = x_ref.shape
    groups = cells // members

    def places():
        for g in range(groups):
            for m in range(0, members, GRID):
                line, row = (m // GRID) % lines, m // GRID // lines
                start = (row * GRID * lines + line) * groups + g
                yield g * members + m, pl.ds(start, GRID, stride=lines * groups)

    for half in range(channels // LANES):
        lanes = slice(half * LANES, (half + 1) * LANES)
        order_ref[half] = arrived_ref[:, lanes].astype(F32)
        for g in range(groups):
            pieces = [order_ref[half, at, :] for k, at in places() if k // members == g]
            at = slice(g * members, (g + 1) * members)
            x_ref[at, lanes] = jnp.concatenate(pieces, axis=0).astype(BF16)
    dim = channels // heads
    per_half = LANES // dim
    halves = channels // LANES
    scale = dim ** (-0.5)
    packed_ref[...] = dot(x_ref[...], w_qkv_ref[...]).astype(BF16)
    att_grad_ref[...] = dot(cot_ref[...], w_out_ref[...], ((1,), (1,))).astype(BF16)
    bias_sum_ref[...] = jnp.zeros(bias_sum_ref.shape, F32)
    tall = per_half * members
    mask = (
        lax.broadcasted_iota(jnp.int32, (tall, LANES), 0) // members
        == lax.broadcasted_iota(jnp.int32, (tall, LANES), 1) // dim
    ).astype(F32).astype(BF16)
    owner = lax.broadcasted_iota(jnp.int32, (members, 2 * LANES), 1) % LANES // dim
    zero = jnp.zeros((members, LANES), BF16)

    def by_head(pair):
        return jnp.concatenate(
            [jnp.concatenate([v] * per_half, axis=0) * mask for v in pair], axis=1
        )

    def diagonal(pair):
        return jnp.concatenate(
            [
                jnp.concatenate([pair[0], zero], axis=1),
                jnp.concatenate([zero, pair[1]], axis=1),
            ],
            axis=0,
        )

    def collect(v):
        parts = [v[h * members : (h + 1) * members] for h in range(per_half)]
        picked = parts[-1]
        for h in range(per_half - 1):
            picked = jnp.where(owner == h, parts[h], picked)
        return [picked[:, :LANES], picked[:, LANES:]]

    def blocks(v):
        return [v[:members, :LANES], v[members:, LANES:]]

    def over_members(v, reduce):
        parted = v.reshape(per_half, members, 2 * members)
        small = reduce(parted, axis=1, keepdims=True)
        return jnp.broadcast_to(small, parted.shape).reshape(v.shape)

    def pair_step(g, carry):
        at = [pl.ds(pl.multiple_of((2 * g + k) * members, 16), members) for k in range(2)]
        for half in range(halves):
            def lanes(part):
                start = part * channels + half * LANES
                return slice(start, start + LANES)

            q, k, v = ([packed_ref[at[n], lanes(part)] for n in range(2)] for part in range(3))
            cot = [att_grad_ref[at[n], lanes(0)] for n in range(2)]
            q_diag, cot_diag = diagonal(q), diagonal(cot)
            k_tall, v_tall = by_head(k), by_head(v)
            scores = dot(k_tall, q_diag, ((1,), (1,))) * scale + bias_ref[half]
            grad_probs = dot(v_tall, cot_diag, ((1,), (1,)))
            lifted = jnp.exp(scores - over_members(scores, jnp.max))
            soft = lifted * (1.0 / over_members(lifted, jnp.sum))
            soft_low = soft.astype(BF16)
            grad_scores = soft * (grad_probs - over_members(grad_probs * soft, jnp.sum))
            bias_sum_ref[half] += grad_scores
            scaled = (grad_scores * scale).astype(BF16)
            attended = blocks(dot(soft_low, v_tall, ((0,), (0,))))
            grad_q = blocks(dot(scaled, k_tall, ((0,), (0,))))
            grad_v = collect(dot(soft_low, cot_diag))
            grad_k = collect(dot(scaled, q_diag))
            for n in range(2):
                att_ref[at[n], lanes(0)] = attended[n].astype(BF16)
                for part, value in enumerate((grad_q, grad_k, grad_v)):
                    packed_grad_ref[at[n], lanes(part)] = value[n].astype(BF16)
        return carry

    lax.fori_loop(0, cells // members // 2, pair_step, 0, unroll=2)
    grad = dot(packed_grad_ref[...], w_qkv_ref[...], ((1,), (1,)))
    for half in range(halves):
        lanes = slice(half * LANES, (half + 1) * LANES)
        for k, at in places():
            order_ref[half, at, :] = grad[k : k + GRID, lanes]
        grad_ref[:, lanes] = order_ref[half].astype(BF16)
    for half in range(halves):
        both = bias_sum_ref[half]
        bias_out_ref[half] = both[:, :members] + both[:, members:]


def run_attention(arrived, cot, w_qkv, w_out, bias_tall, heads, lines):
    cells, channels = cot.shape
    halves, tall, members2 = bias_tall.shape
    members = members2 // 2
    vmem = pl.BlockSpec(memory_space=pltpu.VMEM)
    return pl.pallas_call(
        functools.partial(attention_kernel, members, heads, lines),
        in_specs=[vmem] * 5,
        out_specs=[vmem] * 5,
        out_shape=[
            jax.ShapeDtypeStruct((cells, channels), BF16),
            jax.ShapeDtypeStruct((cells, channels), BF16),
            jax.ShapeDtypeStruct((cells, channels), BF16),
            jax.ShapeDtypeStruct((cells, 3 * channels), BF16),
            jax.ShapeDtypeStruct((halves, tall, members), F32),
        ],
        scratch_shapes=[
            pltpu.VMEM((channels // LANES, cells, LANES), F32),
            pltpu.VMEM((cells, 3 * channels), BF16),
            pltpu.VMEM((cells, channels), BF16),
            pltpu.VMEM(bias_tall.shape, F32),
        ],
        compiler_params=PARAMS,
        cost_estimate=estimate(14),
        name="attention",
    )(arrived.reshape(cells, channels), cot, w_qkv, w_out, bias_tall)


def attention_weights_kernel(x_ref, packed_grad_ref, att_ref, cot_ref, bias_ref, out_ref):
    channels = x_ref.shape[1]
    wide = 3 * channels
    out_ref[:, :wide] = dot(x_ref[...], packed_grad_ref[...], ((0,), (0,))).astype(BF16)
    out_ref[:, wide : wide + channels] = dot(att_ref[...], cot_ref[...], ((0,), (0,))).astype(BF16)
    bias = jnp.concatenate([bias_ref[half] for half in range(bias_ref.shape[0])], axis=1)
    out_ref[:, wide + channels :] = bias.astype(BF16)


def run_attention_weights(x, packed_grad, att, cot, bias):
    channels = x.shape[1]
    vmem = pl.BlockSpec(memory_space=pltpu.VMEM)
    width = 4 * channels + bias.shape[0] * bias.shape[2]
    return pl.pallas_call(
        attention_weights_kernel,
        in_specs=[vmem] * 5,
        out_specs=vmem,
        out_shape=jax.ShapeDtypeStruct((channels, width), BF16),
        compiler_params=PARAMS,
        cost_estimate=estimate(5),
        name="attention_weights",
    )(x, packed_grad, att, cot, bias)


def mixed_back_kernel(
    stride, bands,
    recv_ref, mixed_ref, cot_ref, gain_ref, act_ref, gate_ref, w_projt_ref,
    grad_ref, low_ref, norm_ref, project_ref, gate_grad_ref,
    turned_ref, total_ref,
):
    rows, cols, channels = mixed_ref.shape

    @pl.when(pl.program_id(0) == 0)
    def _():
        gain = gain_ref[...].astype(F32)
        lines = 4

        def some_rows(c, total):
            pieces = []
            for k in range(lines):
                i = c * lines + k
                a, p = lax.rem(i, stride), i // stride
                pieces += [recv_ref[a * bands + band, p] for band in range(bands)]
            grad = jnp.concatenate(pieces, axis=0).astype(F32)
            at = pl.ds(c * lines, lines)
            flat = lambda ref: ref[at].reshape(lines * cols, channels).astype(F32)
            unit, rstd = norm_rows(flat(mixed_ref))
            back = flat(cot_ref) + norm_rows_back(unit, rstd, gain, grad)
            grad_ref[at] = back.reshape(lines, cols, channels)
            low_ref[at] = back.astype(BF16).reshape(lines, cols, channels)
            return total + fold_rows(grad * unit)

        total = lax.fori_loop(
            0, rows // lines, some_rows, jnp.zeros((8, channels), F32), unroll=2
        )
        norm_ref[...] = jnp.sum(total, axis=0, keepdims=True)
        turned_ref[...] = low_ref[...].reshape(rows * cols, channels).T

    flat = act_ref[...].reshape(rows * cols, BLOCK)
    product = dot(turned_ref[...], flat)
    total = jnp.sum(product * w_projt_ref[...].astype(F32), axis=0, keepdims=True)
    step, steps = pl.program_id(0), pl.num_programs(0)
    total_ref[step] = total
    project_ref[...] = (product * gate_ref[...]).T.astype(BF16)

    @pl.when(step == steps - 1)
    def _():
        sums = [total_ref[e] for e in range(total_ref.shape[0])]
        high = [v.astype(BF16).astype(F32) for v in sums]
        terms = jnp.concatenate(high + [v - w for v, w in zip(sums, high)], axis=0)
        gate_grad_ref[...] = jnp.broadcast_to(terms.astype(BF16)[None], gate_grad_ref.shape)


def run_mixed_back(count, stride, recv, mixed, cot, gain, act, gate, w_project_t):
    rows, cols, channels = mixed.shape
    expanded = act.shape[2]
    return pl.pallas_call(
        functools.partial(mixed_back_kernel, stride, cols // SIDE),
        grid=(expanded // BLOCK,),
        in_specs=[
            whole(recv.shape), whole(mixed.shape), whole(cot.shape), whole(gain.shape),
            last_block(act.shape), last_block(gate.shape), last_block(w_project_t.shape),
        ],
        out_specs=[
            whole(mixed.shape), whole(mixed.shape), whole((1, channels)),
            last_block((BLOCK, expanded)), whole((count, 2 * expanded // BLOCK, BLOCK)),
        ],
        out_shape=[
            jax.ShapeDtypeStruct(mixed.shape, F32),
            jax.ShapeDtypeStruct(mixed.shape, BF16),
            jax.ShapeDtypeStruct((1, channels), F32),
            jax.ShapeDtypeStruct((BLOCK, expanded), BF16),
            jax.ShapeDtypeStruct((count, 2 * expanded // BLOCK, BLOCK), BF16),
        ],
        scratch_shapes=[
            pltpu.VMEM((channels, rows * cols), BF16),
            pltpu.VMEM((expanded // BLOCK, 1, BLOCK), F32),
        ],
        compiler_params=PARAMS,
        cost_estimate=estimate(7),
        name="mixed_back",
    )(recv, mixed, cot, gain, act, gate, w_project_t)


def unpack_kernel(late_ref, expand_ref, depth_ref, norm0_ref, norm1_ref):
    channels, expanded = expand_ref.shape
    expand_ref[...] = late_ref[:, :expanded].astype(F32)
    tail = late_ref[:, expanded:].astype(F32)
    pieces = expanded // LANES
    for t in range(9):
        for k in range(pieces):
            row = t * pieces + k
            lanes = slice(k * LANES, (k + 1) * LANES)
            depth_ref[t // 3, t % 3 : t % 3 + 1, lanes] = tail[row : row + 1]
    start = 9 * pieces
    half = channels // LANES
    for k in range(half):
        lanes = slice(k * LANES, (k + 1) * LANES)
        norm0_ref[:, lanes] = tail[start + k : start + k + 1]
        norm1_ref[:, lanes] = tail[start + half + k : start + half + k + 1]


def run_unpack(late, expanded):
    channels = late.shape[0]
    vmem = pl.BlockSpec(memory_space=pltpu.VMEM)
    return pl.pallas_call(
        unpack_kernel,
        in_specs=[vmem],
        out_specs=[vmem] * 4,
        out_shape=[
            jax.ShapeDtypeStruct((channels, expanded), F32),
            jax.ShapeDtypeStruct((3, 3, expanded), F32),
            jax.ShapeDtypeStruct((1, channels), F32),
            jax.ShapeDtypeStruct((1, channels), F32),
        ],
        compiler_params=PARAMS,
        cost_estimate=estimate(100),
        name="unpack",
    )(late)


def expand_back_kernel(
    cells_total,
    parts_ref, hidden_ref, gate_all_ref, w_sq_ref, w_ex_ref,
    low_ref, up_ref, down_ref, side_ref, w_projt_ref, gate_ref, slope_ref, side_slope_ref,
    spread_slope_ref, spread_ref, w_dep_ref, turned_ref, w_exp_ref, gain_ref, norm1_ref,
    weights_ref, first_ref, logit_ref, pre_ref,
    main_ref, side_grad_ref, window_ref, expanded_ref, pool_ref, tail_ref, norm_ref,
):
    rows, cols, channels = low_ref.shape
    side = 8
    wide = cols + side
    step = pl.program_id(0)
    steps = pl.num_programs(0)

    @pl.when(step == 0)
    def _():
        gate = gate_all_ref[...]
        blocks = pool_ref.shape[0]
        terms = jnp.sum(parts_ref[...].astype(F32), axis=0)
        gate_grad = jnp.concatenate(
            [terms[e : e + 1] + terms[blocks + e : blocks + e + 1] for e in range(blocks)], axis=1
        )
        logit = gate_grad * gate * (1.0 - gate)
        hidden = hidden_ref[...]
        sig = jax.nn.sigmoid(hidden)
        pre = dot_exact(logit, w_ex_ref[...].astype(F32), ((1,), (1,))) * (
            sig + hidden * sig * (1.0 - sig)
        )
        logit_ref[...] = logit
        pre_ref[...] = pre
        pooled = dot_exact(pre, w_sq_ref[...].astype(F32), ((1,), (1,))) / cells_total
        for e in range(blocks):
            pool_ref[e] = pooled[:, e * BLOCK : (e + 1) * BLOCK]
        first_ref[...] = jnp.zeros(first_ref.shape, F32)
        tail_ref[...] = jnp.zeros(tail_ref.shape, F32)
        norm_ref[...] = jnp.zeros(norm_ref.shape, F32)

    w_projt = w_projt_ref[...]
    main_ref[pl.ds(0, cols), :] = dot(up_ref[0], w_projt)
    main_ref[pl.ds(cols, rows * cols), :] = dot(
        low_ref[...].reshape(rows * cols, channels), w_projt
    )
    main_ref[pl.ds((rows + 1) * cols, cols), :] = dot(down_ref[0], w_projt)
    side_grad_ref[...] = dot(side_ref[...], w_projt)

    @pl.loop(0, rows + 2, unroll=3)
    def _(i):
        for h in range(BLOCK // LANES):
            lanes = slice(h * LANES, (h + 1) * LANES)
            gate = gate_ref[:, lanes]
            pooled = pool_ref[step][:, lanes]
            gated = main_ref[pl.ds(pl.multiple_of(i * cols, 16), cols), lanes]
            main = (gated * gate + pooled) * slope_ref[i, :, lanes].astype(F32)
            gated = side_grad_ref[pl.ds(pl.multiple_of(i * side, side), side), lanes]
            edge = (gated * gate + pooled) * side_slope_ref[i, :, lanes]
            grad = jnp.concatenate([main, edge], axis=0)
            window_ref[0, i, :, lanes] = pltpu.roll(grad, wide - 1, 0)[:cols]
            window_ref[1, i, :, lanes] = grad[:cols]
            window_ref[2, i, :, lanes] = pltpu.roll(grad, 1, 0)[:cols]

    for h in range(BLOCK // LANES):
        lanes = slice(h * LANES, (h + 1) * LANES)
        taps = w_dep_ref[:, :, lanes].astype(F32)

        def back_row(i, sums):
            spread = spread_ref[i, :, lanes].astype(F32)
            total = jnp.zeros((cols, LANES), F32)
            new_sums = []
            for a in range(3):
                for b in range(3):
                    window = window_ref[b, i + 2 - a, :, lanes]
                    total = total + window * taps[a, b : b + 1]
                    new_sums.append(sums[a * 3 + b] + fold_rows(window * spread))
            grad = total * spread_slope_ref[i, :, lanes].astype(F32)
            expanded_ref[pl.ds(pl.multiple_of(i * cols, 16), cols), lanes] = grad.astype(BF16)
            return tuple(new_sums)

        sums = lax.fori_loop(0, rows, back_row, (jnp.zeros((8, LANES), F32),) * 9, unroll=2)
        for t in range(9):
            row = t * (steps * BLOCK // LANES) + step * (BLOCK // LANES) + h
            tail_ref[pl.ds(row, 1), :] = jnp.sum(sums[t], axis=0, keepdims=True)

    grad_expanded = expanded_ref[...]
    w_exp = w_exp_ref[...]
    weights = dot(turned_ref[...], grad_expanded)
    weights_ref[:, pl.ds(pl.multiple_of(step * BLOCK, BLOCK), BLOCK)] = weights.astype(BF16)
    norm_ref[...] += jnp.sum(weights * w_exp.astype(F32), axis=1, keepdims=True)
    first_ref[...] += dot(grad_expanded, w_exp, ((1,), (1,)))

    @pl.when(step == steps - 1)
    def _():
        norm = norm_ref[...].T[0:1] / gain_ref[...].astype(F32)
        start = 9 * steps * (BLOCK // LANES)
        for k in range(channels // LANES):
            piece = slice(k * LANES, (k + 1) * LANES)
            tail_ref[start + k : start + k + 1, :] = norm[:, piece]
            at = start + channels // LANES + k
            tail_ref[at : at + 1, :] = norm1_ref[:, piece]
        weights_ref[:, steps * BLOCK :] = tail_ref[...].astype(BF16)


def run_expand_back(
    cells_total, parts, hidden, gate, w_squeeze, w_excite, low, up, down, side,
    w_project_t, slope, side_slope, spread_slope, spread, w_depth, turned, w_expand, gain, norm1,
):
    rows, cols, channels = low.shape
    expanded = w_expand.shape[1]
    steps = expanded // BLOCK
    return pl.pallas_call(
        functools.partial(expand_back_kernel, cells_total),
        grid=(steps,),
        in_specs=[
            pl.BlockSpec(
                (parts.shape[0], 2 * steps, BLOCK), lambda e: (0, parts.shape[1] // (2 * steps) - 1, 0)
            ),
            whole(hidden.shape), whole(gate.shape),
            whole(w_squeeze.shape), whole(w_excite.shape),
            whole(low.shape), whole(up.shape), whole(down.shape), whole(side.shape),
            last_block(w_project_t.shape), last_block(gate.shape), last_block(slope.shape),
            last_block(side_slope.shape), last_block(spread_slope.shape), last_block(spread.shape),
            last_block(w_depth.shape), whole(turned.shape), last_block(w_expand.shape),
            whole(gain.shape), whole(norm1.shape),
        ],
        out_specs=[
            whole((channels, expanded + LANES)), whole((rows * cols, channels)),
            whole((1, expanded)), whole(hidden.shape),
        ],
        out_shape=[
            jax.ShapeDtypeStruct((channels, expanded + LANES), BF16),
            jax.ShapeDtypeStruct((rows * cols, channels), F32),
            jax.ShapeDtypeStruct((1, expanded), F32),
            jax.ShapeDtypeStruct(hidden.shape, F32),
        ],
        scratch_shapes=[
            pltpu.VMEM(((rows + 2) * cols, BLOCK), F32),
            pltpu.VMEM(((rows + 2) * 8, BLOCK), F32),
            pltpu.VMEM((3, rows + 2, cols, BLOCK), F32),
            pltpu.VMEM((rows * cols, BLOCK), BF16),
            pltpu.VMEM((steps, 1, BLOCK), F32),
            pltpu.VMEM((channels, LANES), F32),
            pltpu.VMEM((channels, LANES), F32),
        ],
        compiler_params=PARAMS,
        cost_estimate=estimate(14),
        name="expand_back",
    )(
        parts, hidden, gate, w_squeeze, w_excite, low, up, down, side, w_project_t, gate,
        slope, side_slope, spread_slope, spread, w_depth, turned, w_expand, gain, norm1,
    )


def image_back_kernel(image_ref, gain_ref, first_ref, mixed_ref, out_ref):
    unit, rstd = norm_rows(image_ref[...].astype(F32))
    grad = first_ref[...]
    back = mixed_ref[...] + norm_rows_back(unit, rstd, gain_ref[...].astype(F32), grad)
    out_ref[...] = back.astype(BF16)


def run_image_back(image, gain, first, mixed):
    cells, channels = image.shape
    block = pl.BlockSpec((cells // 4, channels), lambda r: (r, 0))
    return pl.pallas_call(
        image_back_kernel,
        grid=(4,),
        in_specs=[block, whole(gain.shape), block, block],
        out_specs=block,
        out_shape=jax.ShapeDtypeStruct((cells, channels), BF16),
        compiler_params=PARAMS,
        cost_estimate=estimate(4),
        name="image_back",
    )(image, gain, first, mixed)


def shift(cells, axis, step):
    count = lax.axis_size(axis)
    pairs = [(i, i + step) for i in range(count) if 0 <= i + step < count]
    return lax.ppermute(cells, axis, pairs)


def halo_rows(cells, width):
    up = shift(cells[cells.shape[0] - width :], "row", 1)
    down = shift(cells[:width], "row", -1)
    return up, down


def halo_sides(cells, up, down, width):
    rows, cols, channels = cells.shape
    first = jnp.concatenate([up[:, :width], cells[:, :width], down[:, :width]], axis=0)
    last = jnp.concatenate(
        [up[:, cols - width :], cells[:, cols - width :], down[:, cols - width :]], axis=0
    )
    left = shift(last, "col", 1)
    right = shift(first, "col", -1)
    gap = jnp.zeros((rows + 2 * width, 8 - 2 * width, channels), cells.dtype)
    side = jnp.concatenate([right, gap, left], axis=1)
    return side.reshape(-1, channels)


def hand_around(blocks):
    return lax.all_to_all(blocks, AXES, split_axis=0, concat_axis=0, tiled=True)


def sum_shares(matrix):
    rows, columns = matrix.shape
    count = lax.axis_size("row") * lax.axis_size("col")
    share = rows // count
    arrived = hand_around(matrix.reshape(count, share, columns))
    total = jnp.sum(arrived.astype(F32), axis=0).astype(BF16)
    sent = jnp.broadcast_to(total[None], (count, share, columns))
    return hand_around(sent).reshape(rows, columns)


def sum_steps():
    return [("col", 1, 2), ("row", 1, lax.axis_size("row")), ("col", 2, lax.axis_size("col") // 2)]


def send_on(v, axis, stride, size, k):
    pairs = []
    for i in range(lax.axis_size(axis)):
        place = i // stride % size
        pairs.append((i, i + ((place + k) % size - place) * stride))
    return lax.ppermute(v, axis, pairs)


def sum_parts(matrix, axis, stride, size):
    place = lax.axis_index(axis) // stride % size
    parts = matrix.reshape(size, matrix.shape[0] // size, matrix.shape[1])
    part = lambda i: lax.dynamic_index_in_dim(parts, i % size, 0, False)
    total = part(place).astype(F32)
    for k in range(1, size):
        total = total + send_on(part(place + k), axis, stride, size, k).astype(F32)
    return total.astype(BF16)


def stack_kernel(*refs):
    for k, ref in enumerate(refs[:-1]):
        refs[-1][k] = ref[...]


def join_parts(blocks, axis, stride, size):
    arrived = [blocks] + [send_on(blocks, axis, stride, size, k) for k in range(1, size)]
    vmem = pl.BlockSpec(memory_space=pltpu.VMEM)
    stacked = pl.pallas_call(
        stack_kernel,
        in_specs=[vmem] * size,
        out_specs=vmem,
        out_shape=jax.ShapeDtypeStruct((size,) + blocks.shape, blocks.dtype),
        compiler_params=PARAMS,
        cost_estimate=estimate(1),
        name="stack",
    )(*arrived)
    return stacked.reshape((size * blocks.shape[0],) + blocks.shape[1:])


def unpack_weights_kernel(
    sizes, places_ref, near_ref, far_ref, qkv_ref, out_ref, bias_ref, project_ref
):
    channels = out_ref.shape[2]
    cuts = (0, 3 * channels, 4 * channels, 4 * channels + bias_ref.shape[2])
    pairs, over_row, rest = sizes
    for pair, source in enumerate((near_ref, far_ref)):
        for r in range(over_row):
            for c in range(rest):
                block = source[r * rest + c].astype(F32)
                at = lax.rem(places_ref[0] + pairs - pair, pairs)
                at = at * over_row + lax.rem(places_ref[1] + over_row - r, over_row)
                at = at * rest + lax.rem(places_ref[2] + rest - c, rest)
                for k, ref in enumerate((qkv_ref, out_ref, bias_ref)):
                    ref[at] = block[:, cuts[k] : cuts[k + 1]]
                for e in range(project_ref.shape[0]):
                    start = cuts[3] + e * channels
                    project_ref[e, at] = block[:, start : start + channels]


def run_unpack_weights(steps, near, far, channels, expanded, bias_width):
    count, rows, _ = near.shape
    count *= 2
    places = jnp.stack([lax.axis_index(axis) // stride % size for axis, stride, size in steps])
    vmem = pl.BlockSpec(memory_space=pltpu.VMEM)
    blocks = lambda width: jax.ShapeDtypeStruct((count, rows, width), F32)
    return pl.pallas_call(
        functools.partial(unpack_weights_kernel, tuple(size for _, _, size in steps)),
        in_specs=[pl.BlockSpec(memory_space=pltpu.SMEM), vmem, vmem],
        out_specs=[vmem] * 4,
        out_shape=[
            blocks(3 * channels), blocks(channels), blocks(bias_width),
            jax.ShapeDtypeStruct((expanded // BLOCK, count, rows, channels), F32),
        ],
        compiler_params=PARAMS,
        cost_estimate=estimate(2),
        name="unpack_weights",
    )(places.astype(jnp.int32), near, far)


def swap_groups(blocks, parity):
    groups = None
    if parity > 1:
        over_row = lax.axis_size("row")
        over_col = lax.axis_size("col")
        groups = [
            [r * over_col + c for r in range(over_row) for c in range(k, over_col, parity)]
            for k in range(parity)
        ]
    return lax.all_to_all(
        blocks, AXES, split_axis=0, concat_axis=0, tiled=True, axis_index_groups=groups
    )


def on_device(
    image, out_cotangent, norm0_gain, w_expand, w_depth, w_squeeze, w_excite, w_project,
    norm1_gain, w_qkv, w_out, attn_bias,
):
    rows, cols, channels = image.shape
    over_row = lax.axis_size("row")
    over_col = lax.axis_size("col")
    count = over_row * over_col
    cells_total = rows * cols * count
    stride = rows * over_row // GRID
    parity = over_col // GRID
    lines = rows // stride
    bands = cols // SIDE
    members = GRID * GRID
    expanded = w_expand.shape[1]

    def into_members(arrived):
        parted = arrived.reshape(over_row, GRID, lines, SIDE, channels)
        return parted.transpose(3, 0, 2, 1, 4).reshape(SIDE * members, channels)

    def out_of_members(values):
        parted = values.reshape(SIDE, over_row, lines, GRID, channels)
        return parted.transpose(1, 3, 2, 0, 4).reshape(-1, lines, SIDE, channels)

    row, col = lax.axis_index("row"), lax.axis_index("col")
    flags = jnp.stack([row > 0, row < over_row - 1, col > 0, col < over_col - 1]).astype(F32)
    gain_first = norm0_gain.reshape(1, channels)
    gain_second = norm1_gain.reshape(1, channels)
    w_project_t = w_project.T
    heads = attn_bias.shape[0]
    halves = channels // LANES
    bias_tall = attn_bias.transpose(0, 2, 1).reshape(halves, heads // halves * members, members)
    bias_tall = jnp.concatenate([bias_tall, bias_tall], axis=2)

    up, down = halo_rows(image, 2)
    normed_first, turned_first, spread, spread_slope = run_expand(image, gain_first, w_expand)
    up, down, spread = lax.optimization_barrier((up, down, spread))
    side = halo_sides(image, up, down, 2)
    cot_sent = (
        out_cotangent.reshape(lines, stride, bands, SIDE, channels)
        .transpose(1, 2, 0, 3, 4)
        .reshape(stride * bands, lines, SIDE, channels)
    )
    cot_members = into_members(swap_groups(cot_sent, parity))
    ring, act, pool = run_depthwise(count, up, down, side, gain_first, w_expand, w_depth, spread)
    pooled, hidden, gate, mixed, normed_sent = run_mix(
        cells_total, stride, hand_around(pool), w_squeeze, w_excite, act, image, w_project,
        gain_second, cot_members,
    )
    slope, side_slope = run_slope(flags, ring, w_depth, spread)
    normed_arrived = swap_groups(normed_sent, parity)
    normed_arrived, slope = lax.optimization_barrier((normed_arrived, slope))
    normed_members, attended, grad_normed, packed_grad, grad_bias = run_attention(
        normed_arrived, cot_members, w_qkv, w_out, bias_tall, heads, lines
    )
    grad_normed_home = swap_groups(grad_normed.reshape(normed_sent.shape), parity)
    weights = run_attention_weights(normed_members, packed_grad, attended, cot_members, grad_bias)
    grad_normed_home, weights = lax.optimization_barrier((grad_normed_home, weights))
    grad_mixed, grad_low, grad_norm1, grad_project, gate_grad = run_mixed_back(
        count, stride, grad_normed_home, mixed, out_cotangent, gain_second, act, gate, w_project_t
    )
    attended_sent = out_of_members(attended)
    if parity == 1:
        both = hand_around(
            jnp.concatenate([attended_sent.reshape(count, -1, channels), gate_grad], axis=1)
        )
        parts = both
        attended_home = both[:, : lines * SIDE].reshape(attended_sent.shape)
    else:
        parts = hand_around(gate_grad)
        attended_home = swap_groups(attended_sent, parity)
    up, down = halo_rows(grad_low, 1)
    side = halo_sides(grad_low, up, down, 1)
    weights = jnp.concatenate([weights, grad_project], axis=1)
    weights, _ = lax.optimization_barrier((weights, up))
    steps = sum_steps()
    for step in steps:
        weights = sum_parts(weights, *step)
    late, grad_first, logit, pre = run_expand_back(
        cells_total, parts, hidden, gate, w_squeeze, w_excite, grad_low, up, down, side,
        w_project_t, slope, side_slope, spread_slope, spread, w_depth, turned_first, w_expand,
        gain_first, grad_norm1,
    )
    weights, _ = lax.optimization_barrier((weights, late))
    weights = weights[None]
    for step in steps[:0:-1]:
        weights = join_parts(weights, *step)
    other = send_on(weights, *steps[0], 1)
    grad_qkv, grad_out_proj, grad_bias, grad_project = run_unpack_weights(
        steps, weights, other, channels, expanded, halves * members
    )
    grad_expand, grad_depth, grad_norm0, grad_norm1 = run_unpack(sum_shares(late), expanded)
    grad_image = run_image_back(
        image.reshape(-1, channels), gain_first, grad_first, grad_mixed.reshape(-1, channels)
    )
    attended_map = (
        attended_home.reshape(stride, bands, lines, SIDE, channels)
        .transpose(2, 0, 1, 3, 4)
        .reshape(rows * cols, channels)
    )
    block_out = (mixed.reshape(-1, channels).astype(F32) + dot(attended_map, w_out)).astype(BF16)

    silu = jax.nn.silu(hidden)
    grad_squeeze = pooled.reshape(expanded, 1) * pre
    grad_excite = silu.reshape(-1, 1) * logit

    grad_bias = (
        grad_bias.reshape(heads // halves, members, halves, members)
        .transpose(2, 0, 3, 1)
        .reshape(attn_bias.shape)
    )
    return (
        block_out.reshape(image.shape),
        grad_image.reshape(image.shape),
        grad_norm0[0],
        grad_expand,
        grad_depth,
        grad_squeeze,
        grad_excite,
        grad_project.reshape(w_project.shape),
        grad_norm1[0],
        grad_qkv.reshape(w_qkv.shape),
        grad_out_proj.reshape(w_out.shape),
        grad_bias,
    )


def solution(mesh):
    cells = P("row", "col", None)
    return jax.shard_map(
        on_device,
        mesh=mesh,
        in_specs=(cells, cells) + (P(),) * 10,
        out_specs=(cells, cells) + (P(),) * 10,
        check_vma=False,
    )
```

```python
import functools
import math

import jax
import jax.numpy as jnp
from jax import lax
from jax.experimental import pallas as pl
from jax.experimental.pallas import tpu as pltpu
from jax.sharding import PartitionSpec as P

GRID = 8
AXES = ("row", "col")
BLOCK = 256
LANES = 128
SIDE = 16
GELU_A = math.sqrt(2.0 / math.pi)
GELU_B = GELU_A * 0.044715
F32 = jnp.float32
BF16 = jnp.bfloat16
PARAMS = pltpu.CompilerParams(vmem_limit_bytes=56 * 1024 * 1024)


def estimate(us):
    return pl.CostEstimate(flops=int(us * 1.1e9), bytes_accessed=int(us * 3.6e6), transcendentals=0)


def dot(left, right, contract=((1,), (0,))):
    return lax.dot_general(left, right, (contract, ((), ())), preferred_element_type=F32)


def dot_exact(vector, right, contract):
    tall = jnp.broadcast_to(vector, (8, vector.shape[1]))
    product = lax.dot_general(
        tall, right, (contract, ((), ())), precision=lax.Precision.HIGHEST, preferred_element_type=F32
    )
    return product[0:1]


def gelu_and_slope(x, with_slope=True):
    square = x * x
    t = jnp.tanh(x * (GELU_A + GELU_B * square))
    half = 0.5 + 0.5 * t
    value = x * half
    if not with_slope:
        return value, None
    slope = half + (value * (1.0 - t)) * (GELU_A + (3.0 * GELU_B) * square)
    return value, slope


def norm_rows(x):
    average = jnp.mean(x, axis=-1, keepdims=True)
    centered = x - average
    variance = jnp.mean(centered * centered, axis=-1, keepdims=True)
    rstd = lax.rsqrt(variance + 1e-05)
    return centered * rstd, rstd


def norm_rows_back(unit, rstd, gain, grad):
    unit_grad = grad * gain
    first = jnp.mean(unit_grad, axis=-1, keepdims=True)
    second = jnp.mean(unit_grad * unit, axis=-1, keepdims=True)
    return rstd * (unit_grad - first - unit * second)


def fold_rows(x):
    return jnp.sum(x.reshape(x.shape[0] // 8, 8, x.shape[1]), axis=0)


def whole(shape):
    return pl.BlockSpec(shape, lambda e: (0,) * len(shape))


def last_block(shape):
    lead = (0,) * (len(shape) - 1)
    return pl.BlockSpec(shape[:-1] + (BLOCK,), lambda e: lead + (e,))


def expand_kernel(
    image_ref, gain_ref, w_exp_ref,
    normed_ref, turned_ref, spread_ref, slope_ref,
    expanded_ref,
):
    rows, cols, channels = image_ref.shape

    @pl.when(pl.program_id(0) == 0)
    def _():
        gain = gain_ref[...].astype(F32)

        @pl.loop(0, rows // 4)
        def _(c):
            flat = image_ref[pl.ds(c * 4, 4)].reshape(4 * cols, channels)
            unit, _ = norm_rows(flat.astype(F32))
            at = pl.ds(pl.multiple_of(c * 4 * cols, 16), 4 * cols)
            normed_ref[at, :] = (unit * gain).astype(BF16)

        turned_ref[...] = normed_ref[...].T

    expanded_ref[...] = dot(normed_ref[...], w_exp_ref[...])

    @pl.loop(0, rows, unroll=4)
    def _(r):
        for h in range(BLOCK // LANES):
            lanes = slice(h * LANES, (h + 1) * LANES)
            x = expanded_ref[pl.ds(pl.multiple_of(r * cols, 16), cols), lanes]
            value, slope = gelu_and_slope(x)
            spread_ref[r, :, lanes] = value.astype(BF16)
            slope_ref[r, :, lanes] = slope.astype(BF16)


def run_expand(image, gain, w_expand):
    rows, cols, channels = image.shape
    expanded = w_expand.shape[1]
    return pl.pallas_call(
        expand_kernel,
        grid=(expanded // BLOCK,),
        in_specs=[whole(image.shape), whole(gain.shape), last_block(w_expand.shape)],
        out_specs=[
            whole((rows * cols, channels)), whole((channels, rows * cols)),
            last_block((rows, cols, expanded)), last_block((rows, cols, expanded)),
        ],
        out_shape=[
            jax.ShapeDtypeStruct((rows * cols, channels), BF16),
            jax.ShapeDtypeStruct((channels, rows * cols), BF16),
            jax.ShapeDtypeStruct((rows, cols, expanded), BF16),
            jax.ShapeDtypeStruct((rows, cols, expanded), BF16),
        ],
        scratch_shapes=[pltpu.VMEM((rows * cols, BLOCK), F32)],
        compiler_params=PARAMS,
        cost_estimate=estimate(14),
        name="expand",
    )(image, gain, w_expand)


def depthwise_kernel(
    up_ref, down_ref, side_ref, gain_ref, w_exp_ref, w_dep_ref, spread_ref,
    ring_ref, act_ref, pool_ref,
    ring_normed_ref, ring_wide_ref,
):
    rows, cols, _ = spread_ref.shape
    channels = up_ref.shape[2]
    over = 4 * cols
    side = 8

    @pl.when(pl.program_id(0) == 0)
    def _():
        gain = gain_ref[...].astype(F32)

        def put(at, values):
            unit, _ = norm_rows(values.astype(F32))
            ring_normed_ref[at : at + values.shape[0], :] = (unit * gain).astype(BF16)

        put(0, up_ref[...].reshape(2 * cols, channels))
        put(2 * cols, down_ref[...].reshape(2 * cols, channels))
        put(over, side_ref[...])

    ring_wide_ref[...] = dot(ring_normed_ref[...], w_exp_ref[...])
    tile = 32

    @pl.loop(0, ring_wide_ref.shape[0] // tile, unroll=True)
    def _(t):
        at = pl.ds(pl.multiple_of(t * tile, tile), tile)
        value, _ = gelu_and_slope(ring_wide_ref[at, :], False)
        low = value.astype(BF16)
        ring_ref[at, :] = low
        ring_wide_ref[at, :] = low.astype(F32)

    for h in range(BLOCK // LANES):
        lanes = slice(h * LANES, (h + 1) * LANES)
        taps = w_dep_ref[:, :, lanes].astype(F32)
        w = [[taps[a, b : b + 1] for b in range(3)] for a in range(3)]

        def line(r, main):
            at = pl.multiple_of(over + (r + 2) * side, side)
            return jnp.concatenate([main, ring_wide_ref[pl.ds(at, side), lanes]], axis=0)

        def conv(i, x, total):
            u = [x[0] * w[0][b] + x[1] * w[1][b] + x[2] * w[2][b] for b in range(3)]
            wide = cols + side
            pre = pltpu.roll(u[0], 1, 0) + u[1] + pltpu.roll(u[2], wide - 1, 0)
            value, _ = gelu_and_slope(pre[:cols], False)
            act_ref[i, :, lanes] = value.astype(BF16)
            return total + fold_rows(value)

        def step(i, carry):
            first, second, total = carry
            third = line(i + 1, spread_ref[i + 1, :, lanes].astype(F32))
            return second, third, conv(i, (first, second, third), total)

        carry = (
            line(-1, ring_wide_ref[cols : 2 * cols, lanes]),
            line(0, spread_ref[0, :, lanes].astype(F32)),
            jnp.zeros((8, LANES), F32),
        )
        first, second, total = lax.fori_loop(0, rows - 1, step, carry, unroll=5)
        third = line(rows, ring_wide_ref[2 * cols : 3 * cols, lanes])
        total = conv(rows - 1, (first, second, third), total)
        total = jnp.sum(total, axis=0, keepdims=True)
        pool_ref[:, :, lanes] = jnp.broadcast_to(total[None], (pool_ref.shape[0], 1, LANES))


def run_depthwise(count, up, down, side, gain, w_expand, w_depth, spread):
    rows, cols, expanded = spread.shape
    channels = up.shape[2]
    ring = 4 * cols + 8 * (rows + 4)
    return pl.pallas_call(
        depthwise_kernel,
        grid=(expanded // BLOCK,),
        in_specs=[
            whole(up.shape), whole(down.shape), whole(side.shape), whole(gain.shape),
            last_block(w_expand.shape), last_block(w_depth.shape), last_block(spread.shape),
        ],
        out_specs=[
            last_block((ring, expanded)), last_block(spread.shape), last_block((count, 1, expanded)),
        ],
        out_shape=[
            jax.ShapeDtypeStruct((ring, expanded), BF16),
            jax.ShapeDtypeStruct(spread.shape, BF16),
            jax.ShapeDtypeStruct((count, 1, expanded), F32),
        ],
        scratch_shapes=[pltpu.VMEM((ring, channels), BF16), pltpu.VMEM((ring, BLOCK), F32)],
        compiler_params=PARAMS,
        cost_estimate=estimate(1),
        name="depthwise",
    )(up, down, side, gain, w_expand, w_depth, spread)


def slope_kernel(flags_ref, ring_ref, w_dep_ref, spread_ref, main_ref, side_out_ref, wide_ref):
    rows, cols, _ = spread_ref.shape
    over = 4 * cols
    side = 8
    wide = cols + side

    for k, r in enumerate((0, 1, rows + 2, rows + 3)):
        wide_ref[r, :cols, :] = ring_ref[k * cols : (k + 1) * cols, :].astype(F32)
    sides = ring_ref[over:, :].astype(F32)
    for r in range(rows + 4):
        wide_ref[r, cols:, :] = sides[r * side : (r + 1) * side]

    @pl.loop(0, rows)
    def _(r):
        wide_ref[r + 2, :cols, :] = spread_ref[r].astype(F32)

    place = lax.broadcasted_iota(jnp.int32, (side, LANES), 0)
    side_mask = jnp.where(
        place == side - 1, flags_ref[2], jnp.where(place == 0, flags_ref[3], 1.0)
    ).astype(F32)

    @pl.loop(0, rows + 2)
    def _(i):
        keep = jnp.where(i == 0, flags_ref[0], jnp.where(i == rows + 1, flags_ref[1], 1.0))
        for h in range(BLOCK // LANES):
            lanes = slice(h * LANES, (h + 1) * LANES)
            taps = w_dep_ref[:, :, lanes].astype(F32)
            x = [wide_ref[i + a, :, lanes] for a in range(3)]
            u = [sum(x[a] * taps[a, b : b + 1] for a in range(3)) for b in range(3)]
            pre = pltpu.roll(u[0], 1, 0) + u[1] + pltpu.roll(u[2], wide - 1, 0)
            _, slope = gelu_and_slope(pre)
            slope = slope * keep
            main_ref[i, :, lanes] = slope[:cols].astype(BF16)
            side_out_ref[i, :, lanes] = slope[cols:] * side_mask


def run_slope(flags, ring, w_depth, spread):
    rows, cols, expanded = spread.shape
    return pl.pallas_call(
        slope_kernel,
        grid=(expanded // BLOCK,),
        in_specs=[
            pl.BlockSpec(memory_space=pltpu.SMEM),
            last_block(ring.shape), last_block(w_depth.shape), last_block(spread.shape),
        ],
        out_specs=[last_block((rows + 2, cols, expanded)), last_block((rows + 2, 8, expanded))],
        out_shape=[
            jax.ShapeDtypeStruct((rows + 2, cols, expanded), BF16),
            jax.ShapeDtypeStruct((rows + 2, 8, expanded), F32),
        ],
        scratch_shapes=[pltpu.VMEM((rows + 4, cols + 8, BLOCK), F32)],
        compiler_params=PARAMS,
        cost_estimate=estimate(13),
        name="slope",
    )(flags, ring, w_depth, spread)


def mix_kernel(
    cells_total, stride, bands,
    parts_ref, w_sq_ref, w_ex_ref, act_ref, image_ref, w_proj_ref, gain_ref, after_ref,
    pooled_ref, hidden_ref, gate_ref, mixed_ref, send_ref,
):
    step = pl.program_id(0)

    @pl.when(step == 0)
    def _():
        pooled = jnp.sum(parts_ref[...], axis=0) / cells_total
        hidden = dot_exact(pooled, w_sq_ref[...].astype(F32), ((1,), (0,)))
        silu = hidden * jax.nn.sigmoid(hidden)
        pooled_ref[...] = pooled
        hidden_ref[...] = hidden
        gate_ref[...] = jax.nn.sigmoid(dot_exact(silu, w_ex_ref[...].astype(F32), ((1,), (0,))))

    lines, cols, channels = image_ref.shape
    flat = act_ref[...].reshape(lines * cols, act_ref.shape[2])
    gated = (flat.astype(F32) * gate_ref[...]).astype(BF16)
    product = dot(gated, w_proj_ref[...])
    mixed = (image_ref[...].reshape(lines * cols, channels).astype(F32) + product).astype(BF16)
    mixed_ref[...] = mixed.reshape(lines, cols, channels)
    unit, _ = norm_rows(mixed.astype(F32))
    normed = (unit * gain_ref[...].astype(F32)).astype(BF16)
    for k in range(lines):
        line = step * lines + k
        for band in range(bands):
            start = k * cols + band * SIDE
            send_ref[lax.rem(line, stride) * bands + band, line // stride] = normed[
                start : start + SIDE
            ]


def run_mix(cells_total, stride, parts, w_squeeze, w_excite, act, image, w_project, gain, after):
    rows, cols, channels = image.shape
    expanded = act.shape[2]
    lines = 4
    bands = cols // SIDE
    block = lambda width: pl.BlockSpec((lines, cols, width), lambda r: (r, 0, 0))
    send = (stride * bands, rows // stride, SIDE, channels)
    return pl.pallas_call(
        functools.partial(mix_kernel, cells_total, stride, bands),
        grid=(rows // lines,),
        in_specs=[
            whole(parts.shape), whole(w_squeeze.shape), whole(w_excite.shape),
            block(expanded), block(channels), whole(w_project.shape), whole(gain.shape),
            pl.BlockSpec(memory_space=pl.ANY),
        ],
        out_specs=[
            whole((1, expanded)), whole((1, w_squeeze.shape[1])), whole((1, expanded)),
            block(channels), whole(send),
        ],
        out_shape=[
            jax.ShapeDtypeStruct((1, expanded), F32),
            jax.ShapeDtypeStruct((1, w_squeeze.shape[1]), F32),
            jax.ShapeDtypeStruct((1, expanded), F32),
            jax.ShapeDtypeStruct(image.shape, BF16),
            jax.ShapeDtypeStruct(send, BF16),
        ],
        compiler_params=PARAMS,
        cost_estimate=estimate(5),
        name="mix",
    )(parts, w_squeeze, w_excite, act, image, w_project, gain, after)


def attention_kernel(
    members, heads, lines,
    arrived_ref, cot_ref, w_qkv_ref, w_out_ref, bias_ref,
    x_ref, att_ref, sent_ref, grad_ref, packed_grad_ref, bias_out_ref,
    order_ref, packed_ref, att_grad_ref, bias_sum_ref,
):
    cells, channels = x_ref.shape
    groups = cells // members

    def places():
        for g in range(groups):
            for m in range(0, members, GRID):
                line, row = (m // GRID) % lines, m // GRID // lines
                start = (row * GRID * lines + line) * groups + g
                yield g * members + m, pl.ds(start, GRID, stride=lines * groups)

    for half in range(channels // LANES):
        lanes = slice(half * LANES, (half + 1) * LANES)
        order_ref[half] = arrived_ref[:, lanes].astype(F32)
        for g in range(groups):
            pieces = [order_ref[half, at, :] for k, at in places() if k // members == g]
            at = slice(g * members, (g + 1) * members)
            x_ref[at, lanes] = jnp.concatenate(pieces, axis=0).astype(BF16)
    dim = channels // heads
    per_half = LANES // dim
    halves = channels // LANES
    scale = dim ** (-0.5)
    packed_ref[...] = dot(x_ref[...], w_qkv_ref[...]).astype(BF16)
    att_grad_ref[...] = dot(cot_ref[...], w_out_ref[...], ((1,), (1,))).astype(BF16)
    bias_sum_ref[...] = jnp.zeros(bias_sum_ref.shape, F32)
    tall = per_half * members
    mask = (
        lax.broadcasted_iota(jnp.int32, (tall, LANES), 0) // members
        == lax.broadcasted_iota(jnp.int32, (tall, LANES), 1) // dim
    ).astype(F32).astype(BF16)
    owner = lax.broadcasted_iota(jnp.int32, (members, 2 * LANES), 1) % LANES // dim
    zero = jnp.zeros((members, LANES), BF16)

    def by_head(pair):
        return jnp.concatenate(
            [jnp.concatenate([v] * per_half, axis=0) * mask for v in pair], axis=1
        )

    def diagonal(pair):
        return jnp.concatenate(
            [
                jnp.concatenate([pair[0], zero], axis=1),
                jnp.concatenate([zero, pair[1]], axis=1),
            ],
            axis=0,
        )

    def collect(v):
        parts = [v[h * members : (h + 1) * members] for h in range(per_half)]
        picked = parts[-1]
        for h in range(per_half - 1):
            picked = jnp.where(owner == h, parts[h], picked)
        return [picked[:, :LANES], picked[:, LANES:]]

    def blocks(v):
        return [v[:members, :LANES], v[members:, LANES:]]

    def over_members(v, reduce):
        parted = v.reshape(per_half, members, 2 * members)
        small = reduce(parted, axis=1, keepdims=True)
        return jnp.broadcast_to(small, parted.shape).reshape(v.shape)

    def pair_step(g, carry):
        at = [pl.ds(pl.multiple_of((2 * g + k) * members, 16), members) for k in range(2)]
        for half in range(halves):
            def lanes(part):
                start = part * channels + half * LANES
                return slice(start, start + LANES)

            q, k, v = ([packed_ref[at[n], lanes(part)] for n in range(2)] for part in range(3))
            cot = [att_grad_ref[at[n], lanes(0)] for n in range(2)]
            q_diag, cot_diag = diagonal(q), diagonal(cot)
            k_tall, v_tall = by_head(k), by_head(v)
            scores = dot(k_tall, q_diag, ((1,), (1,))) * scale + bias_ref[half]
            grad_probs = dot(v_tall, cot_diag, ((1,), (1,)))
            lifted = jnp.exp(scores - over_members(scores, jnp.max))
            soft = lifted * (1.0 / over_members(lifted, jnp.sum))
            soft_low = soft.astype(BF16)
            grad_scores = soft * (grad_probs - over_members(grad_probs * soft, jnp.sum))
            bias_sum_ref[half] += grad_scores
            scaled = (grad_scores * scale).astype(BF16)
            attended = blocks(dot(soft_low, v_tall, ((0,), (0,))))
            grad_q = blocks(dot(scaled, k_tall, ((0,), (0,))))
            grad_v = collect(dot(soft_low, cot_diag))
            grad_k = collect(dot(scaled, q_diag))
            for n in range(2):
                att_ref[at[n], lanes(0)] = attended[n].astype(BF16)
                for part, value in enumerate((grad_q, grad_k, grad_v)):
                    packed_grad_ref[at[n], lanes(part)] = value[n].astype(BF16)
        return carry

    lax.fori_loop(0, cells // members // 2, pair_step, 0, unroll=2)
    grad = dot(packed_grad_ref[...], w_qkv_ref[...], ((1,), (1,)))
    attended = att_ref[...].astype(F32)
    for half in range(halves):
        lanes = slice(half * LANES, (half + 1) * LANES)
        for k, at in places():
            order_ref[half, at, :] = grad[k : k + GRID, lanes]
        grad_ref[:, lanes] = order_ref[half].astype(BF16)
        for k, at in places():
            order_ref[half, at, :] = attended[k : k + GRID, lanes]
        for n in range(sent_ref.shape[0]):
            rows = lines * groups
            sent_ref[n, :rows, lanes] = order_ref[half, n * rows : (n + 1) * rows, :].astype(BF16)
    for half in range(halves):
        both = bias_sum_ref[half]
        bias_out_ref[half] = both[:, :members] + both[:, members:]


def run_attention(arrived, cot, w_qkv, w_out, bias_tall, heads, lines, room):
    cells, channels = cot.shape
    devices, _, groups, _ = arrived.shape
    halves, tall, members2 = bias_tall.shape
    members = members2 // 2
    vmem = pl.BlockSpec(memory_space=pltpu.VMEM)
    return pl.pallas_call(
        functools.partial(attention_kernel, members, heads, lines),
        in_specs=[vmem] * 5,
        out_specs=[vmem] * 6,
        out_shape=[
            jax.ShapeDtypeStruct((cells, channels), BF16),
            jax.ShapeDtypeStruct((cells, channels), BF16),
            jax.ShapeDtypeStruct((devices, lines * groups + room, channels), BF16),
            jax.ShapeDtypeStruct((cells, channels), BF16),
            jax.ShapeDtypeStruct((cells, 3 * channels), BF16),
            jax.ShapeDtypeStruct((halves, tall, members), F32),
        ],
        scratch_shapes=[
            pltpu.VMEM((channels // LANES, cells, LANES), F32),
            pltpu.VMEM((cells, 3 * channels), BF16),
            pltpu.VMEM((cells, channels), BF16),
            pltpu.VMEM(bias_tall.shape, F32),
        ],
        compiler_params=PARAMS,
        cost_estimate=estimate(14),
        name="attention",
    )(arrived.reshape(cells, channels), cot, w_qkv, w_out, bias_tall)


def attention_weights_kernel(x_ref, packed_grad_ref, att_ref, cot_ref, bias_ref, out_ref):
    channels = x_ref.shape[1]
    wide = 3 * channels
    out_ref[:, :wide] = dot(x_ref[...], packed_grad_ref[...], ((0,), (0,))).astype(BF16)
    out_ref[:, wide : wide + channels] = dot(att_ref[...], cot_ref[...], ((0,), (0,))).astype(BF16)
    bias = jnp.concatenate([bias_ref[half] for half in range(bias_ref.shape[0])], axis=1)
    out_ref[:, wide + channels :] = bias.astype(BF16)


def run_attention_weights(x, packed_grad, att, cot, bias):
    channels = x.shape[1]
    vmem = pl.BlockSpec(memory_space=pltpu.VMEM)
    width = 4 * channels + bias.shape[0] * bias.shape[2]
    return pl.pallas_call(
        attention_weights_kernel,
        in_specs=[vmem] * 5,
        out_specs=vmem,
        out_shape=jax.ShapeDtypeStruct((channels, width), BF16),
        compiler_params=PARAMS,
        cost_estimate=estimate(5),
        name="attention_weights",
    )(x, packed_grad, att, cot, bias)


def mixed_back_kernel(
    stride, bands,
    recv_ref, mixed_ref, cot_ref, gain_ref, act_ref, gate_ref, w_projt_ref, sent_ref,
    grad_ref, low_ref, norm_ref, project_ref, gate_grad_ref,
    turned_ref, total_ref,
):
    rows, cols, channels = mixed_ref.shape

    @pl.when(pl.program_id(0) == 0)
    def _():
        gain = gain_ref[...].astype(F32)
        lines = 4

        def some_rows(c, total):
            pieces = []
            for k in range(lines):
                i = c * lines + k
                a, p = lax.rem(i, stride), i // stride
                pieces += [recv_ref[a * bands + band, p] for band in range(bands)]
            grad = jnp.concatenate(pieces, axis=0).astype(F32)
            at = pl.ds(c * lines, lines)
            flat = lambda ref: ref[at].reshape(lines * cols, channels).astype(F32)
            unit, rstd = norm_rows(flat(mixed_ref))
            back = flat(cot_ref) + norm_rows_back(unit, rstd, gain, grad)
            grad_ref[at] = back.reshape(lines, cols, channels)
            low_ref[at] = back.astype(BF16).reshape(lines, cols, channels)
            return total + fold_rows(grad * unit)

        total = lax.fori_loop(
            0, rows // lines, some_rows, jnp.zeros((8, channels), F32), unroll=2
        )
        norm_ref[...] = jnp.sum(total, axis=0, keepdims=True)
        turned_ref[...] = low_ref[...].reshape(rows * cols, channels).T

    flat = act_ref[...].reshape(rows * cols, BLOCK)
    product = dot(turned_ref[...], flat)
    total = jnp.sum(product * w_projt_ref[...].astype(F32), axis=0, keepdims=True)
    step, steps = pl.program_id(0), pl.num_programs(0)
    total_ref[step] = total
    project_ref[...] = (product * gate_ref[...]).T.astype(BF16)

    @pl.when(step == steps - 1)
    def _():
        sums = [total_ref[e] for e in range(total_ref.shape[0])]
        high = [v.astype(BF16).astype(F32) for v in sums]
        terms = jnp.concatenate(high + [v - w for v, w in zip(sums, high)], axis=0)
        gate_grad_ref[...] = jnp.broadcast_to(terms.astype(BF16)[None], gate_grad_ref.shape)


def run_mixed_back(stride, recv, mixed, cot, gain, act, gate, w_project_t, sent):
    rows, cols, channels = mixed.shape
    expanded = act.shape[2]
    terms = 2 * expanded // BLOCK
    return pl.pallas_call(
        functools.partial(mixed_back_kernel, stride, cols // SIDE),
        grid=(expanded // BLOCK,),
        in_specs=[
            whole(recv.shape), whole(mixed.shape), whole(cot.shape), whole(gain.shape),
            last_block(act.shape), last_block(gate.shape), last_block(w_project_t.shape),
            pl.BlockSpec(memory_space=pl.ANY),
        ],
        out_specs=[
            whole(mixed.shape), whole(mixed.shape), whole((1, channels)),
            last_block((BLOCK, expanded)),
            pl.BlockSpec((sent.shape[0], terms, BLOCK), lambda e: (0, sent.shape[1] // terms - 1, 0)),
        ],
        out_shape=[
            jax.ShapeDtypeStruct(mixed.shape, F32),
            jax.ShapeDtypeStruct(mixed.shape, BF16),
            jax.ShapeDtypeStruct((1, channels), F32),
            jax.ShapeDtypeStruct((BLOCK, expanded), BF16),
            jax.ShapeDtypeStruct(sent.shape, BF16),
        ],
        scratch_shapes=[
            pltpu.VMEM((channels, rows * cols), BF16),
            pltpu.VMEM((expanded // BLOCK, 1, BLOCK), F32),
        ],
        compiler_params=PARAMS,
        cost_estimate=estimate(7),
        input_output_aliases={7: 4},
        name="mixed_back",
    )(recv, mixed, cot, gain, act, gate, w_project_t, sent)


def unpack_kernel(late_ref, expand_ref, depth_ref, norm0_ref, norm1_ref):
    channels, expanded = expand_ref.shape
    expand_ref[...] = late_ref[:, :expanded].astype(F32)
    tail = late_ref[:, expanded:].astype(F32)
    pieces = expanded // LANES
    for t in range(9):
        for k in range(pieces):
            row = t * pieces + k
            lanes = slice(k * LANES, (k + 1) * LANES)
            depth_ref[t // 3, t % 3 : t % 3 + 1, lanes] = tail[row : row + 1]
    start = 9 * pieces
    half = channels // LANES
    for k in range(half):
        lanes = slice(k * LANES, (k + 1) * LANES)
        norm0_ref[:, lanes] = tail[start + k : start + k + 1]
        norm1_ref[:, lanes] = tail[start + half + k : start + half + k + 1]


def run_unpack(late, expanded):
    channels = late.shape[0]
    vmem = pl.BlockSpec(memory_space=pltpu.VMEM)
    return pl.pallas_call(
        unpack_kernel,
        in_specs=[vmem],
        out_specs=[vmem] * 4,
        out_shape=[
            jax.ShapeDtypeStruct((channels, expanded), F32),
            jax.ShapeDtypeStruct((3, 3, expanded), F32),
            jax.ShapeDtypeStruct((1, channels), F32),
            jax.ShapeDtypeStruct((1, channels), F32),
        ],
        compiler_params=PARAMS,
        cost_estimate=estimate(100),
        name="unpack",
    )(late)


def expand_back_kernel(
    cells_total,
    parts_ref, hidden_ref, gate_all_ref, w_sq_ref, w_ex_ref,
    low_ref, up_ref, down_ref, side_ref, w_projt_ref, gate_ref, slope_ref, side_slope_ref,
    spread_slope_ref, spread_ref, w_dep_ref, turned_ref, w_exp_ref, gain_ref, norm1_ref,
    weights_ref, first_ref, logit_ref, pre_ref,
    main_ref, side_grad_ref, window_ref, expanded_ref, pool_ref, tail_ref, norm_ref,
):
    rows, cols, channels = low_ref.shape
    side = 8
    wide = cols + side
    step = pl.program_id(0)
    steps = pl.num_programs(0)

    @pl.when(step == 0)
    def _():
        gate = gate_all_ref[...]
        blocks = pool_ref.shape[0]
        terms = jnp.sum(parts_ref[...].astype(F32), axis=0)
        gate_grad = jnp.concatenate(
            [terms[e : e + 1] + terms[blocks + e : blocks + e + 1] for e in range(blocks)], axis=1
        )
        logit = gate_grad * gate * (1.0 - gate)
        hidden = hidden_ref[...]
        sig = jax.nn.sigmoid(hidden)
        pre = dot_exact(logit, w_ex_ref[...].astype(F32), ((1,), (1,))) * (
            sig + hidden * sig * (1.0 - sig)
        )
        logit_ref[...] = logit
        pre_ref[...] = pre
        pooled = dot_exact(pre, w_sq_ref[...].astype(F32), ((1,), (1,))) / cells_total
        for e in range(blocks):
            pool_ref[e] = pooled[:, e * BLOCK : (e + 1) * BLOCK]
        first_ref[...] = jnp.zeros(first_ref.shape, F32)
        tail_ref[...] = jnp.zeros(tail_ref.shape, F32)
        norm_ref[...] = jnp.zeros(norm_ref.shape, F32)

    w_projt = w_projt_ref[...]
    main_ref[pl.ds(0, cols), :] = dot(up_ref[0], w_projt)
    main_ref[pl.ds(cols, rows * cols), :] = dot(
        low_ref[...].reshape(rows * cols, channels), w_projt
    )
    main_ref[pl.ds((rows + 1) * cols, cols), :] = dot(down_ref[0], w_projt)
    side_grad_ref[...] = dot(side_ref[...], w_projt)

    @pl.loop(0, rows + 2, unroll=3)
    def _(i):
        for h in range(BLOCK // LANES):
            lanes = slice(h * LANES, (h + 1) * LANES)
            gate = gate_ref[:, lanes]
            pooled = pool_ref[step][:, lanes]
            gated = main_ref[pl.ds(pl.multiple_of(i * cols, 16), cols), lanes]
            main = (gated * gate + pooled) * slope_ref[i, :, lanes].astype(F32)
            gated = side_grad_ref[pl.ds(pl.multiple_of(i * side, side), side), lanes]
            edge = (gated * gate + pooled) * side_slope_ref[i, :, lanes]
            grad = jnp.concatenate([main, edge], axis=0)
            window_ref[0, i, :, lanes] = pltpu.roll(grad, wide - 1, 0)[:cols]
            window_ref[1, i, :, lanes] = grad[:cols]
            window_ref[2, i, :, lanes] = pltpu.roll(grad, 1, 0)[:cols]

    for h in range(BLOCK // LANES):
        lanes = slice(h * LANES, (h + 1) * LANES)
        taps = w_dep_ref[:, :, lanes].astype(F32)

        def back_row(i, sums):
            spread = spread_ref[i, :, lanes].astype(F32)
            total = jnp.zeros((cols, LANES), F32)
            new_sums = []
            for a in range(3):
                for b in range(3):
                    window = window_ref[b, i + 2 - a, :, lanes]
                    total = total + window * taps[a, b : b + 1]
                    new_sums.append(sums[a * 3 + b] + fold_rows(window * spread))
            grad = total * spread_slope_ref[i, :, lanes].astype(F32)
            expanded_ref[pl.ds(pl.multiple_of(i * cols, 16), cols), lanes] = grad.astype(BF16)
            return tuple(new_sums)

        sums = lax.fori_loop(0, rows, back_row, (jnp.zeros((8, LANES), F32),) * 9, unroll=2)
        for t in range(9):
            row = t * (steps * BLOCK // LANES) + step * (BLOCK // LANES) + h
            tail_ref[pl.ds(row, 1), :] = jnp.sum(sums[t], axis=0, keepdims=True)

    grad_expanded = expanded_ref[...]
    w_exp = w_exp_ref[...]
    weights = dot(turned_ref[...], grad_expanded)
    weights_ref[:, pl.ds(pl.multiple_of(step * BLOCK, BLOCK), BLOCK)] = weights.astype(BF16)
    norm_ref[...] += jnp.sum(weights * w_exp.astype(F32), axis=1, keepdims=True)
    first_ref[...] += dot(grad_expanded, w_exp, ((1,), (1,)))

    @pl.when(step == steps - 1)
    def _():
        norm = norm_ref[...].T[0:1] / gain_ref[...].astype(F32)
        start = 9 * steps * (BLOCK // LANES)
        for k in range(channels // LANES):
            piece = slice(k * LANES, (k + 1) * LANES)
            tail_ref[start + k : start + k + 1, :] = norm[:, piece]
            at = start + channels // LANES + k
            tail_ref[at : at + 1, :] = norm1_ref[:, piece]
        weights_ref[:, steps * BLOCK :] = tail_ref[...].astype(BF16)


def run_expand_back(
    cells_total, parts, hidden, gate, w_squeeze, w_excite, low, up, down, side,
    w_project_t, slope, side_slope, spread_slope, spread, w_depth, turned, w_expand, gain, norm1,
):
    rows, cols, channels = low.shape
    expanded = w_expand.shape[1]
    steps = expanded // BLOCK
    return pl.pallas_call(
        functools.partial(expand_back_kernel, cells_total),
        grid=(steps,),
        in_specs=[
            pl.BlockSpec(
                (parts.shape[0], 2 * steps, BLOCK), lambda e: (0, parts.shape[1] // (2 * steps) - 1, 0)
            ),
            whole(hidden.shape), whole(gate.shape),
            whole(w_squeeze.shape), whole(w_excite.shape),
            whole(low.shape), whole(up.shape), whole(down.shape), whole(side.shape),
            last_block(w_project_t.shape), last_block(gate.shape), last_block(slope.shape),
            last_block(side_slope.shape), last_block(spread_slope.shape), last_block(spread.shape),
            last_block(w_depth.shape), whole(turned.shape), last_block(w_expand.shape),
            whole(gain.shape), whole(norm1.shape),
        ],
        out_specs=[
            whole((channels, expanded + LANES)), whole((rows * cols, channels)),
            whole((1, expanded)), whole(hidden.shape),
        ],
        out_shape=[
            jax.ShapeDtypeStruct((channels, expanded + LANES), BF16),
            jax.ShapeDtypeStruct((rows * cols, channels), F32),
            jax.ShapeDtypeStruct((1, expanded), F32),
            jax.ShapeDtypeStruct(hidden.shape, F32),
        ],
        scratch_shapes=[
            pltpu.VMEM(((rows + 2) * cols, BLOCK), F32),
            pltpu.VMEM(((rows + 2) * 8, BLOCK), F32),
            pltpu.VMEM((3, rows + 2, cols, BLOCK), F32),
            pltpu.VMEM((rows * cols, BLOCK), BF16),
            pltpu.VMEM((steps, 1, BLOCK), F32),
            pltpu.VMEM((channels, LANES), F32),
            pltpu.VMEM((channels, LANES), F32),
        ],
        compiler_params=PARAMS,
        cost_estimate=estimate(14),
        name="expand_back",
    )(
        parts, hidden, gate, w_squeeze, w_excite, low, up, down, side, w_project_t, gate,
        slope, side_slope, spread_slope, spread, w_depth, turned, w_expand, gain, norm1,
    )


def image_back_kernel(image_ref, gain_ref, first_ref, mixed_ref, out_ref):
    unit, rstd = norm_rows(image_ref[...].astype(F32))
    grad = first_ref[...]
    back = mixed_ref[...] + norm_rows_back(unit, rstd, gain_ref[...].astype(F32), grad)
    out_ref[...] = back.astype(BF16)


def run_image_back(image, gain, first, mixed):
    cells, channels = image.shape
    block = pl.BlockSpec((cells // 4, channels), lambda r: (r, 0))
    return pl.pallas_call(
        image_back_kernel,
        grid=(4,),
        in_specs=[block, whole(gain.shape), block, block],
        out_specs=block,
        out_shape=jax.ShapeDtypeStruct((cells, channels), BF16),
        compiler_params=PARAMS,
        cost_estimate=estimate(4),
        name="image_back",
    )(image, gain, first, mixed)


def shift(cells, axis, step):
    count = lax.axis_size(axis)
    pairs = [(i, i + step) for i in range(count) if 0 <= i + step < count]
    return lax.ppermute(cells, axis, pairs)


def halo_rows(cells, width):
    up = shift(cells[cells.shape[0] - width :], "row", 1)
    down = shift(cells[:width], "row", -1)
    return up, down


def halo_sides(cells, up, down, width):
    rows, cols, channels = cells.shape
    first = jnp.concatenate([up[:, :width], cells[:, :width], down[:, :width]], axis=0)
    last = jnp.concatenate(
        [up[:, cols - width :], cells[:, cols - width :], down[:, cols - width :]], axis=0
    )
    left = shift(last, "col", 1)
    right = shift(first, "col", -1)
    gap = jnp.zeros((rows + 2 * width, 8 - 2 * width, channels), cells.dtype)
    side = jnp.concatenate([right, gap, left], axis=1)
    return side.reshape(-1, channels)


def hand_around(blocks):
    return lax.all_to_all(blocks, AXES, split_axis=0, concat_axis=0, tiled=True)


def sum_shares(matrix):
    rows, columns = matrix.shape
    count = lax.axis_size("row") * lax.axis_size("col")
    share = rows // count
    arrived = hand_around(matrix.reshape(count, share, columns))
    total = jnp.sum(arrived.astype(F32), axis=0).astype(BF16)
    sent = jnp.broadcast_to(total[None], (count, share, columns))
    return hand_around(sent).reshape(rows, columns)


def sum_steps():
    return [("col", 1, 2), ("row", 1, lax.axis_size("row")), ("col", 2, lax.axis_size("col") // 2)]


def send_on(v, axis, stride, size, k):
    pairs = []
    for i in range(lax.axis_size(axis)):
        place = i // stride % size
        pairs.append((i, i + ((place + k) % size - place) * stride))
    return lax.ppermute(v, axis, pairs)


def sum_parts(matrix, axis, stride, size):
    place = lax.axis_index(axis) // stride % size
    parts = matrix.reshape(size, matrix.shape[0] // size, matrix.shape[1])
    part = lambda i: lax.dynamic_index_in_dim(parts, i % size, 0, False)
    total = part(place).astype(F32)
    for k in range(1, size):
        total = total + send_on(part(place + k), axis, stride, size, k).astype(F32)
    return total.astype(BF16)


def sum_ordered_kernel(size, place_ref, *refs):
    out_ref, held_ref = refs[size:]
    for k in range(size):
        held_ref[lax.rem(place_ref[0] + size - k, size)] = refs[k][...]
    total = held_ref[0].astype(F32)
    for j in range(1, size):
        total = total + held_ref[j].astype(F32)
    out_ref[...] = total.astype(BF16)


def sum_whole(matrix, axis, stride, size):
    arrived = [matrix] + [send_on(matrix, axis, stride, size, k) for k in range(1, size)]
    place = (lax.axis_index(axis) // stride % size).astype(jnp.int32).reshape(1)
    vmem = pl.BlockSpec(memory_space=pltpu.VMEM)
    return pl.pallas_call(
        functools.partial(sum_ordered_kernel, size),
        in_specs=[pl.BlockSpec(memory_space=pltpu.SMEM)] + [vmem] * size,
        out_specs=vmem,
        out_shape=jax.ShapeDtypeStruct(matrix.shape, BF16),
        scratch_shapes=[pltpu.VMEM((size,) + matrix.shape, BF16)],
        compiler_params=PARAMS,
        cost_estimate=estimate(1),
        name="sum_ordered",
    )(place, *arrived)


def stack_kernel(*refs):
    for k, ref in enumerate(refs[:-1]):
        refs[-1][k] = ref[...]


def join_parts(blocks, axis, stride, size):
    arrived = [blocks] + [send_on(blocks, axis, stride, size, k) for k in range(1, size)]
    vmem = pl.BlockSpec(memory_space=pltpu.VMEM)
    stacked = pl.pallas_call(
        stack_kernel,
        in_specs=[vmem] * size,
        out_specs=vmem,
        out_shape=jax.ShapeDtypeStruct((size,) + blocks.shape, blocks.dtype),
        compiler_params=PARAMS,
        cost_estimate=estimate(1),
        name="stack",
    )(*arrived)
    return stacked.reshape((size * blocks.shape[0],) + blocks.shape[1:])


def unpack_weights_kernel(
    sizes, places_ref, near_ref, far_ref, qkv_ref, out_ref, bias_ref, project_ref
):
    channels = out_ref.shape[2]
    cuts = (0, 3 * channels, 4 * channels, 4 * channels + bias_ref.shape[2])
    pairs, over_row = sizes
    for pair, source in enumerate((near_ref, far_ref)):
        for r in range(over_row):
            block = source[r].astype(F32)
            at = lax.rem(places_ref[0] + pairs - pair, pairs)
            at = at * over_row + lax.rem(places_ref[1] + over_row - r, over_row)
            for k, ref in enumerate((qkv_ref, out_ref, bias_ref)):
                ref[at] = block[:, cuts[k] : cuts[k + 1]]
            for e in range(project_ref.shape[0]):
                start = cuts[3] + e * channels
                project_ref[e, at] = block[:, start : start + channels]


def run_unpack_weights(steps, near, far, channels, expanded, bias_width):
    count, rows, _ = near.shape
    count *= 2
    places = jnp.stack([lax.axis_index(axis) // stride % size for axis, stride, size in steps])
    vmem = pl.BlockSpec(memory_space=pltpu.VMEM)
    blocks = lambda width: jax.ShapeDtypeStruct((count, rows, width), F32)
    return pl.pallas_call(
        functools.partial(unpack_weights_kernel, tuple(size for _, _, size in steps)),
        in_specs=[pl.BlockSpec(memory_space=pltpu.SMEM), vmem, vmem],
        out_specs=[vmem] * 4,
        out_shape=[
            blocks(3 * channels), blocks(channels), blocks(bias_width),
            jax.ShapeDtypeStruct((expanded // BLOCK, count, rows, channels), F32),
        ],
        compiler_params=PARAMS,
        cost_estimate=estimate(2),
        name="unpack_weights",
    )(places.astype(jnp.int32), near, far)


def swap_groups(blocks, parity):
    groups = None
    if parity > 1:
        over_row = lax.axis_size("row")
        over_col = lax.axis_size("col")
        groups = [
            [r * over_col + c for r in range(over_row) for c in range(k, over_col, parity)]
            for k in range(parity)
        ]
    return lax.all_to_all(
        blocks, AXES, split_axis=0, concat_axis=0, tiled=True, axis_index_groups=groups
    )


def on_device(
    image, out_cotangent, norm0_gain, w_expand, w_depth, w_squeeze, w_excite, w_project,
    norm1_gain, w_qkv, w_out, attn_bias,
):
    rows, cols, channels = image.shape
    over_row = lax.axis_size("row")
    over_col = lax.axis_size("col")
    count = over_row * over_col
    cells_total = rows * cols * count
    stride = rows * over_row // GRID
    parity = over_col // GRID
    lines = rows // stride
    bands = cols // SIDE
    members = GRID * GRID
    expanded = w_expand.shape[1]

    def into_members(arrived):
        parted = arrived.reshape(over_row, GRID, lines, SIDE, channels)
        return parted.transpose(3, 0, 2, 1, 4).reshape(SIDE * members, channels)

    row, col = lax.axis_index("row"), lax.axis_index("col")
    flags = jnp.stack([row > 0, row < over_row - 1, col > 0, col < over_col - 1]).astype(F32)
    gain_first = norm0_gain.reshape(1, channels)
    gain_second = norm1_gain.reshape(1, channels)
    w_project_t = w_project.T
    heads = attn_bias.shape[0]
    halves = channels // LANES
    bias_tall = attn_bias.transpose(0, 2, 1).reshape(halves, heads // halves * members, members)
    bias_tall = jnp.concatenate([bias_tall, bias_tall], axis=2)

    up, down = halo_rows(image, 2)
    normed_first, turned_first, spread, spread_slope = run_expand(image, gain_first, w_expand)
    up, down, spread = lax.optimization_barrier((up, down, spread))
    side = halo_sides(image, up, down, 2)
    cot_sent = (
        out_cotangent.reshape(lines, stride, bands, SIDE, channels)
        .transpose(1, 2, 0, 3, 4)
        .reshape(stride * bands, lines, SIDE, channels)
    )
    cot_members = into_members(swap_groups(cot_sent, parity))
    ring, act, pool = run_depthwise(count, up, down, side, gain_first, w_expand, w_depth, spread)
    pooled, hidden, gate, mixed, normed_sent = run_mix(
        cells_total, stride, hand_around(pool), w_squeeze, w_excite, act, image, w_project,
        gain_second, cot_members,
    )
    slope, side_slope = run_slope(flags, ring, w_depth, spread)
    normed_arrived = swap_groups(normed_sent, parity)
    normed_arrived, slope = lax.optimization_barrier((normed_arrived, slope))
    terms = 2 * expanded // BLOCK
    normed_members, attended, attended_sent, grad_normed, packed_grad, grad_bias = run_attention(
        normed_arrived, cot_members, w_qkv, w_out, bias_tall, heads, lines,
        terms if parity == 1 else 0,
    )
    grad_normed_home = swap_groups(grad_normed.reshape(normed_sent.shape), parity)
    weights = run_attention_weights(normed_members, packed_grad, attended, cot_members, grad_bias)
    grad_normed_home, weights = lax.optimization_barrier((grad_normed_home, weights))
    gate_sent = attended_sent if parity == 1 else jnp.zeros((count, terms, BLOCK), BF16)
    grad_mixed, grad_low, grad_norm1, grad_project, gate_sent = run_mixed_back(
        stride, grad_normed_home, mixed, out_cotangent, gain_second, act, gate, w_project_t, gate_sent
    )
    parts = hand_around(gate_sent)
    if parity == 1:
        attended_home = parts[:, : lines * SIDE]
    else:
        attended_home = swap_groups(attended_sent, parity)
    gate_sent, grad_low = lax.optimization_barrier((gate_sent, grad_low))
    up, down = halo_rows(grad_low, 1)
    side = halo_sides(grad_low, up, down, 1)
    weights = jnp.concatenate([weights, grad_project], axis=1)
    weights, _ = lax.optimization_barrier((weights, up))
    steps = sum_steps()
    for step in steps[:2]:
        weights = sum_parts(weights, *step)
    weights = sum_whole(weights, *steps[2])
    late, grad_first, logit, pre = run_expand_back(
        cells_total, parts, hidden, gate, w_squeeze, w_excite, grad_low, up, down, side,
        w_project_t, slope, side_slope, spread_slope, spread, w_depth, turned_first, w_expand,
        gain_first, grad_norm1,
    )
    weights = join_parts(weights[None], *steps[1])
    other = send_on(weights, *steps[0], 1)
    grad_qkv, grad_out_proj, grad_bias, grad_project = run_unpack_weights(
        steps[:2], weights, other, channels, expanded, halves * members
    )
    grad_expand, grad_depth, grad_norm0, grad_norm1 = run_unpack(sum_shares(late), expanded)
    grad_image = run_image_back(
        image.reshape(-1, channels), gain_first, grad_first, grad_mixed.reshape(-1, channels)
    )
    attended_map = (
        attended_home.reshape(stride, bands, lines, SIDE, channels)
        .transpose(2, 0, 1, 3, 4)
        .reshape(rows * cols, channels)
    )
    block_out = (mixed.reshape(-1, channels).astype(F32) + dot(attended_map, w_out)).astype(BF16)

    silu = jax.nn.silu(hidden)
    grad_squeeze = pooled.reshape(expanded, 1) * pre
    grad_excite = silu.reshape(-1, 1) * logit

    grad_bias = (
        grad_bias.reshape(heads // halves, members, halves, members)
        .transpose(2, 0, 3, 1)
        .reshape(attn_bias.shape)
    )
    return (
        block_out.reshape(image.shape),
        grad_image.reshape(image.shape),
        grad_norm0[0],
        grad_expand,
        grad_depth,
        grad_squeeze,
        grad_excite,
        grad_project.reshape(w_project.shape),
        grad_norm1[0],
        grad_qkv.reshape(w_qkv.shape),
        grad_out_proj.reshape(w_out.shape),
        grad_bias,
    )


def solution(mesh):
    cells = P("row", "col", None)
    return jax.shard_map(
        on_device,
        mesh=mesh,
        in_specs=(cells, cells) + (P(),) * 10,
        out_specs=(cells, cells) + (P(),) * 10,
        check_vma=False,
    )
```

```python
import functools
import math

import jax
import jax.numpy as jnp
from jax import lax
from jax.experimental import pallas as pl
from jax.experimental.pallas import tpu as pltpu
from jax.sharding import PartitionSpec as P

GRID = 8
AXES = ("row", "col")
BLOCK = 256
LANES = 128
SIDE = 16
GELU_A = math.sqrt(2.0 / math.pi)
GELU_B = GELU_A * 0.044715
F32 = jnp.float32
BF16 = jnp.bfloat16
PARAMS = pltpu.CompilerParams(vmem_limit_bytes=56 * 1024 * 1024)


def estimate(us):
    return pl.CostEstimate(flops=int(us * 1.1e9), bytes_accessed=int(us * 3.6e6), transcendentals=0)


def dot(left, right, contract=((1,), (0,))):
    return lax.dot_general(left, right, (contract, ((), ())), preferred_element_type=F32)


def dot_exact(vector, right, contract):
    tall = jnp.broadcast_to(vector, (8, vector.shape[1]))
    product = lax.dot_general(
        tall, right, (contract, ((), ())), precision=lax.Precision.HIGHEST, preferred_element_type=F32
    )
    return product[0:1]


def gelu_and_slope(x, with_slope=True):
    square = x * x
    t = jnp.tanh(x * (GELU_A + GELU_B * square))
    half = 0.5 + 0.5 * t
    value = x * half
    if not with_slope:
        return value, None
    slope = half + (value * (1.0 - t)) * (GELU_A + (3.0 * GELU_B) * square)
    return value, slope


def norm_rows(x):
    average = jnp.mean(x, axis=-1, keepdims=True)
    centered = x - average
    variance = jnp.mean(centered * centered, axis=-1, keepdims=True)
    rstd = lax.rsqrt(variance + 1e-05)
    return centered * rstd, rstd


def norm_rows_back(unit, rstd, gain, grad):
    unit_grad = grad * gain
    first = jnp.mean(unit_grad, axis=-1, keepdims=True)
    second = jnp.mean(unit_grad * unit, axis=-1, keepdims=True)
    return rstd * (unit_grad - first - unit * second)


def fold_rows(x):
    return jnp.sum(x.reshape(x.shape[0] // 8, 8, x.shape[1]), axis=0)


def whole(shape):
    return pl.BlockSpec(shape, lambda e: (0,) * len(shape))


def last_block(shape):
    lead = (0,) * (len(shape) - 1)
    return pl.BlockSpec(shape[:-1] + (BLOCK,), lambda e: lead + (e,))


def expand_kernel(
    image_ref, gain_ref, w_exp_ref,
    normed_ref, turned_ref, spread_ref, slope_ref,
    expanded_ref,
):
    rows, cols, channels = image_ref.shape

    @pl.when(pl.program_id(0) == 0)
    def _():
        gain = gain_ref[...].astype(F32)

        @pl.loop(0, rows // 4)
        def _(c):
            flat = image_ref[pl.ds(c * 4, 4)].reshape(4 * cols, channels)
            unit, _ = norm_rows(flat.astype(F32))
            at = pl.ds(pl.multiple_of(c * 4 * cols, 16), 4 * cols)
            normed_ref[at, :] = (unit * gain).astype(BF16)

        turned_ref[...] = normed_ref[...].T

    expanded_ref[...] = dot(normed_ref[...], w_exp_ref[...])

    @pl.loop(0, rows, unroll=4)
    def _(r):
        for h in range(BLOCK // LANES):
            lanes = slice(h * LANES, (h + 1) * LANES)
            x = expanded_ref[pl.ds(pl.multiple_of(r * cols, 16), cols), lanes]
            value, slope = gelu_and_slope(x)
            spread_ref[r, :, lanes] = value.astype(BF16)
            slope_ref[r, :, lanes] = slope.astype(BF16)


def run_expand(image, gain, w_expand):
    rows, cols, channels = image.shape
    expanded = w_expand.shape[1]
    return pl.pallas_call(
        expand_kernel,
        grid=(expanded // BLOCK,),
        in_specs=[whole(image.shape), whole(gain.shape), last_block(w_expand.shape)],
        out_specs=[
            whole((rows * cols, channels)), whole((channels, rows * cols)),
            last_block((rows, cols, expanded)), last_block((rows, cols, expanded)),
        ],
        out_shape=[
            jax.ShapeDtypeStruct((rows * cols, channels), BF16),
            jax.ShapeDtypeStruct((channels, rows * cols), BF16),
            jax.ShapeDtypeStruct((rows, cols, expanded), BF16),
            jax.ShapeDtypeStruct((rows, cols, expanded), BF16),
        ],
        scratch_shapes=[pltpu.VMEM((rows * cols, BLOCK), F32)],
        compiler_params=PARAMS,
        cost_estimate=estimate(14),
        name="expand",
    )(image, gain, w_expand)


def depthwise_kernel(
    up_ref, down_ref, side_ref, gain_ref, w_exp_ref, w_dep_ref, spread_ref,
    ring_ref, act_ref, pool_ref,
    ring_normed_ref, ring_wide_ref,
):
    rows, cols, _ = spread_ref.shape
    channels = up_ref.shape[2]
    over = 4 * cols
    side = 8

    @pl.when(pl.program_id(0) == 0)
    def _():
        gain = gain_ref[...].astype(F32)

        def put(at, values):
            unit, _ = norm_rows(values.astype(F32))
            ring_normed_ref[at : at + values.shape[0], :] = (unit * gain).astype(BF16)

        put(0, up_ref[...].reshape(2 * cols, channels))
        put(2 * cols, down_ref[...].reshape(2 * cols, channels))
        put(over, side_ref[...])

    ring_wide_ref[...] = dot(ring_normed_ref[...], w_exp_ref[...])
    tile = 32

    @pl.loop(0, ring_wide_ref.shape[0] // tile, unroll=True)
    def _(t):
        at = pl.ds(pl.multiple_of(t * tile, tile), tile)
        value, _ = gelu_and_slope(ring_wide_ref[at, :], False)
        low = value.astype(BF16)
        ring_ref[at, :] = low
        ring_wide_ref[at, :] = low.astype(F32)

    for h in range(BLOCK // LANES):
        lanes = slice(h * LANES, (h + 1) * LANES)
        taps = w_dep_ref[:, :, lanes].astype(F32)
        w = [[taps[a, b : b + 1] for b in range(3)] for a in range(3)]

        def line(r, main):
            at = pl.multiple_of(over + (r + 2) * side, side)
            return jnp.concatenate([main, ring_wide_ref[pl.ds(at, side), lanes]], axis=0)

        def conv(i, x, total):
            u = [x[0] * w[0][b] + x[1] * w[1][b] + x[2] * w[2][b] for b in range(3)]
            wide = cols + side
            pre = pltpu.roll(u[0], 1, 0) + u[1] + pltpu.roll(u[2], wide - 1, 0)
            value, _ = gelu_and_slope(pre[:cols], False)
            act_ref[i, :, lanes] = value.astype(BF16)
            return total + fold_rows(value)

        def step(i, carry):
            first, second, total = carry
            third = line(i + 1, spread_ref[i + 1, :, lanes].astype(F32))
            return second, third, conv(i, (first, second, third), total)

        carry = (
            line(-1, ring_wide_ref[cols : 2 * cols, lanes]),
            line(0, spread_ref[0, :, lanes].astype(F32)),
            jnp.zeros((8, LANES), F32),
        )
        first, second, total = lax.fori_loop(0, rows - 1, step, carry, unroll=5)
        third = line(rows, ring_wide_ref[2 * cols : 3 * cols, lanes])
        total = conv(rows - 1, (first, second, third), total)
        total = jnp.sum(total, axis=0, keepdims=True)
        pool_ref[:, :, lanes] = jnp.broadcast_to(total[None], (pool_ref.shape[0], 1, LANES))


def run_depthwise(count, up, down, side, gain, w_expand, w_depth, spread):
    rows, cols, expanded = spread.shape
    channels = up.shape[2]
    ring = 4 * cols + 8 * (rows + 4)
    return pl.pallas_call(
        depthwise_kernel,
        grid=(expanded // BLOCK,),
        in_specs=[
            whole(up.shape), whole(down.shape), whole(side.shape), whole(gain.shape),
            last_block(w_expand.shape), last_block(w_depth.shape), last_block(spread.shape),
        ],
        out_specs=[
            last_block((ring, expanded)), last_block(spread.shape), last_block((count, 1, expanded)),
        ],
        out_shape=[
            jax.ShapeDtypeStruct((ring, expanded), BF16),
            jax.ShapeDtypeStruct(spread.shape, BF16),
            jax.ShapeDtypeStruct((count, 1, expanded), F32),
        ],
        scratch_shapes=[pltpu.VMEM((ring, channels), BF16), pltpu.VMEM((ring, BLOCK), F32)],
        compiler_params=PARAMS,
        cost_estimate=estimate(1),
        name="depthwise",
    )(up, down, side, gain, w_expand, w_depth, spread)


def slope_kernel(flags_ref, ring_ref, w_dep_ref, spread_ref, main_ref, side_out_ref, wide_ref):
    rows, cols, _ = spread_ref.shape
    over = 4 * cols
    side = 8
    wide = cols + side

    for k, r in enumerate((0, 1, rows + 2, rows + 3)):
        wide_ref[r, :cols, :] = ring_ref[k * cols : (k + 1) * cols, :].astype(F32)
    sides = ring_ref[over:, :].astype(F32)
    for r in range(rows + 4):
        wide_ref[r, cols:, :] = sides[r * side : (r + 1) * side]

    @pl.loop(0, rows)
    def _(r):
        wide_ref[r + 2, :cols, :] = spread_ref[r].astype(F32)

    place = lax.broadcasted_iota(jnp.int32, (side, LANES), 0)
    side_mask = jnp.where(
        place == side - 1, flags_ref[2], jnp.where(place == 0, flags_ref[3], 1.0)
    ).astype(F32)

    @pl.loop(0, rows + 2)
    def _(i):
        keep = jnp.where(i == 0, flags_ref[0], jnp.where(i == rows + 1, flags_ref[1], 1.0))
        for h in range(BLOCK // LANES):
            lanes = slice(h * LANES, (h + 1) * LANES)
            taps = w_dep_ref[:, :, lanes].astype(F32)
            x = [wide_ref[i + a, :, lanes] for a in range(3)]
            u = [sum(x[a] * taps[a, b : b + 1] for a in range(3)) for b in range(3)]
            pre = pltpu.roll(u[0], 1, 0) + u[1] + pltpu.roll(u[2], wide - 1, 0)
            _, slope = gelu_and_slope(pre)
            slope = slope * keep
            main_ref[i, :, lanes] = slope[:cols].astype(BF16)
            side_out_ref[i, :, lanes] = slope[cols:] * side_mask


def run_slope(flags, ring, w_depth, spread):
    rows, cols, expanded = spread.shape
    return pl.pallas_call(
        slope_kernel,
        grid=(expanded // BLOCK,),
        in_specs=[
            pl.BlockSpec(memory_space=pltpu.SMEM),
            last_block(ring.shape), last_block(w_depth.shape), last_block(spread.shape),
        ],
        out_specs=[last_block((rows + 2, cols, expanded)), last_block((rows + 2, 8, expanded))],
        out_shape=[
            jax.ShapeDtypeStruct((rows + 2, cols, expanded), BF16),
            jax.ShapeDtypeStruct((rows + 2, 8, expanded), F32),
        ],
        scratch_shapes=[pltpu.VMEM((rows + 4, cols + 8, BLOCK), F32)],
        compiler_params=PARAMS,
        cost_estimate=estimate(13),
        name="slope",
    )(flags, ring, w_depth, spread)


def mix_kernel(
    cells_total, stride, bands,
    parts_ref, w_sq_ref, w_ex_ref, act_ref, image_ref, w_proj_ref, gain_ref, after_ref,
    pooled_ref, hidden_ref, gate_ref, mixed_ref, send_ref,
):
    step = pl.program_id(0)

    @pl.when(step == 0)
    def _():
        pooled = jnp.sum(parts_ref[...], axis=0) / cells_total
        hidden = dot_exact(pooled, w_sq_ref[...].astype(F32), ((1,), (0,)))
        silu = hidden * jax.nn.sigmoid(hidden)
        pooled_ref[...] = pooled
        hidden_ref[...] = hidden
        gate_ref[...] = jax.nn.sigmoid(dot_exact(silu, w_ex_ref[...].astype(F32), ((1,), (0,))))

    lines, cols, channels = image_ref.shape
    flat = act_ref[...].reshape(lines * cols, act_ref.shape[2])
    gated = (flat.astype(F32) * gate_ref[...]).astype(BF16)
    product = dot(gated, w_proj_ref[...])
    mixed = (image_ref[...].reshape(lines * cols, channels).astype(F32) + product).astype(BF16)
    mixed_ref[...] = mixed.reshape(lines, cols, channels)
    unit, _ = norm_rows(mixed.astype(F32))
    normed = (unit * gain_ref[...].astype(F32)).astype(BF16)
    for k in range(lines):
        line = step * lines + k
        for band in range(bands):
            start = k * cols + band * SIDE
            send_ref[lax.rem(line, stride) * bands + band, line // stride] = normed[
                start : start + SIDE
            ]


def run_mix(cells_total, stride, parts, w_squeeze, w_excite, act, image, w_project, gain, after):
    rows, cols, channels = image.shape
    expanded = act.shape[2]
    lines = 4
    bands = cols // SIDE
    block = lambda width: pl.BlockSpec((lines, cols, width), lambda r: (r, 0, 0))
    send = (stride * bands, rows // stride, SIDE, channels)
    return pl.pallas_call(
        functools.partial(mix_kernel, cells_total, stride, bands),
        grid=(rows // lines,),
        in_specs=[
            whole(parts.shape), whole(w_squeeze.shape), whole(w_excite.shape),
            block(expanded), block(channels), whole(w_project.shape), whole(gain.shape),
            pl.BlockSpec(memory_space=pl.ANY),
        ],
        out_specs=[
            whole((1, expanded)), whole((1, w_squeeze.shape[1])), whole((1, expanded)),
            block(channels), whole(send),
        ],
        out_shape=[
            jax.ShapeDtypeStruct((1, expanded), F32),
            jax.ShapeDtypeStruct((1, w_squeeze.shape[1]), F32),
            jax.ShapeDtypeStruct((1, expanded), F32),
            jax.ShapeDtypeStruct(image.shape, BF16),
            jax.ShapeDtypeStruct(send, BF16),
        ],
        compiler_params=PARAMS,
        cost_estimate=estimate(5),
        name="mix",
    )(parts, w_squeeze, w_excite, act, image, w_project, gain, after)


def attention_kernel(
    members, heads, lines,
    arrived_ref, cot_ref, w_qkv_ref, w_out_ref, bias_ref,
    x_ref, att_ref, grad_ref, packed_grad_ref, bias_out_ref,
    order_ref, packed_ref, att_grad_ref, bias_sum_ref,
):
    cells, channels = x_ref.shape
    groups = cells // members

    def places():
        for g in range(groups):
            for m in range(0, members, GRID):
                line, row = (m // GRID) % lines, m // GRID // lines
                start = (row * GRID * lines + line) * groups + g
                yield g * members + m, pl.ds(start, GRID, stride=lines * groups)

    for half in range(channels // LANES):
        lanes = slice(half * LANES, (half + 1) * LANES)
        order_ref[half] = arrived_ref[:, lanes].astype(F32)
        for g in range(groups):
            pieces = [order_ref[half, at, :] for k, at in places() if k // members == g]
            at = slice(g * members, (g + 1) * members)
            x_ref[at, lanes] = jnp.concatenate(pieces, axis=0).astype(BF16)
    dim = channels // heads
    per_half = LANES // dim
    halves = channels // LANES
    scale = dim ** (-0.5)
    packed_ref[...] = dot(x_ref[...], w_qkv_ref[...]).astype(BF16)
    att_grad_ref[...] = dot(cot_ref[...], w_out_ref[...], ((1,), (1,))).astype(BF16)
    bias_sum_ref[...] = jnp.zeros(bias_sum_ref.shape, F32)
    tall = per_half * members
    mask = (
        lax.broadcasted_iota(jnp.int32, (tall, LANES), 0) // members
        == lax.broadcasted_iota(jnp.int32, (tall, LANES), 1) // dim
    ).astype(F32).astype(BF16)
    owner = lax.broadcasted_iota(jnp.int32, (members, 2 * LANES), 1) % LANES // dim
    zero = jnp.zeros((members, LANES), BF16)

    def by_head(pair):
        return jnp.concatenate(
            [jnp.concatenate([v] * per_half, axis=0) * mask for v in pair], axis=1
        )

    def diagonal(pair):
        return jnp.concatenate(
            [
                jnp.concatenate([pair[0], zero], axis=1),
                jnp.concatenate([zero, pair[1]], axis=1),
            ],
            axis=0,
        )

    def collect(v):
        parts = [v[h * members : (h + 1) * members] for h in range(per_half)]
        picked = parts[-1]
        for h in range(per_half - 1):
            picked = jnp.where(owner == h, parts[h], picked)
        return [picked[:, :LANES], picked[:, LANES:]]

    def blocks(v):
        return [v[:members, :LANES], v[members:, LANES:]]

    def over_members(v, reduce):
        parted = v.reshape(per_half, members, 2 * members)
        small = reduce(parted, axis=1, keepdims=True)
        return jnp.broadcast_to(small, parted.shape).reshape(v.shape)

    def pair_step(g, carry):
        at = [pl.ds(pl.multiple_of((2 * g + k) * members, 16), members) for k in range(2)]
        for half in range(halves):
            def lanes(part):
                start = part * channels + half * LANES
                return slice(start, start + LANES)

            q, k, v = ([packed_ref[at[n], lanes(part)] for n in range(2)] for part in range(3))
            cot = [att_grad_ref[at[n], lanes(0)] for n in range(2)]
            q_diag, cot_diag = diagonal(q), diagonal(cot)
            k_tall, v_tall = by_head(k), by_head(v)
            scores = dot(k_tall, q_diag, ((1,), (1,))) * scale + bias_ref[half]
            grad_probs = dot(v_tall, cot_diag, ((1,), (1,)))
            lifted = jnp.exp(scores - over_members(scores, jnp.max))
            soft = lifted * (1.0 / over_members(lifted, jnp.sum))
            soft_low = soft.astype(BF16)
            grad_scores = soft * (grad_probs - over_members(grad_probs * soft, jnp.sum))
            bias_sum_ref[half] += grad_scores
            scaled = (grad_scores * scale).astype(BF16)
            attended = blocks(dot(soft_low, v_tall, ((0,), (0,))))
            grad_q = blocks(dot(scaled, k_tall, ((0,), (0,))))
            grad_v = collect(dot(soft_low, cot_diag))
            grad_k = collect(dot(scaled, q_diag))
            for n in range(2):
                att_ref[at[n], lanes(0)] = attended[n].astype(BF16)
                for part, value in enumerate((grad_q, grad_k, grad_v)):
                    packed_grad_ref[at[n], lanes(part)] = value[n].astype(BF16)
        return carry

    lax.fori_loop(0, cells // members // 2, pair_step, 0, unroll=2)
    grad = dot(packed_grad_ref[...], w_qkv_ref[...], ((1,), (1,)))
    for half in range(halves):
        lanes = slice(half * LANES, (half + 1) * LANES)
        for k, at in places():
            order_ref[half, at, :] = grad[k : k + GRID, lanes]
        grad_ref[:, lanes] = order_ref[half].astype(BF16)
    for half in range(halves):
        both = bias_sum_ref[half]
        bias_out_ref[half] = both[:, :members] + both[:, members:]


def run_attention(arrived, cot, w_qkv, w_out, bias_tall, heads, lines):
    cells, channels = cot.shape
    halves, tall, members2 = bias_tall.shape
    members = members2 // 2
    vmem = pl.BlockSpec(memory_space=pltpu.VMEM)
    return pl.pallas_call(
        functools.partial(attention_kernel, members, heads, lines),
        in_specs=[vmem] * 5,
        out_specs=[vmem] * 5,
        out_shape=[
            jax.ShapeDtypeStruct((cells, channels), BF16),
            jax.ShapeDtypeStruct((cells, channels), BF16),
            jax.ShapeDtypeStruct((cells, channels), BF16),
            jax.ShapeDtypeStruct((cells, 3 * channels), BF16),
            jax.ShapeDtypeStruct((halves, tall, members), F32),
        ],
        scratch_shapes=[
            pltpu.VMEM((channels // LANES, cells, LANES), F32),
            pltpu.VMEM((cells, 3 * channels), BF16),
            pltpu.VMEM((cells, channels), BF16),
            pltpu.VMEM(bias_tall.shape, F32),
        ],
        compiler_params=PARAMS,
        cost_estimate=estimate(14),
        name="attention",
    )(arrived.reshape(cells, channels), cot, w_qkv, w_out, bias_tall)


def attention_weights_kernel(x_ref, packed_grad_ref, att_ref, cot_ref, bias_ref, out_ref):
    channels = x_ref.shape[1]
    wide = 3 * channels
    out_ref[:, :wide] = dot(x_ref[...], packed_grad_ref[...], ((0,), (0,))).astype(BF16)
    out_ref[:, wide : wide + channels] = dot(att_ref[...], cot_ref[...], ((0,), (0,))).astype(BF16)
    bias = jnp.concatenate([bias_ref[half] for half in range(bias_ref.shape[0])], axis=1)
    out_ref[:, wide + channels :] = bias.astype(BF16)


def run_attention_weights(x, packed_grad, att, cot, bias):
    channels = x.shape[1]
    vmem = pl.BlockSpec(memory_space=pltpu.VMEM)
    width = 4 * channels + bias.shape[0] * bias.shape[2]
    return pl.pallas_call(
        attention_weights_kernel,
        in_specs=[vmem] * 5,
        out_specs=vmem,
        out_shape=jax.ShapeDtypeStruct((channels, width), BF16),
        compiler_params=PARAMS,
        cost_estimate=estimate(5),
        name="attention_weights",
    )(x, packed_grad, att, cot, bias)


def mixed_back_kernel(
    stride, bands,
    recv_ref, mixed_ref, cot_ref, gain_ref, act_ref, gate_ref, w_projt_ref,
    grad_ref, low_ref, norm_ref, project_ref, gate_grad_ref,
    turned_ref, total_ref,
):
    rows, cols, channels = mixed_ref.shape

    @pl.when(pl.program_id(0) == 0)
    def _():
        gain = gain_ref[...].astype(F32)
        lines = 4

        def some_rows(c, total):
            pieces = []
            for k in range(lines):
                i = c * lines + k
                a, p = lax.rem(i, stride), i // stride
                pieces += [recv_ref[a * bands + band, p] for band in range(bands)]
            grad = jnp.concatenate(pieces, axis=0).astype(F32)
            at = pl.ds(c * lines, lines)
            flat = lambda ref: ref[at].reshape(lines * cols, channels).astype(F32)
            unit, rstd = norm_rows(flat(mixed_ref))
            back = flat(cot_ref) + norm_rows_back(unit, rstd, gain, grad)
            grad_ref[at] = back.reshape(lines, cols, channels)
            low_ref[at] = back.astype(BF16).reshape(lines, cols, channels)
            return total + fold_rows(grad * unit)

        total = lax.fori_loop(
            0, rows // lines, some_rows, jnp.zeros((8, channels), F32), unroll=2
        )
        norm_ref[...] = jnp.sum(total, axis=0, keepdims=True)
        turned_ref[...] = low_ref[...].reshape(rows * cols, channels).T

    flat = act_ref[...].reshape(rows * cols, BLOCK)
    product = dot(turned_ref[...], flat)
    total = jnp.sum(product * w_projt_ref[...].astype(F32), axis=0, keepdims=True)
    step, steps = pl.program_id(0), pl.num_programs(0)
    total_ref[step] = total
    project_ref[...] = (product * gate_ref[...]).T.astype(BF16)

    @pl.when(step == steps - 1)
    def _():
        sums = [total_ref[e] for e in range(total_ref.shape[0])]
        high = [v.astype(BF16).astype(F32) for v in sums]
        terms = jnp.concatenate(high + [v - w for v, w in zip(sums, high)], axis=0)
        gate_grad_ref[...] = jnp.broadcast_to(terms.astype(BF16)[None], gate_grad_ref.shape)


def run_mixed_back(count, stride, recv, mixed, cot, gain, act, gate, w_project_t):
    rows, cols, channels = mixed.shape
    expanded = act.shape[2]
    return pl.pallas_call(
        functools.partial(mixed_back_kernel, stride, cols // SIDE),
        grid=(expanded // BLOCK,),
        in_specs=[
            whole(recv.shape), whole(mixed.shape), whole(cot.shape), whole(gain.shape),
            last_block(act.shape), last_block(gate.shape), last_block(w_project_t.shape),
        ],
        out_specs=[
            whole(mixed.shape), whole(mixed.shape), whole((1, channels)),
            last_block((BLOCK, expanded)), whole((count, 2 * expanded // BLOCK, BLOCK)),
        ],
        out_shape=[
            jax.ShapeDtypeStruct(mixed.shape, F32),
            jax.ShapeDtypeStruct(mixed.shape, BF16),
            jax.ShapeDtypeStruct((1, channels), F32),
            jax.ShapeDtypeStruct((BLOCK, expanded), BF16),
            jax.ShapeDtypeStruct((count, 2 * expanded // BLOCK, BLOCK), BF16),
        ],
        scratch_shapes=[
            pltpu.VMEM((channels, rows * cols), BF16),
            pltpu.VMEM((expanded // BLOCK, 1, BLOCK), F32),
        ],
        compiler_params=PARAMS,
        cost_estimate=estimate(7),
        name="mixed_back",
    )(recv, mixed, cot, gain, act, gate, w_project_t)


def unpack_kernel(
    place_ref, near_ref, far_ref, expand_ref, depth_ref, norm0_ref, norm1_ref, tail_ref
):
    expanded = expand_ref.shape[2]
    for pair, source in enumerate((near_ref, far_ref)):
        at = lax.rem(place_ref[0] + pair, 2)
        expand_ref[at] = source[:, :expanded].astype(F32)
        tail_ref[at] = source[:, expanded:].astype(F32)
    tail = tail_ref[0]
    pieces = expanded // LANES
    for t in range(9):
        for k in range(pieces):
            row = t * pieces + k
            lanes = slice(k * LANES, (k + 1) * LANES)
            depth_ref[t // 3, t % 3 : t % 3 + 1, lanes] = tail[row : row + 1]
    start = 9 * pieces
    half = norm0_ref.shape[1] // LANES
    for k in range(half):
        lanes = slice(k * LANES, (k + 1) * LANES)
        norm0_ref[:, lanes] = tail[start + k : start + k + 1]
        norm1_ref[:, lanes] = tail[start + half + k : start + half + k + 1]


def run_unpack(near, far, expanded):
    rows = near.shape[0]
    channels = 2 * rows
    place = (lax.axis_index("col") % 2).astype(jnp.int32).reshape(1)
    vmem = pl.BlockSpec(memory_space=pltpu.VMEM)
    return pl.pallas_call(
        unpack_kernel,
        in_specs=[pl.BlockSpec(memory_space=pltpu.SMEM), vmem, vmem],
        out_specs=[vmem] * 4,
        out_shape=[
            jax.ShapeDtypeStruct((2, rows, expanded), F32),
            jax.ShapeDtypeStruct((3, 3, expanded), F32),
            jax.ShapeDtypeStruct((1, channels), F32),
            jax.ShapeDtypeStruct((1, channels), F32),
        ],
        scratch_shapes=[pltpu.VMEM((2, rows, near.shape[1] - expanded), F32)],
        compiler_params=PARAMS,
        cost_estimate=estimate(2),
        name="unpack",
    )(place, near, far)


def expand_back_kernel(
    cells_total,
    parts_ref, hidden_ref, gate_all_ref, w_sq_ref, w_ex_ref,
    low_ref, up_ref, down_ref, side_ref, w_projt_ref, gate_ref, slope_ref, side_slope_ref,
    spread_slope_ref, spread_ref, w_dep_ref, turned_ref, w_exp_ref, gain_ref, norm1_ref,
    weights_ref, first_ref, logit_ref, pre_ref,
    main_ref, side_grad_ref, window_ref, expanded_ref, pool_ref, tail_ref, norm_ref,
):
    rows, cols, channels = low_ref.shape
    side = 8
    wide = cols + side
    step = pl.program_id(0)
    steps = pl.num_programs(0)

    @pl.when(step == 0)
    def _():
        gate = gate_all_ref[...]
        blocks = pool_ref.shape[0]
        terms = jnp.sum(parts_ref[...].astype(F32), axis=0)
        gate_grad = jnp.concatenate(
            [terms[e : e + 1] + terms[blocks + e : blocks + e + 1] for e in range(blocks)], axis=1
        )
        logit = gate_grad * gate * (1.0 - gate)
        hidden = hidden_ref[...]
        sig = jax.nn.sigmoid(hidden)
        pre = dot_exact(logit, w_ex_ref[...].astype(F32), ((1,), (1,))) * (
            sig + hidden * sig * (1.0 - sig)
        )
        logit_ref[...] = logit
        pre_ref[...] = pre
        pooled = dot_exact(pre, w_sq_ref[...].astype(F32), ((1,), (1,))) / cells_total
        for e in range(blocks):
            pool_ref[e] = pooled[:, e * BLOCK : (e + 1) * BLOCK]
        first_ref[...] = jnp.zeros(first_ref.shape, F32)
        tail_ref[...] = jnp.zeros(tail_ref.shape, F32)
        norm_ref[...] = jnp.zeros(norm_ref.shape, F32)

    w_projt = w_projt_ref[...]
    main_ref[pl.ds(0, cols), :] = dot(up_ref[0], w_projt)
    main_ref[pl.ds(cols, rows * cols), :] = dot(
        low_ref[...].reshape(rows * cols, channels), w_projt
    )
    main_ref[pl.ds((rows + 1) * cols, cols), :] = dot(down_ref[0], w_projt)
    side_grad_ref[...] = dot(side_ref[...], w_projt)

    @pl.loop(0, rows + 2, unroll=3)
    def _(i):
        for h in range(BLOCK // LANES):
            lanes = slice(h * LANES, (h + 1) * LANES)
            gate = gate_ref[:, lanes]
            pooled = pool_ref[step][:, lanes]
            gated = main_ref[pl.ds(pl.multiple_of(i * cols, 16), cols), lanes]
            main = (gated * gate + pooled) * slope_ref[i, :, lanes].astype(F32)
            gated = side_grad_ref[pl.ds(pl.multiple_of(i * side, side), side), lanes]
            edge = (gated * gate + pooled) * side_slope_ref[i, :, lanes]
            grad = jnp.concatenate([main, edge], axis=0)
            window_ref[0, i, :, lanes] = pltpu.roll(grad, wide - 1, 0)[:cols]
            window_ref[1, i, :, lanes] = grad[:cols]
            window_ref[2, i, :, lanes] = pltpu.roll(grad, 1, 0)[:cols]

    for h in range(BLOCK // LANES):
        lanes = slice(h * LANES, (h + 1) * LANES)
        taps = w_dep_ref[:, :, lanes].astype(F32)

        def back_row(i, sums):
            spread = spread_ref[i, :, lanes].astype(F32)
            total = jnp.zeros((cols, LANES), F32)
            new_sums = []
            for a in range(3):
                for b in range(3):
                    window = window_ref[b, i + 2 - a, :, lanes]
                    total = total + window * taps[a, b : b + 1]
                    new_sums.append(sums[a * 3 + b] + fold_rows(window * spread))
            grad = total * spread_slope_ref[i, :, lanes].astype(F32)
            expanded_ref[pl.ds(pl.multiple_of(i * cols, 16), cols), lanes] = grad.astype(BF16)
            return tuple(new_sums)

        sums = lax.fori_loop(0, rows, back_row, (jnp.zeros((8, LANES), F32),) * 9, unroll=2)
        for t in range(9):
            row = t * (steps * BLOCK // LANES) + step * (BLOCK // LANES) + h
            tail_ref[pl.ds(row, 1), :] = jnp.sum(sums[t], axis=0, keepdims=True)

    grad_expanded = expanded_ref[...]
    w_exp = w_exp_ref[...]
    weights = dot(turned_ref[...], grad_expanded)
    weights_ref[:, pl.ds(pl.multiple_of(step * BLOCK, BLOCK), BLOCK)] = weights.astype(BF16)
    norm_ref[...] += jnp.sum(weights * w_exp.astype(F32), axis=1, keepdims=True)
    first_ref[...] += dot(grad_expanded, w_exp, ((1,), (1,)))

    @pl.when(step == steps - 1)
    def _():
        norm = norm_ref[...].T[0:1] / gain_ref[...].astype(F32)
        start = 9 * steps * (BLOCK // LANES)
        for k in range(channels // LANES):
            piece = slice(k * LANES, (k + 1) * LANES)
            tail_ref[start + k : start + k + 1, :] = norm[:, piece]
            at = start + channels // LANES + k
            tail_ref[at : at + 1, :] = norm1_ref[:, piece]
        weights_ref[:, steps * BLOCK :] = tail_ref[...].astype(BF16)


def run_expand_back(
    cells_total, parts, hidden, gate, w_squeeze, w_excite, low, up, down, side,
    w_project_t, slope, side_slope, spread_slope, spread, w_depth, turned, w_expand, gain, norm1,
):
    rows, cols, channels = low.shape
    expanded = w_expand.shape[1]
    steps = expanded // BLOCK
    return pl.pallas_call(
        functools.partial(expand_back_kernel, cells_total),
        grid=(steps,),
        in_specs=[
            pl.BlockSpec(
                (parts.shape[0], 2 * steps, BLOCK), lambda e: (0, parts.shape[1] // (2 * steps) - 1, 0)
            ),
            whole(hidden.shape), whole(gate.shape),
            whole(w_squeeze.shape), whole(w_excite.shape),
            whole(low.shape), whole(up.shape), whole(down.shape), whole(side.shape),
            last_block(w_project_t.shape), last_block(gate.shape), last_block(slope.shape),
            last_block(side_slope.shape), last_block(spread_slope.shape), last_block(spread.shape),
            last_block(w_depth.shape), whole(turned.shape), last_block(w_expand.shape),
            whole(gain.shape), whole(norm1.shape),
        ],
        out_specs=[
            whole((channels, expanded + LANES)), whole((rows * cols, channels)),
            whole((1, expanded)), whole(hidden.shape),
        ],
        out_shape=[
            jax.ShapeDtypeStruct((channels, expanded + LANES), BF16),
            jax.ShapeDtypeStruct((rows * cols, channels), F32),
            jax.ShapeDtypeStruct((1, expanded), F32),
            jax.ShapeDtypeStruct(hidden.shape, F32),
        ],
        scratch_shapes=[
            pltpu.VMEM(((rows + 2) * cols, BLOCK), F32),
            pltpu.VMEM(((rows + 2) * 8, BLOCK), F32),
            pltpu.VMEM((3, rows + 2, cols, BLOCK), F32),
            pltpu.VMEM((rows * cols, BLOCK), BF16),
            pltpu.VMEM((steps, 1, BLOCK), F32),
            pltpu.VMEM((channels, LANES), F32),
            pltpu.VMEM((channels, LANES), F32),
        ],
        compiler_params=PARAMS,
        cost_estimate=estimate(14),
        name="expand_back",
    )(
        parts, hidden, gate, w_squeeze, w_excite, low, up, down, side, w_project_t, gate,
        slope, side_slope, spread_slope, spread, w_depth, turned, w_expand, gain, norm1,
    )


def image_back_kernel(image_ref, gain_ref, first_ref, mixed_ref, out_ref):
    unit, rstd = norm_rows(image_ref[...].astype(F32))
    grad = first_ref[...]
    back = mixed_ref[...] + norm_rows_back(unit, rstd, gain_ref[...].astype(F32), grad)
    out_ref[...] = back.astype(BF16)


def run_image_back(image, gain, first, mixed):
    cells, channels = image.shape
    block = pl.BlockSpec((cells // 4, channels), lambda r: (r, 0))
    return pl.pallas_call(
        image_back_kernel,
        grid=(4,),
        in_specs=[block, whole(gain.shape), block, block],
        out_specs=block,
        out_shape=jax.ShapeDtypeStruct((cells, channels), BF16),
        compiler_params=PARAMS,
        cost_estimate=estimate(4),
        name="image_back",
    )(image, gain, first, mixed)


def shift(cells, axis, step):
    count = lax.axis_size(axis)
    pairs = [(i, i + step) for i in range(count) if 0 <= i + step < count]
    return lax.ppermute(cells, axis, pairs)


def halo_rows(cells, width):
    up = shift(cells[cells.shape[0] - width :], "row", 1)
    down = shift(cells[:width], "row", -1)
    return up, down


def halo_sides(cells, up, down, width):
    rows, cols, channels = cells.shape
    first = jnp.concatenate([up[:, :width], cells[:, :width], down[:, :width]], axis=0)
    last = jnp.concatenate(
        [up[:, cols - width :], cells[:, cols - width :], down[:, cols - width :]], axis=0
    )
    left = shift(last, "col", 1)
    right = shift(first, "col", -1)
    gap = jnp.zeros((rows + 2 * width, 8 - 2 * width, channels), cells.dtype)
    side = jnp.concatenate([right, gap, left], axis=1)
    return side.reshape(-1, channels)


def hand_around(blocks):
    return lax.all_to_all(blocks, AXES, split_axis=0, concat_axis=0, tiled=True)


def sum_steps():
    return [("col", 1, 2), ("row", 1, lax.axis_size("row")), ("col", 2, lax.axis_size("col") // 2)]


def send_on(v, axis, stride, size, k):
    pairs = []
    for i in range(lax.axis_size(axis)):
        place = i // stride % size
        pairs.append((i, i + ((place + k) % size - place) * stride))
    return lax.ppermute(v, axis, pairs)


def sum_parts(matrix, axis, stride, size):
    place = lax.axis_index(axis) // stride % size
    parts = matrix.reshape(size, matrix.shape[0] // size, matrix.shape[1])
    part = lambda i: lax.dynamic_index_in_dim(parts, i % size, 0, False)
    total = part(place).astype(F32)
    for k in range(1, size):
        total = total + send_on(part(place + k), axis, stride, size, k).astype(F32)
    return total.astype(BF16)


def sum_shares(matrix):
    rows, columns = matrix.shape
    count = lax.axis_size("row") * lax.axis_size("col")
    pair = ("col", 1, 2)
    half = sum_parts(matrix, *pair)
    same_core = [list(range(k, count, 2)) for k in range(2)]

    def around(blocks):
        return lax.all_to_all(
            blocks, AXES, split_axis=0, concat_axis=0, tiled=True, axis_index_groups=same_core
        )

    arrived = around(half.reshape(count // 2, rows // count, columns))
    total = jnp.sum(arrived.astype(F32), axis=0).astype(BF16)
    sent = jnp.broadcast_to(total[None], (count // 2,) + total.shape)
    gathered = around(sent).reshape(rows // 2, columns)
    return gathered, send_on(gathered, *pair, 1)


def stack_kernel(*refs):
    for k, ref in enumerate(refs[:-1]):
        refs[-1][k] = ref[...]


def join_parts(blocks, axis, stride, size):
    arrived = [blocks] + [send_on(blocks, axis, stride, size, k) for k in range(1, size)]
    vmem = pl.BlockSpec(memory_space=pltpu.VMEM)
    stacked = pl.pallas_call(
        stack_kernel,
        in_specs=[vmem] * size,
        out_specs=vmem,
        out_shape=jax.ShapeDtypeStruct((size,) + blocks.shape, blocks.dtype),
        compiler_params=PARAMS,
        cost_estimate=estimate(1),
        name="stack",
    )(*arrived)
    return stacked.reshape((size * blocks.shape[0],) + blocks.shape[1:])


def unpack_weights_kernel(
    sizes, places_ref, near_ref, far_ref, qkv_ref, out_ref, bias_ref, project_ref
):
    channels = out_ref.shape[2]
    cuts = (0, 3 * channels, 4 * channels, 4 * channels + bias_ref.shape[2])
    pairs, over_row, rest = sizes
    for pair, source in enumerate((near_ref, far_ref)):
        for r in range(over_row):
            for c in range(rest):
                block = source[r * rest + c].astype(F32)
                at = lax.rem(places_ref[0] + pairs - pair, pairs)
                at = at * over_row + lax.rem(places_ref[1] + over_row - r, over_row)
                at = at * rest + lax.rem(places_ref[2] + rest - c, rest)
                for k, ref in enumerate((qkv_ref, out_ref, bias_ref)):
                    ref[at] = block[:, cuts[k] : cuts[k + 1]]
                for e in range(project_ref.shape[0]):
                    start = cuts[3] + e * channels
                    project_ref[e, at] = block[:, start : start + channels]


def run_unpack_weights(steps, near, far, channels, expanded, bias_width):
    count, rows, _ = near.shape
    count *= 2
    places = jnp.stack([lax.axis_index(axis) // stride % size for axis, stride, size in steps])
    vmem = pl.BlockSpec(memory_space=pltpu.VMEM)
    blocks = lambda width: jax.ShapeDtypeStruct((count, rows, width), F32)
    return pl.pallas_call(
        functools.partial(unpack_weights_kernel, tuple(size for _, _, size in steps)),
        in_specs=[pl.BlockSpec(memory_space=pltpu.SMEM), vmem, vmem],
        out_specs=[vmem] * 4,
        out_shape=[
            blocks(3 * channels), blocks(channels), blocks(bias_width),
            jax.ShapeDtypeStruct((expanded // BLOCK, count, rows, channels), F32),
        ],
        compiler_params=PARAMS,
        cost_estimate=estimate(2),
        name="unpack_weights",
    )(places.astype(jnp.int32), near, far)


def swap_groups(blocks, parity):
    groups = None
    if parity > 1:
        over_row = lax.axis_size("row")
        over_col = lax.axis_size("col")
        groups = [
            [r * over_col + c for r in range(over_row) for c in range(k, over_col, parity)]
            for k in range(parity)
        ]
    return lax.all_to_all(
        blocks, AXES, split_axis=0, concat_axis=0, tiled=True, axis_index_groups=groups
    )


def on_device(
    image, out_cotangent, norm0_gain, w_expand, w_depth, w_squeeze, w_excite, w_project,
    norm1_gain, w_qkv, w_out, attn_bias,
):
    rows, cols, channels = image.shape
    over_row = lax.axis_size("row")
    over_col = lax.axis_size("col")
    count = over_row * over_col
    cells_total = rows * cols * count
    stride = rows * over_row // GRID
    parity = over_col // GRID
    lines = rows // stride
    bands = cols // SIDE
    members = GRID * GRID
    expanded = w_expand.shape[1]

    def into_members(arrived):
        parted = arrived.reshape(over_row, GRID, lines, SIDE, channels)
        return parted.transpose(3, 0, 2, 1, 4).reshape(SIDE * members, channels)

    def out_of_members(values):
        parted = values.reshape(SIDE, over_row, lines, GRID, channels)
        return parted.transpose(1, 3, 2, 0, 4).reshape(-1, lines, SIDE, channels)

    row, col = lax.axis_index("row"), lax.axis_index("col")
    flags = jnp.stack([row > 0, row < over_row - 1, col > 0, col < over_col - 1]).astype(F32)
    gain_first = norm0_gain.reshape(1, channels)
    gain_second = norm1_gain.reshape(1, channels)
    w_project_t = w_project.T
    heads = attn_bias.shape[0]
    halves = channels // LANES
    bias_tall = attn_bias.transpose(0, 2, 1).reshape(halves, heads // halves * members, members)
    bias_tall = jnp.concatenate([bias_tall, bias_tall], axis=2)

    up, down = halo_rows(image, 2)
    normed_first, turned_first, spread, spread_slope = run_expand(image, gain_first, w_expand)
    up, down, spread = lax.optimization_barrier((up, down, spread))
    side = halo_sides(image, up, down, 2)
    cot_sent = (
        out_cotangent.reshape(lines, stride, bands, SIDE, channels)
        .transpose(1, 2, 0, 3, 4)
        .reshape(stride * bands, lines, SIDE, channels)
    )
    cot_members = into_members(swap_groups(cot_sent, parity))
    ring, act, pool = run_depthwise(count, up, down, side, gain_first, w_expand, w_depth, spread)
    pooled, hidden, gate, mixed, normed_sent = run_mix(
        cells_total, stride, hand_around(pool), w_squeeze, w_excite, act, image, w_project,
        gain_second, cot_members,
    )
    slope, side_slope = run_slope(flags, ring, w_depth, spread)
    normed_arrived = swap_groups(normed_sent, parity)
    normed_arrived, slope = lax.optimization_barrier((normed_arrived, slope))
    normed_members, attended, grad_normed, packed_grad, grad_bias = run_attention(
        normed_arrived, cot_members, w_qkv, w_out, bias_tall, heads, lines
    )
    grad_normed_home = swap_groups(grad_normed.reshape(normed_sent.shape), parity)
    weights = run_attention_weights(normed_members, packed_grad, attended, cot_members, grad_bias)
    grad_normed_home, weights = lax.optimization_barrier((grad_normed_home, weights))
    grad_mixed, grad_low, grad_norm1, grad_project, gate_grad = run_mixed_back(
        count, stride, grad_normed_home, mixed, out_cotangent, gain_second, act, gate, w_project_t
    )
    attended_sent = out_of_members(attended)
    if parity == 1:
        both = hand_around(
            jnp.concatenate([attended_sent.reshape(count, -1, channels), gate_grad], axis=1)
        )
        parts = both
        attended_home = both[:, : lines * SIDE].reshape(attended_sent.shape)
    else:
        parts = hand_around(gate_grad)
        attended_home = swap_groups(attended_sent, parity)
    up, down = halo_rows(grad_low, 1)
    side = halo_sides(grad_low, up, down, 1)
    weights = jnp.concatenate([weights, grad_project], axis=1)
    weights, _ = lax.optimization_barrier((weights, up))
    steps = sum_steps()
    for step in steps:
        weights = sum_parts(weights, *step)
    late, grad_first, logit, pre = run_expand_back(
        cells_total, parts, hidden, gate, w_squeeze, w_excite, grad_low, up, down, side,
        w_project_t, slope, side_slope, spread_slope, spread, w_depth, turned_first, w_expand,
        gain_first, grad_norm1,
    )
    weights, _ = lax.optimization_barrier((weights, late))
    weights = weights[None]
    for step in steps[:0:-1]:
        weights = join_parts(weights, *step)
    other = send_on(weights, *steps[0], 1)
    grad_qkv, grad_out_proj, grad_bias, grad_project = run_unpack_weights(
        steps, weights, other, channels, expanded, halves * members
    )
    grad_expand, grad_depth, grad_norm0, grad_norm1 = run_unpack(*sum_shares(late), expanded)
    grad_image = run_image_back(
        image.reshape(-1, channels), gain_first, grad_first, grad_mixed.reshape(-1, channels)
    )
    attended_map = (
        attended_home.reshape(stride, bands, lines, SIDE, channels)
        .transpose(2, 0, 1, 3, 4)
        .reshape(rows * cols, channels)
    )
    block_out = (mixed.reshape(-1, channels).astype(F32) + dot(attended_map, w_out)).astype(BF16)

    silu = jax.nn.silu(hidden)
    grad_squeeze = pooled.reshape(expanded, 1) * pre
    grad_excite = silu.reshape(-1, 1) * logit

    grad_bias = (
        grad_bias.reshape(heads // halves, members, halves, members)
        .transpose(2, 0, 3, 1)
        .reshape(attn_bias.shape)
    )
    return (
        block_out.reshape(image.shape),
        grad_image.reshape(image.shape),
        grad_norm0[0],
        grad_expand.reshape(w_expand.shape),
        grad_depth,
        grad_squeeze,
        grad_excite,
        grad_project.reshape(w_project.shape),
        grad_norm1[0],
        grad_qkv.reshape(w_qkv.shape),
        grad_out_proj.reshape(w_out.shape),
        grad_bias,
    )


def solution(mesh):
    cells = P("row", "col", None)
    return jax.shard_map(
        on_device,
        mesh=mesh,
        in_specs=(cells, cells) + (P(),) * 10,
        out_specs=(cells, cells) + (P(),) * 10,
        check_vma=False,
    )
```

```python
import functools
import math

import jax
import jax.numpy as jnp
from jax import lax
from jax.experimental import pallas as pl
from jax.experimental.pallas import tpu as pltpu
from jax.sharding import PartitionSpec as P

GRID = 8
AXES = ("row", "col")
BLOCK = 256
LANES = 128
SIDE = 16
GELU_A = math.sqrt(2.0 / math.pi)
GELU_B = GELU_A * 0.044715
F32 = jnp.float32
BF16 = jnp.bfloat16
PARAMS = pltpu.CompilerParams(vmem_limit_bytes=56 * 1024 * 1024)


def estimate(us):
    return pl.CostEstimate(flops=int(us * 1.1e9), bytes_accessed=int(us * 3.6e6), transcendentals=0)


def dot(left, right, contract=((1,), (0,))):
    return lax.dot_general(left, right, (contract, ((), ())), preferred_element_type=F32)


def dot_exact(vector, right, contract):
    tall = jnp.broadcast_to(vector, (8, vector.shape[1]))
    product = lax.dot_general(
        tall, right, (contract, ((), ())), precision=lax.Precision.HIGHEST, preferred_element_type=F32
    )
    return product[0:1]


def gelu_and_slope(x, with_slope=True):
    square = x * x
    t = jnp.tanh(x * (GELU_A + GELU_B * square))
    half = 0.5 + 0.5 * t
    value = x * half
    if not with_slope:
        return value, None
    slope = half + (value * (1.0 - t)) * (GELU_A + (3.0 * GELU_B) * square)
    return value, slope


def norm_rows(x):
    average = jnp.mean(x, axis=-1, keepdims=True)
    centered = x - average
    variance = jnp.mean(centered * centered, axis=-1, keepdims=True)
    rstd = lax.rsqrt(variance + 1e-05)
    return centered * rstd, rstd


def norm_rows_back(unit, rstd, gain, grad):
    unit_grad = grad * gain
    first = jnp.mean(unit_grad, axis=-1, keepdims=True)
    second = jnp.mean(unit_grad * unit, axis=-1, keepdims=True)
    return rstd * (unit_grad - first - unit * second)


def fold_rows(x):
    return jnp.sum(x.reshape(x.shape[0] // 8, 8, x.shape[1]), axis=0)


def whole(shape):
    return pl.BlockSpec(shape, lambda e: (0,) * len(shape))


def last_block(shape):
    lead = (0,) * (len(shape) - 1)
    return pl.BlockSpec(shape[:-1] + (BLOCK,), lambda e: lead + (e,))


def expand_kernel(
    image_ref, gain_ref, w_exp_ref,
    normed_ref, turned_ref, spread_ref, slope_ref,
    expanded_ref,
):
    rows, cols, channels = image_ref.shape

    @pl.when(pl.program_id(0) == 0)
    def _():
        gain = gain_ref[...].astype(F32)

        @pl.loop(0, rows // 4)
        def _(c):
            flat = image_ref[pl.ds(c * 4, 4)].reshape(4 * cols, channels)
            unit, _ = norm_rows(flat.astype(F32))
            at = pl.ds(pl.multiple_of(c * 4 * cols, 16), 4 * cols)
            normed_ref[at, :] = (unit * gain).astype(BF16)

        turned_ref[...] = normed_ref[...].T

    expanded_ref[...] = dot(normed_ref[...], w_exp_ref[...])

    @pl.loop(0, rows, unroll=4)
    def _(r):
        for h in range(BLOCK // LANES):
            lanes = slice(h * LANES, (h + 1) * LANES)
            x = expanded_ref[pl.ds(pl.multiple_of(r * cols, 16), cols), lanes]
            value, slope = gelu_and_slope(x)
            spread_ref[r, :, lanes] = value.astype(BF16)
            slope_ref[r, :, lanes] = slope.astype(BF16)


def run_expand(image, gain, w_expand):
    rows, cols, channels = image.shape
    expanded = w_expand.shape[1]
    return pl.pallas_call(
        expand_kernel,
        grid=(expanded // BLOCK,),
        in_specs=[whole(image.shape), whole(gain.shape), last_block(w_expand.shape)],
        out_specs=[
            whole((rows * cols, channels)), whole((channels, rows * cols)),
            last_block((rows, cols, expanded)), last_block((rows, cols, expanded)),
        ],
        out_shape=[
            jax.ShapeDtypeStruct((rows * cols, channels), BF16),
            jax.ShapeDtypeStruct((channels, rows * cols), BF16),
            jax.ShapeDtypeStruct((rows, cols, expanded), BF16),
            jax.ShapeDtypeStruct((rows, cols, expanded), BF16),
        ],
        scratch_shapes=[pltpu.VMEM((rows * cols, BLOCK), F32)],
        compiler_params=PARAMS,
        cost_estimate=estimate(14),
        name="expand",
    )(image, gain, w_expand)


def depthwise_kernel(
    up_ref, down_ref, side_ref, gain_ref, w_exp_ref, w_dep_ref, spread_ref,
    ring_ref, act_ref, pool_ref,
    ring_normed_ref, ring_wide_ref,
):
    rows, cols, _ = spread_ref.shape
    channels = up_ref.shape[2]
    over = 4 * cols
    side = 8

    @pl.when(pl.program_id(0) == 0)
    def _():
        gain = gain_ref[...].astype(F32)

        def put(at, values):
            unit, _ = norm_rows(values.astype(F32))
            ring_normed_ref[at : at + values.shape[0], :] = (unit * gain).astype(BF16)

        put(0, up_ref[...].reshape(2 * cols, channels))
        put(2 * cols, down_ref[...].reshape(2 * cols, channels))
        put(over, side_ref[...])

    ring_wide_ref[...] = dot(ring_normed_ref[...], w_exp_ref[...])
    tile = 32

    @pl.loop(0, ring_wide_ref.shape[0] // tile, unroll=True)
    def _(t):
        at = pl.ds(pl.multiple_of(t * tile, tile), tile)
        value, _ = gelu_and_slope(ring_wide_ref[at, :], False)
        low = value.astype(BF16)
        ring_ref[at, :] = low
        ring_wide_ref[at, :] = low.astype(F32)

    for h in range(BLOCK // LANES):
        lanes = slice(h * LANES, (h + 1) * LANES)
        taps = w_dep_ref[:, :, lanes].astype(F32)
        w = [[taps[a, b : b + 1] for b in range(3)] for a in range(3)]

        def line(r, main):
            at = pl.multiple_of(over + (r + 2) * side, side)
            return jnp.concatenate([main, ring_wide_ref[pl.ds(at, side), lanes]], axis=0)

        def conv(i, x, total):
            u = [x[0] * w[0][b] + x[1] * w[1][b] + x[2] * w[2][b] for b in range(3)]
            wide = cols + side
            pre = pltpu.roll(u[0], 1, 0) + u[1] + pltpu.roll(u[2], wide - 1, 0)
            value, _ = gelu_and_slope(pre[:cols], False)
            act_ref[i, :, lanes] = value.astype(BF16)
            return total + fold_rows(value)

        def step(i, carry):
            first, second, total = carry
            third = line(i + 1, spread_ref[i + 1, :, lanes].astype(F32))
            return second, third, conv(i, (first, second, third), total)

        carry = (
            line(-1, ring_wide_ref[cols : 2 * cols, lanes]),
            line(0, spread_ref[0, :, lanes].astype(F32)),
            jnp.zeros((8, LANES), F32),
        )
        first, second, total = lax.fori_loop(0, rows - 1, step, carry, unroll=5)
        third = line(rows, ring_wide_ref[2 * cols : 3 * cols, lanes])
        total = conv(rows - 1, (first, second, third), total)
        total = jnp.sum(total, axis=0, keepdims=True)
        pool_ref[:, :, lanes] = jnp.broadcast_to(total[None], (pool_ref.shape[0], 1, LANES))


def run_depthwise(count, up, down, side, gain, w_expand, w_depth, spread):
    rows, cols, expanded = spread.shape
    channels = up.shape[2]
    ring = 4 * cols + 8 * (rows + 4)
    return pl.pallas_call(
        depthwise_kernel,
        grid=(expanded // BLOCK,),
        in_specs=[
            whole(up.shape), whole(down.shape), whole(side.shape), whole(gain.shape),
            last_block(w_expand.shape), last_block(w_depth.shape), last_block(spread.shape),
        ],
        out_specs=[
            last_block((ring, expanded)), last_block(spread.shape), last_block((count, 1, expanded)),
        ],
        out_shape=[
            jax.ShapeDtypeStruct((ring, expanded), BF16),
            jax.ShapeDtypeStruct(spread.shape, BF16),
            jax.ShapeDtypeStruct((count, 1, expanded), F32),
        ],
        scratch_shapes=[pltpu.VMEM((ring, channels), BF16), pltpu.VMEM((ring, BLOCK), F32)],
        compiler_params=PARAMS,
        cost_estimate=estimate(1),
        name="depthwise",
    )(up, down, side, gain, w_expand, w_depth, spread)


def slope_kernel(flags_ref, ring_ref, w_dep_ref, spread_ref, main_ref, side_out_ref, wide_ref):
    rows, cols, _ = spread_ref.shape
    over = 4 * cols
    side = 8
    wide = cols + side

    for k, r in enumerate((0, 1, rows + 2, rows + 3)):
        wide_ref[r, :cols, :] = ring_ref[k * cols : (k + 1) * cols, :].astype(F32)
    sides = ring_ref[over:, :].astype(F32)
    for r in range(rows + 4):
        wide_ref[r, cols:, :] = sides[r * side : (r + 1) * side]

    @pl.loop(0, rows)
    def _(r):
        wide_ref[r + 2, :cols, :] = spread_ref[r].astype(F32)

    place = lax.broadcasted_iota(jnp.int32, (side, LANES), 0)
    side_mask = jnp.where(
        place == side - 1, flags_ref[2], jnp.where(place == 0, flags_ref[3], 1.0)
    ).astype(F32)

    @pl.loop(0, rows + 2)
    def _(i):
        keep = jnp.where(i == 0, flags_ref[0], jnp.where(i == rows + 1, flags_ref[1], 1.0))
        for h in range(BLOCK // LANES):
            lanes = slice(h * LANES, (h + 1) * LANES)
            taps = w_dep_ref[:, :, lanes].astype(F32)
            x = [wide_ref[i + a, :, lanes] for a in range(3)]
            u = [sum(x[a] * taps[a, b : b + 1] for a in range(3)) for b in range(3)]
            pre = pltpu.roll(u[0], 1, 0) + u[1] + pltpu.roll(u[2], wide - 1, 0)
            _, slope = gelu_and_slope(pre)
            slope = slope * keep
            main_ref[i, :, lanes] = slope[:cols].astype(BF16)
            side_out_ref[i, :, lanes] = slope[cols:] * side_mask


def run_slope(flags, ring, w_depth, spread):
    rows, cols, expanded = spread.shape
    return pl.pallas_call(
        slope_kernel,
        grid=(expanded // BLOCK,),
        in_specs=[
            pl.BlockSpec(memory_space=pltpu.SMEM),
            last_block(ring.shape), last_block(w_depth.shape), last_block(spread.shape),
        ],
        out_specs=[last_block((rows + 2, cols, expanded)), last_block((rows + 2, 8, expanded))],
        out_shape=[
            jax.ShapeDtypeStruct((rows + 2, cols, expanded), BF16),
            jax.ShapeDtypeStruct((rows + 2, 8, expanded), F32),
        ],
        scratch_shapes=[pltpu.VMEM((rows + 4, cols + 8, BLOCK), F32)],
        compiler_params=PARAMS,
        cost_estimate=estimate(13),
        name="slope",
    )(flags, ring, w_depth, spread)


def mix_kernel(
    cells_total, stride, bands,
    parts_ref, w_sq_ref, w_ex_ref, act_ref, image_ref, w_proj_ref, gain_ref, after_ref,
    pooled_ref, hidden_ref, gate_ref, mixed_ref, send_ref,
):
    step = pl.program_id(0)

    @pl.when(step == 0)
    def _():
        pooled = jnp.sum(parts_ref[...], axis=0) / cells_total
        hidden = dot_exact(pooled, w_sq_ref[...].astype(F32), ((1,), (0,)))
        silu = hidden * jax.nn.sigmoid(hidden)
        pooled_ref[...] = pooled
        hidden_ref[...] = hidden
        gate_ref[...] = jax.nn.sigmoid(dot_exact(silu, w_ex_ref[...].astype(F32), ((1,), (0,))))

    lines, cols, channels = image_ref.shape
    flat = act_ref[...].reshape(lines * cols, act_ref.shape[2])
    gated = (flat.astype(F32) * gate_ref[...]).astype(BF16)
    product = dot(gated, w_proj_ref[...])
    mixed = (image_ref[...].reshape(lines * cols, channels).astype(F32) + product).astype(BF16)
    mixed_ref[...] = mixed.reshape(lines, cols, channels)
    unit, _ = norm_rows(mixed.astype(F32))
    normed = (unit * gain_ref[...].astype(F32)).astype(BF16)
    for k in range(lines):
        line = step * lines + k
        for band in range(bands):
            start = k * cols + band * SIDE
            send_ref[lax.rem(line, stride) * bands + band, line // stride] = normed[
                start : start + SIDE
            ]


def run_mix(cells_total, stride, parts, w_squeeze, w_excite, act, image, w_project, gain, after):
    rows, cols, channels = image.shape
    expanded = act.shape[2]
    lines = 4
    bands = cols // SIDE
    block = lambda width: pl.BlockSpec((lines, cols, width), lambda r: (r, 0, 0))
    send = (stride * bands, rows // stride, SIDE, channels)
    return pl.pallas_call(
        functools.partial(mix_kernel, cells_total, stride, bands),
        grid=(rows // lines,),
        in_specs=[
            whole(parts.shape), whole(w_squeeze.shape), whole(w_excite.shape),
            block(expanded), block(channels), whole(w_project.shape), whole(gain.shape),
            pl.BlockSpec(memory_space=pl.ANY),
        ],
        out_specs=[
            whole((1, expanded)), whole((1, w_squeeze.shape[1])), whole((1, expanded)),
            block(channels), whole(send),
        ],
        out_shape=[
            jax.ShapeDtypeStruct((1, expanded), F32),
            jax.ShapeDtypeStruct((1, w_squeeze.shape[1]), F32),
            jax.ShapeDtypeStruct((1, expanded), F32),
            jax.ShapeDtypeStruct(image.shape, BF16),
            jax.ShapeDtypeStruct(send, BF16),
        ],
        compiler_params=PARAMS,
        cost_estimate=estimate(5),
        name="mix",
    )(parts, w_squeeze, w_excite, act, image, w_project, gain, after)


def attention_kernel(
    members, heads, lines,
    arrived_ref, att_grad_ref, w_qkv_ref, bias_ref,
    x_ref, att_ref, grad_ref, packed_grad_ref, bias_out_ref,
    order_ref, packed_ref, bias_sum_ref,
):
    cells, channels = x_ref.shape
    groups = cells // members

    def places():
        for g in range(groups):
            for m in range(0, members, GRID):
                line, row = (m // GRID) % lines, m // GRID // lines
                start = (row * GRID * lines + line) * groups + g
                yield g * members + m, pl.ds(start, GRID, stride=lines * groups)

    for half in range(channels // LANES):
        lanes = slice(half * LANES, (half + 1) * LANES)
        order_ref[half] = arrived_ref[:, lanes].astype(F32)
        for g in range(groups):
            pieces = [order_ref[half, at, :] for k, at in places() if k // members == g]
            at = slice(g * members, (g + 1) * members)
            x_ref[at, lanes] = jnp.concatenate(pieces, axis=0).astype(BF16)
    dim = channels // heads
    per_half = LANES // dim
    halves = channels // LANES
    scale = dim ** (-0.5)
    packed_ref[...] = dot(x_ref[...], w_qkv_ref[...]).astype(BF16)
    bias_sum_ref[...] = jnp.zeros(bias_sum_ref.shape, F32)
    tall = per_half * members
    mask = (
        lax.broadcasted_iota(jnp.int32, (tall, LANES), 0) // members
        == lax.broadcasted_iota(jnp.int32, (tall, LANES), 1) // dim
    ).astype(F32).astype(BF16)
    owner = lax.broadcasted_iota(jnp.int32, (members, 2 * LANES), 1) % LANES // dim
    zero = jnp.zeros((members, LANES), BF16)

    def by_head(pair):
        return jnp.concatenate(
            [jnp.concatenate([v] * per_half, axis=0) * mask for v in pair], axis=1
        )

    def diagonal(pair):
        return jnp.concatenate(
            [
                jnp.concatenate([pair[0], zero], axis=1),
                jnp.concatenate([zero, pair[1]], axis=1),
            ],
            axis=0,
        )

    def collect(v):
        parts = [v[h * members : (h + 1) * members] for h in range(per_half)]
        picked = parts[-1]
        for h in range(per_half - 1):
            picked = jnp.where(owner == h, parts[h], picked)
        return [picked[:, :LANES], picked[:, LANES:]]

    def blocks(v):
        return [v[:members, :LANES], v[members:, LANES:]]

    def over_members(v, reduce):
        parted = v.reshape(per_half, members, 2 * members)
        small = reduce(parted, axis=1, keepdims=True)
        return jnp.broadcast_to(small, parted.shape).reshape(v.shape)

    def pair_step(g, carry):
        at = [pl.ds(pl.multiple_of((2 * g + k) * members, 16), members) for k in range(2)]
        for half in range(halves):
            def lanes(part):
                start = part * channels + half * LANES
                return slice(start, start + LANES)

            q, k, v = ([packed_ref[at[n], lanes(part)] for n in range(2)] for part in range(3))
            cot = [att_grad_ref[at[n], lanes(0)] for n in range(2)]
            q_diag, cot_diag = diagonal(q), diagonal(cot)
            k_tall, v_tall = by_head(k), by_head(v)
            scores = dot(k_tall, q_diag, ((1,), (1,))) * scale + bias_ref[half]
            grad_probs = dot(v_tall, cot_diag, ((1,), (1,)))
            lifted = jnp.exp(scores - over_members(scores, jnp.max))
            soft = lifted * (1.0 / over_members(lifted, jnp.sum))
            soft_low = soft.astype(BF16)
            grad_scores = soft * (grad_probs - over_members(grad_probs * soft, jnp.sum))
            bias_sum_ref[half] += grad_scores
            scaled = (grad_scores * scale).astype(BF16)
            attended = blocks(dot(soft_low, v_tall, ((0,), (0,))))
            grad_q = blocks(dot(scaled, k_tall, ((0,), (0,))))
            grad_v = collect(dot(soft_low, cot_diag))
            grad_k = collect(dot(scaled, q_diag))
            for n in range(2):
                att_ref[at[n], lanes(0)] = attended[n].astype(BF16)
                for part, value in enumerate((grad_q, grad_k, grad_v)):
                    packed_grad_ref[at[n], lanes(part)] = value[n].astype(BF16)
        return carry

    lax.fori_loop(0, cells // members // 2, pair_step, 0, unroll=2)
    grad = dot(packed_grad_ref[...], w_qkv_ref[...], ((1,), (1,)))
    for half in range(halves):
        lanes = slice(half * LANES, (half + 1) * LANES)
        for k, at in places():
            order_ref[half, at, :] = grad[k : k + GRID, lanes]
        grad_ref[:, lanes] = order_ref[half].astype(BF16)
    for half in range(halves):
        both = bias_sum_ref[half]
        bias_out_ref[half] = both[:, :members] + both[:, members:]


def run_attention(arrived, att_grad, w_qkv, bias_tall, heads, lines):
    cells, channels = att_grad.shape
    halves, tall, members2 = bias_tall.shape
    members = members2 // 2
    vmem = pl.BlockSpec(memory_space=pltpu.VMEM)
    return pl.pallas_call(
        functools.partial(attention_kernel, members, heads, lines),
        in_specs=[vmem] * 4,
        out_specs=[vmem] * 5,
        out_shape=[
            jax.ShapeDtypeStruct((cells, channels), BF16),
            jax.ShapeDtypeStruct((cells, channels), BF16),
            jax.ShapeDtypeStruct((cells, channels), BF16),
            jax.ShapeDtypeStruct((cells, 3 * channels), BF16),
            jax.ShapeDtypeStruct((halves, tall, members), F32),
        ],
        scratch_shapes=[
            pltpu.VMEM((channels // LANES, cells, LANES), F32),
            pltpu.VMEM((cells, 3 * channels), BF16),
            pltpu.VMEM(bias_tall.shape, F32),
        ],
        compiler_params=PARAMS,
        cost_estimate=estimate(14),
        name="attention",
    )(arrived.reshape(cells, channels), att_grad, w_qkv, bias_tall)


def attention_weights_kernel(x_ref, packed_grad_ref, att_ref, cot_ref, bias_ref, out_ref):
    channels = x_ref.shape[1]
    wide = 3 * channels
    out_ref[:, :wide] = dot(x_ref[...], packed_grad_ref[...], ((0,), (0,))).astype(BF16)
    out_ref[:, wide : wide + channels] = dot(att_ref[...], cot_ref[...], ((0,), (0,))).astype(BF16)
    halves, tall, members = bias_ref.shape
    for h in range(tall // members):
        rows = slice(h * members, (h + 1) * members)
        turned = jnp.concatenate([bias_ref[half, rows, :].T for half in range(halves)], axis=1)
        out_ref[rows, wide + channels :] = turned.astype(BF16)


def run_attention_weights(x, packed_grad, att, cot, bias):
    channels = x.shape[1]
    vmem = pl.BlockSpec(memory_space=pltpu.VMEM)
    width = 4 * channels + bias.shape[0] * bias.shape[2]
    return pl.pallas_call(
        attention_weights_kernel,
        in_specs=[vmem] * 5,
        out_specs=vmem,
        out_shape=jax.ShapeDtypeStruct((channels, width), BF16),
        compiler_params=PARAMS,
        cost_estimate=estimate(5),
        name="attention_weights",
    )(x, packed_grad, att, cot, bias)


def mixed_back_kernel(
    stride, bands,
    recv_ref, mixed_ref, cot_ref, gain_ref, act_ref, gate_ref, w_projt_ref,
    grad_ref, low_ref, norm_ref, project_ref, gate_grad_ref, lines_ref, sides_ref,
    turned_ref, total_ref,
):
    rows, cols, channels = mixed_ref.shape

    @pl.when(pl.program_id(0) == 0)
    def _():
        gain = gain_ref[...].astype(F32)
        lines = 4

        def some_rows(c, total):
            pieces = []
            for k in range(lines):
                i = c * lines + k
                a, p = lax.rem(i, stride), i // stride
                pieces += [recv_ref[a * bands + band, p] for band in range(bands)]
            grad = jnp.concatenate(pieces, axis=0).astype(F32)
            at = pl.ds(c * lines, lines)
            flat = lambda ref: ref[at].reshape(lines * cols, channels).astype(F32)
            unit, rstd = norm_rows(flat(mixed_ref))
            back = flat(cot_ref) + norm_rows_back(unit, rstd, gain, grad)
            grad_ref[at] = back.reshape(lines, cols, channels)
            low_ref[at] = back.astype(BF16).reshape(lines, cols, channels)
            return total + fold_rows(grad * unit)

        total = lax.fori_loop(
            0, rows // lines, some_rows, jnp.zeros((8, channels), F32), unroll=2
        )
        norm_ref[...] = jnp.sum(total, axis=0, keepdims=True)
        lines_ref[0] = low_ref[0]
        lines_ref[1] = low_ref[rows - 1]
        for i in range(rows):
            sides_ref[0, i] = low_ref[i, 0:1, :]
            sides_ref[1, i] = low_ref[i, cols - 1 : cols, :]
        turned_ref[...] = low_ref[...].reshape(rows * cols, channels).T

    flat = act_ref[...].reshape(rows * cols, BLOCK)
    product = dot(turned_ref[...], flat)
    total = jnp.sum(product * w_projt_ref[...].astype(F32), axis=0, keepdims=True)
    step, steps = pl.program_id(0), pl.num_programs(0)
    total_ref[step] = total
    project_ref[...] = (product * gate_ref[...]).T.astype(BF16)

    @pl.when(step == steps - 1)
    def _():
        sums = [total_ref[e] for e in range(total_ref.shape[0])]
        high = [v.astype(BF16).astype(F32) for v in sums]
        terms = jnp.concatenate(high + [v - w for v, w in zip(sums, high)], axis=0)
        gate_grad_ref[...] = jnp.broadcast_to(terms.astype(BF16)[None], gate_grad_ref.shape)


def run_mixed_back(count, stride, recv, mixed, cot, gain, act, gate, w_project_t):
    rows, cols, channels = mixed.shape
    expanded = act.shape[2]
    return pl.pallas_call(
        functools.partial(mixed_back_kernel, stride, cols // SIDE),
        grid=(expanded // BLOCK,),
        in_specs=[
            whole(recv.shape), whole(mixed.shape), whole(cot.shape), whole(gain.shape),
            last_block(act.shape), last_block(gate.shape), last_block(w_project_t.shape),
        ],
        out_specs=[
            whole(mixed.shape), whole(mixed.shape), whole((1, channels)),
            last_block((BLOCK, expanded)), whole((count, 2 * expanded // BLOCK, BLOCK)),
            whole((2, cols, channels)), whole((2, rows, 1, channels)),
        ],
        out_shape=[
            jax.ShapeDtypeStruct(mixed.shape, F32),
            jax.ShapeDtypeStruct(mixed.shape, BF16),
            jax.ShapeDtypeStruct((1, channels), F32),
            jax.ShapeDtypeStruct((BLOCK, expanded), BF16),
            jax.ShapeDtypeStruct((count, 2 * expanded // BLOCK, BLOCK), BF16),
            jax.ShapeDtypeStruct((2, cols, channels), BF16),
            jax.ShapeDtypeStruct((2, rows, 1, channels), BF16),
        ],
        scratch_shapes=[
            pltpu.VMEM((channels, rows * cols), BF16),
            pltpu.VMEM((expanded // BLOCK, 1, BLOCK), F32),
        ],
        compiler_params=PARAMS,
        cost_estimate=estimate(7),
        name="mixed_back",
    )(recv, mixed, cot, gain, act, gate, w_project_t)


def unpack_kernel(
    place_ref, near_ref, far_ref, expand_ref, depth_ref, norm0_ref, norm1_ref, tail_ref
):
    expanded = expand_ref.shape[2]
    for pair, source in enumerate((near_ref, far_ref)):
        at = lax.rem(place_ref[0] + pair, 2)
        expand_ref[at] = source[:, :expanded].astype(F32)
        tail_ref[at] = source[:, expanded:].astype(F32)
    tail = tail_ref[0]
    pieces = expanded // LANES
    for t in range(9):
        for k in range(pieces):
            row = t * pieces + k
            lanes = slice(k * LANES, (k + 1) * LANES)
            depth_ref[t // 3, t % 3 : t % 3 + 1, lanes] = tail[row : row + 1]
    start = 9 * pieces
    half = norm0_ref.shape[1] // LANES
    for k in range(half):
        lanes = slice(k * LANES, (k + 1) * LANES)
        norm0_ref[:, lanes] = tail[start + k : start + k + 1]
        norm1_ref[:, lanes] = tail[start + half + k : start + half + k + 1]


def run_unpack(near, far, expanded):
    rows = near.shape[0]
    channels = 2 * rows
    place = (lax.axis_index("col") % 2).astype(jnp.int32).reshape(1)
    vmem = pl.BlockSpec(memory_space=pltpu.VMEM)
    return pl.pallas_call(
        unpack_kernel,
        in_specs=[pl.BlockSpec(memory_space=pltpu.SMEM), vmem, vmem],
        out_specs=[vmem] * 4,
        out_shape=[
            jax.ShapeDtypeStruct((2, rows, expanded), F32),
            jax.ShapeDtypeStruct((3, 3, expanded), F32),
            jax.ShapeDtypeStruct((1, channels), F32),
            jax.ShapeDtypeStruct((1, channels), F32),
        ],
        scratch_shapes=[pltpu.VMEM((2, rows, near.shape[1] - expanded), F32)],
        compiler_params=PARAMS,
        cost_estimate=estimate(2),
        name="unpack",
    )(place, near, far)


def expand_back_kernel(
    cells_total,
    parts_ref, hidden_ref, gate_all_ref, w_sq_ref, w_ex_ref,
    low_ref, up_ref, down_ref, side_ref, w_projt_ref, gate_ref, slope_ref, side_slope_ref,
    spread_slope_ref, spread_ref, w_dep_ref, turned_ref, w_exp_ref, gain_ref, norm1_ref,
    weights_ref, first_ref, logit_ref, pre_ref,
    main_ref, side_grad_ref, window_ref, expanded_ref, pool_ref, tail_ref, norm_ref,
):
    rows, cols, channels = low_ref.shape
    side = 8
    wide = cols + side
    step = pl.program_id(0)
    steps = pl.num_programs(0)

    @pl.when(step == 0)
    def _():
        gate = gate_all_ref[...]
        blocks = pool_ref.shape[0]
        terms = jnp.sum(parts_ref[...].astype(F32), axis=0)
        gate_grad = jnp.concatenate(
            [terms[e : e + 1] + terms[blocks + e : blocks + e + 1] for e in range(blocks)], axis=1
        )
        logit = gate_grad * gate * (1.0 - gate)
        hidden = hidden_ref[...]
        sig = jax.nn.sigmoid(hidden)
        pre = dot_exact(logit, w_ex_ref[...].astype(F32), ((1,), (1,))) * (
            sig + hidden * sig * (1.0 - sig)
        )
        logit_ref[...] = logit
        pre_ref[...] = pre
        pooled = dot_exact(pre, w_sq_ref[...].astype(F32), ((1,), (1,))) / cells_total
        for e in range(blocks):
            pool_ref[e] = pooled[:, e * BLOCK : (e + 1) * BLOCK]
        first_ref[...] = jnp.zeros(first_ref.shape, F32)
        tail_ref[...] = jnp.zeros(tail_ref.shape, F32)
        norm_ref[...] = jnp.zeros(norm_ref.shape, F32)

    w_projt = w_projt_ref[...]
    main_ref[pl.ds(0, cols), :] = dot(up_ref[0], w_projt)
    main_ref[pl.ds(cols, rows * cols), :] = dot(
        low_ref[...].reshape(rows * cols, channels), w_projt
    )
    main_ref[pl.ds((rows + 1) * cols, cols), :] = dot(down_ref[0], w_projt)
    side_grad_ref[...] = dot(side_ref[...], w_projt)

    @pl.loop(0, rows + 2, unroll=3)
    def _(i):
        for h in range(BLOCK // LANES):
            lanes = slice(h * LANES, (h + 1) * LANES)
            gate = gate_ref[:, lanes]
            pooled = pool_ref[step][:, lanes]
            gated = main_ref[pl.ds(pl.multiple_of(i * cols, 16), cols), lanes]
            main = (gated * gate + pooled) * slope_ref[i, :, lanes].astype(F32)
            gated = side_grad_ref[pl.ds(pl.multiple_of(i * side, side), side), lanes]
            edge = (gated * gate + pooled) * side_slope_ref[i, :, lanes]
            grad = jnp.concatenate([main, edge], axis=0)
            window_ref[0, i, :, lanes] = pltpu.roll(grad, wide - 1, 0)[:cols]
            window_ref[1, i, :, lanes] = grad[:cols]
            window_ref[2, i, :, lanes] = pltpu.roll(grad, 1, 0)[:cols]

    for h in range(BLOCK // LANES):
        lanes = slice(h * LANES, (h + 1) * LANES)
        taps = w_dep_ref[:, :, lanes].astype(F32)

        def back_row(i, sums):
            spread = spread_ref[i, :, lanes].astype(F32)
            total = jnp.zeros((cols, LANES), F32)
            new_sums = []
            for a in range(3):
                for b in range(3):
                    window = window_ref[b, i + 2 - a, :, lanes]
                    total = total + window * taps[a, b : b + 1]
                    new_sums.append(sums[a * 3 + b] + fold_rows(window * spread))
            grad = total * spread_slope_ref[i, :, lanes].astype(F32)
            expanded_ref[pl.ds(pl.multiple_of(i * cols, 16), cols), lanes] = grad.astype(BF16)
            return tuple(new_sums)

        sums = lax.fori_loop(0, rows, back_row, (jnp.zeros((8, LANES), F32),) * 9, unroll=2)
        for t in range(9):
            row = t * (steps * BLOCK // LANES) + step * (BLOCK // LANES) + h
            tail_ref[pl.ds(row, 1), :] = jnp.sum(sums[t], axis=0, keepdims=True)

    grad_expanded = expanded_ref[...]
    w_exp = w_exp_ref[...]
    weights = dot(turned_ref[...], grad_expanded)
    weights_ref[:, pl.ds(pl.multiple_of(step * BLOCK, BLOCK), BLOCK)] = weights.astype(BF16)
    norm_ref[...] += jnp.sum(weights * w_exp.astype(F32), axis=1, keepdims=True)
    first_ref[...] += dot(grad_expanded, w_exp, ((1,), (1,)))

    @pl.when(step == steps - 1)
    def _():
        norm = norm_ref[...].T[0:1] / gain_ref[...].astype(F32)
        start = 9 * steps * (BLOCK // LANES)
        for k in range(channels // LANES):
            piece = slice(k * LANES, (k + 1) * LANES)
            tail_ref[start + k : start + k + 1, :] = norm[:, piece]
            at = start + channels // LANES + k
            tail_ref[at : at + 1, :] = norm1_ref[:, piece]
        weights_ref[:, steps * BLOCK :] = tail_ref[...].astype(BF16)


def run_expand_back(
    cells_total, parts, hidden, gate, w_squeeze, w_excite, low, up, down, side,
    w_project_t, slope, side_slope, spread_slope, spread, w_depth, turned, w_expand, gain, norm1,
):
    rows, cols, channels = low.shape
    expanded = w_expand.shape[1]
    steps = expanded // BLOCK
    return pl.pallas_call(
        functools.partial(expand_back_kernel, cells_total),
        grid=(steps,),
        in_specs=[
            pl.BlockSpec(
                (parts.shape[0], 2 * steps, BLOCK), lambda e: (0, parts.shape[1] // (2 * steps) - 1, 0)
            ),
            whole(hidden.shape), whole(gate.shape),
            whole(w_squeeze.shape), whole(w_excite.shape),
            whole(low.shape), whole(up.shape), whole(down.shape), whole(side.shape),
            last_block(w_project_t.shape), last_block(gate.shape), last_block(slope.shape),
            last_block(side_slope.shape), last_block(spread_slope.shape), last_block(spread.shape),
            last_block(w_depth.shape), whole(turned.shape), last_block(w_expand.shape),
            whole(gain.shape), whole(norm1.shape),
        ],
        out_specs=[
            whole((channels, expanded + LANES)), whole((rows * cols, channels)),
            whole((1, expanded)), whole(hidden.shape),
        ],
        out_shape=[
            jax.ShapeDtypeStruct((channels, expanded + LANES), BF16),
            jax.ShapeDtypeStruct((rows * cols, channels), F32),
            jax.ShapeDtypeStruct((1, expanded), F32),
            jax.ShapeDtypeStruct(hidden.shape, F32),
        ],
        scratch_shapes=[
            pltpu.VMEM(((rows + 2) * cols, BLOCK), F32),
            pltpu.VMEM(((rows + 2) * 8, BLOCK), F32),
            pltpu.VMEM((3, rows + 2, cols, BLOCK), F32),
            pltpu.VMEM((rows * cols, BLOCK), BF16),
            pltpu.VMEM((steps, 1, BLOCK), F32),
            pltpu.VMEM((channels, LANES), F32),
            pltpu.VMEM((channels, LANES), F32),
        ],
        compiler_params=PARAMS,
        cost_estimate=estimate(14),
        name="expand_back",
    )(
        parts, hidden, gate, w_squeeze, w_excite, low, up, down, side, w_project_t, gate,
        slope, side_slope, spread_slope, spread, w_depth, turned, w_expand, gain, norm1,
    )


def image_back_kernel(image_ref, gain_ref, first_ref, mixed_ref, out_ref):
    unit, rstd = norm_rows(image_ref[...].astype(F32))
    grad = first_ref[...]
    back = mixed_ref[...] + norm_rows_back(unit, rstd, gain_ref[...].astype(F32), grad)
    out_ref[...] = back.astype(BF16)


def run_image_back(image, gain, first, mixed):
    cells, channels = image.shape
    block = pl.BlockSpec((cells // 4, channels), lambda r: (r, 0))
    return pl.pallas_call(
        image_back_kernel,
        grid=(4,),
        in_specs=[block, whole(gain.shape), block, block],
        out_specs=block,
        out_shape=jax.ShapeDtypeStruct((cells, channels), BF16),
        compiler_params=PARAMS,
        cost_estimate=estimate(4),
        name="image_back",
    )(image, gain, first, mixed)


def shift(cells, axis, step):
    count = lax.axis_size(axis)
    pairs = [(i, i + step) for i in range(count) if 0 <= i + step < count]
    return lax.ppermute(cells, axis, pairs)


def halo_rows(top, bottom):
    return shift(bottom, "row", 1), shift(top, "row", -1)


def halo_sides(first, last, up, down):
    width = up.shape[0]
    first = jnp.concatenate([up[:, :width], first, down[:, :width]], axis=0)
    last = jnp.concatenate([up[:, -width:], last, down[:, -width:]], axis=0)
    left = shift(last, "col", 1)
    right = shift(first, "col", -1)
    gap = jnp.zeros((first.shape[0], 8 - 2 * width, first.shape[2]), first.dtype)
    return jnp.concatenate([right, gap, left], axis=1).reshape(-1, first.shape[2])


def hand_around(blocks):
    return lax.all_to_all(blocks, AXES, split_axis=0, concat_axis=0, tiled=True)


def sum_steps():
    return [("col", 1, 2), ("row", 1, lax.axis_size("row")), ("col", 2, lax.axis_size("col") // 2)]


def send_on(v, axis, stride, size, k):
    pairs = []
    for i in range(lax.axis_size(axis)):
        place = i // stride % size
        pairs.append((i, i + ((place + k) % size - place) * stride))
    return lax.ppermute(v, axis, pairs)


def sum_parts(matrix, axis, stride, size):
    place = lax.axis_index(axis) // stride % size
    parts = matrix.reshape(size, matrix.shape[0] // size, matrix.shape[1])
    part = lambda i: lax.dynamic_index_in_dim(parts, i % size, 0, False)
    total = part(place).astype(F32)
    for k in range(1, size):
        total = total + send_on(part(place + k), axis, stride, size, k).astype(F32)
    return total.astype(BF16)


def sum_shares(matrix):
    rows, columns = matrix.shape
    count = lax.axis_size("row") * lax.axis_size("col")
    pair = ("col", 1, 2)
    half = sum_parts(matrix, *pair)
    same_core = [list(range(k, count, 2)) for k in range(2)]

    def around(blocks):
        return lax.all_to_all(
            blocks, AXES, split_axis=0, concat_axis=0, tiled=True, axis_index_groups=same_core
        )

    arrived = around(half.reshape(count // 2, rows // count, columns))
    total = jnp.sum(arrived.astype(F32), axis=0).astype(BF16)
    sent = jnp.broadcast_to(total[None], (count // 2,) + total.shape)
    gathered = around(sent).reshape(rows // 2, columns)
    return gathered, send_on(gathered, *pair, 1)


def stack_kernel(*refs):
    for k, ref in enumerate(refs[:-1]):
        refs[-1][k] = ref[...]


def join_parts(blocks, axis, stride, size):
    arrived = [blocks] + [send_on(blocks, axis, stride, size, k) for k in range(1, size)]
    vmem = pl.BlockSpec(memory_space=pltpu.VMEM)
    stacked = pl.pallas_call(
        stack_kernel,
        in_specs=[vmem] * size,
        out_specs=vmem,
        out_shape=jax.ShapeDtypeStruct((size,) + blocks.shape, blocks.dtype),
        compiler_params=PARAMS,
        cost_estimate=estimate(1),
        name="stack",
    )(*arrived)
    return stacked.reshape((size * blocks.shape[0],) + blocks.shape[1:])


def unpack_weights_kernel(
    sizes, places_ref, near_ref, far_ref, qkv_ref, out_ref, bias_ref, project_ref
):
    channels = out_ref.shape[2]
    halves, members = bias_ref.shape[0], bias_ref.shape[3]
    cuts = (0, 3 * channels, 4 * channels, 4 * channels + halves * members)
    pairs, over_row, rest = sizes
    for pair, source in enumerate((near_ref, far_ref)):
        for r in range(over_row):
            for c in range(rest):
                block = source[r * rest + c].astype(F32)
                at = lax.rem(places_ref[0] + pairs - pair, pairs)
                at = at * over_row + lax.rem(places_ref[1] + over_row - r, over_row)
                at = at * rest + lax.rem(places_ref[2] + rest - c, rest)
                qkv_ref[at] = block[:, : cuts[1]]
                out_ref[at] = block[:, cuts[1] : cuts[2]]
                for half in range(halves):
                    start = cuts[2] + half * members
                    bias_ref[half, at] = block[:, start : start + members]
                for e in range(project_ref.shape[0]):
                    start = cuts[3] + e * channels
                    project_ref[e, at] = block[:, start : start + channels]


def run_unpack_weights(steps, near, far, channels, expanded, halves, members):
    count, rows, _ = near.shape
    count *= 2
    places = jnp.stack([lax.axis_index(axis) // stride % size for axis, stride, size in steps])
    vmem = pl.BlockSpec(memory_space=pltpu.VMEM)
    blocks = lambda width: jax.ShapeDtypeStruct((count, rows, width), F32)
    return pl.pallas_call(
        functools.partial(unpack_weights_kernel, tuple(size for _, _, size in steps)),
        in_specs=[pl.BlockSpec(memory_space=pltpu.SMEM), vmem, vmem],
        out_specs=[vmem] * 4,
        out_shape=[
            blocks(3 * channels), blocks(channels),
            jax.ShapeDtypeStruct((halves, count, rows, members), F32),
            jax.ShapeDtypeStruct((expanded // BLOCK, count, rows, channels), F32),
        ],
        compiler_params=PARAMS,
        cost_estimate=estimate(2),
        name="unpack_weights",
    )(places.astype(jnp.int32), near, far)


def swap_groups(blocks, parity):
    groups = None
    if parity > 1:
        over_row = lax.axis_size("row")
        over_col = lax.axis_size("col")
        groups = [
            [r * over_col + c for r in range(over_row) for c in range(k, over_col, parity)]
            for k in range(parity)
        ]
    return lax.all_to_all(
        blocks, AXES, split_axis=0, concat_axis=0, tiled=True, axis_index_groups=groups
    )


def on_device(
    image, out_cotangent, norm0_gain, w_expand, w_depth, w_squeeze, w_excite, w_project,
    norm1_gain, w_qkv, w_out, attn_bias,
):
    rows, cols, channels = image.shape
    over_row = lax.axis_size("row")
    over_col = lax.axis_size("col")
    count = over_row * over_col
    cells_total = rows * cols * count
    stride = rows * over_row // GRID
    parity = over_col // GRID
    lines = rows // stride
    bands = cols // SIDE
    members = GRID * GRID
    expanded = w_expand.shape[1]

    def into_members(arrived):
        parted = arrived.reshape(over_row, GRID, lines, SIDE, channels)
        return parted.transpose(3, 0, 2, 1, 4).reshape(SIDE * members, channels)

    def out_of_members(values):
        parted = values.reshape(SIDE, over_row, lines, GRID, channels)
        return parted.transpose(1, 3, 2, 0, 4).reshape(-1, lines, SIDE, channels)

    row, col = lax.axis_index("row"), lax.axis_index("col")
    flags = jnp.stack([row > 0, row < over_row - 1, col > 0, col < over_col - 1]).astype(F32)
    gain_first = norm0_gain.reshape(1, channels)
    gain_second = norm1_gain.reshape(1, channels)
    w_project_t = w_project.T
    heads = attn_bias.shape[0]
    halves = channels // LANES
    bias_tall = attn_bias.transpose(0, 2, 1).reshape(halves, heads // halves * members, members)
    bias_tall = jnp.concatenate([bias_tall, bias_tall], axis=2)

    up, down = halo_rows(image[:2], image[-2:])
    normed_first, turned_first, spread, spread_slope = run_expand(image, gain_first, w_expand)
    up, down, spread = lax.optimization_barrier((up, down, spread))
    side = halo_sides(image[:, :2], image[:, -2:], up, down)
    cot_sent = (
        out_cotangent.reshape(lines, stride, bands, SIDE, channels)
        .transpose(1, 2, 0, 3, 4)
        .reshape(stride * bands, lines, SIDE, channels)
    )
    cot_members = into_members(swap_groups(cot_sent, parity))
    ring, act, pool = run_depthwise(count, up, down, side, gain_first, w_expand, w_depth, spread)
    pooled, hidden, gate, mixed, normed_sent = run_mix(
        cells_total, stride, hand_around(pool), w_squeeze, w_excite, act, image, w_project,
        gain_second, cot_members,
    )
    slope, side_slope = run_slope(flags, ring, w_depth, spread)
    normed_arrived = swap_groups(normed_sent, parity)
    att_grad = dot(cot_members, w_out, ((1,), (1,))).astype(BF16)
    normed_arrived, slope, att_grad = lax.optimization_barrier((normed_arrived, slope, att_grad))
    normed_members, attended, grad_normed, packed_grad, grad_bias = run_attention(
        normed_arrived, att_grad, w_qkv, bias_tall, heads, lines
    )
    grad_normed_home = swap_groups(grad_normed.reshape(normed_sent.shape), parity)
    weights = run_attention_weights(normed_members, packed_grad, attended, cot_members, grad_bias)
    grad_normed_home, weights = lax.optimization_barrier((grad_normed_home, weights))
    grad_mixed, grad_low, grad_norm1, grad_project, gate_grad, edge_lines, edge_sides = run_mixed_back(
        count, stride, grad_normed_home, mixed, out_cotangent, gain_second, act, gate, w_project_t
    )
    attended_sent = out_of_members(attended)
    if parity == 1:
        both = hand_around(
            jnp.concatenate([attended_sent.reshape(count, -1, channels), gate_grad], axis=1)
        )
        parts = both
        attended_home = both[:, : lines * SIDE].reshape(attended_sent.shape)
    else:
        parts = hand_around(gate_grad)
        attended_home = swap_groups(attended_sent, parity)
    up, down = halo_rows(edge_lines[:1], edge_lines[1:])
    side = halo_sides(edge_sides[0], edge_sides[1], up, down)
    weights = jnp.concatenate([weights, grad_project], axis=1)
    weights, _ = lax.optimization_barrier((weights, up))
    steps = sum_steps()
    for step in steps[:2]:
        weights = sum_parts(weights, *step)
    late, grad_first, logit, pre = run_expand_back(
        cells_total, parts, hidden, gate, w_squeeze, w_excite, grad_low, up, down, side,
        w_project_t, slope, side_slope, spread_slope, spread, w_depth, turned_first, w_expand,
        gain_first, grad_norm1,
    )
    weights, _ = lax.optimization_barrier((weights, late))
    weights = sum_parts(weights, *steps[2])
    weights = weights[None]
    for step in steps[:0:-1]:
        weights = join_parts(weights, *step)
    other = send_on(weights, *steps[0], 1)
    grad_qkv, grad_out_proj, grad_bias, grad_project = run_unpack_weights(
        steps, weights, other, channels, expanded, halves, members
    )
    grad_expand, grad_depth, grad_norm0, grad_norm1 = run_unpack(*sum_shares(late), expanded)
    grad_image = run_image_back(
        image.reshape(-1, channels), gain_first, grad_first, grad_mixed.reshape(-1, channels)
    )
    attended_map = (
        attended_home.reshape(stride, bands, lines, SIDE, channels)
        .transpose(2, 0, 1, 3, 4)
        .reshape(rows * cols, channels)
    )
    block_out = (mixed.reshape(-1, channels).astype(F32) + dot(attended_map, w_out)).astype(BF16)

    silu = jax.nn.silu(hidden)
    grad_squeeze = pooled.reshape(expanded, 1) * pre
    grad_excite = silu.reshape(-1, 1) * logit

    return (
        block_out.reshape(image.shape),
        grad_image.reshape(image.shape),
        grad_norm0[0],
        grad_expand.reshape(w_expand.shape),
        grad_depth,
        grad_squeeze,
        grad_excite,
        grad_project.reshape(w_project.shape),
        grad_norm1[0],
        grad_qkv.reshape(w_qkv.shape),
        grad_out_proj.reshape(w_out.shape),
        grad_bias.reshape(attn_bias.shape),
    )


def solution(mesh):
    cells = P("row", "col", None)
    return jax.shard_map(
        on_device,
        mesh=mesh,
        in_specs=(cells, cells) + (P(),) * 10,
        out_specs=(cells, cells) + (P(),) * 10,
        check_vma=False,
    )
```

```python
import functools
import math

import jax
import jax.numpy as jnp
from jax import lax
from jax.experimental import pallas as pl
from jax.experimental.pallas import tpu as pltpu
from jax.sharding import PartitionSpec as P

GRID = 8
AXES = ("row", "col")
BLOCK = 256
LANES = 128
SIDE = 16
GELU_A = math.sqrt(2.0 / math.pi)
GELU_B = GELU_A * 0.044715
F32 = jnp.float32
BF16 = jnp.bfloat16
PARAMS = pltpu.CompilerParams(vmem_limit_bytes=56 * 1024 * 1024)


def estimate(us):
    return pl.CostEstimate(flops=int(us * 1.1e9), bytes_accessed=int(us * 3.6e6), transcendentals=0)


def dot(left, right, contract=((1,), (0,))):
    return lax.dot_general(left, right, (contract, ((), ())), preferred_element_type=F32)


def dot_exact(vector, right, contract):
    tall = jnp.broadcast_to(vector, (8, vector.shape[1]))
    product = lax.dot_general(
        tall, right, (contract, ((), ())), precision=lax.Precision.HIGHEST, preferred_element_type=F32
    )
    return product[0:1]


def gelu_and_slope(x, with_slope=True):
    square = x * x
    t = jnp.tanh(x * (GELU_A + GELU_B * square))
    half = 0.5 + 0.5 * t
    value = x * half
    if not with_slope:
        return value, None
    slope = half + (value * (1.0 - t)) * (GELU_A + (3.0 * GELU_B) * square)
    return value, slope


def norm_rows(x):
    average = jnp.mean(x, axis=-1, keepdims=True)
    centered = x - average
    variance = jnp.mean(centered * centered, axis=-1, keepdims=True)
    rstd = lax.rsqrt(variance + 1e-05)
    return centered * rstd, rstd


def norm_rows_back(unit, rstd, gain, grad):
    unit_grad = grad * gain
    first = jnp.mean(unit_grad, axis=-1, keepdims=True)
    second = jnp.mean(unit_grad * unit, axis=-1, keepdims=True)
    return rstd * (unit_grad - first - unit * second)


def fold_rows(x):
    return jnp.sum(x.reshape(x.shape[0] // 8, 8, x.shape[1]), axis=0)


def whole(shape):
    return pl.BlockSpec(shape, lambda e: (0,) * len(shape))


def last_block(shape):
    lead = (0,) * (len(shape) - 1)
    return pl.BlockSpec(shape[:-1] + (BLOCK,), lambda e: lead + (e,))


def expand_kernel(
    image_ref, gain_ref, w_exp_ref,
    normed_ref, turned_ref, spread_ref, slope_ref,
    expanded_ref,
):
    rows, cols, channels = image_ref.shape

    @pl.when(pl.program_id(0) == 0)
    def _():
        gain = gain_ref[...].astype(F32)

        @pl.loop(0, rows // 4)
        def _(c):
            flat = image_ref[pl.ds(c * 4, 4)].reshape(4 * cols, channels)
            unit, _ = norm_rows(flat.astype(F32))
            at = pl.ds(pl.multiple_of(c * 4 * cols, 16), 4 * cols)
            normed_ref[at, :] = (unit * gain).astype(BF16)

        turned_ref[...] = normed_ref[...].T

    expanded_ref[...] = dot(normed_ref[...], w_exp_ref[...])

    @pl.loop(0, rows, unroll=4)
    def _(r):
        for h in range(BLOCK // LANES):
            lanes = slice(h * LANES, (h + 1) * LANES)
            x = expanded_ref[pl.ds(pl.multiple_of(r * cols, 16), cols), lanes]
            value, slope = gelu_and_slope(x)
            spread_ref[r, :, lanes] = value.astype(BF16)
            slope_ref[r, :, lanes] = slope.astype(BF16)


def run_expand(image, gain, w_expand):
    rows, cols, channels = image.shape
    expanded = w_expand.shape[1]
    return pl.pallas_call(
        expand_kernel,
        grid=(expanded // BLOCK,),
        in_specs=[whole(image.shape), whole(gain.shape), last_block(w_expand.shape)],
        out_specs=[
            whole((rows * cols, channels)), whole((channels, rows * cols)),
            last_block((rows, cols, expanded)), last_block((rows, cols, expanded)),
        ],
        out_shape=[
            jax.ShapeDtypeStruct((rows * cols, channels), BF16),
            jax.ShapeDtypeStruct((channels, rows * cols), BF16),
            jax.ShapeDtypeStruct((rows, cols, expanded), BF16),
            jax.ShapeDtypeStruct((rows, cols, expanded), BF16),
        ],
        scratch_shapes=[pltpu.VMEM((rows * cols, BLOCK), F32)],
        compiler_params=PARAMS,
        cost_estimate=estimate(14),
        name="expand",
    )(image, gain, w_expand)


def depthwise_kernel(
    up_ref, down_ref, side_ref, gain_ref, w_exp_ref, w_dep_ref, spread_ref,
    ring_ref, act_ref, pool_ref,
    ring_normed_ref, ring_wide_ref,
):
    rows, cols, _ = spread_ref.shape
    channels = up_ref.shape[2]
    over = 4 * cols
    side = 8

    @pl.when(pl.program_id(0) == 0)
    def _():
        gain = gain_ref[...].astype(F32)

        def put(at, values):
            unit, _ = norm_rows(values.astype(F32))
            ring_normed_ref[at : at + values.shape[0], :] = (unit * gain).astype(BF16)

        put(0, up_ref[...].reshape(2 * cols, channels))
        put(2 * cols, down_ref[...].reshape(2 * cols, channels))
        put(over, side_ref[...])

    ring_wide_ref[...] = dot(ring_normed_ref[...], w_exp_ref[...])
    tile = 32

    @pl.loop(0, ring_wide_ref.shape[0] // tile, unroll=True)
    def _(t):
        at = pl.ds(pl.multiple_of(t * tile, tile), tile)
        value, _ = gelu_and_slope(ring_wide_ref[at, :], False)
        low = value.astype(BF16)
        ring_ref[at, :] = low
        ring_wide_ref[at, :] = low.astype(F32)

    for h in range(BLOCK // LANES):
        lanes = slice(h * LANES, (h + 1) * LANES)
        taps = w_dep_ref[:, :, lanes].astype(F32)
        w = [[taps[a, b : b + 1] for b in range(3)] for a in range(3)]

        def line(r, main):
            at = pl.multiple_of(over + (r + 2) * side, side)
            return jnp.concatenate([main, ring_wide_ref[pl.ds(at, side), lanes]], axis=0)

        def conv(i, x, total):
            u = [x[0] * w[0][b] + x[1] * w[1][b] + x[2] * w[2][b] for b in range(3)]
            wide = cols + side
            pre = pltpu.roll(u[0], 1, 0) + u[1] + pltpu.roll(u[2], wide - 1, 0)
            value, _ = gelu_and_slope(pre[:cols], False)
            act_ref[i, :, lanes] = value.astype(BF16)
            return total + fold_rows(value)

        def step(i, carry):
            first, second, total = carry
            third = line(i + 1, spread_ref[i + 1, :, lanes].astype(F32))
            return second, third, conv(i, (first, second, third), total)

        carry = (
            line(-1, ring_wide_ref[cols : 2 * cols, lanes]),
            line(0, spread_ref[0, :, lanes].astype(F32)),
            jnp.zeros((8, LANES), F32),
        )
        first, second, total = lax.fori_loop(0, rows - 1, step, carry, unroll=5)
        third = line(rows, ring_wide_ref[2 * cols : 3 * cols, lanes])
        total = conv(rows - 1, (first, second, third), total)
        total = jnp.sum(total, axis=0, keepdims=True)
        pool_ref[:, :, lanes] = jnp.broadcast_to(total[None], (pool_ref.shape[0], 1, LANES))


def run_depthwise(count, up, down, side, gain, w_expand, w_depth, spread):
    rows, cols, expanded = spread.shape
    channels = up.shape[2]
    ring = 4 * cols + 8 * (rows + 4)
    return pl.pallas_call(
        depthwise_kernel,
        grid=(expanded // BLOCK,),
        in_specs=[
            whole(up.shape), whole(down.shape), whole(side.shape), whole(gain.shape),
            last_block(w_expand.shape), last_block(w_depth.shape), last_block(spread.shape),
        ],
        out_specs=[
            last_block((ring, expanded)), last_block(spread.shape), last_block((count, 1, expanded)),
        ],
        out_shape=[
            jax.ShapeDtypeStruct((ring, expanded), BF16),
            jax.ShapeDtypeStruct(spread.shape, BF16),
            jax.ShapeDtypeStruct((count, 1, expanded), F32),
        ],
        scratch_shapes=[pltpu.VMEM((ring, channels), BF16), pltpu.VMEM((ring, BLOCK), F32)],
        compiler_params=PARAMS,
        cost_estimate=estimate(1),
        name="depthwise",
    )(up, down, side, gain, w_expand, w_depth, spread)


def slope_kernel(flags_ref, ring_ref, w_dep_ref, spread_ref, main_ref, side_out_ref, wide_ref):
    rows, cols, _ = spread_ref.shape
    over = 4 * cols
    side = 8
    wide = cols + side

    for k, r in enumerate((0, 1, rows + 2, rows + 3)):
        wide_ref[r, :cols, :] = ring_ref[k * cols : (k + 1) * cols, :].astype(F32)
    sides = ring_ref[over:, :].astype(F32)
    for r in range(rows + 4):
        wide_ref[r, cols:, :] = sides[r * side : (r + 1) * side]

    @pl.loop(0, rows)
    def _(r):
        wide_ref[r + 2, :cols, :] = spread_ref[r].astype(F32)

    place = lax.broadcasted_iota(jnp.int32, (side, LANES), 0)
    side_mask = jnp.where(
        place == side - 1, flags_ref[2], jnp.where(place == 0, flags_ref[3], 1.0)
    ).astype(F32)

    @pl.loop(0, rows + 2)
    def _(i):
        keep = jnp.where(i == 0, flags_ref[0], jnp.where(i == rows + 1, flags_ref[1], 1.0))
        for h in range(BLOCK // LANES):
            lanes = slice(h * LANES, (h + 1) * LANES)
            taps = w_dep_ref[:, :, lanes].astype(F32)
            x = [wide_ref[i + a, :, lanes] for a in range(3)]
            u = [sum(x[a] * taps[a, b : b + 1] for a in range(3)) for b in range(3)]
            pre = pltpu.roll(u[0], 1, 0) + u[1] + pltpu.roll(u[2], wide - 1, 0)
            _, slope = gelu_and_slope(pre)
            slope = slope * keep
            main_ref[i, :, lanes] = slope[:cols].astype(BF16)
            side_out_ref[i, :, lanes] = slope[cols:] * side_mask


def run_slope(flags, ring, w_depth, spread):
    rows, cols, expanded = spread.shape
    return pl.pallas_call(
        slope_kernel,
        grid=(expanded // BLOCK,),
        in_specs=[
            pl.BlockSpec(memory_space=pltpu.SMEM),
            last_block(ring.shape), last_block(w_depth.shape), last_block(spread.shape),
        ],
        out_specs=[last_block((rows + 2, cols, expanded)), last_block((rows + 2, 8, expanded))],
        out_shape=[
            jax.ShapeDtypeStruct((rows + 2, cols, expanded), BF16),
            jax.ShapeDtypeStruct((rows + 2, 8, expanded), F32),
        ],
        scratch_shapes=[pltpu.VMEM((rows + 4, cols + 8, BLOCK), F32)],
        compiler_params=PARAMS,
        cost_estimate=estimate(13),
        name="slope",
    )(flags, ring, w_depth, spread)


def mix_kernel(
    cells_total, stride, bands,
    parts_ref, w_sq_ref, w_ex_ref, act_ref, image_ref, w_proj_ref, gain_ref, after_ref,
    pooled_ref, hidden_ref, gate_ref, mixed_ref, send_ref,
):
    step = pl.program_id(0)

    @pl.when(step == 0)
    def _():
        pooled = jnp.sum(parts_ref[...], axis=0) / cells_total
        hidden = dot_exact(pooled, w_sq_ref[...].astype(F32), ((1,), (0,)))
        silu = hidden * jax.nn.sigmoid(hidden)
        pooled_ref[...] = pooled
        hidden_ref[...] = hidden
        gate_ref[...] = jax.nn.sigmoid(dot_exact(silu, w_ex_ref[...].astype(F32), ((1,), (0,))))

    lines, cols, channels = image_ref.shape
    flat = act_ref[...].reshape(lines * cols, act_ref.shape[2])
    gated = (flat.astype(F32) * gate_ref[...]).astype(BF16)
    product = dot(gated, w_proj_ref[...])
    mixed = (image_ref[...].reshape(lines * cols, channels).astype(F32) + product).astype(BF16)
    mixed_ref[...] = mixed.reshape(lines, cols, channels)
    unit, _ = norm_rows(mixed.astype(F32))
    normed = (unit * gain_ref[...].astype(F32)).astype(BF16)
    for k in range(lines):
        line = step * lines + k
        for band in range(bands):
            start = k * cols + band * SIDE
            send_ref[lax.rem(line, stride) * bands + band, line // stride] = normed[
                start : start + SIDE
            ]


def run_mix(cells_total, stride, parts, w_squeeze, w_excite, act, image, w_project, gain, after):
    rows, cols, channels = image.shape
    expanded = act.shape[2]
    lines = 4
    bands = cols // SIDE
    block = lambda width: pl.BlockSpec((lines, cols, width), lambda r: (r, 0, 0))
    send = (stride * bands, rows // stride, SIDE, channels)
    return pl.pallas_call(
        functools.partial(mix_kernel, cells_total, stride, bands),
        grid=(rows // lines,),
        in_specs=[
            whole(parts.shape), whole(w_squeeze.shape), whole(w_excite.shape),
            block(expanded), block(channels), whole(w_project.shape), whole(gain.shape),
            pl.BlockSpec(memory_space=pl.ANY),
        ],
        out_specs=[
            whole((1, expanded)), whole((1, w_squeeze.shape[1])), whole((1, expanded)),
            block(channels), whole(send),
        ],
        out_shape=[
            jax.ShapeDtypeStruct((1, expanded), F32),
            jax.ShapeDtypeStruct((1, w_squeeze.shape[1]), F32),
            jax.ShapeDtypeStruct((1, expanded), F32),
            jax.ShapeDtypeStruct(image.shape, BF16),
            jax.ShapeDtypeStruct(send, BF16),
        ],
        compiler_params=PARAMS,
        cost_estimate=estimate(5),
        name="mix",
    )(parts, w_squeeze, w_excite, act, image, w_project, gain, after)


def attention_kernel(
    members, heads, lines,
    arrived_ref, att_grad_ref, w_qkv_ref, bias_ref,
    x_ref, att_ref, grad_ref, packed_grad_ref, bias_out_ref,
    order_ref, packed_ref, bias_sum_ref,
):
    cells, channels = x_ref.shape
    groups = cells // members

    def places():
        for g in range(groups):
            for m in range(0, members, GRID):
                line, row = (m // GRID) % lines, m // GRID // lines
                start = (row * GRID * lines + line) * groups + g
                yield g * members + m, pl.ds(start, GRID, stride=lines * groups)

    for half in range(channels // LANES):
        lanes = slice(half * LANES, (half + 1) * LANES)
        order_ref[half] = arrived_ref[:, lanes].astype(F32)
        for g in range(groups):
            pieces = [order_ref[half, at, :] for k, at in places() if k // members == g]
            at = slice(g * members, (g + 1) * members)
            x_ref[at, lanes] = jnp.concatenate(pieces, axis=0).astype(BF16)
    dim = channels // heads
    per_half = LANES // dim
    halves = channels // LANES
    scale = dim ** (-0.5)
    packed_ref[...] = dot(x_ref[...], w_qkv_ref[...]).astype(BF16)
    bias_sum_ref[...] = jnp.zeros(bias_sum_ref.shape, F32)
    tall = per_half * members
    mask = (
        lax.broadcasted_iota(jnp.int32, (tall, LANES), 0) // members
        == lax.broadcasted_iota(jnp.int32, (tall, LANES), 1) // dim
    ).astype(F32).astype(BF16)
    owner = lax.broadcasted_iota(jnp.int32, (members, 2 * LANES), 1) % LANES // dim
    zero = jnp.zeros((members, LANES), BF16)

    def by_head(pair):
        return jnp.concatenate(
            [jnp.concatenate([v] * per_half, axis=0) * mask for v in pair], axis=1
        )

    def diagonal(pair):
        return jnp.concatenate(
            [
                jnp.concatenate([pair[0], zero], axis=1),
                jnp.concatenate([zero, pair[1]], axis=1),
            ],
            axis=0,
        )

    def collect(v):
        parts = [v[h * members : (h + 1) * members] for h in range(per_half)]
        picked = parts[-1]
        for h in range(per_half - 1):
            picked = jnp.where(owner == h, parts[h], picked)
        return [picked[:, :LANES], picked[:, LANES:]]

    def blocks(v):
        return [v[:members, :LANES], v[members:, LANES:]]

    def over_members(v, reduce):
        parted = v.reshape(per_half, members, 2 * members)
        small = reduce(parted, axis=1, keepdims=True)
        return jnp.broadcast_to(small, parted.shape).reshape(v.shape)

    def pair_step(g, carry):
        at = [pl.ds(pl.multiple_of((2 * g + k) * members, 16), members) for k in range(2)]
        for half in range(halves):
            def lanes(part):
                start = part * channels + half * LANES
                return slice(start, start + LANES)

            q, k, v = ([packed_ref[at[n], lanes(part)] for n in range(2)] for part in range(3))
            cot = [att_grad_ref[at[n], lanes(0)] for n in range(2)]
            q_diag, cot_diag = diagonal(q), diagonal(cot)
            k_tall, v_tall = by_head(k), by_head(v)
            scores = dot(k_tall, q_diag, ((1,), (1,))) * scale + bias_ref[half]
            grad_probs = dot(v_tall, cot_diag, ((1,), (1,)))
            lifted = jnp.exp(scores - over_members(scores, jnp.max))
            soft = lifted * (1.0 / over_members(lifted, jnp.sum))
            soft_low = soft.astype(BF16)
            grad_scores = soft * (grad_probs - over_members(grad_probs * soft, jnp.sum))
            bias_sum_ref[half] += grad_scores
            scaled = (grad_scores * scale).astype(BF16)
            attended = blocks(dot(soft_low, v_tall, ((0,), (0,))))
            grad_q = blocks(dot(scaled, k_tall, ((0,), (0,))))
            grad_v = collect(dot(soft_low, cot_diag))
            grad_k = collect(dot(scaled, q_diag))
            for n in range(2):
                att_ref[at[n], lanes(0)] = attended[n].astype(BF16)
                for part, value in enumerate((grad_q, grad_k, grad_v)):
                    packed_grad_ref[at[n], lanes(part)] = value[n].astype(BF16)
        return carry

    lax.fori_loop(0, cells // members // 2, pair_step, 0, unroll=2)
    grad = dot(packed_grad_ref[...], w_qkv_ref[...], ((1,), (1,)))
    for half in range(halves):
        lanes = slice(half * LANES, (half + 1) * LANES)
        for k, at in places():
            order_ref[half, at, :] = grad[k : k + GRID, lanes]
        grad_ref[:, lanes] = order_ref[half].astype(BF16)
    for half in range(halves):
        both = bias_sum_ref[half]
        bias_out_ref[half] = both[:, :members] + both[:, members:]


def run_attention(arrived, att_grad, w_qkv, bias_tall, heads, lines):
    cells, channels = att_grad.shape
    halves, tall, members2 = bias_tall.shape
    members = members2 // 2
    vmem = pl.BlockSpec(memory_space=pltpu.VMEM)
    return pl.pallas_call(
        functools.partial(attention_kernel, members, heads, lines),
        in_specs=[vmem] * 4,
        out_specs=[vmem] * 5,
        out_shape=[
            jax.ShapeDtypeStruct((cells, channels), BF16),
            jax.ShapeDtypeStruct((cells, channels), BF16),
            jax.ShapeDtypeStruct((cells, channels), BF16),
            jax.ShapeDtypeStruct((cells, 3 * channels), BF16),
            jax.ShapeDtypeStruct((halves, tall, members), F32),
        ],
        scratch_shapes=[
            pltpu.VMEM((channels // LANES, cells, LANES), F32),
            pltpu.VMEM((cells, 3 * channels), BF16),
            pltpu.VMEM(bias_tall.shape, F32),
        ],
        compiler_params=PARAMS,
        cost_estimate=estimate(14),
        name="attention",
    )(arrived.reshape(cells, channels), att_grad, w_qkv, bias_tall)


def attention_weights_kernel(x_ref, packed_grad_ref, att_ref, cot_ref, bias_ref, out_ref):
    channels = x_ref.shape[1]
    wide = 3 * channels
    out_ref[:, :wide] = dot(x_ref[...], packed_grad_ref[...], ((0,), (0,))).astype(BF16)
    out_ref[:, wide : wide + channels] = dot(att_ref[...], cot_ref[...], ((0,), (0,))).astype(BF16)
    halves, tall, members = bias_ref.shape
    for h in range(tall // members):
        rows = slice(h * members, (h + 1) * members)
        turned = jnp.concatenate([bias_ref[half, rows, :].T for half in range(halves)], axis=1)
        out_ref[rows, wide + channels :] = turned.astype(BF16)


def run_attention_weights(x, packed_grad, att, cot, bias):
    channels = x.shape[1]
    vmem = pl.BlockSpec(memory_space=pltpu.VMEM)
    width = 4 * channels + bias.shape[0] * bias.shape[2]
    return pl.pallas_call(
        attention_weights_kernel,
        in_specs=[vmem] * 5,
        out_specs=vmem,
        out_shape=jax.ShapeDtypeStruct((channels, width), BF16),
        compiler_params=PARAMS,
        cost_estimate=estimate(5),
        name="attention_weights",
    )(x, packed_grad, att, cot, bias)


def mixed_back_kernel(
    stride, bands,
    recv_ref, mixed_ref, cot_ref, gain_ref, act_ref, gate_ref, w_projt_ref,
    grad_ref, low_ref, norm_ref, project_ref, gate_grad_ref, lines_ref, sides_ref,
    turned_ref, total_ref,
):
    rows, cols, channels = mixed_ref.shape

    @pl.when(pl.program_id(0) == 0)
    def _():
        gain = gain_ref[...].astype(F32)
        lines = 4

        def some_rows(c, total):
            pieces = []
            for k in range(lines):
                i = c * lines + k
                a, p = lax.rem(i, stride), i // stride
                pieces += [recv_ref[a * bands + band, p] for band in range(bands)]
            grad = jnp.concatenate(pieces, axis=0).astype(F32)
            at = pl.ds(c * lines, lines)
            flat = lambda ref: ref[at].reshape(lines * cols, channels).astype(F32)
            unit, rstd = norm_rows(flat(mixed_ref))
            back = flat(cot_ref) + norm_rows_back(unit, rstd, gain, grad)
            grad_ref[at] = back.reshape(lines, cols, channels)
            low_ref[at] = back.astype(BF16).reshape(lines, cols, channels)
            return total + fold_rows(grad * unit)

        total = lax.fori_loop(
            0, rows // lines, some_rows, jnp.zeros((8, channels), F32), unroll=2
        )
        norm_ref[...] = jnp.sum(total, axis=0, keepdims=True)
        lines_ref[0] = low_ref[0]
        lines_ref[1] = low_ref[rows - 1]
        for i in range(rows):
            sides_ref[0, i] = low_ref[i, 0:1, :]
            sides_ref[1, i] = low_ref[i, cols - 1 : cols, :]
        turned_ref[...] = low_ref[...].reshape(rows * cols, channels).T

    flat = act_ref[...].reshape(rows * cols, BLOCK)
    product = dot(turned_ref[...], flat)
    total = jnp.sum(product * w_projt_ref[...].astype(F32), axis=0, keepdims=True)
    step, steps = pl.program_id(0), pl.num_programs(0)
    total_ref[step] = total
    project_ref[...] = (product * gate_ref[...]).T.astype(BF16)

    @pl.when(step == steps - 1)
    def _():
        sums = [total_ref[e] for e in range(total_ref.shape[0])]
        high = [v.astype(BF16).astype(F32) for v in sums]
        terms = jnp.concatenate(high + [v - w for v, w in zip(sums, high)], axis=0)
        gate_grad_ref[...] = jnp.broadcast_to(terms.astype(BF16)[None], gate_grad_ref.shape)


def run_mixed_back(count, stride, recv, mixed, cot, gain, act, gate, w_project_t):
    rows, cols, channels = mixed.shape
    expanded = act.shape[2]
    return pl.pallas_call(
        functools.partial(mixed_back_kernel, stride, cols // SIDE),
        grid=(expanded // BLOCK,),
        in_specs=[
            whole(recv.shape), whole(mixed.shape), whole(cot.shape), whole(gain.shape),
            last_block(act.shape), last_block(gate.shape), last_block(w_project_t.shape),
        ],
        out_specs=[
            whole(mixed.shape), whole(mixed.shape), whole((1, channels)),
            last_block((BLOCK, expanded)), whole((count, 2 * expanded // BLOCK, BLOCK)),
            whole((2, cols, channels)), whole((2, rows, 1, channels)),
        ],
        out_shape=[
            jax.ShapeDtypeStruct(mixed.shape, F32),
            jax.ShapeDtypeStruct(mixed.shape, BF16),
            jax.ShapeDtypeStruct((1, channels), F32),
            jax.ShapeDtypeStruct((BLOCK, expanded), BF16),
            jax.ShapeDtypeStruct((count, 2 * expanded // BLOCK, BLOCK), BF16),
            jax.ShapeDtypeStruct((2, cols, channels), BF16),
            jax.ShapeDtypeStruct((2, rows, 1, channels), BF16),
        ],
        scratch_shapes=[
            pltpu.VMEM((channels, rows * cols), BF16),
            pltpu.VMEM((expanded // BLOCK, 1, BLOCK), F32),
        ],
        compiler_params=PARAMS,
        cost_estimate=estimate(7),
        name="mixed_back",
    )(recv, mixed, cot, gain, act, gate, w_project_t)


def unpack_kernel(
    place_ref, near_ref, far_ref, expand_ref, depth_ref, norm0_ref, norm1_ref, tail_ref
):
    expanded = expand_ref.shape[2]
    for pair, source in enumerate((near_ref, far_ref)):
        at = lax.rem(place_ref[0] + pair, 2)
        expand_ref[at] = source[:, :expanded].astype(F32)
        tail_ref[at] = source[:, expanded:].astype(F32)
    tail = tail_ref[0]
    pieces = expanded // LANES
    for t in range(9):
        for k in range(pieces):
            row = t * pieces + k
            lanes = slice(k * LANES, (k + 1) * LANES)
            depth_ref[t // 3, t % 3 : t % 3 + 1, lanes] = tail[row : row + 1]
    start = 9 * pieces
    half = norm0_ref.shape[1] // LANES
    for k in range(half):
        lanes = slice(k * LANES, (k + 1) * LANES)
        norm0_ref[:, lanes] = tail[start + k : start + k + 1]
        norm1_ref[:, lanes] = tail[start + half + k : start + half + k + 1]


def run_unpack(near, far, expanded):
    rows = near.shape[0]
    channels = 2 * rows
    place = (lax.axis_index("col") % 2).astype(jnp.int32).reshape(1)
    vmem = pl.BlockSpec(memory_space=pltpu.VMEM)
    return pl.pallas_call(
        unpack_kernel,
        in_specs=[pl.BlockSpec(memory_space=pltpu.SMEM), vmem, vmem],
        out_specs=[vmem] * 4,
        out_shape=[
            jax.ShapeDtypeStruct((2, rows, expanded), F32),
            jax.ShapeDtypeStruct((3, 3, expanded), F32),
            jax.ShapeDtypeStruct((1, channels), F32),
            jax.ShapeDtypeStruct((1, channels), F32),
        ],
        scratch_shapes=[pltpu.VMEM((2, rows, near.shape[1] - expanded), F32)],
        compiler_params=PARAMS,
        cost_estimate=estimate(2),
        name="unpack",
    )(place, near, far)


def expand_back_kernel(
    cells_total,
    parts_ref, hidden_ref, gate_all_ref, w_sq_ref, w_ex_ref,
    low_ref, up_ref, down_ref, side_ref, w_projt_ref, gate_ref, slope_ref, side_slope_ref,
    spread_slope_ref, spread_ref, w_dep_ref, turned_ref, w_exp_ref, gain_ref, norm1_ref,
    weights_ref, first_ref, logit_ref, pre_ref,
    main_ref, side_grad_ref, window_ref, expanded_ref, pool_ref, tail_ref, norm_ref, weights_sum_ref,
):
    rows, cols, channels = low_ref.shape
    side = 8
    wide = cols + side
    step = pl.program_id(0)
    steps = pl.num_programs(0)

    @pl.when(step == 0)
    def _():
        gate = gate_all_ref[...]
        blocks = pool_ref.shape[0]
        terms = jnp.sum(parts_ref[...].astype(F32), axis=0)
        gate_grad = jnp.concatenate(
            [terms[e : e + 1] + terms[blocks + e : blocks + e + 1] for e in range(blocks)], axis=1
        )
        logit = gate_grad * gate * (1.0 - gate)
        hidden = hidden_ref[...]
        sig = jax.nn.sigmoid(hidden)
        pre = dot_exact(logit, w_ex_ref[...].astype(F32), ((1,), (1,))) * (
            sig + hidden * sig * (1.0 - sig)
        )
        logit_ref[...] = logit
        pre_ref[...] = pre
        pooled = dot_exact(pre, w_sq_ref[...].astype(F32), ((1,), (1,))) / cells_total
        for e in range(blocks):
            pool_ref[e] = pooled[:, e * BLOCK : (e + 1) * BLOCK]
        first_ref[...] = jnp.zeros(first_ref.shape, F32)
        tail_ref[...] = jnp.zeros(tail_ref.shape, F32)
        norm_ref[...] = jnp.zeros(norm_ref.shape, F32)

    w_projt = w_projt_ref[...]
    w_exp = w_exp_ref[...]
    two = 2 * cols

    def gate_rows(p):
        at = pl.ds(pl.multiple_of(cols + p * two, 16), two)
        main_ref[at, :] = dot(low_ref[pl.ds(2 * p, 2)].reshape(two, channels), w_projt)

    def window_row(i):
        for h in range(BLOCK // LANES):
            lanes = slice(h * LANES, (h + 1) * LANES)
            gate = gate_ref[:, lanes]
            pooled = pool_ref[step][:, lanes]
            gated = main_ref[pl.ds(pl.multiple_of(i * cols, 16), cols), lanes]
            main = (gated * gate + pooled) * slope_ref[i, :, lanes].astype(F32)
            gated = side_grad_ref[pl.ds(pl.multiple_of(i * side, side), side), lanes]
            edge = (gated * gate + pooled) * side_slope_ref[i, :, lanes]
            grad = jnp.concatenate([main, edge], axis=0)
            window_ref[0, i, :, lanes] = pltpu.roll(grad, wide - 1, 0)[:cols]
            window_ref[1, i, :, lanes] = grad[:cols]
            window_ref[2, i, :, lanes] = pltpu.roll(grad, 1, 0)[:cols]

    side_grad_ref[...] = dot(side_ref[...], w_projt)
    main_ref[pl.ds(0, cols), :] = dot(up_ref[0], w_projt)
    main_ref[pl.ds((rows + 1) * cols, cols), :] = dot(down_ref[0], w_projt)
    gate_rows(0)
    window_row(0)
    window_row(rows + 1)

    @pl.loop(0, rows // 2 - 1)
    def _(p):
        window_row(2 * p + 1)
        window_row(2 * p + 2)
        gate_rows(p + 1)

    window_row(rows - 1)
    window_row(rows)

    weights_sum_ref[...] = jnp.zeros(weights_sum_ref.shape, F32)

    def back_rows(p, sums):
        sums = list(sums)
        for r in range(2):
            i = 2 * p + r
            for h in range(BLOCK // LANES):
                lanes = slice(h * LANES, (h + 1) * LANES)
                taps = w_dep_ref[:, :, lanes].astype(F32)
                spread = spread_ref[i, :, lanes].astype(F32)
                total = jnp.zeros((cols, LANES), F32)
                for a in range(3):
                    for b in range(3):
                        window = window_ref[b, i + 2 - a, :, lanes]
                        total = total + window * taps[a, b : b + 1]
                        sums[h * 9 + a * 3 + b] += fold_rows(window * spread)
                grad = total * spread_slope_ref[i, :, lanes].astype(F32)
                at = pl.ds(pl.multiple_of(i * cols, 16), cols)
                expanded_ref[at, lanes] = grad.astype(BF16)
        return tuple(sums)

    def use_rows(p):
        at = pl.ds(pl.multiple_of(p * two, LANES), two)
        grad = expanded_ref[at, :]
        first_ref[at, :] += dot(grad, w_exp, ((1,), (1,)))
        weights_sum_ref[...] += dot(turned_ref[:, at], grad)

    def back_step(p, sums):
        use_rows(p - 1)
        return back_rows(p, sums)

    sums = back_rows(0, (jnp.zeros((8, LANES), F32),) * (9 * BLOCK // LANES))
    sums = lax.fori_loop(1, rows // 2, back_step, sums)
    use_rows(rows // 2 - 1)
    for h in range(BLOCK // LANES):
        for t in range(9):
            row = t * (steps * BLOCK // LANES) + step * (BLOCK // LANES) + h
            tail_ref[pl.ds(row, 1), :] = jnp.sum(sums[h * 9 + t], axis=0, keepdims=True)

    weights = weights_sum_ref[...]
    weights_ref[:, pl.ds(pl.multiple_of(step * BLOCK, BLOCK), BLOCK)] = weights.astype(BF16)
    norm_ref[...] += jnp.sum(weights * w_exp.astype(F32), axis=1, keepdims=True)

    @pl.when(step == steps - 1)
    def _():
        norm = norm_ref[...].T[0:1] / gain_ref[...].astype(F32)
        start = 9 * steps * (BLOCK // LANES)
        for k in range(channels // LANES):
            piece = slice(k * LANES, (k + 1) * LANES)
            tail_ref[start + k : start + k + 1, :] = norm[:, piece]
            at = start + channels // LANES + k
            tail_ref[at : at + 1, :] = norm1_ref[:, piece]
        weights_ref[:, steps * BLOCK :] = tail_ref[...].astype(BF16)


def run_expand_back(
    cells_total, parts, hidden, gate, w_squeeze, w_excite, low, up, down, side,
    w_project_t, slope, side_slope, spread_slope, spread, w_depth, turned, w_expand, gain, norm1,
):
    rows, cols, channels = low.shape
    expanded = w_expand.shape[1]
    steps = expanded // BLOCK
    return pl.pallas_call(
        functools.partial(expand_back_kernel, cells_total),
        grid=(steps,),
        in_specs=[
            pl.BlockSpec(
                (parts.shape[0], 2 * steps, BLOCK), lambda e: (0, parts.shape[1] // (2 * steps) - 1, 0)
            ),
            whole(hidden.shape), whole(gate.shape),
            whole(w_squeeze.shape), whole(w_excite.shape),
            whole(low.shape), whole(up.shape), whole(down.shape), whole(side.shape),
            last_block(w_project_t.shape), last_block(gate.shape), last_block(slope.shape),
            last_block(side_slope.shape), last_block(spread_slope.shape), last_block(spread.shape),
            last_block(w_depth.shape), whole(turned.shape), last_block(w_expand.shape),
            whole(gain.shape), whole(norm1.shape),
        ],
        out_specs=[
            whole((channels, expanded + LANES)), whole((rows * cols, channels)),
            whole((1, expanded)), whole(hidden.shape),
        ],
        out_shape=[
            jax.ShapeDtypeStruct((channels, expanded + LANES), BF16),
            jax.ShapeDtypeStruct((rows * cols, channels), F32),
            jax.ShapeDtypeStruct((1, expanded), F32),
            jax.ShapeDtypeStruct(hidden.shape, F32),
        ],
        scratch_shapes=[
            pltpu.VMEM(((rows + 2) * cols, BLOCK), F32),
            pltpu.VMEM(((rows + 2) * 8, BLOCK), F32),
            pltpu.VMEM((3, rows + 2, cols, BLOCK), F32),
            pltpu.VMEM((rows * cols, BLOCK), BF16),
            pltpu.VMEM((steps, 1, BLOCK), F32),
            pltpu.VMEM((channels, LANES), F32),
            pltpu.VMEM((channels, LANES), F32),
            pltpu.VMEM((channels, BLOCK), F32),
        ],
        compiler_params=PARAMS,
        cost_estimate=estimate(14),
        name="expand_back",
    )(
        parts, hidden, gate, w_squeeze, w_excite, low, up, down, side, w_project_t, gate,
        slope, side_slope, spread_slope, spread, w_depth, turned, w_expand, gain, norm1,
    )


def image_back_kernel(image_ref, gain_ref, first_ref, mixed_ref, out_ref):
    unit, rstd = norm_rows(image_ref[...].astype(F32))
    grad = first_ref[...]
    back = mixed_ref[...] + norm_rows_back(unit, rstd, gain_ref[...].astype(F32), grad)
    out_ref[...] = back.astype(BF16)


def run_image_back(image, gain, first, mixed):
    cells, channels = image.shape
    block = pl.BlockSpec((cells // 4, channels), lambda r: (r, 0))
    return pl.pallas_call(
        image_back_kernel,
        grid=(4,),
        in_specs=[block, whole(gain.shape), block, block],
        out_specs=block,
        out_shape=jax.ShapeDtypeStruct((cells, channels), BF16),
        compiler_params=PARAMS,
        cost_estimate=estimate(4),
        name="image_back",
    )(image, gain, first, mixed)


def shift(cells, axis, step):
    count = lax.axis_size(axis)
    pairs = [(i, i + step) for i in range(count) if 0 <= i + step < count]
    return lax.ppermute(cells, axis, pairs)


def halo_rows(top, bottom):
    return shift(bottom, "row", 1), shift(top, "row", -1)


def halo_sides(first, last, up, down):
    width = up.shape[0]
    first = jnp.concatenate([up[:, :width], first, down[:, :width]], axis=0)
    last = jnp.concatenate([up[:, -width:], last, down[:, -width:]], axis=0)
    left = shift(last, "col", 1)
    right = shift(first, "col", -1)
    gap = jnp.zeros((first.shape[0], 8 - 2 * width, first.shape[2]), first.dtype)
    return jnp.concatenate([right, gap, left], axis=1).reshape(-1, first.shape[2])


def hand_around(blocks):
    return lax.all_to_all(blocks, AXES, split_axis=0, concat_axis=0, tiled=True)


def sum_steps():
    return [("col", 1, 2), ("row", 1, lax.axis_size("row")), ("col", 2, lax.axis_size("col") // 2)]


def send_on(v, axis, stride, size, k):
    pairs = []
    for i in range(lax.axis_size(axis)):
        place = i // stride % size
        pairs.append((i, i + ((place + k) % size - place) * stride))
    return lax.ppermute(v, axis, pairs)


def sum_parts(matrix, axis, stride, size):
    place = lax.axis_index(axis) // stride % size
    parts = matrix.reshape(size, matrix.shape[0] // size, matrix.shape[1])
    part = lambda i: lax.dynamic_index_in_dim(parts, i % size, 0, False)
    total = part(place).astype(F32)
    for k in range(1, size):
        total = total + send_on(part(place + k), axis, stride, size, k).astype(F32)
    return total.astype(BF16)


def sum_shares(matrix):
    rows, columns = matrix.shape
    count = lax.axis_size("row") * lax.axis_size("col")
    pair = ("col", 1, 2)
    half = sum_parts(matrix, *pair)
    same_core = [list(range(k, count, 2)) for k in range(2)]

    def around(blocks):
        return lax.all_to_all(
            blocks, AXES, split_axis=0, concat_axis=0, tiled=True, axis_index_groups=same_core
        )

    arrived = around(half.reshape(count // 2, rows // count, columns))
    total = jnp.sum(arrived.astype(F32), axis=0).astype(BF16)
    sent = jnp.broadcast_to(total[None], (count // 2,) + total.shape)
    gathered = around(sent).reshape(rows // 2, columns)
    return gathered, send_on(gathered, *pair, 1)


def stack_kernel(*refs):
    for k, ref in enumerate(refs[:-1]):
        refs[-1][k] = ref[...]


def join_parts(blocks, axis, stride, size):
    arrived = [blocks] + [send_on(blocks, axis, stride, size, k) for k in range(1, size)]
    vmem = pl.BlockSpec(memory_space=pltpu.VMEM)
    stacked = pl.pallas_call(
        stack_kernel,
        in_specs=[vmem] * size,
        out_specs=vmem,
        out_shape=jax.ShapeDtypeStruct((size,) + blocks.shape, blocks.dtype),
        compiler_params=PARAMS,
        cost_estimate=estimate(1),
        name="stack",
    )(*arrived)
    return stacked.reshape((size * blocks.shape[0],) + blocks.shape[1:])


def unpack_weights_kernel(
    sizes, places_ref, near_ref, far_ref, qkv_ref, out_ref, bias_ref, project_ref
):
    channels = out_ref.shape[2]
    halves, members = bias_ref.shape[0], bias_ref.shape[3]
    cuts = (0, 3 * channels, 4 * channels, 4 * channels + halves * members)
    pairs, over_row, rest = sizes
    for pair, source in enumerate((near_ref, far_ref)):
        for r in range(over_row):
            for c in range(rest):
                block = source[r * rest + c].astype(F32)
                at = lax.rem(places_ref[0] + pairs - pair, pairs)
                at = at * over_row + lax.rem(places_ref[1] + over_row - r, over_row)
                at = at * rest + lax.rem(places_ref[2] + rest - c, rest)
                qkv_ref[at] = block[:, : cuts[1]]
                out_ref[at] = block[:, cuts[1] : cuts[2]]
                for half in range(halves):
                    start = cuts[2] + half * members
                    bias_ref[half, at] = block[:, start : start + members]
                for e in range(project_ref.shape[0]):
                    start = cuts[3] + e * channels
                    project_ref[e, at] = block[:, start : start + channels]


def run_unpack_weights(steps, near, far, channels, expanded, halves, members):
    count, rows, _ = near.shape
    count *= 2
    places = jnp.stack([lax.axis_index(axis) // stride % size for axis, stride, size in steps])
    vmem = pl.BlockSpec(memory_space=pltpu.VMEM)
    blocks = lambda width: jax.ShapeDtypeStruct((count, rows, width), F32)
    return pl.pallas_call(
        functools.partial(unpack_weights_kernel, tuple(size for _, _, size in steps)),
        in_specs=[pl.BlockSpec(memory_space=pltpu.SMEM), vmem, vmem],
        out_specs=[vmem] * 4,
        out_shape=[
            blocks(3 * channels), blocks(channels),
            jax.ShapeDtypeStruct((halves, count, rows, members), F32),
            jax.ShapeDtypeStruct((expanded // BLOCK, count, rows, channels), F32),
        ],
        compiler_params=PARAMS,
        cost_estimate=estimate(2),
        name="unpack_weights",
    )(places.astype(jnp.int32), near, far)


def swap_groups(blocks, parity):
    groups = None
    if parity > 1:
        over_row = lax.axis_size("row")
        over_col = lax.axis_size("col")
        groups = [
            [r * over_col + c for r in range(over_row) for c in range(k, over_col, parity)]
            for k in range(parity)
        ]
    return lax.all_to_all(
        blocks, AXES, split_axis=0, concat_axis=0, tiled=True, axis_index_groups=groups
    )


def on_device(
    image, out_cotangent, norm0_gain, w_expand, w_depth, w_squeeze, w_excite, w_project,
    norm1_gain, w_qkv, w_out, attn_bias,
):
    rows, cols, channels = image.shape
    over_row = lax.axis_size("row")
    over_col = lax.axis_size("col")
    count = over_row * over_col
    cells_total = rows * cols * count
    stride = rows * over_row // GRID
    parity = over_col // GRID
    lines = rows // stride
    bands = cols // SIDE
    members = GRID * GRID
    expanded = w_expand.shape[1]

    def into_members(arrived):
        parted = arrived.reshape(over_row, GRID, lines, SIDE, channels)
        return parted.transpose(3, 0, 2, 1, 4).reshape(SIDE * members, channels)

    def out_of_members(values):
        parted = values.reshape(SIDE, over_row, lines, GRID, channels)
        return parted.transpose(1, 3, 2, 0, 4).reshape(-1, lines, SIDE, channels)

    row, col = lax.axis_index("row"), lax.axis_index("col")
    flags = jnp.stack([row > 0, row < over_row - 1, col > 0, col < over_col - 1]).astype(F32)
    gain_first = norm0_gain.reshape(1, channels)
    gain_second = norm1_gain.reshape(1, channels)
    w_project_t = w_project.T
    heads = attn_bias.shape[0]
    halves = channels // LANES
    bias_tall = attn_bias.transpose(0, 2, 1).reshape(halves, heads // halves * members, members)
    bias_tall = jnp.concatenate([bias_tall, bias_tall], axis=2)

    up, down = halo_rows(image[:2], image[-2:])
    normed_first, turned_first, spread, spread_slope = run_expand(image, gain_first, w_expand)
    up, down, spread = lax.optimization_barrier((up, down, spread))
    side = halo_sides(image[:, :2], image[:, -2:], up, down)
    cot_sent = (
        out_cotangent.reshape(lines, stride, bands, SIDE, channels)
        .transpose(1, 2, 0, 3, 4)
        .reshape(stride * bands, lines, SIDE, channels)
    )
    cot_members = into_members(swap_groups(cot_sent, parity))
    ring, act, pool = run_depthwise(count, up, down, side, gain_first, w_expand, w_depth, spread)
    pooled, hidden, gate, mixed, normed_sent = run_mix(
        cells_total, stride, hand_around(pool), w_squeeze, w_excite, act, image, w_project,
        gain_second, cot_members,
    )
    slope, side_slope = run_slope(flags, ring, w_depth, spread)
    normed_arrived = swap_groups(normed_sent, parity)
    att_grad = dot(cot_members, w_out, ((1,), (1,))).astype(BF16)
    normed_arrived, slope, att_grad = lax.optimization_barrier((normed_arrived, slope, att_grad))
    normed_members, attended, grad_normed, packed_grad, grad_bias = run_attention(
        normed_arrived, att_grad, w_qkv, bias_tall, heads, lines
    )
    grad_normed_home = swap_groups(grad_normed.reshape(normed_sent.shape), parity)
    weights = run_attention_weights(normed_members, packed_grad, attended, cot_members, grad_bias)
    grad_normed_home, weights = lax.optimization_barrier((grad_normed_home, weights))
    grad_mixed, grad_low, grad_norm1, grad_project, gate_grad, edge_lines, edge_sides = run_mixed_back(
        count, stride, grad_normed_home, mixed, out_cotangent, gain_second, act, gate, w_project_t
    )
    attended_sent = out_of_members(attended)
    if parity == 1:
        both = hand_around(
            jnp.concatenate([attended_sent.reshape(count, -1, channels), gate_grad], axis=1)
        )
        parts = both
        attended_home = both[:, : lines * SIDE].reshape(attended_sent.shape)
    else:
        parts = hand_around(gate_grad)
        attended_home = swap_groups(attended_sent, parity)
    up, down = halo_rows(edge_lines[:1], edge_lines[1:])
    edge_sides, parts = lax.optimization_barrier((edge_sides, parts))
    side = halo_sides(edge_sides[0], edge_sides[1], up, down)
    weights = jnp.concatenate([weights, grad_project], axis=1)
    weights, _ = lax.optimization_barrier((weights, up))
    steps = sum_steps()
    for step in steps:
        weights = sum_parts(weights, *step)
    late, grad_first, logit, pre = run_expand_back(
        cells_total, parts, hidden, gate, w_squeeze, w_excite, grad_low, up, down, side,
        w_project_t, slope, side_slope, spread_slope, spread, w_depth, turned_first, w_expand,
        gain_first, grad_norm1,
    )
    weights, _ = lax.optimization_barrier((weights, late))
    weights = weights[None]
    for step in steps[:0:-1]:
        weights = join_parts(weights, *step)
    other = send_on(weights, *steps[0], 1)
    grad_qkv, grad_out_proj, grad_bias, grad_project = run_unpack_weights(
        steps, weights, other, channels, expanded, halves, members
    )
    grad_expand, grad_depth, grad_norm0, grad_norm1 = run_unpack(*sum_shares(late), expanded)
    grad_image = run_image_back(
        image.reshape(-1, channels), gain_first, grad_first, grad_mixed.reshape(-1, channels)
    )
    attended_map = (
        attended_home.reshape(stride, bands, lines, SIDE, channels)
        .transpose(2, 0, 1, 3, 4)
        .reshape(rows * cols, channels)
    )
    block_out = (mixed.reshape(-1, channels).astype(F32) + dot(attended_map, w_out)).astype(BF16)

    silu = jax.nn.silu(hidden)
    grad_squeeze = pooled.reshape(expanded, 1) * pre
    grad_excite = silu.reshape(-1, 1) * logit

    return (
        block_out.reshape(image.shape),
        grad_image.reshape(image.shape),
        grad_norm0[0],
        grad_expand.reshape(w_expand.shape),
        grad_depth,
        grad_squeeze,
        grad_excite,
        grad_project.reshape(w_project.shape),
        grad_norm1[0],
        grad_qkv.reshape(w_qkv.shape),
        grad_out_proj.reshape(w_out.shape),
        grad_bias.reshape(attn_bias.shape),
    )


def solution(mesh):
    cells = P("row", "col", None)
    return jax.shard_map(
        on_device,
        mesh=mesh,
        in_specs=(cells, cells) + (P(),) * 10,
        out_specs=(cells, cells) + (P(),) * 10,
        check_vma=False,
    )
```

```python
import functools
import math

import jax
import jax.numpy as jnp
from jax import lax
from jax.experimental import pallas as pl
from jax.experimental.pallas import tpu as pltpu
from jax.sharding import PartitionSpec as P

GRID = 8
AXES = ("row", "col")
BLOCK = 256
LANES = 128
SIDE = 16
GELU_A = math.sqrt(2.0 / math.pi)
GELU_B = GELU_A * 0.044715
F32 = jnp.float32
BF16 = jnp.bfloat16
PARAMS = pltpu.CompilerParams(vmem_limit_bytes=24 * 1024 * 1024)


def estimate(us):
    return pl.CostEstimate(flops=int(us * 1.1e9), bytes_accessed=int(us * 3.6e6), transcendentals=0)


def dot(left, right, contract=((1,), (0,))):
    return lax.dot_general(left, right, (contract, ((), ())), preferred_element_type=F32)


def dot_exact(vector, right, contract):
    tall = jnp.broadcast_to(vector, (8, vector.shape[1]))
    product = lax.dot_general(
        tall, right, (contract, ((), ())), precision=lax.Precision.HIGHEST, preferred_element_type=F32
    )
    return product[0:1]


def gelu_and_slope(x, with_slope=True):
    square = x * x
    t = jnp.tanh(x * (GELU_A + GELU_B * square))
    half = 0.5 + 0.5 * t
    value = x * half
    if not with_slope:
        return value, None
    slope = half + (value * (1.0 - t)) * (GELU_A + (3.0 * GELU_B) * square)
    return value, slope


def norm_rows(x):
    average = jnp.mean(x, axis=-1, keepdims=True)
    centered = x - average
    variance = jnp.mean(centered * centered, axis=-1, keepdims=True)
    rstd = lax.rsqrt(variance + 1e-05)
    return centered * rstd, rstd


def norm_rows_back(unit, rstd, gain, grad):
    unit_grad = grad * gain
    first = jnp.mean(unit_grad, axis=-1, keepdims=True)
    second = jnp.mean(unit_grad * unit, axis=-1, keepdims=True)
    return rstd * (unit_grad - first - unit * second)


def fold_rows(x):
    return jnp.sum(x.reshape(x.shape[0] // 8, 8, x.shape[1]), axis=0)


def whole(shape):
    return pl.BlockSpec(shape, lambda e: (0,) * len(shape))


def last_block(shape):
    lead = (0,) * (len(shape) - 1)
    return pl.BlockSpec(shape[:-1] + (BLOCK,), lambda e: lead + (e,))


def expand_kernel(
    image_ref, gain_ref, w_exp_ref,
    normed_ref, turned_ref, spread_ref, slope_ref,
    expanded_ref,
):
    rows, cols, channels = image_ref.shape

    @pl.when(pl.program_id(0) == 0)
    def _():
        gain = gain_ref[...].astype(F32)

        @pl.loop(0, rows // 4)
        def _(c):
            flat = image_ref[pl.ds(c * 4, 4)].reshape(4 * cols, channels)
            unit, _ = norm_rows(flat.astype(F32))
            at = pl.ds(pl.multiple_of(c * 4 * cols, 16), 4 * cols)
            normed_ref[at, :] = (unit * gain).astype(BF16)

        turned_ref[...] = normed_ref[...].T

    expanded_ref[...] = dot(normed_ref[...], w_exp_ref[...])

    @pl.loop(0, rows, unroll=4)
    def _(r):
        for h in range(BLOCK // LANES):
            lanes = slice(h * LANES, (h + 1) * LANES)
            x = expanded_ref[pl.ds(pl.multiple_of(r * cols, 16), cols), lanes]
            value, slope = gelu_and_slope(x)
            spread_ref[r, :, lanes] = value.astype(BF16)
            slope_ref[r, :, lanes] = slope.astype(BF16)


def run_expand(image, gain, w_expand):
    rows, cols, channels = image.shape
    expanded = w_expand.shape[1]
    return pl.pallas_call(
        expand_kernel,
        grid=(expanded // BLOCK,),
        in_specs=[whole(image.shape), whole(gain.shape), last_block(w_expand.shape)],
        out_specs=[
            whole((rows * cols, channels)), whole((channels, rows * cols)),
            last_block((rows, cols, expanded)), last_block((rows, cols, expanded)),
        ],
        out_shape=[
            jax.ShapeDtypeStruct((rows * cols, channels), BF16),
            jax.ShapeDtypeStruct((channels, rows * cols), BF16),
            jax.ShapeDtypeStruct((rows, cols, expanded), BF16),
            jax.ShapeDtypeStruct((rows, cols, expanded), BF16),
        ],
        scratch_shapes=[pltpu.VMEM((rows * cols, BLOCK), F32)],
        compiler_params=PARAMS,
        cost_estimate=estimate(14),
        name="expand",
    )(image, gain, w_expand)


def depthwise_kernel(
    up_ref, down_ref, side_ref, gain_ref, w_exp_ref, w_dep_ref, spread_ref,
    ring_ref, act_ref, pool_ref,
    ring_normed_ref, ring_wide_ref,
):
    rows, cols, _ = spread_ref.shape
    channels = up_ref.shape[2]
    over = 4 * cols
    side = 8

    @pl.when(pl.program_id(0) == 0)
    def _():
        gain = gain_ref[...].astype(F32)

        def put(at, values):
            unit, _ = norm_rows(values.astype(F32))
            ring_normed_ref[at : at + values.shape[0], :] = (unit * gain).astype(BF16)

        put(0, up_ref[...].reshape(2 * cols, channels))
        put(2 * cols, down_ref[...].reshape(2 * cols, channels))
        put(over, side_ref[...])

    ring_wide_ref[...] = dot(ring_normed_ref[...], w_exp_ref[...])
    tile = 32

    @pl.loop(0, ring_wide_ref.shape[0] // tile, unroll=True)
    def _(t):
        at = pl.ds(pl.multiple_of(t * tile, tile), tile)
        value, _ = gelu_and_slope(ring_wide_ref[at, :], False)
        low = value.astype(BF16)
        ring_ref[at, :] = low
        ring_wide_ref[at, :] = low.astype(F32)

    for h in range(BLOCK // LANES):
        lanes = slice(h * LANES, (h + 1) * LANES)
        taps = w_dep_ref[:, :, lanes].astype(F32)
        w = [[taps[a, b : b + 1] for b in range(3)] for a in range(3)]

        def line(r, main):
            at = pl.multiple_of(over + (r + 2) * side, side)
            return jnp.concatenate([main, ring_wide_ref[pl.ds(at, side), lanes]], axis=0)

        def conv(i, x, total):
            u = [x[0] * w[0][b] + x[1] * w[1][b] + x[2] * w[2][b] for b in range(3)]
            wide = cols + side
            pre = pltpu.roll(u[0], 1, 0) + u[1] + pltpu.roll(u[2], wide - 1, 0)
            value, _ = gelu_and_slope(pre[:cols], False)
            act_ref[i, :, lanes] = value.astype(BF16)
            return total + fold_rows(value)

        def step(i, carry):
            first, second, total = carry
            third = line(i + 1, spread_ref[i + 1, :, lanes].astype(F32))
            return second, third, conv(i, (first, second, third), total)

        carry = (
            line(-1, ring_wide_ref[cols : 2 * cols, lanes]),
            line(0, spread_ref[0, :, lanes].astype(F32)),
            jnp.zeros((8, LANES), F32),
        )
        first, second, total = lax.fori_loop(0, rows - 1, step, carry, unroll=5)
        third = line(rows, ring_wide_ref[2 * cols : 3 * cols, lanes])
        total = conv(rows - 1, (first, second, third), total)
        total = jnp.sum(total, axis=0, keepdims=True)
        pool_ref[:, :, lanes] = jnp.broadcast_to(total[None], (pool_ref.shape[0], 1, LANES))


def run_depthwise(count, up, down, side, gain, w_expand, w_depth, spread):
    rows, cols, expanded = spread.shape
    channels = up.shape[2]
    ring = 4 * cols + 8 * (rows + 4)
    return pl.pallas_call(
        depthwise_kernel,
        grid=(expanded // BLOCK,),
        in_specs=[
            whole(up.shape), whole(down.shape), whole(side.shape), whole(gain.shape),
            last_block(w_expand.shape), last_block(w_depth.shape), last_block(spread.shape),
        ],
        out_specs=[
            last_block((ring, expanded)), last_block(spread.shape), last_block((count, 1, expanded)),
        ],
        out_shape=[
            jax.ShapeDtypeStruct((ring, expanded), BF16),
            jax.ShapeDtypeStruct(spread.shape, BF16),
            jax.ShapeDtypeStruct((count, 1, expanded), F32),
        ],
        scratch_shapes=[pltpu.VMEM((ring, channels), BF16), pltpu.VMEM((ring, BLOCK), F32)],
        compiler_params=PARAMS,
        cost_estimate=estimate(1),
        name="depthwise",
    )(up, down, side, gain, w_expand, w_depth, spread)


def slope_kernel(flags_ref, ring_ref, w_dep_ref, spread_ref, main_ref, side_out_ref, wide_ref):
    rows, cols, _ = spread_ref.shape
    over = 4 * cols
    side = 8
    wide = cols + side

    for k, r in enumerate((0, 1, rows + 2, rows + 3)):
        wide_ref[r, :cols, :] = ring_ref[k * cols : (k + 1) * cols, :].astype(F32)
    sides = ring_ref[over:, :].astype(F32)
    for r in range(rows + 4):
        wide_ref[r, cols:, :] = sides[r * side : (r + 1) * side]

    @pl.loop(0, rows)
    def _(r):
        wide_ref[r + 2, :cols, :] = spread_ref[r].astype(F32)

    place = lax.broadcasted_iota(jnp.int32, (side, LANES), 0)
    side_mask = jnp.where(
        place == side - 1, flags_ref[2], jnp.where(place == 0, flags_ref[3], 1.0)
    ).astype(F32)

    @pl.loop(0, rows + 2)
    def _(i):
        keep = jnp.where(i == 0, flags_ref[0], jnp.where(i == rows + 1, flags_ref[1], 1.0))
        for h in range(BLOCK // LANES):
            lanes = slice(h * LANES, (h + 1) * LANES)
            taps = w_dep_ref[:, :, lanes].astype(F32)
            x = [wide_ref[i + a, :, lanes] for a in range(3)]
            u = [sum(x[a] * taps[a, b : b + 1] for a in range(3)) for b in range(3)]
            pre = pltpu.roll(u[0], 1, 0) + u[1] + pltpu.roll(u[2], wide - 1, 0)
            _, slope = gelu_and_slope(pre)
            slope = slope * keep
            main_ref[i, :, lanes] = slope[:cols].astype(BF16)
            side_out_ref[i, :, lanes] = slope[cols:] * side_mask


def run_slope(flags, ring, w_depth, spread):
    rows, cols, expanded = spread.shape
    return pl.pallas_call(
        slope_kernel,
        grid=(expanded // BLOCK,),
        in_specs=[
            pl.BlockSpec(memory_space=pltpu.SMEM),
            last_block(ring.shape), last_block(w_depth.shape), last_block(spread.shape),
        ],
        out_specs=[last_block((rows + 2, cols, expanded)), last_block((rows + 2, 8, expanded))],
        out_shape=[
            jax.ShapeDtypeStruct((rows + 2, cols, expanded), BF16),
            jax.ShapeDtypeStruct((rows + 2, 8, expanded), F32),
        ],
        scratch_shapes=[pltpu.VMEM((rows + 4, cols + 8, BLOCK), F32)],
        compiler_params=PARAMS,
        cost_estimate=estimate(13),
        name="slope",
    )(flags, ring, w_depth, spread)


def mix_kernel(
    cells_total, stride, bands,
    parts_ref, w_sq_ref, w_ex_ref, act_ref, image_ref, w_proj_ref, gain_ref, after_ref,
    pooled_ref, hidden_ref, gate_ref, mixed_ref, send_ref,
):
    step = pl.program_id(0)

    @pl.when(step == 0)
    def _():
        pooled = jnp.sum(parts_ref[...], axis=0) / cells_total
        hidden = dot_exact(pooled, w_sq_ref[...].astype(F32), ((1,), (0,)))
        silu = hidden * jax.nn.sigmoid(hidden)
        pooled_ref[...] = pooled
        hidden_ref[...] = hidden
        gate_ref[...] = jax.nn.sigmoid(dot_exact(silu, w_ex_ref[...].astype(F32), ((1,), (0,))))

    lines, cols, channels = image_ref.shape
    flat = act_ref[...].reshape(lines * cols, act_ref.shape[2])
    gated = (flat.astype(F32) * gate_ref[...]).astype(BF16)
    product = dot(gated, w_proj_ref[...])
    mixed = (image_ref[...].reshape(lines * cols, channels).astype(F32) + product).astype(BF16)
    mixed_ref[...] = mixed.reshape(lines, cols, channels)
    unit, _ = norm_rows(mixed.astype(F32))
    normed = (unit * gain_ref[...].astype(F32)).astype(BF16)
    for k in range(lines):
        line = step * lines + k
        for band in range(bands):
            start = k * cols + band * SIDE
            send_ref[lax.rem(line, stride) * bands + band, line // stride] = normed[
                start : start + SIDE
            ]


def run_mix(cells_total, stride, parts, w_squeeze, w_excite, act, image, w_project, gain, after):
    rows, cols, channels = image.shape
    expanded = act.shape[2]
    lines = 4
    bands = cols // SIDE
    block = lambda width: pl.BlockSpec((lines, cols, width), lambda r: (r, 0, 0))
    send = (stride * bands, rows // stride, SIDE, channels)
    return pl.pallas_call(
        functools.partial(mix_kernel, cells_total, stride, bands),
        grid=(rows // lines,),
        in_specs=[
            whole(parts.shape), whole(w_squeeze.shape), whole(w_excite.shape),
            block(expanded), block(channels), whole(w_project.shape), whole(gain.shape),
            pl.BlockSpec(memory_space=pl.ANY),
        ],
        out_specs=[
            whole((1, expanded)), whole((1, w_squeeze.shape[1])), whole((1, expanded)),
            block(channels), whole(send),
        ],
        out_shape=[
            jax.ShapeDtypeStruct((1, expanded), F32),
            jax.ShapeDtypeStruct((1, w_squeeze.shape[1]), F32),
            jax.ShapeDtypeStruct((1, expanded), F32),
            jax.ShapeDtypeStruct(image.shape, BF16),
            jax.ShapeDtypeStruct(send, BF16),
        ],
        compiler_params=PARAMS,
        cost_estimate=estimate(5),
        name="mix",
    )(parts, w_squeeze, w_excite, act, image, w_project, gain, after)


def attention_kernel(
    members, heads, lines,
    arrived_ref, att_grad_ref, w_qkv_ref, bias_ref,
    x_ref, att_ref, grad_ref, packed_grad_ref, bias_out_ref,
    order_ref, packed_ref, bias_sum_ref,
):
    cells, channels = x_ref.shape
    groups = cells // members

    def places():
        for g in range(groups):
            for m in range(0, members, GRID):
                line, row = (m // GRID) % lines, m // GRID // lines
                start = (row * GRID * lines + line) * groups + g
                yield g * members + m, pl.ds(start, GRID, stride=lines * groups)

    for half in range(channels // LANES):
        lanes = slice(half * LANES, (half + 1) * LANES)
        order_ref[half] = arrived_ref[:, lanes].astype(F32)
        for g in range(groups):
            pieces = [order_ref[half, at, :] for k, at in places() if k // members == g]
            at = slice(g * members, (g + 1) * members)
            x_ref[at, lanes] = jnp.concatenate(pieces, axis=0).astype(BF16)
    dim = channels // heads
    per_half = LANES // dim
    halves = channels // LANES
    scale = dim ** (-0.5)
    packed_ref[...] = dot(x_ref[...], w_qkv_ref[...]).astype(BF16)
    bias_sum_ref[...] = jnp.zeros(bias_sum_ref.shape, F32)
    tall = per_half * members
    mask = (
        lax.broadcasted_iota(jnp.int32, (tall, LANES), 0) // members
        == lax.broadcasted_iota(jnp.int32, (tall, LANES), 1) // dim
    ).astype(F32).astype(BF16)
    owner = lax.broadcasted_iota(jnp.int32, (members, 2 * LANES), 1) % LANES // dim
    zero = jnp.zeros((members, LANES), BF16)

    def by_head(pair):
        return jnp.concatenate(
            [jnp.concatenate([v] * per_half, axis=0) * mask for v in pair], axis=1
        )

    def diagonal(pair):
        return jnp.concatenate(
            [
                jnp.concatenate([pair[0], zero], axis=1),
                jnp.concatenate([zero, pair[1]], axis=1),
            ],
            axis=0,
        )

    def collect(v):
        parts = [v[h * members : (h + 1) * members] for h in range(per_half)]
        picked = parts[-1]
        for h in range(per_half - 1):
            picked = jnp.where(owner == h, parts[h], picked)
        return [picked[:, :LANES], picked[:, LANES:]]

    def blocks(v):
        return [v[:members, :LANES], v[members:, LANES:]]

    def over_members(v, reduce):
        parted = v.reshape(per_half, members, 2 * members)
        small = reduce(parted, axis=1, keepdims=True)
        return jnp.broadcast_to(small, parted.shape).reshape(v.shape)

    def pair_step(g, carry):
        at = [pl.ds(pl.multiple_of((2 * g + k) * members, 16), members) for k in range(2)]
        for half in range(halves):
            def lanes(part):
                start = part * channels + half * LANES
                return slice(start, start + LANES)

            q, k, v = ([packed_ref[at[n], lanes(part)] for n in range(2)] for part in range(3))
            cot = [att_grad_ref[at[n], lanes(0)] for n in range(2)]
            q_diag, cot_diag = diagonal(q), diagonal(cot)
            k_tall, v_tall = by_head(k), by_head(v)
            scores = dot(k_tall, q_diag, ((1,), (1,))) * scale + bias_ref[half]
            grad_probs = dot(v_tall, cot_diag, ((1,), (1,)))
            lifted = jnp.exp(scores - over_members(scores, jnp.max))
            soft = lifted * (1.0 / over_members(lifted, jnp.sum))
            soft_low = soft.astype(BF16)
            grad_scores = soft * (grad_probs - over_members(grad_probs * soft, jnp.sum))
            bias_sum_ref[half] += grad_scores
            scaled = (grad_scores * scale).astype(BF16)
            attended = blocks(dot(soft_low, v_tall, ((0,), (0,))))
            grad_q = blocks(dot(scaled, k_tall, ((0,), (0,))))
            grad_v = collect(dot(soft_low, cot_diag))
            grad_k = collect(dot(scaled, q_diag))
            for n in range(2):
                att_ref[at[n], lanes(0)] = attended[n].astype(BF16)
                for part, value in enumerate((grad_q, grad_k, grad_v)):
                    packed_grad_ref[at[n], lanes(part)] = value[n].astype(BF16)
        return carry

    lax.fori_loop(0, cells // members // 2, pair_step, 0, unroll=2)
    grad = dot(packed_grad_ref[...], w_qkv_ref[...], ((1,), (1,)))
    for half in range(halves):
        lanes = slice(half * LANES, (half + 1) * LANES)
        for k, at in places():
            order_ref[half, at, :] = grad[k : k + GRID, lanes]
        grad_ref[:, lanes] = order_ref[half].astype(BF16)
    for half in range(halves):
        both = bias_sum_ref[half]
        bias_out_ref[half] = both[:, :members] + both[:, members:]


def run_attention(arrived, att_grad, w_qkv, bias_tall, heads, lines):
    cells, channels = att_grad.shape
    halves, tall, members2 = bias_tall.shape
    members = members2 // 2
    vmem = pl.BlockSpec(memory_space=pltpu.VMEM)
    return pl.pallas_call(
        functools.partial(attention_kernel, members, heads, lines),
        in_specs=[vmem] * 4,
        out_specs=[vmem] * 5,
        out_shape=[
            jax.ShapeDtypeStruct((cells, channels), BF16),
            jax.ShapeDtypeStruct((cells, channels), BF16),
            jax.ShapeDtypeStruct((cells, channels), BF16),
            jax.ShapeDtypeStruct((cells, 3 * channels), BF16),
            jax.ShapeDtypeStruct((halves, tall, members), F32),
        ],
        scratch_shapes=[
            pltpu.VMEM((channels // LANES, cells, LANES), F32),
            pltpu.VMEM((cells, 3 * channels), BF16),
            pltpu.VMEM(bias_tall.shape, F32),
        ],
        compiler_params=PARAMS,
        cost_estimate=estimate(14),
        name="attention",
    )(arrived.reshape(cells, channels), att_grad, w_qkv, bias_tall)


def attention_weights_kernel(x_ref, packed_grad_ref, att_ref, cot_ref, bias_ref, out_ref):
    channels = x_ref.shape[1]
    wide = 3 * channels
    out_ref[:, :wide] = dot(x_ref[...], packed_grad_ref[...], ((0,), (0,))).astype(BF16)
    out_ref[:, wide : wide + channels] = dot(att_ref[...], cot_ref[...], ((0,), (0,))).astype(BF16)
    halves, tall, members = bias_ref.shape
    for h in range(tall // members):
        rows = slice(h * members, (h + 1) * members)
        turned = jnp.concatenate([bias_ref[half, rows, :].T for half in range(halves)], axis=1)
        out_ref[rows, wide + channels :] = turned.astype(BF16)


def run_attention_weights(x, packed_grad, att, cot, bias):
    channels = x.shape[1]
    vmem = pl.BlockSpec(memory_space=pltpu.VMEM)
    width = 4 * channels + bias.shape[0] * bias.shape[2]
    return pl.pallas_call(
        attention_weights_kernel,
        in_specs=[vmem] * 5,
        out_specs=vmem,
        out_shape=jax.ShapeDtypeStruct((channels, width), BF16),
        compiler_params=PARAMS,
        cost_estimate=estimate(5),
        name="attention_weights",
    )(x, packed_grad, att, cot, bias)


def mixed_back_kernel(
    stride, bands,
    recv_ref, mixed_ref, cot_ref, gain_ref, act_ref, gate_ref, w_projt_ref,
    grad_ref, low_ref, norm_ref, project_ref, gate_grad_ref,
    turned_ref, total_ref,
):
    rows, cols, channels = mixed_ref.shape

    @pl.when(pl.program_id(0) == 0)
    def _():
        gain = gain_ref[...].astype(F32)
        lines = 4

        def some_rows(c, total):
            pieces = []
            for k in range(lines):
                i = c * lines + k
                a, p = lax.rem(i, stride), i // stride
                pieces += [recv_ref[a * bands + band, p] for band in range(bands)]
            grad = jnp.concatenate(pieces, axis=0).astype(F32)
            at = pl.ds(c * lines, lines)
            flat = lambda ref: ref[at].reshape(lines * cols, channels).astype(F32)
            unit, rstd = norm_rows(flat(mixed_ref))
            back = flat(cot_ref) + norm_rows_back(unit, rstd, gain, grad)
            grad_ref[at] = back.reshape(lines, cols, channels)
            low_ref[at] = back.astype(BF16).reshape(lines, cols, channels)
            return total + fold_rows(grad * unit)

        total = lax.fori_loop(
            0, rows // lines, some_rows, jnp.zeros((8, channels), F32), unroll=2
        )
        norm_ref[...] = jnp.sum(total, axis=0, keepdims=True)
        turned_ref[...] = low_ref[...].reshape(rows * cols, channels).T

    flat = act_ref[...].reshape(rows * cols, BLOCK)
    product = dot(turned_ref[...], flat)
    total = jnp.sum(product * w_projt_ref[...].astype(F32), axis=0, keepdims=True)
    step, steps = pl.program_id(0), pl.num_programs(0)
    total_ref[step] = total
    project_ref[...] = (product * gate_ref[...]).T.astype(BF16)

    @pl.when(step == steps - 1)
    def _():
        sums = [total_ref[e] for e in range(total_ref.shape[0])]
        high = [v.astype(BF16).astype(F32) for v in sums]
        terms = jnp.concatenate(high + [v - w for v, w in zip(sums, high)], axis=0)
        gate_grad_ref[...] = jnp.broadcast_to(terms.astype(BF16)[None], gate_grad_ref.shape)


def run_mixed_back(count, stride, recv, mixed, cot, gain, act, gate, w_project_t):
    rows, cols, channels = mixed.shape
    expanded = act.shape[2]
    return pl.pallas_call(
        functools.partial(mixed_back_kernel, stride, cols // SIDE),
        grid=(expanded // BLOCK,),
        in_specs=[
            whole(recv.shape), whole(mixed.shape), whole(cot.shape), whole(gain.shape),
            last_block(act.shape), last_block(gate.shape), last_block(w_project_t.shape),
        ],
        out_specs=[
            whole(mixed.shape), whole(mixed.shape), whole((1, channels)),
            last_block((BLOCK, expanded)), whole((count, 2 * expanded // BLOCK, BLOCK)),
        ],
        out_shape=[
            jax.ShapeDtypeStruct(mixed.shape, F32),
            jax.ShapeDtypeStruct(mixed.shape, BF16),
            jax.ShapeDtypeStruct((1, channels), F32),
            jax.ShapeDtypeStruct((BLOCK, expanded), BF16),
            jax.ShapeDtypeStruct((count, 2 * expanded // BLOCK, BLOCK), BF16),
        ],
        scratch_shapes=[
            pltpu.VMEM((channels, rows * cols), BF16),
            pltpu.VMEM((expanded // BLOCK, 1, BLOCK), F32),
        ],
        compiler_params=PARAMS,
        cost_estimate=estimate(7),
        name="mixed_back",
    )(recv, mixed, cot, gain, act, gate, w_project_t)


def unpack_kernel(
    place_ref, near_ref, far_ref, expand_ref, depth_ref, norm0_ref, norm1_ref, tail_ref
):
    expanded = expand_ref.shape[2]
    for pair, source in enumerate((near_ref, far_ref)):
        at = lax.rem(place_ref[0] + pair, 2)
        expand_ref[at] = source[:, :expanded].astype(F32)
        tail_ref[at] = source[:, expanded:].astype(F32)
    tail = tail_ref[0]
    pieces = expanded // LANES
    for t in range(9):
        for k in range(pieces):
            row = t * pieces + k
            lanes = slice(k * LANES, (k + 1) * LANES)
            depth_ref[t // 3, t % 3 : t % 3 + 1, lanes] = tail[row : row + 1]
    start = 9 * pieces
    half = norm0_ref.shape[1] // LANES
    for k in range(half):
        lanes = slice(k * LANES, (k + 1) * LANES)
        norm0_ref[:, lanes] = tail[start + k : start + k + 1]
        norm1_ref[:, lanes] = tail[start + half + k : start + half + k + 1]


def run_unpack(near, far, expanded):
    rows = near.shape[0]
    channels = 2 * rows
    place = (lax.axis_index("col") % 2).astype(jnp.int32).reshape(1)
    vmem = pl.BlockSpec(memory_space=pltpu.VMEM)
    return pl.pallas_call(
        unpack_kernel,
        in_specs=[pl.BlockSpec(memory_space=pltpu.SMEM), vmem, vmem],
        out_specs=[vmem] * 4,
        out_shape=[
            jax.ShapeDtypeStruct((2, rows, expanded), F32),
            jax.ShapeDtypeStruct((3, 3, expanded), F32),
            jax.ShapeDtypeStruct((1, channels), F32),
            jax.ShapeDtypeStruct((1, channels), F32),
        ],
        scratch_shapes=[pltpu.VMEM((2, rows, near.shape[1] - expanded), F32)],
        compiler_params=PARAMS,
        cost_estimate=estimate(2),
        name="unpack",
    )(place, near, far)


def expand_back_kernel(
    cells_total,
    parts_ref, hidden_ref, gate_all_ref, w_sq_ref, w_ex_ref,
    low_ref, up_ref, down_ref, side_ref, w_projt_ref, gate_ref, slope_ref, side_slope_ref,
    spread_slope_ref, spread_ref, w_dep_ref, turned_ref, w_exp_ref, gain_ref, norm1_ref,
    weights_ref, first_ref, logit_ref, pre_ref,
    main_ref, side_grad_ref, window_ref, expanded_ref, pool_ref, tail_ref, norm_ref,
):
    rows, cols, channels = low_ref.shape
    side = 8
    wide = cols + side
    step = pl.program_id(0)
    steps = pl.num_programs(0)

    @pl.when(step == 0)
    def _():
        gate = gate_all_ref[...]
        blocks = pool_ref.shape[0]
        terms = jnp.sum(parts_ref[...].astype(F32), axis=0)
        gate_grad = jnp.concatenate(
            [terms[e : e + 1] + terms[blocks + e : blocks + e + 1] for e in range(blocks)], axis=1
        )
        logit = gate_grad * gate * (1.0 - gate)
        hidden = hidden_ref[...]
        sig = jax.nn.sigmoid(hidden)
        pre = dot_exact(logit, w_ex_ref[...].astype(F32), ((1,), (1,))) * (
            sig + hidden * sig * (1.0 - sig)
        )
        logit_ref[...] = logit
        pre_ref[...] = pre
        pooled = dot_exact(pre, w_sq_ref[...].astype(F32), ((1,), (1,))) / cells_total
        for e in range(blocks):
            pool_ref[e] = pooled[:, e * BLOCK : (e + 1) * BLOCK]
        first_ref[...] = jnp.zeros(first_ref.shape, F32)
        tail_ref[...] = jnp.zeros(tail_ref.shape, F32)
        norm_ref[...] = jnp.zeros(norm_ref.shape, F32)

    w_projt = w_projt_ref[...]
    main_ref[pl.ds(0, cols), :] = dot(up_ref[0], w_projt)
    main_ref[pl.ds(cols, rows * cols), :] = dot(
        low_ref[...].reshape(rows * cols, channels), w_projt
    )
    main_ref[pl.ds((rows + 1) * cols, cols), :] = dot(down_ref[0], w_projt)
    side_grad_ref[...] = dot(side_ref[...], w_projt)

    @pl.loop(0, rows + 2, unroll=3)
    def _(i):
        for h in range(BLOCK // LANES):
            lanes = slice(h * LANES, (h + 1) * LANES)
            gate = gate_ref[:, lanes]
            pooled = pool_ref[step][:, lanes]
            gated = main_ref[pl.ds(pl.multiple_of(i * cols, 16), cols), lanes]
            main = (gated * gate + pooled) * slope_ref[i, :, lanes].astype(F32)
            gated = side_grad_ref[pl.ds(pl.multiple_of(i * side, side), side), lanes]
            edge = (gated * gate + pooled) * side_slope_ref[i, :, lanes]
            grad = jnp.concatenate([main, edge], axis=0)
            window_ref[0, i, :, lanes] = pltpu.roll(grad, wide - 1, 0)[:cols]
            window_ref[1, i, :, lanes] = grad[:cols]
            window_ref[2, i, :, lanes] = pltpu.roll(grad, 1, 0)[:cols]

    for h in range(BLOCK // LANES):
        lanes = slice(h * LANES, (h + 1) * LANES)
        taps = w_dep_ref[:, :, lanes].astype(F32)

        def back_row(i, sums):
            spread = spread_ref[i, :, lanes].astype(F32)
            total = jnp.zeros((cols, LANES), F32)
            new_sums = []
            for a in range(3):
                for b in range(3):
                    window = window_ref[b, i + 2 - a, :, lanes]
                    total = total + window * taps[a, b : b + 1]
                    new_sums.append(sums[a * 3 + b] + fold_rows(window * spread))
            grad = total * spread_slope_ref[i, :, lanes].astype(F32)
            expanded_ref[pl.ds(pl.multiple_of(i * cols, 16), cols), lanes] = grad.astype(BF16)
            return tuple(new_sums)

        sums = lax.fori_loop(0, rows, back_row, (jnp.zeros((8, LANES), F32),) * 9, unroll=2)
        for t in range(9):
            row = t * (steps * BLOCK // LANES) + step * (BLOCK // LANES) + h
            tail_ref[pl.ds(row, 1), :] = jnp.sum(sums[t], axis=0, keepdims=True)

    grad_expanded = expanded_ref[...]
    w_exp = w_exp_ref[...]
    weights = dot(turned_ref[...], grad_expanded)
    weights_ref[:, pl.ds(pl.multiple_of(step * BLOCK, BLOCK), BLOCK)] = weights.astype(BF16)
    norm_ref[...] += jnp.sum(weights * w_exp.astype(F32), axis=1, keepdims=True)
    first_ref[...] += dot(grad_expanded, w_exp, ((1,), (1,)))

    @pl.when(step == steps - 1)
    def _():
        norm = norm_ref[...].T[0:1] / gain_ref[...].astype(F32)
        start = 9 * steps * (BLOCK // LANES)
        for k in range(channels // LANES):
            piece = slice(k * LANES, (k + 1) * LANES)
            tail_ref[start + k : start + k + 1, :] = norm[:, piece]
            at = start + channels // LANES + k
            tail_ref[at : at + 1, :] = norm1_ref[:, piece]
        weights_ref[:, steps * BLOCK :] = tail_ref[...].astype(BF16)


def run_expand_back(
    cells_total, parts, hidden, gate, w_squeeze, w_excite, low, up, down, side,
    w_project_t, slope, side_slope, spread_slope, spread, w_depth, turned, w_expand, gain, norm1,
):
    rows, cols, channels = low.shape
    expanded = w_expand.shape[1]
    steps = expanded // BLOCK
    return pl.pallas_call(
        functools.partial(expand_back_kernel, cells_total),
        grid=(steps,),
        in_specs=[
            pl.BlockSpec(
                (parts.shape[0], 2 * steps, BLOCK), lambda e: (0, parts.shape[1] // (2 * steps) - 1, 0)
            ),
            whole(hidden.shape), whole(gate.shape),
            whole(w_squeeze.shape), whole(w_excite.shape),
            whole(low.shape), whole(up.shape), whole(down.shape), whole(side.shape),
            last_block(w_project_t.shape), last_block(gate.shape), last_block(slope.shape),
            last_block(side_slope.shape), last_block(spread_slope.shape), last_block(spread.shape),
            last_block(w_depth.shape), whole(turned.shape), last_block(w_expand.shape),
            whole(gain.shape), whole(norm1.shape),
        ],
        out_specs=[
            whole((channels, expanded + LANES)), whole((rows * cols, channels)),
            whole((1, expanded)), whole(hidden.shape),
        ],
        out_shape=[
            jax.ShapeDtypeStruct((channels, expanded + LANES), BF16),
            jax.ShapeDtypeStruct((rows * cols, channels), F32),
            jax.ShapeDtypeStruct((1, expanded), F32),
            jax.ShapeDtypeStruct(hidden.shape, F32),
        ],
        scratch_shapes=[
            pltpu.VMEM(((rows + 2) * cols, BLOCK), F32),
            pltpu.VMEM(((rows + 2) * 8, BLOCK), F32),
            pltpu.VMEM((3, rows + 2, cols, BLOCK), F32),
            pltpu.VMEM((rows * cols, BLOCK), BF16),
            pltpu.VMEM((steps, 1, BLOCK), F32),
            pltpu.VMEM((channels, LANES), F32),
            pltpu.VMEM((channels, LANES), F32),
        ],
        compiler_params=PARAMS,
        cost_estimate=estimate(14),
        name="expand_back",
    )(
        parts, hidden, gate, w_squeeze, w_excite, low, up, down, side, w_project_t, gate,
        slope, side_slope, spread_slope, spread, w_depth, turned, w_expand, gain, norm1,
    )


def image_back_kernel(image_ref, gain_ref, first_ref, mixed_ref, out_ref):
    unit, rstd = norm_rows(image_ref[...].astype(F32))
    grad = first_ref[...]
    back = mixed_ref[...] + norm_rows_back(unit, rstd, gain_ref[...].astype(F32), grad)
    out_ref[...] = back.astype(BF16)


def run_image_back(image, gain, first, mixed):
    cells, channels = image.shape
    block = pl.BlockSpec((cells // 4, channels), lambda r: (r, 0))
    return pl.pallas_call(
        image_back_kernel,
        grid=(4,),
        in_specs=[block, whole(gain.shape), block, block],
        out_specs=block,
        out_shape=jax.ShapeDtypeStruct((cells, channels), BF16),
        compiler_params=PARAMS,
        cost_estimate=estimate(4),
        name="image_back",
    )(image, gain, first, mixed)


def shift(cells, axis, step):
    count = lax.axis_size(axis)
    pairs = [(i, i + step) for i in range(count) if 0 <= i + step < count]
    return lax.ppermute(cells, axis, pairs)


def halo_rows(cells, width):
    up = shift(cells[cells.shape[0] - width :], "row", 1)
    down = shift(cells[:width], "row", -1)
    return up, down


def halo_sides(cells, up, down, width):
    rows, cols, channels = cells.shape
    first = jnp.concatenate([up[:, :width], cells[:, :width], down[:, :width]], axis=0)
    last = jnp.concatenate(
        [up[:, cols - width :], cells[:, cols - width :], down[:, cols - width :]], axis=0
    )
    left = shift(last, "col", 1)
    right = shift(first, "col", -1)
    gap = jnp.zeros((rows + 2 * width, 8 - 2 * width, channels), cells.dtype)
    side = jnp.concatenate([right, gap, left], axis=1)
    return side.reshape(-1, channels)


def hand_around(blocks):
    return lax.all_to_all(blocks, AXES, split_axis=0, concat_axis=0, tiled=True)


def sum_steps():
    return [("col", 1, 2), ("row", 1, lax.axis_size("row")), ("col", 2, lax.axis_size("col") // 2)]


def send_on(v, axis, stride, size, k):
    pairs = []
    for i in range(lax.axis_size(axis)):
        place = i // stride % size
        pairs.append((i, i + ((place + k) % size - place) * stride))
    return lax.ppermute(v, axis, pairs)


def sum_parts(matrix, axis, stride, size):
    place = lax.axis_index(axis) // stride % size
    parts = matrix.reshape(size, matrix.shape[0] // size, matrix.shape[1])
    part = lambda i: lax.dynamic_index_in_dim(parts, i % size, 0, False)
    total = part(place).astype(F32)
    for k in range(1, size):
        total = total + send_on(part(place + k), axis, stride, size, k).astype(F32)
    return total.astype(BF16)


def sum_shares(matrix):
    rows, columns = matrix.shape
    count = lax.axis_size("row") * lax.axis_size("col")
    pair = ("col", 1, 2)
    half = sum_parts(matrix, *pair)
    same_core = [list(range(k, count, 2)) for k in range(2)]

    def around(blocks):
        return lax.all_to_all(
            blocks, AXES, split_axis=0, concat_axis=0, tiled=True, axis_index_groups=same_core
        )

    arrived = around(half.reshape(count // 2, rows // count, columns))
    total = jnp.sum(arrived.astype(F32), axis=0).astype(BF16)
    sent = jnp.broadcast_to(total[None], (count // 2,) + total.shape)
    gathered = around(sent).reshape(rows // 2, columns)
    return gathered, send_on(gathered, *pair, 1)


def stack_kernel(*refs):
    for k, ref in enumerate(refs[:-1]):
        refs[-1][k] = ref[...]


def join_parts(blocks, axis, stride, size):
    arrived = [blocks] + [send_on(blocks, axis, stride, size, k) for k in range(1, size)]
    vmem = pl.BlockSpec(memory_space=pltpu.VMEM)
    stacked = pl.pallas_call(
        stack_kernel,
        in_specs=[vmem] * size,
        out_specs=vmem,
        out_shape=jax.ShapeDtypeStruct((size,) + blocks.shape, blocks.dtype),
        compiler_params=PARAMS,
        cost_estimate=estimate(1),
        name="stack",
    )(*arrived)
    return stacked.reshape((size * blocks.shape[0],) + blocks.shape[1:])


def unpack_weights_kernel(
    sizes, places_ref, near_ref, far_ref, qkv_ref, out_ref, bias_ref, project_ref
):
    channels = out_ref.shape[2]
    halves, members = bias_ref.shape[0], bias_ref.shape[3]
    cuts = (0, 3 * channels, 4 * channels, 4 * channels + halves * members)
    pairs, over_row, rest = sizes
    for pair, source in enumerate((near_ref, far_ref)):
        for r in range(over_row):
            for c in range(rest):
                block = source[r * rest + c].astype(F32)
                at = lax.rem(places_ref[0] + pairs - pair, pairs)
                at = at * over_row + lax.rem(places_ref[1] + over_row - r, over_row)
                at = at * rest + lax.rem(places_ref[2] + rest - c, rest)
                qkv_ref[at] = block[:, : cuts[1]]
                out_ref[at] = block[:, cuts[1] : cuts[2]]
                for half in range(halves):
                    start = cuts[2] + half * members
                    bias_ref[half, at] = block[:, start : start + members]
                for e in range(project_ref.shape[0]):
                    start = cuts[3] + e * channels
                    project_ref[e, at] = block[:, start : start + channels]


def run_unpack_weights(steps, near, far, channels, expanded, halves, members):
    count, rows, _ = near.shape
    count *= 2
    places = jnp.stack([lax.axis_index(axis) // stride % size for axis, stride, size in steps])
    vmem = pl.BlockSpec(memory_space=pltpu.VMEM)
    blocks = lambda width: jax.ShapeDtypeStruct((count, rows, width), F32)
    return pl.pallas_call(
        functools.partial(unpack_weights_kernel, tuple(size for _, _, size in steps)),
        in_specs=[pl.BlockSpec(memory_space=pltpu.SMEM), vmem, vmem],
        out_specs=[vmem] * 4,
        out_shape=[
            blocks(3 * channels), blocks(channels),
            jax.ShapeDtypeStruct((halves, count, rows, members), F32),
            jax.ShapeDtypeStruct((expanded // BLOCK, count, rows, channels), F32),
        ],
        compiler_params=PARAMS,
        cost_estimate=estimate(2),
        name="unpack_weights",
    )(places.astype(jnp.int32), near, far)


def swap_groups(blocks, parity):
    groups = None
    if parity > 1:
        over_row = lax.axis_size("row")
        over_col = lax.axis_size("col")
        groups = [
            [r * over_col + c for r in range(over_row) for c in range(k, over_col, parity)]
            for k in range(parity)
        ]
    return lax.all_to_all(
        blocks, AXES, split_axis=0, concat_axis=0, tiled=True, axis_index_groups=groups
    )


def on_device(
    image, out_cotangent, norm0_gain, w_expand, w_depth, w_squeeze, w_excite, w_project,
    norm1_gain, w_qkv, w_out, attn_bias,
):
    rows, cols, channels = image.shape
    over_row = lax.axis_size("row")
    over_col = lax.axis_size("col")
    count = over_row * over_col
    cells_total = rows * cols * count
    stride = rows * over_row // GRID
    parity = over_col // GRID
    lines = rows // stride
    bands = cols // SIDE
    members = GRID * GRID
    expanded = w_expand.shape[1]

    def into_members(arrived):
        parted = arrived.reshape(over_row, GRID, lines, SIDE, channels)
        return parted.transpose(3, 0, 2, 1, 4).reshape(SIDE * members, channels)

    def out_of_members(values):
        parted = values.reshape(SIDE, over_row, lines, GRID, channels)
        return parted.transpose(1, 3, 2, 0, 4).reshape(-1, lines, SIDE, channels)

    row, col = lax.axis_index("row"), lax.axis_index("col")
    flags = jnp.stack([row > 0, row < over_row - 1, col > 0, col < over_col - 1]).astype(F32)
    gain_first = norm0_gain.reshape(1, channels)
    gain_second = norm1_gain.reshape(1, channels)
    w_project_t = w_project.T
    heads = attn_bias.shape[0]
    halves = channels // LANES
    bias_tall = attn_bias.transpose(0, 2, 1).reshape(halves, heads // halves * members, members)
    bias_tall = jnp.concatenate([bias_tall, bias_tall], axis=2)

    up, down = halo_rows(image, 2)
    normed_first, turned_first, spread, spread_slope = run_expand(image, gain_first, w_expand)
    up, down, spread = lax.optimization_barrier((up, down, spread))
    side = halo_sides(image, up, down, 2)
    cot_sent = (
        out_cotangent.reshape(lines, stride, bands, SIDE, channels)
        .transpose(1, 2, 0, 3, 4)
        .reshape(stride * bands, lines, SIDE, channels)
    )
    cot_members = into_members(swap_groups(cot_sent, parity))
    ring, act, pool = run_depthwise(count, up, down, side, gain_first, w_expand, w_depth, spread)
    pooled, hidden, gate, mixed, normed_sent = run_mix(
        cells_total, stride, hand_around(pool), w_squeeze, w_excite, act, image, w_project,
        gain_second, cot_members,
    )
    slope, side_slope = run_slope(flags, ring, w_depth, spread)
    normed_arrived = swap_groups(normed_sent, parity)
    att_grad = dot(cot_members, w_out, ((1,), (1,))).astype(BF16)
    normed_arrived, slope, att_grad = lax.optimization_barrier((normed_arrived, slope, att_grad))
    normed_members, attended, grad_normed, packed_grad, grad_bias = run_attention(
        normed_arrived, att_grad, w_qkv, bias_tall, heads, lines
    )
    grad_normed_home = swap_groups(grad_normed.reshape(normed_sent.shape), parity)
    weights = run_attention_weights(normed_members, packed_grad, attended, cot_members, grad_bias)
    grad_normed_home, weights = lax.optimization_barrier((grad_normed_home, weights))
    grad_mixed, grad_low, grad_norm1, grad_project, gate_grad = run_mixed_back(
        count, stride, grad_normed_home, mixed, out_cotangent, gain_second, act, gate, w_project_t
    )
    attended_sent = out_of_members(attended)
    if parity == 1:
        both = hand_around(
            jnp.concatenate([attended_sent.reshape(count, -1, channels), gate_grad], axis=1)
        )
        parts = both
        attended_home = both[:, : lines * SIDE].reshape(attended_sent.shape)
    else:
        parts = hand_around(gate_grad)
        attended_home = swap_groups(attended_sent, parity)
    up, down = halo_rows(grad_low, 1)
    side = halo_sides(grad_low, up, down, 1)
    weights = jnp.concatenate([weights, grad_project], axis=1)
    weights, _ = lax.optimization_barrier((weights, up))
    steps = sum_steps()
    for step in steps:
        weights = sum_parts(weights, *step)
    late, grad_first, logit, pre = run_expand_back(
        cells_total, parts, hidden, gate, w_squeeze, w_excite, grad_low, up, down, side,
        w_project_t, slope, side_slope, spread_slope, spread, w_depth, turned_first, w_expand,
        gain_first, grad_norm1,
    )
    weights, _ = lax.optimization_barrier((weights, late))
    weights = weights[None]
    for step in steps[:0:-1]:
        weights = join_parts(weights, *step)
    other = send_on(weights, *steps[0], 1)
    grad_qkv, grad_out_proj, grad_bias, grad_project = run_unpack_weights(
        steps, weights, other, channels, expanded, halves, members
    )
    grad_expand, grad_depth, grad_norm0, grad_norm1 = run_unpack(*sum_shares(late), expanded)
    grad_image = run_image_back(
        image.reshape(-1, channels), gain_first, grad_first, grad_mixed.reshape(-1, channels)
    )
    attended_map = (
        attended_home.reshape(stride, bands, lines, SIDE, channels)
        .transpose(2, 0, 1, 3, 4)
        .reshape(rows * cols, channels)
    )
    block_out = (mixed.reshape(-1, channels).astype(F32) + dot(attended_map, w_out)).astype(BF16)

    silu = jax.nn.silu(hidden)
    grad_squeeze = pooled.reshape(expanded, 1) * pre
    grad_excite = silu.reshape(-1, 1) * logit

    return (
        block_out.reshape(image.shape),
        grad_image.reshape(image.shape),
        grad_norm0[0],
        grad_expand.reshape(w_expand.shape),
        grad_depth,
        grad_squeeze,
        grad_excite,
        grad_project.reshape(w_project.shape),
        grad_norm1[0],
        grad_qkv.reshape(w_qkv.shape),
        grad_out_proj.reshape(w_out.shape),
        grad_bias.reshape(attn_bias.shape),
    )


def solution(mesh):
    cells = P("row", "col", None)
    return jax.shard_map(
        on_device,
        mesh=mesh,
        in_specs=(cells, cells) + (P(),) * 10,
        out_specs=(cells, cells) + (P(),) * 10,
        check_vma=False,
    )
```

```python
import functools
import math

import jax
import jax.numpy as jnp
from jax import lax
from jax.experimental import pallas as pl
from jax.experimental.pallas import tpu as pltpu
from jax.sharding import PartitionSpec as P

GRID = 8
AXES = ("row", "col")
BLOCK = 256
LANES = 128
SIDE = 16
GELU_A = math.sqrt(2.0 / math.pi)
GELU_B = GELU_A * 0.044715
F32 = jnp.float32
BF16 = jnp.bfloat16
PARAMS = pltpu.CompilerParams(vmem_limit_bytes=56 * 1024 * 1024)
SMALL = pltpu.CompilerParams(vmem_limit_bytes=24 * 1024 * 1024)


def estimate(us):
    return pl.CostEstimate(flops=int(us * 1.1e9), bytes_accessed=int(us * 3.6e6), transcendentals=0)


def dot(left, right, contract=((1,), (0,))):
    return lax.dot_general(left, right, (contract, ((), ())), preferred_element_type=F32)


def dot_exact(vector, right, contract):
    tall = jnp.broadcast_to(vector, (8, vector.shape[1]))
    product = lax.dot_general(
        tall, right, (contract, ((), ())), precision=lax.Precision.HIGHEST, preferred_element_type=F32
    )
    return product[0:1]


def gelu_and_slope(x, with_slope=True):
    square = x * x
    t = jnp.tanh(x * (GELU_A + GELU_B * square))
    half = 0.5 + 0.5 * t
    value = x * half
    if not with_slope:
        return value, None
    slope = half + (value * (1.0 - t)) * (GELU_A + (3.0 * GELU_B) * square)
    return value, slope


def norm_rows(x):
    average = jnp.mean(x, axis=-1, keepdims=True)
    centered = x - average
    variance = jnp.mean(centered * centered, axis=-1, keepdims=True)
    rstd = lax.rsqrt(variance + 1e-05)
    return centered * rstd, rstd


def norm_rows_back(unit, rstd, gain, grad):
    unit_grad = grad * gain
    first = jnp.mean(unit_grad, axis=-1, keepdims=True)
    second = jnp.mean(unit_grad * unit, axis=-1, keepdims=True)
    return rstd * (unit_grad - first - unit * second)


def fold_rows(x):
    return jnp.sum(x.reshape(x.shape[0] // 8, 8, x.shape[1]), axis=0)


def whole(shape):
    return pl.BlockSpec(shape, lambda e: (0,) * len(shape))


def last_block(shape):
    lead = (0,) * (len(shape) - 1)
    return pl.BlockSpec(shape[:-1] + (BLOCK,), lambda e: lead + (e,))


def expand_kernel(
    image_ref, gain_ref, w_exp_ref,
    normed_ref, turned_ref, spread_ref, slope_ref,
    expanded_ref,
):
    rows, cols, channels = image_ref.shape

    @pl.when(pl.program_id(0) == 0)
    def _():
        gain = gain_ref[...].astype(F32)

        @pl.loop(0, rows // 4)
        def _(c):
            flat = image_ref[pl.ds(c * 4, 4)].reshape(4 * cols, channels)
            unit, _ = norm_rows(flat.astype(F32))
            at = pl.ds(pl.multiple_of(c * 4 * cols, 16), 4 * cols)
            normed_ref[at, :] = (unit * gain).astype(BF16)

        turned_ref[...] = normed_ref[...].T

    expanded_ref[...] = dot(normed_ref[...], w_exp_ref[...])

    @pl.loop(0, rows, unroll=4)
    def _(r):
        for h in range(BLOCK // LANES):
            lanes = slice(h * LANES, (h + 1) * LANES)
            x = expanded_ref[pl.ds(pl.multiple_of(r * cols, 16), cols), lanes]
            value, slope = gelu_and_slope(x)
            spread_ref[r, :, lanes] = value.astype(BF16)
            slope_ref[r, :, lanes] = slope.astype(BF16)


def run_expand(image, gain, w_expand):
    rows, cols, channels = image.shape
    expanded = w_expand.shape[1]
    return pl.pallas_call(
        expand_kernel,
        grid=(expanded // BLOCK,),
        in_specs=[whole(image.shape), whole(gain.shape), last_block(w_expand.shape)],
        out_specs=[
            whole((rows * cols, channels)), whole((channels, rows * cols)),
            last_block((rows, cols, expanded)), last_block((rows, cols, expanded)),
        ],
        out_shape=[
            jax.ShapeDtypeStruct((rows * cols, channels), BF16),
            jax.ShapeDtypeStruct((channels, rows * cols), BF16),
            jax.ShapeDtypeStruct((rows, cols, expanded), BF16),
            jax.ShapeDtypeStruct((rows, cols, expanded), BF16),
        ],
        scratch_shapes=[pltpu.VMEM((rows * cols, BLOCK), F32)],
        compiler_params=PARAMS,
        cost_estimate=estimate(14),
        name="expand",
    )(image, gain, w_expand)


def depthwise_kernel(
    up_ref, down_ref, side_ref, gain_ref, w_exp_ref, w_dep_ref, spread_ref,
    ring_ref, act_ref, pool_ref,
    ring_normed_ref, ring_wide_ref,
):
    rows, cols, _ = spread_ref.shape
    channels = up_ref.shape[2]
    over = 4 * cols
    side = 8

    @pl.when(pl.program_id(0) == 0)
    def _():
        gain = gain_ref[...].astype(F32)

        def put(at, values):
            unit, _ = norm_rows(values.astype(F32))
            ring_normed_ref[at : at + values.shape[0], :] = (unit * gain).astype(BF16)

        put(0, up_ref[...].reshape(2 * cols, channels))
        put(2 * cols, down_ref[...].reshape(2 * cols, channels))
        put(over, side_ref[...])

    ring_wide_ref[...] = dot(ring_normed_ref[...], w_exp_ref[...])
    tile = 32

    @pl.loop(0, ring_wide_ref.shape[0] // tile, unroll=True)
    def _(t):
        at = pl.ds(pl.multiple_of(t * tile, tile), tile)
        value, _ = gelu_and_slope(ring_wide_ref[at, :], False)
        low = value.astype(BF16)
        ring_ref[at, :] = low
        ring_wide_ref[at, :] = low.astype(F32)

    for h in range(BLOCK // LANES):
        lanes = slice(h * LANES, (h + 1) * LANES)
        taps = w_dep_ref[:, :, lanes].astype(F32)
        w = [[taps[a, b : b + 1] for b in range(3)] for a in range(3)]

        def line(r, main):
            at = pl.multiple_of(over + (r + 2) * side, side)
            return jnp.concatenate([main, ring_wide_ref[pl.ds(at, side), lanes]], axis=0)

        def conv(i, x, total):
            u = [x[0] * w[0][b] + x[1] * w[1][b] + x[2] * w[2][b] for b in range(3)]
            wide = cols + side
            pre = pltpu.roll(u[0], 1, 0) + u[1] + pltpu.roll(u[2], wide - 1, 0)
            value, _ = gelu_and_slope(pre[:cols], False)
            act_ref[i, :, lanes] = value.astype(BF16)
            return total + fold_rows(value)

        def step(i, carry):
            first, second, total = carry
            third = line(i + 1, spread_ref[i + 1, :, lanes].astype(F32))
            return second, third, conv(i, (first, second, third), total)

        carry = (
            line(-1, ring_wide_ref[cols : 2 * cols, lanes]),
            line(0, spread_ref[0, :, lanes].astype(F32)),
            jnp.zeros((8, LANES), F32),
        )
        first, second, total = lax.fori_loop(0, rows - 1, step, carry, unroll=5)
        third = line(rows, ring_wide_ref[2 * cols : 3 * cols, lanes])
        total = conv(rows - 1, (first, second, third), total)
        total = jnp.sum(total, axis=0, keepdims=True)
        pool_ref[:, :, lanes] = jnp.broadcast_to(total[None], (pool_ref.shape[0], 1, LANES))


def run_depthwise(count, up, down, side, gain, w_expand, w_depth, spread):
    rows, cols, expanded = spread.shape
    channels = up.shape[2]
    ring = 4 * cols + 8 * (rows + 4)
    return pl.pallas_call(
        depthwise_kernel,
        grid=(expanded // BLOCK,),
        in_specs=[
            whole(up.shape), whole(down.shape), whole(side.shape), whole(gain.shape),
            last_block(w_expand.shape), last_block(w_depth.shape), last_block(spread.shape),
        ],
        out_specs=[
            last_block((ring, expanded)), last_block(spread.shape), last_block((count, 1, expanded)),
        ],
        out_shape=[
            jax.ShapeDtypeStruct((ring, expanded), BF16),
            jax.ShapeDtypeStruct(spread.shape, BF16),
            jax.ShapeDtypeStruct((count, 1, expanded), F32),
        ],
        scratch_shapes=[pltpu.VMEM((ring, channels), BF16), pltpu.VMEM((ring, BLOCK), F32)],
        compiler_params=PARAMS,
        cost_estimate=estimate(1),
        name="depthwise",
    )(up, down, side, gain, w_expand, w_depth, spread)


def slope_kernel(flags_ref, ring_ref, w_dep_ref, spread_ref, main_ref, side_out_ref, wide_ref):
    rows, cols, _ = spread_ref.shape
    over = 4 * cols
    side = 8
    wide = cols + side

    for k, r in enumerate((0, 1, rows + 2, rows + 3)):
        wide_ref[r, :cols, :] = ring_ref[k * cols : (k + 1) * cols, :].astype(F32)
    sides = ring_ref[over:, :].astype(F32)
    for r in range(rows + 4):
        wide_ref[r, cols:, :] = sides[r * side : (r + 1) * side]

    @pl.loop(0, rows)
    def _(r):
        wide_ref[r + 2, :cols, :] = spread_ref[r].astype(F32)

    place = lax.broadcasted_iota(jnp.int32, (side, LANES), 0)
    side_mask = jnp.where(
        place == side - 1, flags_ref[2], jnp.where(place == 0, flags_ref[3], 1.0)
    ).astype(F32)

    @pl.loop(0, rows + 2)
    def _(i):
        keep = jnp.where(i == 0, flags_ref[0], jnp.where(i == rows + 1, flags_ref[1], 1.0))
        for h in range(BLOCK // LANES):
            lanes = slice(h * LANES, (h + 1) * LANES)
            taps = w_dep_ref[:, :, lanes].astype(F32)
            x = [wide_ref[i + a, :, lanes] for a in range(3)]
            u = [sum(x[a] * taps[a, b : b + 1] for a in range(3)) for b in range(3)]
            pre = pltpu.roll(u[0], 1, 0) + u[1] + pltpu.roll(u[2], wide - 1, 0)
            _, slope = gelu_and_slope(pre)
            slope = slope * keep
            main_ref[i, :, lanes] = slope[:cols].astype(BF16)
            side_out_ref[i, :, lanes] = slope[cols:] * side_mask


def run_slope(flags, ring, w_depth, spread):
    rows, cols, expanded = spread.shape
    return pl.pallas_call(
        slope_kernel,
        grid=(expanded // BLOCK,),
        in_specs=[
            pl.BlockSpec(memory_space=pltpu.SMEM),
            last_block(ring.shape), last_block(w_depth.shape), last_block(spread.shape),
        ],
        out_specs=[last_block((rows + 2, cols, expanded)), last_block((rows + 2, 8, expanded))],
        out_shape=[
            jax.ShapeDtypeStruct((rows + 2, cols, expanded), BF16),
            jax.ShapeDtypeStruct((rows + 2, 8, expanded), F32),
        ],
        scratch_shapes=[pltpu.VMEM((rows + 4, cols + 8, BLOCK), F32)],
        compiler_params=PARAMS,
        cost_estimate=estimate(13),
        name="slope",
    )(flags, ring, w_depth, spread)


def mix_kernel(
    cells_total, stride, bands,
    parts_ref, w_sq_ref, w_ex_ref, act_ref, image_ref, w_proj_ref, gain_ref, after_ref,
    pooled_ref, hidden_ref, gate_ref, mixed_ref, send_ref,
):
    step = pl.program_id(0)

    @pl.when(step == 0)
    def _():
        pooled = jnp.sum(parts_ref[...], axis=0) / cells_total
        hidden = dot_exact(pooled, w_sq_ref[...].astype(F32), ((1,), (0,)))
        silu = hidden * jax.nn.sigmoid(hidden)
        pooled_ref[...] = pooled
        hidden_ref[...] = hidden
        gate_ref[...] = jax.nn.sigmoid(dot_exact(silu, w_ex_ref[...].astype(F32), ((1,), (0,))))

    lines, cols, channels = image_ref.shape
    flat = act_ref[...].reshape(lines * cols, act_ref.shape[2])
    gated = (flat.astype(F32) * gate_ref[...]).astype(BF16)
    product = dot(gated, w_proj_ref[...])
    mixed = (image_ref[...].reshape(lines * cols, channels).astype(F32) + product).astype(BF16)
    mixed_ref[...] = mixed.reshape(lines, cols, channels)
    unit, _ = norm_rows(mixed.astype(F32))
    normed = (unit * gain_ref[...].astype(F32)).astype(BF16)
    for k in range(lines):
        line = step * lines + k
        for band in range(bands):
            start = k * cols + band * SIDE
            send_ref[lax.rem(line, stride) * bands + band, line // stride] = normed[
                start : start + SIDE
            ]


def run_mix(cells_total, stride, parts, w_squeeze, w_excite, act, image, w_project, gain, after):
    rows, cols, channels = image.shape
    expanded = act.shape[2]
    lines = 4
    bands = cols // SIDE
    block = lambda width: pl.BlockSpec((lines, cols, width), lambda r: (r, 0, 0))
    send = (stride * bands, rows // stride, SIDE, channels)
    return pl.pallas_call(
        functools.partial(mix_kernel, cells_total, stride, bands),
        grid=(rows // lines,),
        in_specs=[
            whole(parts.shape), whole(w_squeeze.shape), whole(w_excite.shape),
            block(expanded), block(channels), whole(w_project.shape), whole(gain.shape),
            pl.BlockSpec(memory_space=pl.ANY),
        ],
        out_specs=[
            whole((1, expanded)), whole((1, w_squeeze.shape[1])), whole((1, expanded)),
            block(channels), whole(send),
        ],
        out_shape=[
            jax.ShapeDtypeStruct((1, expanded), F32),
            jax.ShapeDtypeStruct((1, w_squeeze.shape[1]), F32),
            jax.ShapeDtypeStruct((1, expanded), F32),
            jax.ShapeDtypeStruct(image.shape, BF16),
            jax.ShapeDtypeStruct(send, BF16),
        ],
        compiler_params=SMALL,
        cost_estimate=estimate(5),
        name="mix",
    )(parts, w_squeeze, w_excite, act, image, w_project, gain, after)


def attention_kernel(
    members, heads, lines,
    arrived_ref, att_grad_ref, w_qkv_ref, bias_ref,
    x_ref, att_ref, grad_ref, packed_grad_ref, bias_out_ref,
    order_ref, packed_ref, bias_sum_ref,
):
    cells, channels = x_ref.shape
    groups = cells // members

    def places():
        for g in range(groups):
            for m in range(0, members, GRID):
                line, row = (m // GRID) % lines, m // GRID // lines
                start = (row * GRID * lines + line) * groups + g
                yield g * members + m, pl.ds(start, GRID, stride=lines * groups)

    for half in range(channels // LANES):
        lanes = slice(half * LANES, (half + 1) * LANES)
        order_ref[half] = arrived_ref[:, lanes].astype(F32)
        for g in range(groups):
            pieces = [order_ref[half, at, :] for k, at in places() if k // members == g]
            at = slice(g * members, (g + 1) * members)
            x_ref[at, lanes] = jnp.concatenate(pieces, axis=0).astype(BF16)
    dim = channels // heads
    per_half = LANES // dim
    halves = channels // LANES
    scale = dim ** (-0.5)
    packed_ref[...] = dot(x_ref[...], w_qkv_ref[...]).astype(BF16)
    bias_sum_ref[...] = jnp.zeros(bias_sum_ref.shape, F32)
    tall = per_half * members
    mask = (
        lax.broadcasted_iota(jnp.int32, (tall, LANES), 0) // members
        == lax.broadcasted_iota(jnp.int32, (tall, LANES), 1) // dim
    ).astype(F32).astype(BF16)
    owner = lax.broadcasted_iota(jnp.int32, (members, 2 * LANES), 1) % LANES // dim
    zero = jnp.zeros((members, LANES), BF16)

    def by_head(pair):
        return jnp.concatenate(
            [jnp.concatenate([v] * per_half, axis=0) * mask for v in pair], axis=1
        )

    def diagonal(pair):
        return jnp.concatenate(
            [
                jnp.concatenate([pair[0], zero], axis=1),
                jnp.concatenate([zero, pair[1]], axis=1),
            ],
            axis=0,
        )

    def collect(v):
        parts = [v[h * members : (h + 1) * members] for h in range(per_half)]
        picked = parts[-1]
        for h in range(per_half - 1):
            picked = jnp.where(owner == h, parts[h], picked)
        return [picked[:, :LANES], picked[:, LANES:]]

    def blocks(v):
        return [v[:members, :LANES], v[members:, LANES:]]

    def over_members(v, reduce):
        parted = v.reshape(per_half, members, 2 * members)
        small = reduce(parted, axis=1, keepdims=True)
        return jnp.broadcast_to(small, parted.shape).reshape(v.shape)

    def pair_step(g, carry):
        at = [pl.ds(pl.multiple_of((2 * g + k) * members, 16), members) for k in range(2)]
        for half in range(halves):
            def lanes(part):
                start = part * channels + half * LANES
                return slice(start, start + LANES)

            q, k, v = ([packed_ref[at[n], lanes(part)] for n in range(2)] for part in range(3))
            cot = [att_grad_ref[at[n], lanes(0)] for n in range(2)]
            q_diag, cot_diag = diagonal(q), diagonal(cot)
            k_tall, v_tall = by_head(k), by_head(v)
            scores = dot(k_tall, q_diag, ((1,), (1,))) * scale + bias_ref[half]
            grad_probs = dot(v_tall, cot_diag, ((1,), (1,)))
            lifted = jnp.exp(scores - over_members(scores, jnp.max))
            soft = lifted * (1.0 / over_members(lifted, jnp.sum))
            soft_low = soft.astype(BF16)
            grad_scores = soft * (grad_probs - over_members(grad_probs * soft, jnp.sum))
            bias_sum_ref[half] += grad_scores
            scaled = (grad_scores * scale).astype(BF16)
            attended = blocks(dot(soft_low, v_tall, ((0,), (0,))))
            grad_q = blocks(dot(scaled, k_tall, ((0,), (0,))))
            grad_v = collect(dot(soft_low, cot_diag))
            grad_k = collect(dot(scaled, q_diag))
            for n in range(2):
                att_ref[at[n], lanes(0)] = attended[n].astype(BF16)
                for part, value in enumerate((grad_q, grad_k, grad_v)):
                    packed_grad_ref[at[n], lanes(part)] = value[n].astype(BF16)
        return carry

    lax.fori_loop(0, cells // members // 2, pair_step, 0, unroll=2)
    grad = dot(packed_grad_ref[...], w_qkv_ref[...], ((1,), (1,)))
    for half in range(halves):
        lanes = slice(half * LANES, (half + 1) * LANES)
        for k, at in places():
            order_ref[half, at, :] = grad[k : k + GRID, lanes]
        grad_ref[:, lanes] = order_ref[half].astype(BF16)
    for half in range(halves):
        both = bias_sum_ref[half]
        bias_out_ref[half] = both[:, :members] + both[:, members:]


def run_attention(arrived, att_grad, w_qkv, bias_tall, heads, lines):
    cells, channels = att_grad.shape
    halves, tall, members2 = bias_tall.shape
    members = members2 // 2
    vmem = pl.BlockSpec(memory_space=pltpu.VMEM)
    return pl.pallas_call(
        functools.partial(attention_kernel, members, heads, lines),
        in_specs=[vmem] * 4,
        out_specs=[vmem] * 5,
        out_shape=[
            jax.ShapeDtypeStruct((cells, channels), BF16),
            jax.ShapeDtypeStruct((cells, channels), BF16),
            jax.ShapeDtypeStruct((cells, channels), BF16),
            jax.ShapeDtypeStruct((cells, 3 * channels), BF16),
            jax.ShapeDtypeStruct((halves, tall, members), F32),
        ],
        scratch_shapes=[
            pltpu.VMEM((channels // LANES, cells, LANES), F32),
            pltpu.VMEM((cells, 3 * channels), BF16),
            pltpu.VMEM(bias_tall.shape, F32),
        ],
        compiler_params=PARAMS,
        cost_estimate=estimate(14),
        name="attention",
    )(arrived.reshape(cells, channels), att_grad, w_qkv, bias_tall)


def attention_weights_kernel(x_ref, packed_grad_ref, att_ref, cot_ref, bias_ref, out_ref):
    channels = x_ref.shape[1]
    wide = 3 * channels
    out_ref[:, :wide] = dot(x_ref[...], packed_grad_ref[...], ((0,), (0,))).astype(BF16)
    out_ref[:, wide : wide + channels] = dot(att_ref[...], cot_ref[...], ((0,), (0,))).astype(BF16)
    halves, tall, members = bias_ref.shape
    for h in range(tall // members):
        rows = slice(h * members, (h + 1) * members)
        turned = jnp.concatenate([bias_ref[half, rows, :].T for half in range(halves)], axis=1)
        out_ref[rows, wide + channels :] = turned.astype(BF16)


def run_attention_weights(x, packed_grad, att, cot, bias):
    channels = x.shape[1]
    vmem = pl.BlockSpec(memory_space=pltpu.VMEM)
    width = 4 * channels + bias.shape[0] * bias.shape[2]
    return pl.pallas_call(
        attention_weights_kernel,
        in_specs=[vmem] * 5,
        out_specs=vmem,
        out_shape=jax.ShapeDtypeStruct((channels, width), BF16),
        compiler_params=PARAMS,
        cost_estimate=estimate(5),
        name="attention_weights",
    )(x, packed_grad, att, cot, bias)


def mixed_back_kernel(
    stride, bands,
    recv_ref, mixed_ref, cot_ref, gain_ref, act_ref, gate_ref, w_projt_ref,
    grad_ref, low_ref, norm_ref, project_ref, gate_grad_ref,
    turned_ref, total_ref,
):
    rows, cols, channels = mixed_ref.shape

    @pl.when(pl.program_id(0) == 0)
    def _():
        gain = gain_ref[...].astype(F32)
        lines = 4

        def some_rows(c, total):
            pieces = []
            for k in range(lines):
                i = c * lines + k
                a, p = lax.rem(i, stride), i // stride
                pieces += [recv_ref[a * bands + band, p] for band in range(bands)]
            grad = jnp.concatenate(pieces, axis=0).astype(F32)
            at = pl.ds(c * lines, lines)
            flat = lambda ref: ref[at].reshape(lines * cols, channels).astype(F32)
            unit, rstd = norm_rows(flat(mixed_ref))
            back = flat(cot_ref) + norm_rows_back(unit, rstd, gain, grad)
            grad_ref[at] = back.reshape(lines, cols, channels)
            low_ref[at] = back.astype(BF16).reshape(lines, cols, channels)
            return total + fold_rows(grad * unit)

        total = lax.fori_loop(
            0, rows // lines, some_rows, jnp.zeros((8, channels), F32), unroll=2
        )
        norm_ref[...] = jnp.sum(total, axis=0, keepdims=True)
        turned_ref[...] = low_ref[...].reshape(rows * cols, channels).T

    flat = act_ref[...].reshape(rows * cols, BLOCK)
    product = dot(turned_ref[...], flat)
    total = jnp.sum(product * w_projt_ref[...].astype(F32), axis=0, keepdims=True)
    step, steps = pl.program_id(0), pl.num_programs(0)
    total_ref[step] = total
    project_ref[...] = (product * gate_ref[...]).T.astype(BF16)

    @pl.when(step == steps - 1)
    def _():
        sums = [total_ref[e] for e in range(total_ref.shape[0])]
        high = [v.astype(BF16).astype(F32) for v in sums]
        terms = jnp.concatenate(high + [v - w for v, w in zip(sums, high)], axis=0)
        gate_grad_ref[...] = jnp.broadcast_to(terms.astype(BF16)[None], gate_grad_ref.shape)


def run_mixed_back(count, stride, recv, mixed, cot, gain, act, gate, w_project_t):
    rows, cols, channels = mixed.shape
    expanded = act.shape[2]
    return pl.pallas_call(
        functools.partial(mixed_back_kernel, stride, cols // SIDE),
        grid=(expanded // BLOCK,),
        in_specs=[
            whole(recv.shape), whole(mixed.shape), whole(cot.shape), whole(gain.shape),
            last_block(act.shape), last_block(gate.shape), last_block(w_project_t.shape),
        ],
        out_specs=[
            whole(mixed.shape), whole(mixed.shape), whole((1, channels)),
            last_block((BLOCK, expanded)), whole((count, 2 * expanded // BLOCK, BLOCK)),
        ],
        out_shape=[
            jax.ShapeDtypeStruct(mixed.shape, F32),
            jax.ShapeDtypeStruct(mixed.shape, BF16),
            jax.ShapeDtypeStruct((1, channels), F32),
            jax.ShapeDtypeStruct((BLOCK, expanded), BF16),
            jax.ShapeDtypeStruct((count, 2 * expanded // BLOCK, BLOCK), BF16),
        ],
        scratch_shapes=[
            pltpu.VMEM((channels, rows * cols), BF16),
            pltpu.VMEM((expanded // BLOCK, 1, BLOCK), F32),
        ],
        compiler_params=PARAMS,
        cost_estimate=estimate(7),
        name="mixed_back",
    )(recv, mixed, cot, gain, act, gate, w_project_t)


def unpack_kernel(
    place_ref, near_ref, far_ref, expand_ref, depth_ref, norm0_ref, norm1_ref, tail_ref
):
    expanded = expand_ref.shape[2]
    for pair, source in enumerate((near_ref, far_ref)):
        at = lax.rem(place_ref[0] + pair, 2)
        expand_ref[at] = source[:, :expanded].astype(F32)
        tail_ref[at] = source[:, expanded:].astype(F32)
    tail = tail_ref[0]
    pieces = expanded // LANES
    for t in range(9):
        for k in range(pieces):
            row = t * pieces + k
            lanes = slice(k * LANES, (k + 1) * LANES)
            depth_ref[t // 3, t % 3 : t % 3 + 1, lanes] = tail[row : row + 1]
    start = 9 * pieces
    half = norm0_ref.shape[1] // LANES
    for k in range(half):
        lanes = slice(k * LANES, (k + 1) * LANES)
        norm0_ref[:, lanes] = tail[start + k : start + k + 1]
        norm1_ref[:, lanes] = tail[start + half + k : start + half + k + 1]


def run_unpack(near, far, expanded):
    rows = near.shape[0]
    channels = 2 * rows
    place = (lax.axis_index("col") % 2).astype(jnp.int32).reshape(1)
    vmem = pl.BlockSpec(memory_space=pltpu.VMEM)
    return pl.pallas_call(
        unpack_kernel,
        in_specs=[pl.BlockSpec(memory_space=pltpu.SMEM), vmem, vmem],
        out_specs=[vmem] * 4,
        out_shape=[
            jax.ShapeDtypeStruct((2, rows, expanded), F32),
            jax.ShapeDtypeStruct((3, 3, expanded), F32),
            jax.ShapeDtypeStruct((1, channels), F32),
            jax.ShapeDtypeStruct((1, channels), F32),
        ],
        scratch_shapes=[pltpu.VMEM((2, rows, near.shape[1] - expanded), F32)],
        compiler_params=SMALL,
        cost_estimate=estimate(2),
        name="unpack",
    )(place, near, far)


def expand_back_kernel(
    cells_total,
    parts_ref, hidden_ref, gate_all_ref, w_sq_ref, w_ex_ref,
    low_ref, up_ref, down_ref, side_ref, w_projt_ref, gate_ref, slope_ref, side_slope_ref,
    spread_slope_ref, spread_ref, w_dep_ref, turned_ref, w_exp_ref, gain_ref, norm1_ref,
    weights_ref, first_ref, logit_ref, pre_ref,
    main_ref, side_grad_ref, window_ref, expanded_ref, pool_ref, tail_ref, norm_ref,
):
    rows, cols, channels = low_ref.shape
    side = 8
    wide = cols + side
    step = pl.program_id(0)
    steps = pl.num_programs(0)

    @pl.when(step == 0)
    def _():
        gate = gate_all_ref[...]
        blocks = pool_ref.shape[0]
        terms = jnp.sum(parts_ref[...].astype(F32), axis=0)
        gate_grad = jnp.concatenate(
            [terms[e : e + 1] + terms[blocks + e : blocks + e + 1] for e in range(blocks)], axis=1
        )
        logit = gate_grad * gate * (1.0 - gate)
        hidden = hidden_ref[...]
        sig = jax.nn.sigmoid(hidden)
        pre = dot_exact(logit, w_ex_ref[...].astype(F32), ((1,), (1,))) * (
            sig + hidden * sig * (1.0 - sig)
        )
        logit_ref[...] = logit
        pre_ref[...] = pre
        pooled = dot_exact(pre, w_sq_ref[...].astype(F32), ((1,), (1,))) / cells_total
        for e in range(blocks):
            pool_ref[e] = pooled[:, e * BLOCK : (e + 1) * BLOCK]
        first_ref[...] = jnp.zeros(first_ref.shape, F32)
        tail_ref[...] = jnp.zeros(tail_ref.shape, F32)
        norm_ref[...] = jnp.zeros(norm_ref.shape, F32)

    w_projt = w_projt_ref[...]
    main_ref[pl.ds(0, cols), :] = dot(up_ref[0], w_projt)
    main_ref[pl.ds(cols, rows * cols), :] = dot(
        low_ref[...].reshape(rows * cols, channels), w_projt
    )
    main_ref[pl.ds((rows + 1) * cols, cols), :] = dot(down_ref[0], w_projt)
    side_grad_ref[...] = dot(side_ref[...], w_projt)

    @pl.loop(0, rows + 2, unroll=3)
    def _(i):
        for h in range(BLOCK // LANES):
            lanes = slice(h * LANES, (h + 1) * LANES)
            gate = gate_ref[:, lanes]
            pooled = pool_ref[step][:, lanes]
            gated = main_ref[pl.ds(pl.multiple_of(i * cols, 16), cols), lanes]
            main = (gated * gate + pooled) * slope_ref[i, :, lanes].astype(F32)
            gated = side_grad_ref[pl.ds(pl.multiple_of(i * side, side), side), lanes]
            edge = (gated * gate + pooled) * side_slope_ref[i, :, lanes]
            grad = jnp.concatenate([main, edge], axis=0)
            window_ref[0, i, :, lanes] = pltpu.roll(grad, wide - 1, 0)[:cols]
            window_ref[1, i, :, lanes] = grad[:cols]
            window_ref[2, i, :, lanes] = pltpu.roll(grad, 1, 0)[:cols]

    for h in range(BLOCK // LANES):
        lanes = slice(h * LANES, (h + 1) * LANES)
        taps = w_dep_ref[:, :, lanes].astype(F32)

        def back_row(i, sums):
            spread = spread_ref[i, :, lanes].astype(F32)
            total = jnp.zeros((cols, LANES), F32)
            new_sums = []
            for a in range(3):
                for b in range(3):
                    window = window_ref[b, i + 2 - a, :, lanes]
                    total = total + window * taps[a, b : b + 1]
                    new_sums.append(sums[a * 3 + b] + fold_rows(window * spread))
            grad = total * spread_slope_ref[i, :, lanes].astype(F32)
            expanded_ref[pl.ds(pl.multiple_of(i * cols, 16), cols), lanes] = grad.astype(BF16)
            return tuple(new_sums)

        sums = lax.fori_loop(0, rows, back_row, (jnp.zeros((8, LANES), F32),) * 9, unroll=2)
        for t in range(9):
            row = t * (steps * BLOCK // LANES) + step * (BLOCK // LANES) + h
            tail_ref[pl.ds(row, 1), :] = jnp.sum(sums[t], axis=0, keepdims=True)

    grad_expanded = expanded_ref[...]
    w_exp = w_exp_ref[...]
    weights = dot(turned_ref[...], grad_expanded)
    weights_ref[:, pl.ds(pl.multiple_of(step * BLOCK, BLOCK), BLOCK)] = weights.astype(BF16)
    norm_ref[...] += jnp.sum(weights * w_exp.astype(F32), axis=1, keepdims=True)
    first_ref[...] += dot(grad_expanded, w_exp, ((1,), (1,)))

    @pl.when(step == steps - 1)
    def _():
        norm = norm_ref[...].T[0:1] / gain_ref[...].astype(F32)
        start = 9 * steps * (BLOCK // LANES)
        for k in range(channels // LANES):
            piece = slice(k * LANES, (k + 1) * LANES)
            tail_ref[start + k : start + k + 1, :] = norm[:, piece]
            at = start + channels // LANES + k
            tail_ref[at : at + 1, :] = norm1_ref[:, piece]
        weights_ref[:, steps * BLOCK :] = tail_ref[...].astype(BF16)


def run_expand_back(
    cells_total, parts, hidden, gate, w_squeeze, w_excite, low, up, down, side,
    w_project_t, slope, side_slope, spread_slope, spread, w_depth, turned, w_expand, gain, norm1,
):
    rows, cols, channels = low.shape
    expanded = w_expand.shape[1]
    steps = expanded // BLOCK
    return pl.pallas_call(
        functools.partial(expand_back_kernel, cells_total),
        grid=(steps,),
        in_specs=[
            pl.BlockSpec(
                (parts.shape[0], 2 * steps, BLOCK), lambda e: (0, parts.shape[1] // (2 * steps) - 1, 0)
            ),
            whole(hidden.shape), whole(gate.shape),
            whole(w_squeeze.shape), whole(w_excite.shape),
            whole(low.shape), whole(up.shape), whole(down.shape), whole(side.shape),
            last_block(w_project_t.shape), last_block(gate.shape), last_block(slope.shape),
            last_block(side_slope.shape), last_block(spread_slope.shape), last_block(spread.shape),
            last_block(w_depth.shape), whole(turned.shape), last_block(w_expand.shape),
            whole(gain.shape), whole(norm1.shape),
        ],
        out_specs=[
            whole((channels, expanded + LANES)), whole((rows * cols, channels)),
            whole((1, expanded)), whole(hidden.shape),
        ],
        out_shape=[
            jax.ShapeDtypeStruct((channels, expanded + LANES), BF16),
            jax.ShapeDtypeStruct((rows * cols, channels), F32),
            jax.ShapeDtypeStruct((1, expanded), F32),
            jax.ShapeDtypeStruct(hidden.shape, F32),
        ],
        scratch_shapes=[
            pltpu.VMEM(((rows + 2) * cols, BLOCK), F32),
            pltpu.VMEM(((rows + 2) * 8, BLOCK), F32),
            pltpu.VMEM((3, rows + 2, cols, BLOCK), F32),
            pltpu.VMEM((rows * cols, BLOCK), BF16),
            pltpu.VMEM((steps, 1, BLOCK), F32),
            pltpu.VMEM((channels, LANES), F32),
            pltpu.VMEM((channels, LANES), F32),
        ],
        compiler_params=PARAMS,
        cost_estimate=estimate(14),
        name="expand_back",
    )(
        parts, hidden, gate, w_squeeze, w_excite, low, up, down, side, w_project_t, gate,
        slope, side_slope, spread_slope, spread, w_depth, turned, w_expand, gain, norm1,
    )


def image_back_kernel(image_ref, gain_ref, first_ref, mixed_ref, out_ref):
    unit, rstd = norm_rows(image_ref[...].astype(F32))
    grad = first_ref[...]
    back = mixed_ref[...] + norm_rows_back(unit, rstd, gain_ref[...].astype(F32), grad)
    out_ref[...] = back.astype(BF16)


def run_image_back(image, gain, first, mixed):
    cells, channels = image.shape
    block = pl.BlockSpec((cells // 4, channels), lambda r: (r, 0))
    return pl.pallas_call(
        image_back_kernel,
        grid=(4,),
        in_specs=[block, whole(gain.shape), block, block],
        out_specs=block,
        out_shape=jax.ShapeDtypeStruct((cells, channels), BF16),
        compiler_params=SMALL,
        cost_estimate=estimate(4),
        name="image_back",
    )(image, gain, first, mixed)


def shift(cells, axis, step):
    count = lax.axis_size(axis)
    pairs = [(i, i + step) for i in range(count) if 0 <= i + step < count]
    return lax.ppermute(cells, axis, pairs)


def halo_rows(cells, width):
    up = shift(cells[cells.shape[0] - width :], "row", 1)
    down = shift(cells[:width], "row", -1)
    return up, down


def halo_sides(cells, up, down, width):
    rows, cols, channels = cells.shape
    first = jnp.concatenate([up[:, :width], cells[:, :width], down[:, :width]], axis=0)
    last = jnp.concatenate(
        [up[:, cols - width :], cells[:, cols - width :], down[:, cols - width :]], axis=0
    )
    left = shift(last, "col", 1)
    right = shift(first, "col", -1)
    gap = jnp.zeros((rows + 2 * width, 8 - 2 * width, channels), cells.dtype)
    side = jnp.concatenate([right, gap, left], axis=1)
    return side.reshape(-1, channels)


def hand_around(blocks):
    return lax.all_to_all(blocks, AXES, split_axis=0, concat_axis=0, tiled=True)


def sum_steps():
    return [("col", 1, 2), ("row", 1, lax.axis_size("row")), ("col", 2, lax.axis_size("col") // 2)]


def send_on(v, axis, stride, size, k):
    pairs = []
    for i in range(lax.axis_size(axis)):
        place = i // stride % size
        pairs.append((i, i + ((place + k) % size - place) * stride))
    return lax.ppermute(v, axis, pairs)


def sum_parts(matrix, axis, stride, size):
    place = lax.axis_index(axis) // stride % size
    parts = matrix.reshape(size, matrix.shape[0] // size, matrix.shape[1])
    part = lambda i: lax.dynamic_index_in_dim(parts, i % size, 0, False)
    total = part(place).astype(F32)
    for k in range(1, size):
        total = total + send_on(part(place + k), axis, stride, size, k).astype(F32)
    return total.astype(BF16)


def sum_shares(matrix):
    rows, columns = matrix.shape
    count = lax.axis_size("row") * lax.axis_size("col")
    pair = ("col", 1, 2)
    half = sum_parts(matrix, *pair)
    same_core = [list(range(k, count, 2)) for k in range(2)]

    def around(blocks):
        return lax.all_to_all(
            blocks, AXES, split_axis=0, concat_axis=0, tiled=True, axis_index_groups=same_core
        )

    arrived = around(half.reshape(count // 2, rows // count, columns))
    total = jnp.sum(arrived.astype(F32), axis=0).astype(BF16)
    sent = jnp.broadcast_to(total[None], (count // 2,) + total.shape)
    gathered = around(sent).reshape(rows // 2, columns)
    return gathered, send_on(gathered, *pair, 1)


def stack_kernel(*refs):
    for k, ref in enumerate(refs[:-1]):
        refs[-1][k] = ref[...]


def join_parts(blocks, axis, stride, size):
    arrived = [blocks] + [send_on(blocks, axis, stride, size, k) for k in range(1, size)]
    vmem = pl.BlockSpec(memory_space=pltpu.VMEM)
    stacked = pl.pallas_call(
        stack_kernel,
        in_specs=[vmem] * size,
        out_specs=vmem,
        out_shape=jax.ShapeDtypeStruct((size,) + blocks.shape, blocks.dtype),
        compiler_params=SMALL,
        cost_estimate=estimate(1),
        name="stack",
    )(*arrived)
    return stacked.reshape((size * blocks.shape[0],) + blocks.shape[1:])


def unpack_weights_kernel(
    sizes, places_ref, near_ref, far_ref, qkv_ref, out_ref, bias_ref, project_ref
):
    channels = out_ref.shape[2]
    halves, members = bias_ref.shape[0], bias_ref.shape[3]
    cuts = (0, 3 * channels, 4 * channels, 4 * channels + halves * members)
    pairs, over_row, rest = sizes
    for pair, source in enumerate((near_ref, far_ref)):
        for r in range(over_row):
            for c in range(rest):
                block = source[r * rest + c].astype(F32)
                at = lax.rem(places_ref[0] + pairs - pair, pairs)
                at = at * over_row + lax.rem(places_ref[1] + over_row - r, over_row)
                at = at * rest + lax.rem(places_ref[2] + rest - c, rest)
                qkv_ref[at] = block[:, : cuts[1]]
                out_ref[at] = block[:, cuts[1] : cuts[2]]
                for half in range(halves):
                    start = cuts[2] + half * members
                    bias_ref[half, at] = block[:, start : start + members]
                for e in range(project_ref.shape[0]):
                    start = cuts[3] + e * channels
                    project_ref[e, at] = block[:, start : start + channels]


def run_unpack_weights(steps, near, far, channels, expanded, halves, members):
    count, rows, _ = near.shape
    count *= 2
    places = jnp.stack([lax.axis_index(axis) // stride % size for axis, stride, size in steps])
    vmem = pl.BlockSpec(memory_space=pltpu.VMEM)
    blocks = lambda width: jax.ShapeDtypeStruct((count, rows, width), F32)
    return pl.pallas_call(
        functools.partial(unpack_weights_kernel, tuple(size for _, _, size in steps)),
        in_specs=[pl.BlockSpec(memory_space=pltpu.SMEM), vmem, vmem],
        out_specs=[vmem] * 4,
        out_shape=[
            blocks(3 * channels), blocks(channels),
            jax.ShapeDtypeStruct((halves, count, rows, members), F32),
            jax.ShapeDtypeStruct((expanded // BLOCK, count, rows, channels), F32),
        ],
        compiler_params=SMALL,
        cost_estimate=estimate(2),
        name="unpack_weights",
    )(places.astype(jnp.int32), near, far)


def swap_groups(blocks, parity):
    groups = None
    if parity > 1:
        over_row = lax.axis_size("row")
        over_col = lax.axis_size("col")
        groups = [
            [r * over_col + c for r in range(over_row) for c in range(k, over_col, parity)]
            for k in range(parity)
        ]
    return lax.all_to_all(
        blocks, AXES, split_axis=0, concat_axis=0, tiled=True, axis_index_groups=groups
    )


def on_device(
    image, out_cotangent, norm0_gain, w_expand, w_depth, w_squeeze, w_excite, w_project,
    norm1_gain, w_qkv, w_out, attn_bias,
):
    rows, cols, channels = image.shape
    over_row = lax.axis_size("row")
    over_col = lax.axis_size("col")
    count = over_row * over_col
    cells_total = rows * cols * count
    stride = rows * over_row // GRID
    parity = over_col // GRID
    lines = rows // stride
    bands = cols // SIDE
    members = GRID * GRID
    expanded = w_expand.shape[1]

    def into_members(arrived):
        parted = arrived.reshape(over_row, GRID, lines, SIDE, channels)
        return parted.transpose(3, 0, 2, 1, 4).reshape(SIDE * members, channels)

    def out_of_members(values):
        parted = values.reshape(SIDE, over_row, lines, GRID, channels)
        return parted.transpose(1, 3, 2, 0, 4).reshape(-1, lines, SIDE, channels)

    row, col = lax.axis_index("row"), lax.axis_index("col")
    flags = jnp.stack([row > 0, row < over_row - 1, col > 0, col < over_col - 1]).astype(F32)
    gain_first = norm0_gain.reshape(1, channels)
    gain_second = norm1_gain.reshape(1, channels)
    w_project_t = w_project.T
    heads = attn_bias.shape[0]
    halves = channels // LANES
    bias_tall = attn_bias.transpose(0, 2, 1).reshape(halves, heads // halves * members, members)
    bias_tall = jnp.concatenate([bias_tall, bias_tall], axis=2)

    up, down = halo_rows(image, 2)
    normed_first, turned_first, spread, spread_slope = run_expand(image, gain_first, w_expand)
    up, down, spread = lax.optimization_barrier((up, down, spread))
    side = halo_sides(image, up, down, 2)
    cot_sent = (
        out_cotangent.reshape(lines, stride, bands, SIDE, channels)
        .transpose(1, 2, 0, 3, 4)
        .reshape(stride * bands, lines, SIDE, channels)
    )
    cot_members = into_members(swap_groups(cot_sent, parity))
    ring, act, pool = run_depthwise(count, up, down, side, gain_first, w_expand, w_depth, spread)
    pooled, hidden, gate, mixed, normed_sent = run_mix(
        cells_total, stride, hand_around(pool), w_squeeze, w_excite, act, image, w_project,
        gain_second, cot_members,
    )
    slope, side_slope = run_slope(flags, ring, w_depth, spread)
    normed_arrived = swap_groups(normed_sent, parity)
    att_grad = dot(cot_members, w_out, ((1,), (1,))).astype(BF16)
    normed_arrived, slope, att_grad = lax.optimization_barrier((normed_arrived, slope, att_grad))
    normed_members, attended, grad_normed, packed_grad, grad_bias = run_attention(
        normed_arrived, att_grad, w_qkv, bias_tall, heads, lines
    )
    grad_normed_home = swap_groups(grad_normed.reshape(normed_sent.shape), parity)
    weights = run_attention_weights(normed_members, packed_grad, attended, cot_members, grad_bias)
    grad_normed_home, weights = lax.optimization_barrier((grad_normed_home, weights))
    grad_mixed, grad_low, grad_norm1, grad_project, gate_grad = run_mixed_back(
        count, stride, grad_normed_home, mixed, out_cotangent, gain_second, act, gate, w_project_t
    )
    attended_sent = out_of_members(attended)
    if parity == 1:
        both = hand_around(
            jnp.concatenate([attended_sent.reshape(count, -1, channels), gate_grad], axis=1)
        )
        parts = both
        attended_home = both[:, : lines * SIDE].reshape(attended_sent.shape)
    else:
        parts = hand_around(gate_grad)
        attended_home = swap_groups(attended_sent, parity)
    up, down = halo_rows(grad_low, 1)
    side = halo_sides(grad_low, up, down, 1)
    weights = jnp.concatenate([weights, grad_project], axis=1)
    weights, _ = lax.optimization_barrier((weights, up))
    steps = sum_steps()
    for step in steps:
        weights = sum_parts(weights, *step)
    late, grad_first, logit, pre = run_expand_back(
        cells_total, parts, hidden, gate, w_squeeze, w_excite, grad_low, up, down, side,
        w_project_t, slope, side_slope, spread_slope, spread, w_depth, turned_first, w_expand,
        gain_first, grad_norm1,
    )
    weights, _ = lax.optimization_barrier((weights, late))
    weights = weights[None]
    for step in steps[:0:-1]:
        weights = join_parts(weights, *step)
    other = send_on(weights, *steps[0], 1)
    grad_qkv, grad_out_proj, grad_bias, grad_project = run_unpack_weights(
        steps, weights, other, channels, expanded, halves, members
    )
    grad_expand, grad_depth, grad_norm0, grad_norm1 = run_unpack(*sum_shares(late), expanded)
    grad_image = run_image_back(
        image.reshape(-1, channels), gain_first, grad_first, grad_mixed.reshape(-1, channels)
    )
    attended_map = (
        attended_home.reshape(stride, bands, lines, SIDE, channels)
        .transpose(2, 0, 1, 3, 4)
        .reshape(rows * cols, channels)
    )
    block_out = (mixed.reshape(-1, channels).astype(F32) + dot(attended_map, w_out)).astype(BF16)

    silu = jax.nn.silu(hidden)
    grad_squeeze = pooled.reshape(expanded, 1) * pre
    grad_excite = silu.reshape(-1, 1) * logit

    return (
        block_out.reshape(image.shape),
        grad_image.reshape(image.shape),
        grad_norm0[0],
        grad_expand.reshape(w_expand.shape),
        grad_depth,
        grad_squeeze,
        grad_excite,
        grad_project.reshape(w_project.shape),
        grad_norm1[0],
        grad_qkv.reshape(w_qkv.shape),
        grad_out_proj.reshape(w_out.shape),
        grad_bias.reshape(attn_bias.shape),
    )


def solution(mesh):
    cells = P("row", "col", None)
    return jax.shard_map(
        on_device,
        mesh=mesh,
        in_specs=(cells, cells) + (P(),) * 10,
        out_specs=(cells, cells) + (P(),) * 10,
        check_vma=False,
    )
```

```python
import functools
import math

import jax
import jax.numpy as jnp
from jax import lax
from jax.experimental import pallas as pl
from jax.experimental.pallas import tpu as pltpu
from jax.sharding import PartitionSpec as P

GRID = 8
AXES = ("row", "col")
BLOCK = 256
LANES = 128
SIDE = 16
GELU_A = math.sqrt(2.0 / math.pi)
GELU_B = GELU_A * 0.044715
F32 = jnp.float32
BF16 = jnp.bfloat16
PARAMS = pltpu.CompilerParams(vmem_limit_bytes=56 * 1024 * 1024)
SMALL = pltpu.CompilerParams(vmem_limit_bytes=24 * 1024 * 1024)


def estimate(us):
    return pl.CostEstimate(flops=int(us * 1.1e9), bytes_accessed=int(us * 3.6e6), transcendentals=0)


def dot(left, right, contract=((1,), (0,))):
    return lax.dot_general(left, right, (contract, ((), ())), preferred_element_type=F32)


def dot_exact(vector, right, contract):
    tall = jnp.broadcast_to(vector, (8, vector.shape[1]))
    product = lax.dot_general(
        tall, right, (contract, ((), ())), precision=lax.Precision.HIGHEST, preferred_element_type=F32
    )
    return product[0:1]


def gelu_and_slope(x, with_slope=True):
    square = x * x
    t = jnp.tanh(x * (GELU_A + GELU_B * square))
    half = 0.5 + 0.5 * t
    value = x * half
    if not with_slope:
        return value, None
    slope = half + (value * (1.0 - t)) * (GELU_A + (3.0 * GELU_B) * square)
    return value, slope


def norm_rows(x):
    average = jnp.mean(x, axis=-1, keepdims=True)
    centered = x - average
    variance = jnp.mean(centered * centered, axis=-1, keepdims=True)
    rstd = lax.rsqrt(variance + 1e-05)
    return centered * rstd, rstd


def norm_rows_back(unit, rstd, gain, grad):
    unit_grad = grad * gain
    first = jnp.mean(unit_grad, axis=-1, keepdims=True)
    second = jnp.mean(unit_grad * unit, axis=-1, keepdims=True)
    return rstd * (unit_grad - first - unit * second)


def fold_rows(x):
    return jnp.sum(x.reshape(x.shape[0] // 8, 8, x.shape[1]), axis=0)


def whole(shape):
    return pl.BlockSpec(shape, lambda e: (0,) * len(shape))


def last_block(shape):
    lead = (0,) * (len(shape) - 1)
    return pl.BlockSpec(shape[:-1] + (BLOCK,), lambda e: lead + (e,))


def expand_kernel(
    image_ref, gain_ref, w_exp_ref,
    normed_ref, spread_ref, pre_ref,
    expanded_ref,
):
    rows, cols, channels = image_ref.shape

    @pl.when(pl.program_id(0) == 0)
    def _():
        gain = gain_ref[...].astype(F32)

        @pl.loop(0, rows // 4)
        def _(c):
            flat = image_ref[pl.ds(c * 4, 4)].reshape(4 * cols, channels)
            unit, _ = norm_rows(flat.astype(F32))
            at = pl.ds(pl.multiple_of(c * 4 * cols, 16), 4 * cols)
            normed_ref[at, :] = (unit * gain).astype(BF16)

    expanded_ref[...] = dot(normed_ref[...], w_exp_ref[...])

    @pl.loop(0, rows, unroll=4)
    def _(r):
        for h in range(BLOCK // LANES):
            lanes = slice(h * LANES, (h + 1) * LANES)
            x = expanded_ref[pl.ds(pl.multiple_of(r * cols, 16), cols), lanes]
            value, _ = gelu_and_slope(x, False)
            spread_ref[r, :, lanes] = value.astype(BF16)
            pre_ref[r, :, lanes] = x.astype(BF16)


def run_expand(image, gain, w_expand):
    rows, cols, channels = image.shape
    expanded = w_expand.shape[1]
    return pl.pallas_call(
        expand_kernel,
        grid=(expanded // BLOCK,),
        in_specs=[whole(image.shape), whole(gain.shape), last_block(w_expand.shape)],
        out_specs=[
            whole((rows * cols, channels)),
            last_block((rows, cols, expanded)), last_block((rows, cols, expanded)),
        ],
        out_shape=[
            jax.ShapeDtypeStruct((rows * cols, channels), BF16),
            jax.ShapeDtypeStruct((rows, cols, expanded), BF16),
            jax.ShapeDtypeStruct((rows, cols, expanded), BF16),
        ],
        scratch_shapes=[pltpu.VMEM((rows * cols, BLOCK), F32)],
        compiler_params=PARAMS,
        cost_estimate=estimate(14),
        name="expand",
    )(image, gain, w_expand)


def depthwise_kernel(
    up_ref, down_ref, side_ref, gain_ref, w_exp_ref, w_dep_ref, spread_ref,
    ring_ref, act_ref, pool_ref,
    ring_normed_ref, ring_wide_ref,
):
    rows, cols, _ = spread_ref.shape
    channels = up_ref.shape[2]
    over = 4 * cols
    side = 8

    @pl.when(pl.program_id(0) == 0)
    def _():
        gain = gain_ref[...].astype(F32)

        def put(at, values):
            unit, _ = norm_rows(values.astype(F32))
            ring_normed_ref[at : at + values.shape[0], :] = (unit * gain).astype(BF16)

        put(0, up_ref[...].reshape(2 * cols, channels))
        put(2 * cols, down_ref[...].reshape(2 * cols, channels))
        put(over, side_ref[...])

    ring_wide_ref[...] = dot(ring_normed_ref[...], w_exp_ref[...])
    tile = 32

    @pl.loop(0, ring_wide_ref.shape[0] // tile, unroll=True)
    def _(t):
        at = pl.ds(pl.multiple_of(t * tile, tile), tile)
        value, _ = gelu_and_slope(ring_wide_ref[at, :], False)
        low = value.astype(BF16)
        ring_ref[at, :] = low
        ring_wide_ref[at, :] = low.astype(F32)

    for h in range(BLOCK // LANES):
        lanes = slice(h * LANES, (h + 1) * LANES)
        taps = w_dep_ref[:, :, lanes].astype(F32)
        w = [[taps[a, b : b + 1] for b in range(3)] for a in range(3)]

        def line(r, main):
            at = pl.multiple_of(over + (r + 2) * side, side)
            return jnp.concatenate([main, ring_wide_ref[pl.ds(at, side), lanes]], axis=0)

        def conv(i, x, total):
            u = [x[0] * w[0][b] + x[1] * w[1][b] + x[2] * w[2][b] for b in range(3)]
            wide = cols + side
            pre = pltpu.roll(u[0], 1, 0) + u[1] + pltpu.roll(u[2], wide - 1, 0)
            value, _ = gelu_and_slope(pre[:cols], False)
            act_ref[i, :, lanes] = value.astype(BF16)
            return total + fold_rows(value)

        def step(i, carry):
            first, second, total = carry
            third = line(i + 1, spread_ref[i + 1, :, lanes].astype(F32))
            return second, third, conv(i, (first, second, third), total)

        carry = (
            line(-1, ring_wide_ref[cols : 2 * cols, lanes]),
            line(0, spread_ref[0, :, lanes].astype(F32)),
            jnp.zeros((8, LANES), F32),
        )
        first, second, total = lax.fori_loop(0, rows - 1, step, carry, unroll=5)
        third = line(rows, ring_wide_ref[2 * cols : 3 * cols, lanes])
        total = conv(rows - 1, (first, second, third), total)
        total = jnp.sum(total, axis=0, keepdims=True)
        pool_ref[:, :, lanes] = jnp.broadcast_to(total[None], (pool_ref.shape[0], 1, LANES))


def run_depthwise(count, up, down, side, gain, w_expand, w_depth, spread):
    rows, cols, expanded = spread.shape
    channels = up.shape[2]
    ring = 4 * cols + 8 * (rows + 4)
    return pl.pallas_call(
        depthwise_kernel,
        grid=(expanded // BLOCK,),
        in_specs=[
            whole(up.shape), whole(down.shape), whole(side.shape), whole(gain.shape),
            last_block(w_expand.shape), last_block(w_depth.shape), last_block(spread.shape),
        ],
        out_specs=[
            last_block((ring, expanded)), last_block(spread.shape), last_block((count, 1, expanded)),
        ],
        out_shape=[
            jax.ShapeDtypeStruct((ring, expanded), BF16),
            jax.ShapeDtypeStruct(spread.shape, BF16),
            jax.ShapeDtypeStruct((count, 1, expanded), F32),
        ],
        scratch_shapes=[pltpu.VMEM((ring, channels), BF16), pltpu.VMEM((ring, BLOCK), F32)],
        compiler_params=PARAMS,
        cost_estimate=estimate(1),
        name="depthwise",
    )(up, down, side, gain, w_expand, w_depth, spread)


def slope_kernel(
    flags_ref, ring_ref, w_dep_ref, spread_ref, pre_ref, normed_ref,
    main_ref, side_out_ref, spread_slope_ref, turned_ref, wide_ref,
):
    rows, cols, _ = spread_ref.shape

    @pl.when(pl.program_id(0) == 0)
    def _():
        turned_ref[...] = normed_ref[...].T

    @pl.loop(0, rows, unroll=4)
    def _(r):
        for h in range(BLOCK // LANES):
            lanes = slice(h * LANES, (h + 1) * LANES)
            _, slope = gelu_and_slope(pre_ref[r, :, lanes].astype(F32))
            spread_slope_ref[r, :, lanes] = slope.astype(BF16)

    over = 4 * cols
    side = 8
    wide = cols + side

    for k, r in enumerate((0, 1, rows + 2, rows + 3)):
        wide_ref[r, :cols, :] = ring_ref[k * cols : (k + 1) * cols, :].astype(F32)
    sides = ring_ref[over:, :].astype(F32)
    for r in range(rows + 4):
        wide_ref[r, cols:, :] = sides[r * side : (r + 1) * side]

    @pl.loop(0, rows)
    def _(r):
        wide_ref[r + 2, :cols, :] = spread_ref[r].astype(F32)

    place = lax.broadcasted_iota(jnp.int32, (side, LANES), 0)
    side_mask = jnp.where(
        place == side - 1, flags_ref[2], jnp.where(place == 0, flags_ref[3], 1.0)
    ).astype(F32)

    @pl.loop(0, rows + 2)
    def _(i):
        keep = jnp.where(i == 0, flags_ref[0], jnp.where(i == rows + 1, flags_ref[1], 1.0))
        for h in range(BLOCK // LANES):
            lanes = slice(h * LANES, (h + 1) * LANES)
            taps = w_dep_ref[:, :, lanes].astype(F32)
            x = [wide_ref[i + a, :, lanes] for a in range(3)]
            u = [sum(x[a] * taps[a, b : b + 1] for a in range(3)) for b in range(3)]
            pre = pltpu.roll(u[0], 1, 0) + u[1] + pltpu.roll(u[2], wide - 1, 0)
            _, slope = gelu_and_slope(pre)
            slope = slope * keep
            main_ref[i, :, lanes] = slope[:cols].astype(BF16)
            side_out_ref[i, :, lanes] = slope[cols:] * side_mask


def run_slope(flags, ring, w_depth, spread, pre, normed):
    rows, cols, expanded = spread.shape
    return pl.pallas_call(
        slope_kernel,
        grid=(expanded // BLOCK,),
        in_specs=[
            pl.BlockSpec(memory_space=pltpu.SMEM),
            last_block(ring.shape), last_block(w_depth.shape), last_block(spread.shape),
            last_block(pre.shape), whole(normed.shape),
        ],
        out_specs=[
            last_block((rows + 2, cols, expanded)), last_block((rows + 2, 8, expanded)),
            last_block(pre.shape), whole(normed.shape[::-1]),
        ],
        out_shape=[
            jax.ShapeDtypeStruct((rows + 2, cols, expanded), BF16),
            jax.ShapeDtypeStruct((rows + 2, 8, expanded), F32),
            jax.ShapeDtypeStruct(pre.shape, BF16),
            jax.ShapeDtypeStruct(normed.shape[::-1], BF16),
        ],
        scratch_shapes=[pltpu.VMEM((rows + 4, cols + 8, BLOCK), F32)],
        compiler_params=PARAMS,
        cost_estimate=estimate(13),
        name="slope",
    )(flags, ring, w_depth, spread, pre, normed)


def mix_kernel(
    cells_total, stride, bands,
    parts_ref, w_sq_ref, w_ex_ref, act_ref, image_ref, w_proj_ref, gain_ref, after_ref,
    pooled_ref, hidden_ref, gate_ref, mixed_ref, send_ref,
):
    step = pl.program_id(0)

    @pl.when(step == 0)
    def _():
        pooled = jnp.sum(parts_ref[...], axis=0) / cells_total
        hidden = dot_exact(pooled, w_sq_ref[...].astype(F32), ((1,), (0,)))
        silu = hidden * jax.nn.sigmoid(hidden)
        pooled_ref[...] = pooled
        hidden_ref[...] = hidden
        gate_ref[...] = jax.nn.sigmoid(dot_exact(silu, w_ex_ref[...].astype(F32), ((1,), (0,))))

    lines, cols, channels = image_ref.shape
    flat = act_ref[...].reshape(lines * cols, act_ref.shape[2])
    gated = (flat.astype(F32) * gate_ref[...]).astype(BF16)
    product = dot(gated, w_proj_ref[...])
    mixed = (image_ref[...].reshape(lines * cols, channels).astype(F32) + product).astype(BF16)
    mixed_ref[...] = mixed.reshape(lines, cols, channels)
    unit, _ = norm_rows(mixed.astype(F32))
    normed = (unit * gain_ref[...].astype(F32)).astype(BF16)
    for k in range(lines):
        line = step * lines + k
        for band in range(bands):
            start = k * cols + band * SIDE
            send_ref[lax.rem(line, stride) * bands + band, line // stride] = normed[
                start : start + SIDE
            ]


def run_mix(cells_total, stride, parts, w_squeeze, w_excite, act, image, w_project, gain, after):
    rows, cols, channels = image.shape
    expanded = act.shape[2]
    lines = 4
    bands = cols // SIDE
    block = lambda width: pl.BlockSpec((lines, cols, width), lambda r: (r, 0, 0))
    send = (stride * bands, rows // stride, SIDE, channels)
    return pl.pallas_call(
        functools.partial(mix_kernel, cells_total, stride, bands),
        grid=(rows // lines,),
        in_specs=[
            whole(parts.shape), whole(w_squeeze.shape), whole(w_excite.shape),
            block(expanded), block(channels), whole(w_project.shape), whole(gain.shape),
            pl.BlockSpec(memory_space=pl.ANY),
        ],
        out_specs=[
            whole((1, expanded)), whole((1, w_squeeze.shape[1])), whole((1, expanded)),
            block(channels), whole(send),
        ],
        out_shape=[
            jax.ShapeDtypeStruct((1, expanded), F32),
            jax.ShapeDtypeStruct((1, w_squeeze.shape[1]), F32),
            jax.ShapeDtypeStruct((1, expanded), F32),
            jax.ShapeDtypeStruct(image.shape, BF16),
            jax.ShapeDtypeStruct(send, BF16),
        ],
        compiler_params=PARAMS,
        cost_estimate=estimate(5),
        name="mix",
    )(parts, w_squeeze, w_excite, act, image, w_project, gain, after)


def attention_kernel(
    members, heads, lines,
    arrived_ref, att_grad_ref, w_qkv_ref, bias_ref,
    x_ref, att_ref, grad_ref, packed_grad_ref, bias_out_ref,
    order_ref, packed_ref, bias_sum_ref,
):
    cells, channels = x_ref.shape
    groups = cells // members

    def places():
        for g in range(groups):
            for m in range(0, members, GRID):
                line, row = (m // GRID) % lines, m // GRID // lines
                start = (row * GRID * lines + line) * groups + g
                yield g * members + m, pl.ds(start, GRID, stride=lines * groups)

    for half in range(channels // LANES):
        lanes = slice(half * LANES, (half + 1) * LANES)
        order_ref[half] = arrived_ref[:, lanes].astype(F32)
        for g in range(groups):
            pieces = [order_ref[half, at, :] for k, at in places() if k // members == g]
            at = slice(g * members, (g + 1) * members)
            x_ref[at, lanes] = jnp.concatenate(pieces, axis=0).astype(BF16)
    dim = channels // heads
    per_half = LANES // dim
    halves = channels // LANES
    scale = dim ** (-0.5)
    packed_ref[...] = dot(x_ref[...], w_qkv_ref[...]).astype(BF16)
    bias_sum_ref[...] = jnp.zeros(bias_sum_ref.shape, F32)
    tall = per_half * members
    mask = (
        lax.broadcasted_iota(jnp.int32, (tall, LANES), 0) // members
        == lax.broadcasted_iota(jnp.int32, (tall, LANES), 1) // dim
    ).astype(F32).astype(BF16)
    owner = lax.broadcasted_iota(jnp.int32, (members, 2 * LANES), 1) % LANES // dim
    zero = jnp.zeros((members, LANES), BF16)

    def by_head(pair):
        return jnp.concatenate(
            [jnp.concatenate([v] * per_half, axis=0) * mask for v in pair], axis=1
        )

    def diagonal(pair):
        return jnp.concatenate(
            [
                jnp.concatenate([pair[0], zero], axis=1),
                jnp.concatenate([zero, pair[1]], axis=1),
            ],
            axis=0,
        )

    def collect(v):
        parts = [v[h * members : (h + 1) * members] for h in range(per_half)]
        picked = parts[-1]
        for h in range(per_half - 1):
            picked = jnp.where(owner == h, parts[h], picked)
        return [picked[:, :LANES], picked[:, LANES:]]

    def blocks(v):
        return [v[:members, :LANES], v[members:, LANES:]]

    def over_members(v, reduce):
        parted = v.reshape(per_half, members, 2 * members)
        small = reduce(parted, axis=1, keepdims=True)
        return jnp.broadcast_to(small, parted.shape).reshape(v.shape)

    def pair_step(g, carry):
        at = [pl.ds(pl.multiple_of((2 * g + k) * members, 16), members) for k in range(2)]
        for half in range(halves):
            def lanes(part):
                start = part * channels + half * LANES
                return slice(start, start + LANES)

            q, k, v = ([packed_ref[at[n], lanes(part)] for n in range(2)] for part in range(3))
            cot = [att_grad_ref[at[n], lanes(0)] for n in range(2)]
            q_diag, cot_diag = diagonal(q), diagonal(cot)
            k_tall, v_tall = by_head(k), by_head(v)
            scores = dot(k_tall, q_diag, ((1,), (1,))) * scale + bias_ref[half]
            grad_probs = dot(v_tall, cot_diag, ((1,), (1,)))
            lifted = jnp.exp(scores - over_members(scores, jnp.max))
            soft = lifted * (1.0 / over_members(lifted, jnp.sum))
            soft_low = soft.astype(BF16)
            grad_scores = soft * (grad_probs - over_members(grad_probs * soft, jnp.sum))
            bias_sum_ref[half] += grad_scores
            scaled = (grad_scores * scale).astype(BF16)
            attended = blocks(dot(soft_low, v_tall, ((0,), (0,))))
            grad_q = blocks(dot(scaled, k_tall, ((0,), (0,))))
            grad_v = collect(dot(soft_low, cot_diag))
            grad_k = collect(dot(scaled, q_diag))
            for n in range(2):
                att_ref[at[n], lanes(0)] = attended[n].astype(BF16)
                for part, value in enumerate((grad_q, grad_k, grad_v)):
                    packed_grad_ref[at[n], lanes(part)] = value[n].astype(BF16)
        return carry

    lax.fori_loop(0, cells // members // 2, pair_step, 0, unroll=2)
    grad = dot(packed_grad_ref[...], w_qkv_ref[...], ((1,), (1,)))
    for half in range(halves):
        lanes = slice(half * LANES, (half + 1) * LANES)
        for k, at in places():
            order_ref[half, at, :] = grad[k : k + GRID, lanes]
        grad_ref[:, lanes] = order_ref[half].astype(BF16)
    for half in range(halves):
        both = bias_sum_ref[half]
        bias_out_ref[half] = both[:, :members] + both[:, members:]


def run_attention(arrived, att_grad, w_qkv, bias_tall, heads, lines):
    cells, channels = att_grad.shape
    halves, tall, members2 = bias_tall.shape
    members = members2 // 2
    vmem = pl.BlockSpec(memory_space=pltpu.VMEM)
    return pl.pallas_call(
        functools.partial(attention_kernel, members, heads, lines),
        in_specs=[vmem] * 4,
        out_specs=[vmem] * 5,
        out_shape=[
            jax.ShapeDtypeStruct((cells, channels), BF16),
            jax.ShapeDtypeStruct((cells, channels), BF16),
            jax.ShapeDtypeStruct((cells, channels), BF16),
            jax.ShapeDtypeStruct((cells, 3 * channels), BF16),
            jax.ShapeDtypeStruct((halves, tall, members), F32),
        ],
        scratch_shapes=[
            pltpu.VMEM((channels // LANES, cells, LANES), F32),
            pltpu.VMEM((cells, 3 * channels), BF16),
            pltpu.VMEM(bias_tall.shape, F32),
        ],
        compiler_params=PARAMS,
        cost_estimate=estimate(14),
        name="attention",
    )(arrived.reshape(cells, channels), att_grad, w_qkv, bias_tall)


def attention_weights_kernel(x_ref, packed_grad_ref, att_ref, cot_ref, bias_ref, out_ref):
    channels = x_ref.shape[1]
    wide = 3 * channels
    out_ref[:, :wide] = dot(x_ref[...], packed_grad_ref[...], ((0,), (0,))).astype(BF16)
    out_ref[:, wide : wide + channels] = dot(att_ref[...], cot_ref[...], ((0,), (0,))).astype(BF16)
    halves, tall, members = bias_ref.shape
    for h in range(tall // members):
        rows = slice(h * members, (h + 1) * members)
        turned = jnp.concatenate([bias_ref[half, rows, :].T for half in range(halves)], axis=1)
        out_ref[rows, wide + channels :] = turned.astype(BF16)


def run_attention_weights(x, packed_grad, att, cot, bias):
    channels = x.shape[1]
    vmem = pl.BlockSpec(memory_space=pltpu.VMEM)
    width = 4 * channels + bias.shape[0] * bias.shape[2]
    return pl.pallas_call(
        attention_weights_kernel,
        in_specs=[vmem] * 5,
        out_specs=vmem,
        out_shape=jax.ShapeDtypeStruct((channels, width), BF16),
        compiler_params=PARAMS,
        cost_estimate=estimate(5),
        name="attention_weights",
    )(x, packed_grad, att, cot, bias)


def mixed_back_kernel(
    stride, bands,
    recv_ref, mixed_ref, cot_ref, gain_ref, act_ref, gate_ref, w_projt_ref,
    low_ref, norm_ref, project_ref, gate_grad_ref,
    turned_ref, total_ref,
):
    rows, cols, channels = mixed_ref.shape

    @pl.when(pl.program_id(0) == 0)
    def _():
        gain = gain_ref[...].astype(F32)
        lines = 4

        def some_rows(c, total):
            pieces = []
            for k in range(lines):
                i = c * lines + k
                a, p = lax.rem(i, stride), i // stride
                pieces += [recv_ref[a * bands + band, p] for band in range(bands)]
            grad = jnp.concatenate(pieces, axis=0).astype(F32)
            at = pl.ds(c * lines, lines)
            flat = lambda ref: ref[at].reshape(lines * cols, channels).astype(F32)
            unit, rstd = norm_rows(flat(mixed_ref))
            back = flat(cot_ref) + norm_rows_back(unit, rstd, gain, grad)
            low_ref[at] = back.astype(BF16).reshape(lines, cols, channels)
            return total + fold_rows(grad * unit)

        total = lax.fori_loop(
            0, rows // lines, some_rows, jnp.zeros((8, channels), F32), unroll=2
        )
        norm_ref[...] = jnp.sum(total, axis=0, keepdims=True)
        turned_ref[...] = low_ref[...].reshape(rows * cols, channels).T

    flat = act_ref[...].reshape(rows * cols, BLOCK)
    product = dot(turned_ref[...], flat)
    total = jnp.sum(product * w_projt_ref[...].astype(F32), axis=0, keepdims=True)
    step, steps = pl.program_id(0), pl.num_programs(0)
    total_ref[step] = total
    project_ref[...] = (product * gate_ref[...]).T.astype(BF16)

    @pl.when(step == steps - 1)
    def _():
        sums = [total_ref[e] for e in range(total_ref.shape[0])]
        high = [v.astype(BF16).astype(F32) for v in sums]
        terms = jnp.concatenate(high + [v - w for v, w in zip(sums, high)], axis=0)
        gate_grad_ref[...] = jnp.broadcast_to(terms.astype(BF16)[None], gate_grad_ref.shape)


def run_mixed_back(count, stride, recv, mixed, cot, gain, act, gate, w_project_t):
    rows, cols, channels = mixed.shape
    expanded = act.shape[2]
    return pl.pallas_call(
        functools.partial(mixed_back_kernel, stride, cols // SIDE),
        grid=(expanded // BLOCK,),
        in_specs=[
            whole(recv.shape), whole(mixed.shape), whole(cot.shape), whole(gain.shape),
            last_block(act.shape), last_block(gate.shape), last_block(w_project_t.shape),
        ],
        out_specs=[
            whole(mixed.shape), whole((1, channels)),
            last_block((BLOCK, expanded)), whole((count, 2 * expanded // BLOCK, BLOCK)),
        ],
        out_shape=[
            jax.ShapeDtypeStruct(mixed.shape, BF16),
            jax.ShapeDtypeStruct((1, channels), F32),
            jax.ShapeDtypeStruct((BLOCK, expanded), BF16),
            jax.ShapeDtypeStruct((count, 2 * expanded // BLOCK, BLOCK), BF16),
        ],
        scratch_shapes=[
            pltpu.VMEM((channels, rows * cols), BF16),
            pltpu.VMEM((expanded // BLOCK, 1, BLOCK), F32),
        ],
        compiler_params=PARAMS,
        cost_estimate=estimate(7),
        name="mixed_back",
    )(recv, mixed, cot, gain, act, gate, w_project_t)


def unpack_kernel(
    place_ref, near_ref, far_ref, expand_ref, depth_ref, norm0_ref, norm1_ref, tail_ref
):
    expanded = expand_ref.shape[2]
    for pair, source in enumerate((near_ref, far_ref)):
        at = lax.rem(place_ref[0] + pair, 2)
        expand_ref[at] = source[:, :expanded].astype(F32)
        tail_ref[at] = source[:, expanded:].astype(F32)
    tail = tail_ref[0]
    pieces = expanded // LANES
    for t in range(9):
        for k in range(pieces):
            row = t * pieces + k
            lanes = slice(k * LANES, (k + 1) * LANES)
            depth_ref[t // 3, t % 3 : t % 3 + 1, lanes] = tail[row : row + 1]
    start = 9 * pieces
    half = norm0_ref.shape[1] // LANES
    for k in range(half):
        lanes = slice(k * LANES, (k + 1) * LANES)
        norm0_ref[:, lanes] = tail[start + k : start + k + 1]
        norm1_ref[:, lanes] = tail[start + half + k : start + half + k + 1]


def run_unpack(near, far, expanded):
    rows = near.shape[0]
    channels = 2 * rows
    place = (lax.axis_index("col") % 2).astype(jnp.int32).reshape(1)
    vmem = pl.BlockSpec(memory_space=pltpu.VMEM)
    return pl.pallas_call(
        unpack_kernel,
        in_specs=[pl.BlockSpec(memory_space=pltpu.SMEM), vmem, vmem],
        out_specs=[vmem] * 4,
        out_shape=[
            jax.ShapeDtypeStruct((2, rows, expanded), F32),
            jax.ShapeDtypeStruct((3, 3, expanded), F32),
            jax.ShapeDtypeStruct((1, channels), F32),
            jax.ShapeDtypeStruct((1, channels), F32),
        ],
        scratch_shapes=[pltpu.VMEM((2, rows, near.shape[1] - expanded), F32)],
        compiler_params=SMALL,
        cost_estimate=estimate(2),
        name="unpack",
    )(place, near, far)


def expand_back_kernel(
    cells_total,
    parts_ref, hidden_ref, gate_all_ref, w_sq_ref, w_ex_ref,
    low_ref, up_ref, down_ref, side_ref, w_projt_ref, gate_ref, slope_ref, side_slope_ref,
    spread_slope_ref, spread_ref, w_dep_ref, turned_ref, w_exp_ref, gain_ref, norm1_ref,
    weights_ref, first_ref, logit_ref, pre_ref,
    main_ref, side_grad_ref, window_ref, expanded_ref, pool_ref, tail_ref, norm_ref,
):
    rows, cols, channels = low_ref.shape
    side = 8
    wide = cols + side
    step = pl.program_id(0)
    steps = pl.num_programs(0)

    @pl.when(step == 0)
    def _():
        gate = gate_all_ref[...]
        blocks = pool_ref.shape[0]
        terms = jnp.sum(parts_ref[...].astype(F32), axis=0)
        gate_grad = jnp.concatenate(
            [terms[e : e + 1] + terms[blocks + e : blocks + e + 1] for e in range(blocks)], axis=1
        )
        logit = gate_grad * gate * (1.0 - gate)
        hidden = hidden_ref[...]
        sig = jax.nn.sigmoid(hidden)
        pre = dot_exact(logit, w_ex_ref[...].astype(F32), ((1,), (1,))) * (
            sig + hidden * sig * (1.0 - sig)
        )
        logit_ref[...] = logit
        pre_ref[...] = pre
        pooled = dot_exact(pre, w_sq_ref[...].astype(F32), ((1,), (1,))) / cells_total
        for e in range(blocks):
            pool_ref[e] = pooled[:, e * BLOCK : (e + 1) * BLOCK]
        first_ref[...] = jnp.zeros(first_ref.shape, F32)
        tail_ref[...] = jnp.zeros(tail_ref.shape, F32)
        norm_ref[...] = jnp.zeros(norm_ref.shape, F32)

    w_projt = w_projt_ref[...]
    main_ref[pl.ds(0, cols), :] = dot(up_ref[0], w_projt)
    main_ref[pl.ds(cols, rows * cols), :] = dot(
        low_ref[...].reshape(rows * cols, channels), w_projt
    )
    main_ref[pl.ds((rows + 1) * cols, cols), :] = dot(down_ref[0], w_projt)
    side_grad_ref[...] = dot(side_ref[...], w_projt)

    @pl.loop(0, rows + 2, unroll=3)
    def _(i):
        for h in range(BLOCK // LANES):
            lanes = slice(h * LANES, (h + 1) * LANES)
            gate = gate_ref[:, lanes]
            pooled = pool_ref[step][:, lanes]
            gated = main_ref[pl.ds(pl.multiple_of(i * cols, 16), cols), lanes]
            main = (gated * gate + pooled) * slope_ref[i, :, lanes].astype(F32)
            gated = side_grad_ref[pl.ds(pl.multiple_of(i * side, side), side), lanes]
            edge = (gated * gate + pooled) * side_slope_ref[i, :, lanes]
            grad = jnp.concatenate([main, edge], axis=0)
            window_ref[0, i, :, lanes] = pltpu.roll(grad, wide - 1, 0)[:cols]
            window_ref[1, i, :, lanes] = grad[:cols]
            window_ref[2, i, :, lanes] = pltpu.roll(grad, 1, 0)[:cols]

    for h in range(BLOCK // LANES):
        lanes = slice(h * LANES, (h + 1) * LANES)
        taps = w_dep_ref[:, :, lanes].astype(F32)

        def back_row(i, sums):
            spread = spread_ref[i, :, lanes].astype(F32)
            total = jnp.zeros((cols, LANES), F32)
            new_sums = []
            for a in range(3):
                for b in range(3):
                    window = window_ref[b, i + 2 - a, :, lanes]
                    total = total + window * taps[a, b : b + 1]
                    new_sums.append(sums[a * 3 + b] + fold_rows(window * spread))
            grad = total * spread_slope_ref[i, :, lanes].astype(F32)
            expanded_ref[pl.ds(pl.multiple_of(i * cols, 16), cols), lanes] = grad.astype(BF16)
            return tuple(new_sums)

        sums = lax.fori_loop(0, rows, back_row, (jnp.zeros((8, LANES), F32),) * 9, unroll=2)
        for t in range(9):
            row = t * (steps * BLOCK // LANES) + step * (BLOCK // LANES) + h
            tail_ref[pl.ds(row, 1), :] = jnp.sum(sums[t], axis=0, keepdims=True)

    grad_expanded = expanded_ref[...]
    w_exp = w_exp_ref[...]
    weights = dot(turned_ref[...], grad_expanded)
    weights_ref[:, pl.ds(pl.multiple_of(step * BLOCK, BLOCK), BLOCK)] = weights.astype(BF16)
    norm_ref[...] += jnp.sum(weights * w_exp.astype(F32), axis=1, keepdims=True)
    first_ref[...] += dot(grad_expanded, w_exp, ((1,), (1,)))

    @pl.when(step == steps - 1)
    def _():
        norm = norm_ref[...].T[0:1] / gain_ref[...].astype(F32)
        start = 9 * steps * (BLOCK // LANES)
        for k in range(channels // LANES):
            piece = slice(k * LANES, (k + 1) * LANES)
            tail_ref[start + k : start + k + 1, :] = norm[:, piece]
            at = start + channels // LANES + k
            tail_ref[at : at + 1, :] = norm1_ref[:, piece]
        weights_ref[:, steps * BLOCK :] = tail_ref[...].astype(BF16)


def run_expand_back(
    cells_total, parts, hidden, gate, w_squeeze, w_excite, low, up, down, side,
    w_project_t, slope, side_slope, spread_slope, spread, w_depth, turned, w_expand, gain, norm1,
):
    rows, cols, channels = low.shape
    expanded = w_expand.shape[1]
    steps = expanded // BLOCK
    return pl.pallas_call(
        functools.partial(expand_back_kernel, cells_total),
        grid=(steps,),
        in_specs=[
            pl.BlockSpec(
                (parts.shape[0], 2 * steps, BLOCK), lambda e: (0, parts.shape[1] // (2 * steps) - 1, 0)
            ),
            whole(hidden.shape), whole(gate.shape),
            whole(w_squeeze.shape), whole(w_excite.shape),
            whole(low.shape), whole(up.shape), whole(down.shape), whole(side.shape),
            last_block(w_project_t.shape), last_block(gate.shape), last_block(slope.shape),
            last_block(side_slope.shape), last_block(spread_slope.shape), last_block(spread.shape),
            last_block(w_depth.shape), whole(turned.shape), last_block(w_expand.shape),
            whole(gain.shape), whole(norm1.shape),
        ],
        out_specs=[
            whole((channels, expanded + LANES)), whole((rows * cols, channels)),
            whole((1, expanded)), whole(hidden.shape),
        ],
        out_shape=[
            jax.ShapeDtypeStruct((channels, expanded + LANES), BF16),
            jax.ShapeDtypeStruct((rows * cols, channels), F32),
            jax.ShapeDtypeStruct((1, expanded), F32),
            jax.ShapeDtypeStruct(hidden.shape, F32),
        ],
        scratch_shapes=[
            pltpu.VMEM(((rows + 2) * cols, BLOCK), F32),
            pltpu.VMEM(((rows + 2) * 8, BLOCK), F32),
            pltpu.VMEM((3, rows + 2, cols, BLOCK), F32),
            pltpu.VMEM((rows * cols, BLOCK), BF16),
            pltpu.VMEM((steps, 1, BLOCK), F32),
            pltpu.VMEM((channels, LANES), F32),
            pltpu.VMEM((channels, LANES), F32),
        ],
        compiler_params=PARAMS,
        cost_estimate=estimate(14),
        name="expand_back",
    )(
        parts, hidden, gate, w_squeeze, w_excite, low, up, down, side, w_project_t, gate,
        slope, side_slope, spread_slope, spread, w_depth, turned, w_expand, gain, norm1,
    )


def image_back_kernel(image_ref, gain_ref, first_ref, mixed_ref, out_ref):
    unit, rstd = norm_rows(image_ref[...].astype(F32))
    grad = first_ref[...]
    back = mixed_ref[...].astype(F32) + norm_rows_back(unit, rstd, gain_ref[...].astype(F32), grad)
    out_ref[...] = back.astype(BF16)


def run_image_back(image, gain, first, mixed):
    cells, channels = image.shape
    block = pl.BlockSpec((cells // 4, channels), lambda r: (r, 0))
    return pl.pallas_call(
        image_back_kernel,
        grid=(4,),
        in_specs=[block, whole(gain.shape), block, block],
        out_specs=block,
        out_shape=jax.ShapeDtypeStruct((cells, channels), BF16),
        compiler_params=SMALL,
        cost_estimate=estimate(4),
        name="image_back",
    )(image, gain, first, mixed)


def shift(cells, axis, step):
    count = lax.axis_size(axis)
    pairs = [(i, i + step) for i in range(count) if 0 <= i + step < count]
    return lax.ppermute(cells, axis, pairs)


def halo_rows(cells, width):
    up = shift(cells[cells.shape[0] - width :], "row", 1)
    down = shift(cells[:width], "row", -1)
    return up, down


def halo_sides(cells, up, down, width):
    rows, cols, channels = cells.shape
    first = jnp.concatenate([up[:, :width], cells[:, :width], down[:, :width]], axis=0)
    last = jnp.concatenate(
        [up[:, cols - width :], cells[:, cols - width :], down[:, cols - width :]], axis=0
    )
    left = shift(last, "col", 1)
    right = shift(first, "col", -1)
    gap = jnp.zeros((rows + 2 * width, 8 - 2 * width, channels), cells.dtype)
    side = jnp.concatenate([right, gap, left], axis=1)
    return side.reshape(-1, channels)


def hand_around(blocks):
    return lax.all_to_all(blocks, AXES, split_axis=0, concat_axis=0, tiled=True)


def sum_steps():
    return [("col", 1, 2), ("row", 1, lax.axis_size("row")), ("col", 2, lax.axis_size("col") // 2)]


def send_on(v, axis, stride, size, k):
    pairs = []
    for i in range(lax.axis_size(axis)):
        place = i // stride % size
        pairs.append((i, i + ((place + k) % size - place) * stride))
    return lax.ppermute(v, axis, pairs)


def sum_parts(matrix, axis, stride, size):
    place = lax.axis_index(axis) // stride % size
    parts = matrix.reshape(size, matrix.shape[0] // size, matrix.shape[1])
    part = lambda i: lax.dynamic_index_in_dim(parts, i % size, 0, False)
    total = part(place).astype(F32)
    for k in range(1, size):
        total = total + send_on(part(place + k), axis, stride, size, k).astype(F32)
    return total.astype(BF16)


def sum_shares(matrix):
    rows, columns = matrix.shape
    count = lax.axis_size("row") * lax.axis_size("col")
    pair = ("col", 1, 2)
    half = sum_parts(matrix, *pair)
    same_core = [list(range(k, count, 2)) for k in range(2)]

    def around(blocks):
        return lax.all_to_all(
            blocks, AXES, split_axis=0, concat_axis=0, tiled=True, axis_index_groups=same_core
        )

    arrived = around(half.reshape(count // 2, rows // count, columns))
    total = jnp.sum(arrived.astype(F32), axis=0).astype(BF16)
    sent = jnp.broadcast_to(total[None], (count // 2,) + total.shape)
    gathered = around(sent).reshape(rows // 2, columns)
    return gathered, send_on(gathered, *pair, 1)


def stack_kernel(*refs):
    for k, ref in enumerate(refs[:-1]):
        refs[-1][k] = ref[...]


def join_parts(blocks, axis, stride, size):
    arrived = [blocks] + [send_on(blocks, axis, stride, size, k) for k in range(1, size)]
    vmem = pl.BlockSpec(memory_space=pltpu.VMEM)
    stacked = pl.pallas_call(
        stack_kernel,
        in_specs=[vmem] * size,
        out_specs=vmem,
        out_shape=jax.ShapeDtypeStruct((size,) + blocks.shape, blocks.dtype),
        compiler_params=SMALL,
        cost_estimate=estimate(1),
        name="stack",
    )(*arrived)
    return stacked.reshape((size * blocks.shape[0],) + blocks.shape[1:])


def unpack_weights_kernel(
    sizes, places_ref, near_ref, far_ref, qkv_ref, out_ref, bias_ref, project_ref
):
    channels = out_ref.shape[2]
    halves, members = bias_ref.shape[0], bias_ref.shape[3]
    cuts = (0, 3 * channels, 4 * channels, 4 * channels + halves * members)
    pairs, over_row, rest = sizes
    for pair, source in enumerate((near_ref, far_ref)):
        for r in range(over_row):
            for c in range(rest):
                block = source[r * rest + c].astype(F32)
                at = lax.rem(places_ref[0] + pairs - pair, pairs)
                at = at * over_row + lax.rem(places_ref[1] + over_row - r, over_row)
                at = at * rest + lax.rem(places_ref[2] + rest - c, rest)
                qkv_ref[at] = block[:, : cuts[1]]
                out_ref[at] = block[:, cuts[1] : cuts[2]]
                for half in range(halves):
                    start = cuts[2] + half * members
                    bias_ref[half, at] = block[:, start : start + members]
                for e in range(project_ref.shape[0]):
                    start = cuts[3] + e * channels
                    project_ref[e, at] = block[:, start : start + channels]


def run_unpack_weights(steps, near, far, channels, expanded, halves, members):
    count, rows, _ = near.shape
    count *= 2
    places = jnp.stack([lax.axis_index(axis) // stride % size for axis, stride, size in steps])
    vmem = pl.BlockSpec(memory_space=pltpu.VMEM)
    blocks = lambda width: jax.ShapeDtypeStruct((count, rows, width), F32)
    return pl.pallas_call(
        functools.partial(unpack_weights_kernel, tuple(size for _, _, size in steps)),
        in_specs=[pl.BlockSpec(memory_space=pltpu.SMEM), vmem, vmem],
        out_specs=[vmem] * 4,
        out_shape=[
            blocks(3 * channels), blocks(channels),
            jax.ShapeDtypeStruct((halves, count, rows, members), F32),
            jax.ShapeDtypeStruct((expanded // BLOCK, count, rows, channels), F32),
        ],
        compiler_params=SMALL,
        cost_estimate=estimate(2),
        name="unpack_weights",
    )(places.astype(jnp.int32), near, far)


def swap_groups(blocks, parity):
    groups = None
    if parity > 1:
        over_row = lax.axis_size("row")
        over_col = lax.axis_size("col")
        groups = [
            [r * over_col + c for r in range(over_row) for c in range(k, over_col, parity)]
            for k in range(parity)
        ]
    return lax.all_to_all(
        blocks, AXES, split_axis=0, concat_axis=0, tiled=True, axis_index_groups=groups
    )


def on_device(
    image, out_cotangent, norm0_gain, w_expand, w_depth, w_squeeze, w_excite, w_project,
    norm1_gain, w_qkv, w_out, attn_bias,
):
    rows, cols, channels = image.shape
    over_row = lax.axis_size("row")
    over_col = lax.axis_size("col")
    count = over_row * over_col
    cells_total = rows * cols * count
    stride = rows * over_row // GRID
    parity = over_col // GRID
    lines = rows // stride
    bands = cols // SIDE
    members = GRID * GRID
    expanded = w_expand.shape[1]

    def into_members(arrived):
        parted = arrived.reshape(over_row, GRID, lines, SIDE, channels)
        return parted.transpose(3, 0, 2, 1, 4).reshape(SIDE * members, channels)

    def out_of_members(values):
        parted = values.reshape(SIDE, over_row, lines, GRID, channels)
        return parted.transpose(1, 3, 2, 0, 4).reshape(-1, lines, SIDE, channels)

    row, col = lax.axis_index("row"), lax.axis_index("col")
    flags = jnp.stack([row > 0, row < over_row - 1, col > 0, col < over_col - 1]).astype(F32)
    gain_first = norm0_gain.reshape(1, channels)
    gain_second = norm1_gain.reshape(1, channels)
    w_project_t = w_project.T
    heads = attn_bias.shape[0]
    halves = channels // LANES
    bias_tall = attn_bias.transpose(0, 2, 1).reshape(halves, heads // halves * members, members)
    bias_tall = jnp.concatenate([bias_tall, bias_tall], axis=2)

    up, down = halo_rows(image, 2)
    normed_first, spread, pre_spread = run_expand(image, gain_first, w_expand)
    up, down, spread = lax.optimization_barrier((up, down, spread))
    side = halo_sides(image, up, down, 2)
    cot_sent = (
        out_cotangent.reshape(lines, stride, bands, SIDE, channels)
        .transpose(1, 2, 0, 3, 4)
        .reshape(stride * bands, lines, SIDE, channels)
    )
    cot_members = into_members(swap_groups(cot_sent, parity))
    ring, act, pool = run_depthwise(count, up, down, side, gain_first, w_expand, w_depth, spread)
    pooled, hidden, gate, mixed, normed_sent = run_mix(
        cells_total, stride, hand_around(pool), w_squeeze, w_excite, act, image, w_project,
        gain_second, cot_members,
    )
    slope, side_slope, spread_slope, turned_first = run_slope(
        flags, ring, w_depth, spread, pre_spread, normed_first
    )
    normed_arrived = swap_groups(normed_sent, parity)
    att_grad = dot(cot_members, w_out, ((1,), (1,))).astype(BF16)
    normed_arrived, slope, att_grad = lax.optimization_barrier((normed_arrived, slope, att_grad))
    normed_members, attended, grad_normed, packed_grad, grad_bias = run_attention(
        normed_arrived, att_grad, w_qkv, bias_tall, heads, lines
    )
    grad_normed_home = swap_groups(grad_normed.reshape(normed_sent.shape), parity)
    weights = run_attention_weights(normed_members, packed_grad, attended, cot_members, grad_bias)
    grad_normed_home, weights = lax.optimization_barrier((grad_normed_home, weights))
    grad_low, grad_norm1, grad_project, gate_grad = run_mixed_back(
        count, stride, grad_normed_home, mixed, out_cotangent, gain_second, act, gate, w_project_t
    )
    attended_sent = out_of_members(attended)
    if parity == 1:
        both = hand_around(
            jnp.concatenate([attended_sent.reshape(count, -1, channels), gate_grad], axis=1)
        )
        parts = both
        attended_home = both[:, : lines * SIDE].reshape(attended_sent.shape)
    else:
        parts = hand_around(gate_grad)
        attended_home = swap_groups(attended_sent, parity)
    up, down = halo_rows(grad_low, 1)
    side = halo_sides(grad_low, up, down, 1)
    weights = jnp.concatenate([weights, grad_project], axis=1)
    weights, _ = lax.optimization_barrier((weights, up))
    steps = sum_steps()
    for step in steps:
        weights = sum_parts(weights, *step)
    late, grad_first, logit, pre = run_expand_back(
        cells_total, parts, hidden, gate, w_squeeze, w_excite, grad_low, up, down, side,
        w_project_t, slope, side_slope, spread_slope, spread, w_depth, turned_first, w_expand,
        gain_first, grad_norm1,
    )
    weights, _ = lax.optimization_barrier((weights, late))
    weights = weights[None]
    for step in steps[:0:-1]:
        weights = join_parts(weights, *step)
    other = send_on(weights, *steps[0], 1)
    grad_qkv, grad_out_proj, grad_bias, grad_project = run_unpack_weights(
        steps, weights, other, channels, expanded, halves, members
    )
    grad_expand, grad_depth, grad_norm0, grad_norm1 = run_unpack(*sum_shares(late), expanded)
    grad_image = run_image_back(
        image.reshape(-1, channels), gain_first, grad_first, grad_low.reshape(-1, channels)
    )
    attended_map = (
        attended_home.reshape(stride, bands, lines, SIDE, channels)
        .transpose(2, 0, 1, 3, 4)
        .reshape(rows * cols, channels)
    )
    block_out = (mixed.reshape(-1, channels).astype(F32) + dot(attended_map, w_out)).astype(BF16)

    silu = jax.nn.silu(hidden)
    grad_squeeze = pooled.reshape(expanded, 1) * pre
    grad_excite = silu.reshape(-1, 1) * logit

    return (
        block_out.reshape(image.shape),
        grad_image.reshape(image.shape),
        grad_norm0[0],
        grad_expand.reshape(w_expand.shape),
        grad_depth,
        grad_squeeze,
        grad_excite,
        grad_project.reshape(w_project.shape),
        grad_norm1[0],
        grad_qkv.reshape(w_qkv.shape),
        grad_out_proj.reshape(w_out.shape),
        grad_bias.reshape(attn_bias.shape),
    )


def solution(mesh):
    cells = P("row", "col", None)
    return jax.shard_map(
        on_device,
        mesh=mesh,
        in_specs=(cells, cells) + (P(),) * 10,
        out_specs=(cells, cells) + (P(),) * 10,
        check_vma=False,
    )
```

```python
import functools
import math

import jax
import jax.numpy as jnp
from jax import lax
from jax.experimental import pallas as pl
from jax.experimental.pallas import tpu as pltpu
from jax.sharding import PartitionSpec as P

GRID = 8
AXES = ("row", "col")
BLOCK = 256
LANES = 128
SIDE = 16
GELU_A = math.sqrt(2.0 / math.pi)
GELU_B = GELU_A * 0.044715
F32 = jnp.float32
BF16 = jnp.bfloat16
PARAMS = pltpu.CompilerParams(vmem_limit_bytes=56 * 1024 * 1024)
SMALL = pltpu.CompilerParams(vmem_limit_bytes=24 * 1024 * 1024)


def estimate(us):
    return pl.CostEstimate(flops=int(us * 1.1e9), bytes_accessed=int(us * 3.6e6), transcendentals=0)


def dot(left, right, contract=((1,), (0,))):
    return lax.dot_general(left, right, (contract, ((), ())), preferred_element_type=F32)


def dot_exact(vector, right, contract):
    tall = jnp.broadcast_to(vector, (8, vector.shape[1]))
    product = lax.dot_general(
        tall, right, (contract, ((), ())), precision=lax.Precision.HIGHEST, preferred_element_type=F32
    )
    return product[0:1]


def gelu_and_slope(x, with_slope=True):
    square = x * x
    t = jnp.tanh(x * (GELU_A + GELU_B * square))
    half = 0.5 + 0.5 * t
    value = x * half
    if not with_slope:
        return value, None
    slope = half + (value * (1.0 - t)) * (GELU_A + (3.0 * GELU_B) * square)
    return value, slope


def norm_rows(x):
    average = jnp.mean(x, axis=-1, keepdims=True)
    centered = x - average
    variance = jnp.mean(centered * centered, axis=-1, keepdims=True)
    rstd = lax.rsqrt(variance + 1e-05)
    return centered * rstd, rstd


def norm_rows_back(unit, rstd, gain, grad):
    unit_grad = grad * gain
    first = jnp.mean(unit_grad, axis=-1, keepdims=True)
    second = jnp.mean(unit_grad * unit, axis=-1, keepdims=True)
    return rstd * (unit_grad - first - unit * second)


def fold_rows(x):
    return jnp.sum(x.reshape(x.shape[0] // 8, 8, x.shape[1]), axis=0)


def whole(shape):
    return pl.BlockSpec(shape, lambda e: (0,) * len(shape))


def last_block(shape):
    lead = (0,) * (len(shape) - 1)
    return pl.BlockSpec(shape[:-1] + (BLOCK,), lambda e: lead + (e,))


def expand_kernel(
    image_ref, gain_ref, w_exp_ref,
    normed_ref, spread_ref, pre_ref,
    expanded_ref,
):
    rows, cols, channels = image_ref.shape

    @pl.when(pl.program_id(0) == 0)
    def _():
        gain = gain_ref[...].astype(F32)

        @pl.loop(0, rows // 4)
        def _(c):
            flat = image_ref[pl.ds(c * 4, 4)].reshape(4 * cols, channels)
            unit, _ = norm_rows(flat.astype(F32))
            at = pl.ds(pl.multiple_of(c * 4 * cols, 16), 4 * cols)
            normed_ref[at, :] = (unit * gain).astype(BF16)

    expanded_ref[...] = dot(normed_ref[...], w_exp_ref[...])

    @pl.loop(0, rows, unroll=4)
    def _(r):
        for h in range(BLOCK // LANES):
            lanes = slice(h * LANES, (h + 1) * LANES)
            x = expanded_ref[pl.ds(pl.multiple_of(r * cols, 16), cols), lanes]
            value, _ = gelu_and_slope(x, False)
            spread_ref[r, :, lanes] = value.astype(BF16)
            pre_ref[r, :, lanes] = x.astype(BF16)


def run_expand(image, gain, w_expand):
    rows, cols, channels = image.shape
    expanded = w_expand.shape[1]
    return pl.pallas_call(
        expand_kernel,
        grid=(expanded // BLOCK,),
        in_specs=[whole(image.shape), whole(gain.shape), last_block(w_expand.shape)],
        out_specs=[
            whole((rows * cols, channels)),
            last_block((rows, cols, expanded)), last_block((rows, cols, expanded)),
        ],
        out_shape=[
            jax.ShapeDtypeStruct((rows * cols, channels), BF16),
            jax.ShapeDtypeStruct((rows, cols, expanded), BF16),
            jax.ShapeDtypeStruct((rows, cols, expanded), BF16),
        ],
        scratch_shapes=[pltpu.VMEM((rows * cols, BLOCK), F32)],
        compiler_params=PARAMS,
        cost_estimate=estimate(14),
        name="expand",
    )(image, gain, w_expand)


def depthwise_kernel(
    up_ref, down_ref, side_ref, gain_ref, w_exp_ref, w_dep_ref, spread_ref,
    ring_ref, act_ref, pool_ref,
    ring_normed_ref, ring_wide_ref,
):
    rows, cols, _ = spread_ref.shape
    channels = up_ref.shape[2]
    over = 4 * cols
    side = 8

    @pl.when(pl.program_id(0) == 0)
    def _():
        gain = gain_ref[...].astype(F32)

        def put(at, values):
            unit, _ = norm_rows(values.astype(F32))
            ring_normed_ref[at : at + values.shape[0], :] = (unit * gain).astype(BF16)

        put(0, up_ref[...].reshape(2 * cols, channels))
        put(2 * cols, down_ref[...].reshape(2 * cols, channels))
        put(over, side_ref[...])

    ring_wide_ref[...] = dot(ring_normed_ref[...], w_exp_ref[...])
    tile = 32

    @pl.loop(0, ring_wide_ref.shape[0] // tile, unroll=True)
    def _(t):
        at = pl.ds(pl.multiple_of(t * tile, tile), tile)
        value, _ = gelu_and_slope(ring_wide_ref[at, :], False)
        low = value.astype(BF16)
        ring_ref[at, :] = low
        ring_wide_ref[at, :] = low.astype(F32)

    for h in range(BLOCK // LANES):
        lanes = slice(h * LANES, (h + 1) * LANES)
        taps = w_dep_ref[:, :, lanes].astype(F32)
        w = [[taps[a, b : b + 1] for b in range(3)] for a in range(3)]

        def line(r, main):
            at = pl.multiple_of(over + (r + 2) * side, side)
            return jnp.concatenate([main, ring_wide_ref[pl.ds(at, side), lanes]], axis=0)

        def conv(i, x, total):
            u = [x[0] * w[0][b] + x[1] * w[1][b] + x[2] * w[2][b] for b in range(3)]
            wide = cols + side
            pre = pltpu.roll(u[0], 1, 0) + u[1] + pltpu.roll(u[2], wide - 1, 0)
            value, _ = gelu_and_slope(pre[:cols], False)
            act_ref[i, :, lanes] = value.astype(BF16)
            return total + fold_rows(value)

        def step(i, carry):
            first, second, total = carry
            third = line(i + 1, spread_ref[i + 1, :, lanes].astype(F32))
            return second, third, conv(i, (first, second, third), total)

        carry = (
            line(-1, ring_wide_ref[cols : 2 * cols, lanes]),
            line(0, spread_ref[0, :, lanes].astype(F32)),
            jnp.zeros((8, LANES), F32),
        )
        first, second, total = lax.fori_loop(0, rows - 1, step, carry, unroll=5)
        third = line(rows, ring_wide_ref[2 * cols : 3 * cols, lanes])
        total = conv(rows - 1, (first, second, third), total)
        total = jnp.sum(total, axis=0, keepdims=True)
        pool_ref[:, :, lanes] = jnp.broadcast_to(total[None], (pool_ref.shape[0], 1, LANES))


def run_depthwise(count, up, down, side, gain, w_expand, w_depth, spread):
    rows, cols, expanded = spread.shape
    channels = up.shape[2]
    ring = 4 * cols + 8 * (rows + 4)
    return pl.pallas_call(
        depthwise_kernel,
        grid=(expanded // BLOCK,),
        in_specs=[
            whole(up.shape), whole(down.shape), whole(side.shape), whole(gain.shape),
            last_block(w_expand.shape), last_block(w_depth.shape), last_block(spread.shape),
        ],
        out_specs=[
            last_block((ring, expanded)), last_block(spread.shape), last_block((count, 1, expanded)),
        ],
        out_shape=[
            jax.ShapeDtypeStruct((ring, expanded), BF16),
            jax.ShapeDtypeStruct(spread.shape, BF16),
            jax.ShapeDtypeStruct((count, 1, expanded), F32),
        ],
        scratch_shapes=[pltpu.VMEM((ring, channels), BF16), pltpu.VMEM((ring, BLOCK), F32)],
        compiler_params=PARAMS,
        cost_estimate=estimate(1),
        name="depthwise",
    )(up, down, side, gain, w_expand, w_depth, spread)


def slope_kernel(
    flags_ref, ring_ref, w_dep_ref, spread_ref, pre_ref, normed_ref,
    main_ref, side_out_ref, spread_slope_ref, turned_ref, wide_ref,
):
    rows, cols, _ = spread_ref.shape

    @pl.when(pl.program_id(0) == 0)
    def _():
        turned_ref[...] = normed_ref[...].T

    @pl.loop(0, rows, unroll=4)
    def _(r):
        for h in range(BLOCK // LANES):
            lanes = slice(h * LANES, (h + 1) * LANES)
            _, slope = gelu_and_slope(pre_ref[r, :, lanes].astype(F32))
            spread_slope_ref[r, :, lanes] = slope.astype(BF16)

    over = 4 * cols
    side = 8
    wide = cols + side

    for k, r in enumerate((0, 1, rows + 2, rows + 3)):
        wide_ref[r, :cols, :] = ring_ref[k * cols : (k + 1) * cols, :].astype(F32)
    sides = ring_ref[over:, :].astype(F32)
    for r in range(rows + 4):
        wide_ref[r, cols:, :] = sides[r * side : (r + 1) * side]

    @pl.loop(0, rows)
    def _(r):
        wide_ref[r + 2, :cols, :] = spread_ref[r].astype(F32)

    place = lax.broadcasted_iota(jnp.int32, (side, LANES), 0)
    side_mask = jnp.where(
        place == side - 1, flags_ref[2], jnp.where(place == 0, flags_ref[3], 1.0)
    ).astype(F32)

    @pl.loop(0, rows + 2)
    def _(i):
        keep = jnp.where(i == 0, flags_ref[0], jnp.where(i == rows + 1, flags_ref[1], 1.0))
        for h in range(BLOCK // LANES):
            lanes = slice(h * LANES, (h + 1) * LANES)
            taps = w_dep_ref[:, :, lanes].astype(F32)
            x = [wide_ref[i + a, :, lanes] for a in range(3)]
            u = [sum(x[a] * taps[a, b : b + 1] for a in range(3)) for b in range(3)]
            pre = pltpu.roll(u[0], 1, 0) + u[1] + pltpu.roll(u[2], wide - 1, 0)
            _, slope = gelu_and_slope(pre)
            slope = slope * keep
            main_ref[i, :, lanes] = slope[:cols].astype(BF16)
            side_out_ref[i, :, lanes] = slope[cols:] * side_mask


def run_slope(flags, ring, w_depth, spread, pre, normed):
    rows, cols, expanded = spread.shape
    return pl.pallas_call(
        slope_kernel,
        grid=(expanded // BLOCK,),
        in_specs=[
            pl.BlockSpec(memory_space=pltpu.SMEM),
            last_block(ring.shape), last_block(w_depth.shape), last_block(spread.shape),
            last_block(pre.shape), whole(normed.shape),
        ],
        out_specs=[
            last_block((rows + 2, cols, expanded)), last_block((rows + 2, 8, expanded)),
            last_block(pre.shape), whole(normed.shape[::-1]),
        ],
        out_shape=[
            jax.ShapeDtypeStruct((rows + 2, cols, expanded), BF16),
            jax.ShapeDtypeStruct((rows + 2, 8, expanded), F32),
            jax.ShapeDtypeStruct(pre.shape, BF16),
            jax.ShapeDtypeStruct(normed.shape[::-1], BF16),
        ],
        scratch_shapes=[pltpu.VMEM((rows + 4, cols + 8, BLOCK), F32)],
        compiler_params=PARAMS,
        cost_estimate=estimate(13),
        name="slope",
    )(flags, ring, w_depth, spread, pre, normed)


def mix_kernel(
    cells_total, stride, bands,
    parts_ref, w_sq_ref, w_ex_ref, act_ref, image_ref, w_proj_ref, gain_ref, after_ref,
    pooled_ref, hidden_ref, gate_ref, mixed_ref, send_ref,
):
    step = pl.program_id(0)

    @pl.when(step == 0)
    def _():
        pooled = jnp.sum(parts_ref[...], axis=0) / cells_total
        hidden = dot_exact(pooled, w_sq_ref[...].astype(F32), ((1,), (0,)))
        silu = hidden * jax.nn.sigmoid(hidden)
        pooled_ref[...] = pooled
        hidden_ref[...] = hidden
        gate_ref[...] = jax.nn.sigmoid(dot_exact(silu, w_ex_ref[...].astype(F32), ((1,), (0,))))

    lines, cols, channels = image_ref.shape
    flat = act_ref[...].reshape(lines * cols, act_ref.shape[2])
    gated = (flat.astype(F32) * gate_ref[...]).astype(BF16)
    product = dot(gated, w_proj_ref[...])
    mixed = (image_ref[...].reshape(lines * cols, channels).astype(F32) + product).astype(BF16)
    mixed_ref[...] = mixed.reshape(lines, cols, channels)
    unit, _ = norm_rows(mixed.astype(F32))
    normed = (unit * gain_ref[...].astype(F32)).astype(BF16)
    for k in range(lines):
        line = step * lines + k
        for band in range(bands):
            start = k * cols + band * SIDE
            send_ref[lax.rem(line, stride) * bands + band, line // stride] = normed[
                start : start + SIDE
            ]


def run_mix(cells_total, stride, parts, w_squeeze, w_excite, act, image, w_project, gain, after):
    rows, cols, channels = image.shape
    expanded = act.shape[2]
    lines = 4
    bands = cols // SIDE
    block = lambda width: pl.BlockSpec((lines, cols, width), lambda r: (r, 0, 0))
    send = (stride * bands, rows // stride, SIDE, channels)
    return pl.pallas_call(
        functools.partial(mix_kernel, cells_total, stride, bands),
        grid=(rows // lines,),
        in_specs=[
            whole(parts.shape), whole(w_squeeze.shape), whole(w_excite.shape),
            block(expanded), block(channels), whole(w_project.shape), whole(gain.shape),
            pl.BlockSpec(memory_space=pl.ANY),
        ],
        out_specs=[
            whole((1, expanded)), whole((1, w_squeeze.shape[1])), whole((1, expanded)),
            block(channels), whole(send),
        ],
        out_shape=[
            jax.ShapeDtypeStruct((1, expanded), F32),
            jax.ShapeDtypeStruct((1, w_squeeze.shape[1]), F32),
            jax.ShapeDtypeStruct((1, expanded), F32),
            jax.ShapeDtypeStruct(image.shape, BF16),
            jax.ShapeDtypeStruct(send, BF16),
        ],
        compiler_params=PARAMS,
        cost_estimate=estimate(5),
        name="mix",
    )(parts, w_squeeze, w_excite, act, image, w_project, gain, after)


def attention_kernel(
    members, heads, lines,
    arrived_ref, att_grad_ref, w_qkv_ref, bias_ref,
    x_ref, att_ref, grad_ref, packed_grad_ref, bias_out_ref,
    order_ref, packed_ref, bias_sum_ref,
):
    cells, channels = x_ref.shape
    groups = cells // members

    def places():
        for g in range(groups):
            for m in range(0, members, GRID):
                line, row = (m // GRID) % lines, m // GRID // lines
                start = (row * GRID * lines + line) * groups + g
                yield g * members + m, pl.ds(start, GRID, stride=lines * groups)

    for half in range(channels // LANES):
        lanes = slice(half * LANES, (half + 1) * LANES)
        order_ref[half] = arrived_ref[:, lanes].astype(F32)
        for g in range(groups):
            pieces = [order_ref[half, at, :] for k, at in places() if k // members == g]
            at = slice(g * members, (g + 1) * members)
            x_ref[at, lanes] = jnp.concatenate(pieces, axis=0).astype(BF16)
    dim = channels // heads
    per_half = LANES // dim
    halves = channels // LANES
    scale = dim ** (-0.5)
    packed_ref[...] = dot(x_ref[...], w_qkv_ref[...]).astype(BF16)
    bias_sum_ref[...] = jnp.zeros(bias_sum_ref.shape, F32)
    tall = per_half * members
    mask = (
        lax.broadcasted_iota(jnp.int32, (tall, LANES), 0) // members
        == lax.broadcasted_iota(jnp.int32, (tall, LANES), 1) // dim
    ).astype(F32).astype(BF16)
    owner = lax.broadcasted_iota(jnp.int32, (members, 2 * LANES), 1) % LANES // dim
    zero = jnp.zeros((members, LANES), BF16)

    def by_head(pair):
        return jnp.concatenate(
            [jnp.concatenate([v] * per_half, axis=0) * mask for v in pair], axis=1
        )

    def diagonal(pair):
        return jnp.concatenate(
            [
                jnp.concatenate([pair[0], zero], axis=1),
                jnp.concatenate([zero, pair[1]], axis=1),
            ],
            axis=0,
        )

    def collect(v):
        parts = [v[h * members : (h + 1) * members] for h in range(per_half)]
        picked = parts[-1]
        for h in range(per_half - 1):
            picked = jnp.where(owner == h, parts[h], picked)
        return [picked[:, :LANES], picked[:, LANES:]]

    def blocks(v):
        return [v[:members, :LANES], v[members:, LANES:]]

    def over_members(v, reduce):
        parted = v.reshape(per_half, members, 2 * members)
        small = reduce(parted, axis=1, keepdims=True)
        return jnp.broadcast_to(small, parted.shape).reshape(v.shape)

    def pair_step(g, carry):
        at = [pl.ds(pl.multiple_of((2 * g + k) * members, 16), members) for k in range(2)]
        for half in range(halves):
            def lanes(part):
                start = part * channels + half * LANES
                return slice(start, start + LANES)

            q, k, v = ([packed_ref[at[n], lanes(part)] for n in range(2)] for part in range(3))
            cot = [att_grad_ref[at[n], lanes(0)] for n in range(2)]
            q_diag, cot_diag = diagonal(q), diagonal(cot)
            k_tall, v_tall = by_head(k), by_head(v)
            scores = dot(k_tall, q_diag, ((1,), (1,))) * scale + bias_ref[half]
            grad_probs = dot(v_tall, cot_diag, ((1,), (1,)))
            lifted = jnp.exp(scores - over_members(scores, jnp.max))
            soft = lifted * (1.0 / over_members(lifted, jnp.sum))
            soft_low = soft.astype(BF16)
            grad_scores = soft * (grad_probs - over_members(grad_probs * soft, jnp.sum))
            bias_sum_ref[half] += grad_scores
            scaled = (grad_scores * scale).astype(BF16)
            attended = blocks(dot(soft_low, v_tall, ((0,), (0,))))
            grad_q = blocks(dot(scaled, k_tall, ((0,), (0,))))
            grad_v = collect(dot(soft_low, cot_diag))
            grad_k = collect(dot(scaled, q_diag))
            for n in range(2):
                att_ref[at[n], lanes(0)] = attended[n].astype(BF16)
                for part, value in enumerate((grad_q, grad_k, grad_v)):
                    packed_grad_ref[at[n], lanes(part)] = value[n].astype(BF16)
        return carry

    lax.fori_loop(0, cells // members // 2, pair_step, 0, unroll=2)
    grad = dot(packed_grad_ref[...], w_qkv_ref[...], ((1,), (1,)))
    for half in range(halves):
        lanes = slice(half * LANES, (half + 1) * LANES)
        for k, at in places():
            order_ref[half, at, :] = grad[k : k + GRID, lanes]
        grad_ref[:, lanes] = order_ref[half].astype(BF16)
    for half in range(halves):
        both = bias_sum_ref[half]
        bias_out_ref[half] = both[:, :members] + both[:, members:]


def run_attention(arrived, att_grad, w_qkv, bias_tall, heads, lines):
    cells, channels = att_grad.shape
    halves, tall, members2 = bias_tall.shape
    members = members2 // 2
    vmem = pl.BlockSpec(memory_space=pltpu.VMEM)
    return pl.pallas_call(
        functools.partial(attention_kernel, members, heads, lines),
        in_specs=[vmem] * 4,
        out_specs=[vmem] * 5,
        out_shape=[
            jax.ShapeDtypeStruct((cells, channels), BF16),
            jax.ShapeDtypeStruct((cells, channels), BF16),
            jax.ShapeDtypeStruct((cells, channels), BF16),
            jax.ShapeDtypeStruct((cells, 3 * channels), BF16),
            jax.ShapeDtypeStruct((halves, tall, members), F32),
        ],
        scratch_shapes=[
            pltpu.VMEM((channels // LANES, cells, LANES), F32),
            pltpu.VMEM((cells, 3 * channels), BF16),
            pltpu.VMEM(bias_tall.shape, F32),
        ],
        compiler_params=PARAMS,
        cost_estimate=estimate(14),
        name="attention",
    )(arrived.reshape(cells, channels), att_grad, w_qkv, bias_tall)


def attention_weights_kernel(x_ref, packed_grad_ref, att_ref, cot_ref, bias_ref, out_ref):
    channels = x_ref.shape[1]
    wide = 3 * channels
    out_ref[:, :wide] = dot(x_ref[...], packed_grad_ref[...], ((0,), (0,))).astype(BF16)
    out_ref[:, wide : wide + channels] = dot(att_ref[...], cot_ref[...], ((0,), (0,))).astype(BF16)
    halves, tall, members = bias_ref.shape
    for h in range(tall // members):
        rows = slice(h * members, (h + 1) * members)
        turned = jnp.concatenate([bias_ref[half, rows, :].T for half in range(halves)], axis=1)
        out_ref[rows, wide + channels :] = turned.astype(BF16)


def run_attention_weights(x, packed_grad, att, cot, bias):
    channels = x.shape[1]
    vmem = pl.BlockSpec(memory_space=pltpu.VMEM)
    width = 4 * channels + bias.shape[0] * bias.shape[2]
    return pl.pallas_call(
        attention_weights_kernel,
        in_specs=[vmem] * 5,
        out_specs=vmem,
        out_shape=jax.ShapeDtypeStruct((channels, width), BF16),
        compiler_params=PARAMS,
        cost_estimate=estimate(5),
        name="attention_weights",
    )(x, packed_grad, att, cot, bias)


def mixed_back_kernel(
    stride, bands,
    recv_ref, mixed_ref, cot_ref, gain_ref, act_ref, gate_ref, w_projt_ref,
    low_ref, norm_ref, project_ref, gate_grad_ref,
    turned_ref, total_ref,
):
    rows, cols, channels = mixed_ref.shape

    @pl.when(pl.program_id(0) == 0)
    def _():
        gain = gain_ref[...].astype(F32)
        lines = 4

        def some_rows(c, total):
            pieces = []
            for k in range(lines):
                i = c * lines + k
                a, p = lax.rem(i, stride), i // stride
                pieces += [recv_ref[a * bands + band, p] for band in range(bands)]
            grad = jnp.concatenate(pieces, axis=0).astype(F32)
            at = pl.ds(c * lines, lines)
            flat = lambda ref: ref[at].reshape(lines * cols, channels).astype(F32)
            unit, rstd = norm_rows(flat(mixed_ref))
            back = flat(cot_ref) + norm_rows_back(unit, rstd, gain, grad)
            low_ref[at] = back.astype(BF16).reshape(lines, cols, channels)
            return total + fold_rows(grad * unit)

        total = lax.fori_loop(
            0, rows // lines, some_rows, jnp.zeros((8, channels), F32), unroll=2
        )
        norm_ref[...] = jnp.sum(total, axis=0, keepdims=True)
        turned_ref[...] = low_ref[...].reshape(rows * cols, channels).T

    flat = act_ref[...].reshape(rows * cols, BLOCK)
    product = dot(turned_ref[...], flat)
    total = jnp.sum(product * w_projt_ref[...].astype(F32), axis=0, keepdims=True)
    step, steps = pl.program_id(0), pl.num_programs(0)
    total_ref[step] = total
    project_ref[...] = (product * gate_ref[...]).T.astype(BF16)

    @pl.when(step == steps - 1)
    def _():
        sums = [total_ref[e] for e in range(total_ref.shape[0])]
        high = [v.astype(BF16).astype(F32) for v in sums]
        terms = jnp.concatenate(high + [v - w for v, w in zip(sums, high)], axis=0)
        gate_grad_ref[...] = jnp.broadcast_to(terms.astype(BF16)[None], gate_grad_ref.shape)


def run_mixed_back(count, stride, recv, mixed, cot, gain, act, gate, w_project_t):
    rows, cols, channels = mixed.shape
    expanded = act.shape[2]
    return pl.pallas_call(
        functools.partial(mixed_back_kernel, stride, cols // SIDE),
        grid=(expanded // BLOCK,),
        in_specs=[
            whole(recv.shape), whole(mixed.shape), whole(cot.shape), whole(gain.shape),
            last_block(act.shape), last_block(gate.shape), last_block(w_project_t.shape),
        ],
        out_specs=[
            whole(mixed.shape), whole((1, channels)),
            last_block((BLOCK, expanded)), whole((count, 2 * expanded // BLOCK, BLOCK)),
        ],
        out_shape=[
            jax.ShapeDtypeStruct(mixed.shape, BF16),
            jax.ShapeDtypeStruct((1, channels), F32),
            jax.ShapeDtypeStruct((BLOCK, expanded), BF16),
            jax.ShapeDtypeStruct((count, 2 * expanded // BLOCK, BLOCK), BF16),
        ],
        scratch_shapes=[
            pltpu.VMEM((channels, rows * cols), BF16),
            pltpu.VMEM((expanded // BLOCK, 1, BLOCK), F32),
        ],
        compiler_params=PARAMS,
        cost_estimate=estimate(7),
        name="mixed_back",
    )(recv, mixed, cot, gain, act, gate, w_project_t)


def core_place():
    return (lax.axis_index("col") % 2).astype(jnp.int32).reshape(1)


def unpack_kernel(
    place_ref, near_ref, far_ref, expand_ref, depth_ref, norm0_ref, norm1_ref, tail_ref
):
    expanded = expand_ref.shape[2]
    for pair, source in enumerate((near_ref, far_ref)):
        at = lax.rem(place_ref[0] + pair, 2)
        expand_ref[at] = source[:, :expanded].astype(F32)
        tail_ref[at] = source[:, expanded:].astype(F32)
    tail = tail_ref[0]
    pieces = expanded // LANES
    for t in range(9):
        for k in range(pieces):
            row = t * pieces + k
            lanes = slice(k * LANES, (k + 1) * LANES)
            depth_ref[t // 3, t % 3 : t % 3 + 1, lanes] = tail[row : row + 1]
    start = 9 * pieces
    half = norm0_ref.shape[1] // LANES
    for k in range(half):
        lanes = slice(k * LANES, (k + 1) * LANES)
        norm0_ref[:, lanes] = tail[start + k : start + k + 1]
        norm1_ref[:, lanes] = tail[start + half + k : start + half + k + 1]


def run_unpack(near, far, expanded):
    rows = near.shape[0]
    channels = 2 * rows
    vmem = pl.BlockSpec(memory_space=pltpu.VMEM)
    return pl.pallas_call(
        unpack_kernel,
        in_specs=[pl.BlockSpec(memory_space=pltpu.SMEM), vmem, vmem],
        out_specs=[vmem] * 4,
        out_shape=[
            jax.ShapeDtypeStruct((2, rows, expanded), F32),
            jax.ShapeDtypeStruct((3, 3, expanded), F32),
            jax.ShapeDtypeStruct((1, channels), F32),
            jax.ShapeDtypeStruct((1, channels), F32),
        ],
        scratch_shapes=[pltpu.VMEM((2, rows, near.shape[1] - expanded), F32)],
        compiler_params=SMALL,
        cost_estimate=estimate(2),
        name="unpack",
    )(core_place(), near, far)


def expand_back_kernel(
    cells_total,
    place_ref, parts_ref, hidden_ref, gate_all_ref, w_sq_ref, w_ex_ref,
    low_ref, up_ref, down_ref, side_ref, w_projt_ref, gate_ref, slope_ref, side_slope_ref,
    spread_slope_ref, spread_ref, w_dep_ref, turned_ref, w_exp_ref, gain_ref, norm1_ref,
    mine_ref, other_ref, first_ref, logit_ref, pre_ref,
    main_ref, side_grad_ref, window_ref, expanded_ref, pool_ref, tail_ref, norm_ref,
):
    rows, cols, channels = low_ref.shape
    side = 8
    wide = cols + side
    step = pl.program_id(0)
    steps = pl.num_programs(0)

    @pl.when(step == 0)
    def _():
        gate = gate_all_ref[...]
        blocks = pool_ref.shape[0]
        terms = jnp.sum(parts_ref[...].astype(F32), axis=0)
        gate_grad = jnp.concatenate(
            [terms[e : e + 1] + terms[blocks + e : blocks + e + 1] for e in range(blocks)], axis=1
        )
        logit = gate_grad * gate * (1.0 - gate)
        hidden = hidden_ref[...]
        sig = jax.nn.sigmoid(hidden)
        pre = dot_exact(logit, w_ex_ref[...].astype(F32), ((1,), (1,))) * (
            sig + hidden * sig * (1.0 - sig)
        )
        logit_ref[...] = logit
        pre_ref[...] = pre
        pooled = dot_exact(pre, w_sq_ref[...].astype(F32), ((1,), (1,))) / cells_total
        for e in range(blocks):
            pool_ref[e] = pooled[:, e * BLOCK : (e + 1) * BLOCK]
        first_ref[...] = jnp.zeros(first_ref.shape, F32)
        tail_ref[...] = jnp.zeros(tail_ref.shape, F32)
        norm_ref[...] = jnp.zeros(norm_ref.shape, F32)

    w_projt = w_projt_ref[...]
    main_ref[pl.ds(0, cols), :] = dot(up_ref[0], w_projt)
    main_ref[pl.ds(cols, rows * cols), :] = dot(
        low_ref[...].reshape(rows * cols, channels), w_projt
    )
    main_ref[pl.ds((rows + 1) * cols, cols), :] = dot(down_ref[0], w_projt)
    side_grad_ref[...] = dot(side_ref[...], w_projt)

    @pl.loop(0, rows + 2, unroll=3)
    def _(i):
        for h in range(BLOCK // LANES):
            lanes = slice(h * LANES, (h + 1) * LANES)
            gate = gate_ref[:, lanes]
            pooled = pool_ref[step][:, lanes]
            gated = main_ref[pl.ds(pl.multiple_of(i * cols, 16), cols), lanes]
            main = (gated * gate + pooled) * slope_ref[i, :, lanes].astype(F32)
            gated = side_grad_ref[pl.ds(pl.multiple_of(i * side, side), side), lanes]
            edge = (gated * gate + pooled) * side_slope_ref[i, :, lanes]
            grad = jnp.concatenate([main, edge], axis=0)
            window_ref[0, i, :, lanes] = pltpu.roll(grad, wide - 1, 0)[:cols]
            window_ref[1, i, :, lanes] = grad[:cols]
            window_ref[2, i, :, lanes] = pltpu.roll(grad, 1, 0)[:cols]

    for h in range(BLOCK // LANES):
        lanes = slice(h * LANES, (h + 1) * LANES)
        taps = w_dep_ref[:, :, lanes].astype(F32)

        def back_row(i, sums):
            spread = spread_ref[i, :, lanes].astype(F32)
            total = jnp.zeros((cols, LANES), F32)
            new_sums = []
            for a in range(3):
                for b in range(3):
                    window = window_ref[b, i + 2 - a, :, lanes]
                    total = total + window * taps[a, b : b + 1]
                    new_sums.append(sums[a * 3 + b] + fold_rows(window * spread))
            grad = total * spread_slope_ref[i, :, lanes].astype(F32)
            expanded_ref[pl.ds(pl.multiple_of(i * cols, 16), cols), lanes] = grad.astype(BF16)
            return tuple(new_sums)

        sums = lax.fori_loop(0, rows, back_row, (jnp.zeros((8, LANES), F32),) * 9, unroll=2)
        for t in range(9):
            row = t * (steps * BLOCK // LANES) + step * (BLOCK // LANES) + h
            tail_ref[pl.ds(row, 1), :] = jnp.sum(sums[t], axis=0, keepdims=True)

    grad_expanded = expanded_ref[...]
    w_exp = w_exp_ref[...]
    weights = dot(turned_ref[...], grad_expanded)


    def keep(at, values):
        half = channels // 2
        for place in range(2):

            @pl.when(place_ref[0] == place)
            def _():
                mine_ref[:, at] = values[place * half : (place + 1) * half]
                other_ref[:, at] = values[(1 - place) * half : (2 - place) * half]

    keep(pl.ds(pl.multiple_of(step * BLOCK, BLOCK), BLOCK), weights.astype(BF16))
    norm_ref[...] += jnp.sum(weights * w_exp.astype(F32), axis=1, keepdims=True)
    first_ref[...] += dot(grad_expanded, w_exp, ((1,), (1,)))

    @pl.when(step == steps - 1)
    def _():
        norm = norm_ref[...].T[0:1] / gain_ref[...].astype(F32)
        start = 9 * steps * (BLOCK // LANES)
        for k in range(channels // LANES):
            piece = slice(k * LANES, (k + 1) * LANES)
            tail_ref[start + k : start + k + 1, :] = norm[:, piece]
            at = start + channels // LANES + k
            tail_ref[at : at + 1, :] = norm1_ref[:, piece]
        keep(slice(mine_ref.shape[1] - LANES, mine_ref.shape[1]), tail_ref[...].astype(BF16))


def run_expand_back(
    cells_total, parts, hidden, gate, w_squeeze, w_excite, low, up, down, side,
    w_project_t, slope, side_slope, spread_slope, spread, w_depth, turned, w_expand, gain, norm1,
):
    rows, cols, channels = low.shape
    expanded = w_expand.shape[1]
    steps = expanded // BLOCK
    return pl.pallas_call(
        functools.partial(expand_back_kernel, cells_total),
        grid=(steps,),
        in_specs=[
            pl.BlockSpec(memory_space=pltpu.SMEM),
            pl.BlockSpec(
                (parts.shape[0], 2 * steps, BLOCK), lambda e: (0, parts.shape[1] // (2 * steps) - 1, 0)
            ),
            whole(hidden.shape), whole(gate.shape),
            whole(w_squeeze.shape), whole(w_excite.shape),
            whole(low.shape), whole(up.shape), whole(down.shape), whole(side.shape),
            last_block(w_project_t.shape), last_block(gate.shape), last_block(slope.shape),
            last_block(side_slope.shape), last_block(spread_slope.shape), last_block(spread.shape),
            last_block(w_depth.shape), whole(turned.shape), last_block(w_expand.shape),
            whole(gain.shape), whole(norm1.shape),
        ],
        out_specs=[
            whole((channels // 2, expanded + LANES)), whole((channels // 2, expanded + LANES)),
            whole((rows * cols, channels)),
            whole((1, expanded)), whole(hidden.shape),
        ],
        out_shape=[
            jax.ShapeDtypeStruct((channels // 2, expanded + LANES), BF16),
            jax.ShapeDtypeStruct((channels // 2, expanded + LANES), BF16),
            jax.ShapeDtypeStruct((rows * cols, channels), F32),
            jax.ShapeDtypeStruct((1, expanded), F32),
            jax.ShapeDtypeStruct(hidden.shape, F32),
        ],
        scratch_shapes=[
            pltpu.VMEM(((rows + 2) * cols, BLOCK), F32),
            pltpu.VMEM(((rows + 2) * 8, BLOCK), F32),
            pltpu.VMEM((3, rows + 2, cols, BLOCK), F32),
            pltpu.VMEM((rows * cols, BLOCK), BF16),
            pltpu.VMEM((steps, 1, BLOCK), F32),
            pltpu.VMEM((channels, LANES), F32),
            pltpu.VMEM((channels, LANES), F32),
        ],
        compiler_params=PARAMS,
        cost_estimate=estimate(14),
        name="expand_back",
    )(
        core_place(), parts, hidden, gate, w_squeeze, w_excite, low, up, down, side, w_project_t, gate,
        slope, side_slope, spread_slope, spread, w_depth, turned, w_expand, gain, norm1,
    )


def image_back_kernel(image_ref, gain_ref, first_ref, mixed_ref, out_ref):
    unit, rstd = norm_rows(image_ref[...].astype(F32))
    grad = first_ref[...]
    back = mixed_ref[...].astype(F32) + norm_rows_back(unit, rstd, gain_ref[...].astype(F32), grad)
    out_ref[...] = back.astype(BF16)


def run_image_back(image, gain, first, mixed):
    cells, channels = image.shape
    block = pl.BlockSpec((cells // 4, channels), lambda r: (r, 0))
    return pl.pallas_call(
        image_back_kernel,
        grid=(4,),
        in_specs=[block, whole(gain.shape), block, block],
        out_specs=block,
        out_shape=jax.ShapeDtypeStruct((cells, channels), BF16),
        compiler_params=SMALL,
        cost_estimate=estimate(4),
        name="image_back",
    )(image, gain, first, mixed)


def shift(cells, axis, step):
    count = lax.axis_size(axis)
    pairs = [(i, i + step) for i in range(count) if 0 <= i + step < count]
    return lax.ppermute(cells, axis, pairs)


def halo_rows(cells, width):
    up = shift(cells[cells.shape[0] - width :], "row", 1)
    down = shift(cells[:width], "row", -1)
    return up, down


def halo_sides(cells, up, down, width):
    rows, cols, channels = cells.shape
    first = jnp.concatenate([up[:, :width], cells[:, :width], down[:, :width]], axis=0)
    last = jnp.concatenate(
        [up[:, cols - width :], cells[:, cols - width :], down[:, cols - width :]], axis=0
    )
    left = shift(last, "col", 1)
    right = shift(first, "col", -1)
    gap = jnp.zeros((rows + 2 * width, 8 - 2 * width, channels), cells.dtype)
    side = jnp.concatenate([right, gap, left], axis=1)
    return side.reshape(-1, channels)


def hand_around(blocks):
    return lax.all_to_all(blocks, AXES, split_axis=0, concat_axis=0, tiled=True)


def sum_steps():
    return [("col", 1, 2), ("row", 1, lax.axis_size("row")), ("col", 2, lax.axis_size("col") // 2)]


def send_on(v, axis, stride, size, k):
    pairs = []
    for i in range(lax.axis_size(axis)):
        place = i // stride % size
        pairs.append((i, i + ((place + k) % size - place) * stride))
    return lax.ppermute(v, axis, pairs)


def sum_parts(matrix, axis, stride, size):
    place = lax.axis_index(axis) // stride % size
    parts = matrix.reshape(size, matrix.shape[0] // size, matrix.shape[1])
    part = lambda i: lax.dynamic_index_in_dim(parts, i % size, 0, False)
    total = part(place).astype(F32)
    for k in range(1, size):
        total = total + send_on(part(place + k), axis, stride, size, k).astype(F32)
    return total.astype(BF16)


def sum_shares(mine, other):
    rows, columns = 2 * mine.shape[0], mine.shape[1]
    count = lax.axis_size("row") * lax.axis_size("col")
    pair = ("col", 1, 2)
    half = (mine.astype(F32) + send_on(other, *pair, 1).astype(F32)).astype(BF16)
    same_core = [list(range(k, count, 2)) for k in range(2)]

    def around(blocks):
        return lax.all_to_all(
            blocks, AXES, split_axis=0, concat_axis=0, tiled=True, axis_index_groups=same_core
        )

    arrived = around(half.reshape(count // 2, rows // count, columns))
    total = jnp.sum(arrived.astype(F32), axis=0).astype(BF16)
    sent = jnp.broadcast_to(total[None], (count // 2,) + total.shape)
    gathered = around(sent).reshape(rows // 2, columns)
    return gathered, send_on(gathered, *pair, 1)


def stack_kernel(*refs):
    for k, ref in enumerate(refs[:-1]):
        refs[-1][k] = ref[...]


def join_parts(blocks, axis, stride, size):
    arrived = [blocks] + [send_on(blocks, axis, stride, size, k) for k in range(1, size)]
    vmem = pl.BlockSpec(memory_space=pltpu.VMEM)
    stacked = pl.pallas_call(
        stack_kernel,
        in_specs=[vmem] * size,
        out_specs=vmem,
        out_shape=jax.ShapeDtypeStruct((size,) + blocks.shape, blocks.dtype),
        compiler_params=SMALL,
        cost_estimate=estimate(1),
        name="stack",
    )(*arrived)
    return stacked.reshape((size * blocks.shape[0],) + blocks.shape[1:])


def unpack_weights_kernel(
    sizes, places_ref, near_ref, far_ref, qkv_ref, out_ref, bias_ref, project_ref
):
    channels = out_ref.shape[2]
    halves, members = bias_ref.shape[0], bias_ref.shape[3]
    cuts = (0, 3 * channels, 4 * channels, 4 * channels + halves * members)
    pairs, over_row, rest = sizes
    for pair, source in enumerate((near_ref, far_ref)):
        for r in range(over_row):
            for c in range(rest):
                block = source[r * rest + c].astype(F32)
                at = lax.rem(places_ref[0] + pairs - pair, pairs)
                at = at * over_row + lax.rem(places_ref[1] + over_row - r, over_row)
                at = at * rest + lax.rem(places_ref[2] + rest - c, rest)
                qkv_ref[at] = block[:, : cuts[1]]
                out_ref[at] = block[:, cuts[1] : cuts[2]]
                for half in range(halves):
                    start = cuts[2] + half * members
                    bias_ref[half, at] = block[:, start : start + members]
                for e in range(project_ref.shape[0]):
                    start = cuts[3] + e * channels
                    project_ref[e, at] = block[:, start : start + channels]


def run_unpack_weights(steps, near, far, channels, expanded, halves, members):
    count, rows, _ = near.shape
    count *= 2
    places = jnp.stack([lax.axis_index(axis) // stride % size for axis, stride, size in steps])
    vmem = pl.BlockSpec(memory_space=pltpu.VMEM)
    blocks = lambda width: jax.ShapeDtypeStruct((count, rows, width), F32)
    return pl.pallas_call(
        functools.partial(unpack_weights_kernel, tuple(size for _, _, size in steps)),
        in_specs=[pl.BlockSpec(memory_space=pltpu.SMEM), vmem, vmem],
        out_specs=[vmem] * 4,
        out_shape=[
            blocks(3 * channels), blocks(channels),
            jax.ShapeDtypeStruct((halves, count, rows, members), F32),
            jax.ShapeDtypeStruct((expanded // BLOCK, count, rows, channels), F32),
        ],
        compiler_params=SMALL,
        cost_estimate=estimate(2),
        name="unpack_weights",
    )(places.astype(jnp.int32), near, far)


def swap_groups(blocks, parity):
    groups = None
    if parity > 1:
        over_row = lax.axis_size("row")
        over_col = lax.axis_size("col")
        groups = [
            [r * over_col + c for r in range(over_row) for c in range(k, over_col, parity)]
            for k in range(parity)
        ]
    return lax.all_to_all(
        blocks, AXES, split_axis=0, concat_axis=0, tiled=True, axis_index_groups=groups
    )


def on_device(
    image, out_cotangent, norm0_gain, w_expand, w_depth, w_squeeze, w_excite, w_project,
    norm1_gain, w_qkv, w_out, attn_bias,
):
    rows, cols, channels = image.shape
    over_row = lax.axis_size("row")
    over_col = lax.axis_size("col")
    count = over_row * over_col
    cells_total = rows * cols * count
    stride = rows * over_row // GRID
    parity = over_col // GRID
    lines = rows // stride
    bands = cols // SIDE
    members = GRID * GRID
    expanded = w_expand.shape[1]

    def into_members(arrived):
        parted = arrived.reshape(over_row, GRID, lines, SIDE, channels)
        return parted.transpose(3, 0, 2, 1, 4).reshape(SIDE * members, channels)

    def out_of_members(values):
        parted = values.reshape(SIDE, over_row, lines, GRID, channels)
        return parted.transpose(1, 3, 2, 0, 4).reshape(-1, lines, SIDE, channels)

    row, col = lax.axis_index("row"), lax.axis_index("col")
    flags = jnp.stack([row > 0, row < over_row - 1, col > 0, col < over_col - 1]).astype(F32)
    gain_first = norm0_gain.reshape(1, channels)
    gain_second = norm1_gain.reshape(1, channels)
    w_project_t = w_project.T
    heads = attn_bias.shape[0]
    halves = channels // LANES
    bias_tall = attn_bias.transpose(0, 2, 1).reshape(halves, heads // halves * members, members)
    bias_tall = jnp.concatenate([bias_tall, bias_tall], axis=2)

    up, down = halo_rows(image, 2)
    normed_first, spread, pre_spread = run_expand(image, gain_first, w_expand)
    up, down, spread = lax.optimization_barrier((up, down, spread))
    side = halo_sides(image, up, down, 2)
    cot_sent = (
        out_cotangent.reshape(lines, stride, bands, SIDE, channels)
        .transpose(1, 2, 0, 3, 4)
        .reshape(stride * bands, lines, SIDE, channels)
    )
    cot_members = into_members(swap_groups(cot_sent, parity))
    ring, act, pool = run_depthwise(count, up, down, side, gain_first, w_expand, w_depth, spread)
    pooled, hidden, gate, mixed, normed_sent = run_mix(
        cells_total, stride, hand_around(pool), w_squeeze, w_excite, act, image, w_project,
        gain_second, cot_members,
    )
    slope, side_slope, spread_slope, turned_first = run_slope(
        flags, ring, w_depth, spread, pre_spread, normed_first
    )
    normed_arrived = swap_groups(normed_sent, parity)
    att_grad = dot(cot_members, w_out, ((1,), (1,))).astype(BF16)
    normed_arrived, slope, att_grad = lax.optimization_barrier((normed_arrived, slope, att_grad))
    normed_members, attended, grad_normed, packed_grad, grad_bias = run_attention(
        normed_arrived, att_grad, w_qkv, bias_tall, heads, lines
    )
    grad_normed_home = swap_groups(grad_normed.reshape(normed_sent.shape), parity)
    weights = run_attention_weights(normed_members, packed_grad, attended, cot_members, grad_bias)
    grad_normed_home, weights = lax.optimization_barrier((grad_normed_home, weights))
    grad_low, grad_norm1, grad_project, gate_grad = run_mixed_back(
        count, stride, grad_normed_home, mixed, out_cotangent, gain_second, act, gate, w_project_t
    )
    attended_sent = out_of_members(attended)
    if parity == 1:
        both = hand_around(
            jnp.concatenate([attended_sent.reshape(count, -1, channels), gate_grad], axis=1)
        )
        parts = both
        attended_home = both[:, : lines * SIDE].reshape(attended_sent.shape)
    else:
        parts = hand_around(gate_grad)
        attended_home = swap_groups(attended_sent, parity)
    up, down = halo_rows(grad_low, 1)
    edge_up, edge_down, parts = lax.optimization_barrier((up, down, parts))
    side = halo_sides(grad_low, edge_up, edge_down, 1)
    weights = jnp.concatenate([weights, grad_project], axis=1)
    weights, _ = lax.optimization_barrier((weights, up))
    steps = sum_steps()
    for step in steps:
        weights = sum_parts(weights, *step)
    grad_low, weights = lax.optimization_barrier((grad_low, weights))
    late, late_other, grad_first, logit, pre = run_expand_back(
        cells_total, parts, hidden, gate, w_squeeze, w_excite, grad_low, up, down, side,
        w_project_t, slope, side_slope, spread_slope, spread, w_depth, turned_first, w_expand,
        gain_first, grad_norm1,
    )
    weights, _ = lax.optimization_barrier((weights, late))
    weights = weights[None]
    for step in steps[:0:-1]:
        weights = join_parts(weights, *step)
    other = send_on(weights, *steps[0], 1)
    grad_qkv, grad_out_proj, grad_bias, grad_project = run_unpack_weights(
        steps, weights, other, channels, expanded, halves, members
    )
    grad_expand, grad_depth, grad_norm0, grad_norm1 = run_unpack(*sum_shares(late, late_other), expanded)
    grad_image = run_image_back(
        image.reshape(-1, channels), gain_first, grad_first, grad_low.reshape(-1, channels)
    )
    attended_map = (
        attended_home.reshape(stride, bands, lines, SIDE, channels)
        .transpose(2, 0, 1, 3, 4)
        .reshape(rows * cols, channels)
    )
    block_out = (mixed.reshape(-1, channels).astype(F32) + dot(attended_map, w_out)).astype(BF16)

    silu = jax.nn.silu(hidden)
    grad_squeeze = pooled.reshape(expanded, 1) * pre
    grad_excite = silu.reshape(-1, 1) * logit

    return (
        block_out.reshape(image.shape),
        grad_image.reshape(image.shape),
        grad_norm0[0],
        grad_expand.reshape(w_expand.shape),
        grad_depth,
        grad_squeeze,
        grad_excite,
        grad_project.reshape(w_project.shape),
        grad_norm1[0],
        grad_qkv.reshape(w_qkv.shape),
        grad_out_proj.reshape(w_out.shape),
        grad_bias.reshape(attn_bias.shape),
    )


def solution(mesh):
    cells = P("row", "col", None)
    return jax.shard_map(
        on_device,
        mesh=mesh,
        in_specs=(cells, cells) + (P(),) * 10,
        out_specs=(cells, cells) + (P(),) * 10,
        check_vma=False,
    )
```

```python
import functools
import math

import jax
import jax.numpy as jnp
from jax import lax
from jax.experimental import pallas as pl
from jax.experimental.pallas import tpu as pltpu
from jax.sharding import PartitionSpec as P

GRID = 8
AXES = ("row", "col")
BLOCK = 256
LANES = 128
SIDE = 16
GELU_A = math.sqrt(2.0 / math.pi)
GELU_B = GELU_A * 0.044715
F32 = jnp.float32
BF16 = jnp.bfloat16
PARAMS = pltpu.CompilerParams(vmem_limit_bytes=56 * 1024 * 1024)
SMALL = pltpu.CompilerParams(vmem_limit_bytes=24 * 1024 * 1024)


def estimate(us):
    return pl.CostEstimate(flops=int(us * 1.1e9), bytes_accessed=int(us * 3.6e6), transcendentals=0)


def dot(left, right, contract=((1,), (0,))):
    return lax.dot_general(left, right, (contract, ((), ())), preferred_element_type=F32)


def dot_exact(vector, right, contract):
    tall = jnp.broadcast_to(vector, (8, vector.shape[1]))
    product = lax.dot_general(
        tall, right, (contract, ((), ())), precision=lax.Precision.HIGHEST, preferred_element_type=F32
    )
    return product[0:1]


def gelu_and_slope(x, with_slope=True):
    square = x * x
    t = jnp.tanh(x * (GELU_A + GELU_B * square))
    half = 0.5 + 0.5 * t
    value = x * half
    if not with_slope:
        return value, None
    slope = half + (value * (1.0 - t)) * (GELU_A + (3.0 * GELU_B) * square)
    return value, slope


def norm_rows(x):
    average = jnp.mean(x, axis=-1, keepdims=True)
    centered = x - average
    variance = jnp.mean(centered * centered, axis=-1, keepdims=True)
    rstd = lax.rsqrt(variance + 1e-05)
    return centered * rstd, rstd


def norm_rows_back(unit, rstd, gain, grad):
    unit_grad = grad * gain
    first = jnp.mean(unit_grad, axis=-1, keepdims=True)
    second = jnp.mean(unit_grad * unit, axis=-1, keepdims=True)
    return rstd * (unit_grad - first - unit * second)


def fold_rows(x):
    return jnp.sum(x.reshape(x.shape[0] // 8, 8, x.shape[1]), axis=0)


def whole(shape):
    return pl.BlockSpec(shape, lambda e: (0,) * len(shape))


def last_block(shape):
    lead = (0,) * (len(shape) - 1)
    return pl.BlockSpec(shape[:-1] + (BLOCK,), lambda e: lead + (e,))


def expand_kernel(
    image_ref, gain_ref, w_exp_ref,
    normed_ref, spread_ref, pre_ref,
    expanded_ref,
):
    rows, cols, channels = image_ref.shape

    @pl.when(pl.program_id(0) == 0)
    def _():
        gain = gain_ref[...].astype(F32)

        @pl.loop(0, rows // 4)
        def _(c):
            flat = image_ref[pl.ds(c * 4, 4)].reshape(4 * cols, channels)
            unit, _ = norm_rows(flat.astype(F32))
            at = pl.ds(pl.multiple_of(c * 4 * cols, 16), 4 * cols)
            normed_ref[at, :] = (unit * gain).astype(BF16)

    expanded_ref[...] = dot(normed_ref[...], w_exp_ref[...])

    @pl.loop(0, rows, unroll=4)
    def _(r):
        for h in range(BLOCK // LANES):
            lanes = slice(h * LANES, (h + 1) * LANES)
            x = expanded_ref[pl.ds(pl.multiple_of(r * cols, 16), cols), lanes]
            value, _ = gelu_and_slope(x, False)
            spread_ref[r, :, lanes] = value.astype(BF16)
            pre_ref[r, :, lanes] = x.astype(BF16)


def run_expand(image, gain, w_expand):
    rows, cols, channels = image.shape
    expanded = w_expand.shape[1]
    return pl.pallas_call(
        expand_kernel,
        grid=(expanded // BLOCK,),
        in_specs=[whole(image.shape), whole(gain.shape), last_block(w_expand.shape)],
        out_specs=[
            whole((rows * cols, channels)),
            last_block((rows, cols, expanded)), last_block((rows, cols, expanded)),
        ],
        out_shape=[
            jax.ShapeDtypeStruct((rows * cols, channels), BF16),
            jax.ShapeDtypeStruct((rows, cols, expanded), BF16),
            jax.ShapeDtypeStruct((rows, cols, expanded), BF16),
        ],
        scratch_shapes=[pltpu.VMEM((rows * cols, BLOCK), F32)],
        compiler_params=PARAMS,
        cost_estimate=estimate(14),
        name="expand",
    )(image, gain, w_expand)


def depthwise_kernel(
    up_ref, down_ref, side_ref, gain_ref, w_exp_ref, w_dep_ref, spread_ref,
    ring_ref, act_ref, pool_ref,
    ring_normed_ref, ring_wide_ref,
):
    rows, cols, _ = spread_ref.shape
    channels = up_ref.shape[2]
    over = 4 * cols
    side = 8

    @pl.when(pl.program_id(0) == 0)
    def _():
        gain = gain_ref[...].astype(F32)

        def put(at, values):
            unit, _ = norm_rows(values.astype(F32))
            ring_normed_ref[at : at + values.shape[0], :] = (unit * gain).astype(BF16)

        put(0, up_ref[...].reshape(2 * cols, channels))
        put(2 * cols, down_ref[...].reshape(2 * cols, channels))
        put(over, side_ref[...])

    ring_wide_ref[...] = dot(ring_normed_ref[...], w_exp_ref[...])
    tile = 32

    @pl.loop(0, ring_wide_ref.shape[0] // tile, unroll=True)
    def _(t):
        at = pl.ds(pl.multiple_of(t * tile, tile), tile)
        value, _ = gelu_and_slope(ring_wide_ref[at, :], False)
        low = value.astype(BF16)
        ring_ref[at, :] = low
        ring_wide_ref[at, :] = low.astype(F32)

    for h in range(BLOCK // LANES):
        lanes = slice(h * LANES, (h + 1) * LANES)
        taps = w_dep_ref[:, :, lanes].astype(F32)
        w = [[taps[a, b : b + 1] for b in range(3)] for a in range(3)]

        def line(r, main):
            at = pl.multiple_of(over + (r + 2) * side, side)
            return jnp.concatenate([main, ring_wide_ref[pl.ds(at, side), lanes]], axis=0)

        def conv(i, x, total):
            u = [x[0] * w[0][b] + x[1] * w[1][b] + x[2] * w[2][b] for b in range(3)]
            wide = cols + side
            pre = pltpu.roll(u[0], 1, 0) + u[1] + pltpu.roll(u[2], wide - 1, 0)
            value, _ = gelu_and_slope(pre[:cols], False)
            act_ref[i, :, lanes] = value.astype(BF16)
            return total + fold_rows(value)

        def step(i, carry):
            first, second, total = carry
            third = line(i + 1, spread_ref[i + 1, :, lanes].astype(F32))
            return second, third, conv(i, (first, second, third), total)

        carry = (
            line(-1, ring_wide_ref[cols : 2 * cols, lanes]),
            line(0, spread_ref[0, :, lanes].astype(F32)),
            jnp.zeros((8, LANES), F32),
        )
        first, second, total = lax.fori_loop(0, rows - 1, step, carry, unroll=5)
        third = line(rows, ring_wide_ref[2 * cols : 3 * cols, lanes])
        total = conv(rows - 1, (first, second, third), total)
        total = jnp.sum(total, axis=0, keepdims=True)
        pool_ref[:, :, lanes] = jnp.broadcast_to(total[None], (pool_ref.shape[0], 1, LANES))


def run_depthwise(count, up, down, side, gain, w_expand, w_depth, spread):
    rows, cols, expanded = spread.shape
    channels = up.shape[2]
    ring = 4 * cols + 8 * (rows + 4)
    return pl.pallas_call(
        depthwise_kernel,
        grid=(expanded // BLOCK,),
        in_specs=[
            whole(up.shape), whole(down.shape), whole(side.shape), whole(gain.shape),
            last_block(w_expand.shape), last_block(w_depth.shape), last_block(spread.shape),
        ],
        out_specs=[
            last_block((ring, expanded)), last_block(spread.shape), last_block((count, 1, expanded)),
        ],
        out_shape=[
            jax.ShapeDtypeStruct((ring, expanded), BF16),
            jax.ShapeDtypeStruct(spread.shape, BF16),
            jax.ShapeDtypeStruct((count, 1, expanded), F32),
        ],
        scratch_shapes=[pltpu.VMEM((ring, channels), BF16), pltpu.VMEM((ring, BLOCK), F32)],
        compiler_params=PARAMS,
        cost_estimate=estimate(1),
        name="depthwise",
    )(up, down, side, gain, w_expand, w_depth, spread)


def slope_kernel(
    flags_ref, ring_ref, w_dep_ref, spread_ref, pre_ref, normed_ref,
    main_ref, side_out_ref, spread_slope_ref, turned_ref, wide_ref,
):
    rows, cols, _ = spread_ref.shape

    @pl.when(pl.program_id(0) == 0)
    def _():
        turned_ref[...] = normed_ref[...].T

    @pl.loop(0, rows, unroll=4)
    def _(r):
        for h in range(BLOCK // LANES):
            lanes = slice(h * LANES, (h + 1) * LANES)
            _, slope = gelu_and_slope(pre_ref[r, :, lanes].astype(F32))
            spread_slope_ref[r, :, lanes] = slope.astype(BF16)

    over = 4 * cols
    side = 8
    wide = cols + side

    for k, r in enumerate((0, 1, rows + 2, rows + 3)):
        wide_ref[r, :cols, :] = ring_ref[k * cols : (k + 1) * cols, :].astype(F32)
    sides = ring_ref[over:, :].astype(F32)
    for r in range(rows + 4):
        wide_ref[r, cols:, :] = sides[r * side : (r + 1) * side]

    @pl.loop(0, rows)
    def _(r):
        wide_ref[r + 2, :cols, :] = spread_ref[r].astype(F32)

    place = lax.broadcasted_iota(jnp.int32, (side, LANES), 0)
    side_mask = jnp.where(
        place == side - 1, flags_ref[2], jnp.where(place == 0, flags_ref[3], 1.0)
    ).astype(F32)

    @pl.loop(0, rows + 2)
    def _(i):
        keep = jnp.where(i == 0, flags_ref[0], jnp.where(i == rows + 1, flags_ref[1], 1.0))
        for h in range(BLOCK // LANES):
            lanes = slice(h * LANES, (h + 1) * LANES)
            taps = w_dep_ref[:, :, lanes].astype(F32)
            x = [wide_ref[i + a, :, lanes] for a in range(3)]
            u = [sum(x[a] * taps[a, b : b + 1] for a in range(3)) for b in range(3)]
            pre = pltpu.roll(u[0], 1, 0) + u[1] + pltpu.roll(u[2], wide - 1, 0)
            _, slope = gelu_and_slope(pre)
            slope = slope * keep
            main_ref[i, :, lanes] = slope[:cols].astype(BF16)
            side_out_ref[i, :, lanes] = slope[cols:] * side_mask


def run_slope(flags, ring, w_depth, spread, pre, normed):
    rows, cols, expanded = spread.shape
    return pl.pallas_call(
        slope_kernel,
        grid=(expanded // BLOCK,),
        in_specs=[
            pl.BlockSpec(memory_space=pltpu.SMEM),
            last_block(ring.shape), last_block(w_depth.shape), last_block(spread.shape),
            last_block(pre.shape), whole(normed.shape),
        ],
        out_specs=[
            last_block((rows + 2, cols, expanded)), last_block((rows + 2, 8, expanded)),
            last_block(pre.shape), whole(normed.shape[::-1]),
        ],
        out_shape=[
            jax.ShapeDtypeStruct((rows + 2, cols, expanded), BF16),
            jax.ShapeDtypeStruct((rows + 2, 8, expanded), F32),
            jax.ShapeDtypeStruct(pre.shape, BF16),
            jax.ShapeDtypeStruct(normed.shape[::-1], BF16),
        ],
        scratch_shapes=[pltpu.VMEM((rows + 4, cols + 8, BLOCK), F32)],
        compiler_params=PARAMS,
        cost_estimate=estimate(13),
        name="slope",
    )(flags, ring, w_depth, spread, pre, normed)


def mix_kernel(
    cells_total, stride, bands,
    parts_ref, w_sq_ref, w_ex_ref, act_ref, image_ref, w_proj_ref, gain_ref, after_ref,
    pooled_ref, hidden_ref, gate_ref, mixed_ref, send_ref,
):
    step = pl.program_id(0)

    @pl.when(step == 0)
    def _():
        pooled = jnp.sum(parts_ref[...], axis=0) / cells_total
        hidden = dot_exact(pooled, w_sq_ref[...].astype(F32), ((1,), (0,)))
        silu = hidden * jax.nn.sigmoid(hidden)
        pooled_ref[...] = pooled
        hidden_ref[...] = hidden
        gate_ref[...] = jax.nn.sigmoid(dot_exact(silu, w_ex_ref[...].astype(F32), ((1,), (0,))))

    lines, cols, channels = image_ref.shape
    flat = act_ref[...].reshape(lines * cols, act_ref.shape[2])
    gated = (flat.astype(F32) * gate_ref[...]).astype(BF16)
    product = dot(gated, w_proj_ref[...])
    mixed = (image_ref[...].reshape(lines * cols, channels).astype(F32) + product).astype(BF16)
    mixed_ref[...] = mixed.reshape(lines, cols, channels)
    unit, _ = norm_rows(mixed.astype(F32))
    normed = (unit * gain_ref[...].astype(F32)).astype(BF16)
    for k in range(lines):
        line = step * lines + k
        for band in range(bands):
            start = k * cols + band * SIDE
            send_ref[lax.rem(line, stride) * bands + band, line // stride] = normed[
                start : start + SIDE
            ]


def run_mix(cells_total, stride, parts, w_squeeze, w_excite, act, image, w_project, gain, after):
    rows, cols, channels = image.shape
    expanded = act.shape[2]
    lines = 4
    bands = cols // SIDE
    block = lambda width: pl.BlockSpec((lines, cols, width), lambda r: (r, 0, 0))
    send = (stride * bands, rows // stride, SIDE, channels)
    return pl.pallas_call(
        functools.partial(mix_kernel, cells_total, stride, bands),
        grid=(rows // lines,),
        in_specs=[
            whole(parts.shape), whole(w_squeeze.shape), whole(w_excite.shape),
            block(expanded), block(channels), whole(w_project.shape), whole(gain.shape),
            pl.BlockSpec(memory_space=pl.ANY),
        ],
        out_specs=[
            whole((1, expanded)), whole((1, w_squeeze.shape[1])), whole((1, expanded)),
            block(channels), whole(send),
        ],
        out_shape=[
            jax.ShapeDtypeStruct((1, expanded), F32),
            jax.ShapeDtypeStruct((1, w_squeeze.shape[1]), F32),
            jax.ShapeDtypeStruct((1, expanded), F32),
            jax.ShapeDtypeStruct(image.shape, BF16),
            jax.ShapeDtypeStruct(send, BF16),
        ],
        compiler_params=PARAMS,
        cost_estimate=estimate(5),
        name="mix",
    )(parts, w_squeeze, w_excite, act, image, w_project, gain, after)


def attention_kernel(
    members, heads, lines,
    arrived_ref, att_grad_ref, w_qkv_ref, bias_ref,
    x_ref, att_ref, grad_ref, packed_grad_ref, bias_out_ref,
    order_ref, packed_ref, bias_sum_ref,
):
    cells, channels = x_ref.shape
    groups = cells // members

    def places():
        for g in range(groups):
            for m in range(0, members, GRID):
                line, row = (m // GRID) % lines, m // GRID // lines
                start = (row * GRID * lines + line) * groups + g
                yield g * members + m, pl.ds(start, GRID, stride=lines * groups)

    for half in range(channels // LANES):
        lanes = slice(half * LANES, (half + 1) * LANES)
        order_ref[half] = arrived_ref[:, lanes].astype(F32)
        for g in range(groups):
            pieces = [order_ref[half, at, :] for k, at in places() if k // members == g]
            at = slice(g * members, (g + 1) * members)
            x_ref[at, lanes] = jnp.concatenate(pieces, axis=0).astype(BF16)
    dim = channels // heads
    per_half = LANES // dim
    halves = channels // LANES
    scale = dim ** (-0.5)
    packed_ref[...] = dot(x_ref[...], w_qkv_ref[...]).astype(BF16)
    bias_sum_ref[...] = jnp.zeros(bias_sum_ref.shape, F32)
    tall = per_half * members
    mask = (
        lax.broadcasted_iota(jnp.int32, (tall, LANES), 0) // members
        == lax.broadcasted_iota(jnp.int32, (tall, LANES), 1) // dim
    ).astype(F32).astype(BF16)
    owner = lax.broadcasted_iota(jnp.int32, (members, 2 * LANES), 1) % LANES // dim
    zero = jnp.zeros((members, LANES), BF16)

    def by_head(pair):
        return jnp.concatenate(
            [jnp.concatenate([v] * per_half, axis=0) * mask for v in pair], axis=1
        )

    def diagonal(pair):
        return jnp.concatenate(
            [
                jnp.concatenate([pair[0], zero], axis=1),
                jnp.concatenate([zero, pair[1]], axis=1),
            ],
            axis=0,
        )

    def collect(v):
        parts = [v[h * members : (h + 1) * members] for h in range(per_half)]
        picked = parts[-1]
        for h in range(per_half - 1):
            picked = jnp.where(owner == h, parts[h], picked)
        return [picked[:, :LANES], picked[:, LANES:]]

    def blocks(v):
        return [v[:members, :LANES], v[members:, LANES:]]

    def over_members(v, reduce):
        parted = v.reshape(per_half, members, 2 * members)
        small = reduce(parted, axis=1, keepdims=True)
        return jnp.broadcast_to(small, parted.shape).reshape(v.shape)

    def pair_step(g, carry):
        at = [pl.ds(pl.multiple_of((2 * g + k) * members, 16), members) for k in range(2)]
        for half in range(halves):
            def lanes(part):
                start = part * channels + half * LANES
                return slice(start, start + LANES)

            q, k, v = ([packed_ref[at[n], lanes(part)] for n in range(2)] for part in range(3))
            cot = [att_grad_ref[at[n], lanes(0)] for n in range(2)]
            q_diag, cot_diag = diagonal(q), diagonal(cot)
            k_tall, v_tall = by_head(k), by_head(v)
            scores = dot(k_tall, q_diag, ((1,), (1,))) * scale + bias_ref[half]
            grad_probs = dot(v_tall, cot_diag, ((1,), (1,)))
            lifted = jnp.exp(scores - over_members(scores, jnp.max))
            soft = lifted * (1.0 / over_members(lifted, jnp.sum))
            soft_low = soft.astype(BF16)
            grad_scores = soft * (grad_probs - over_members(grad_probs * soft, jnp.sum))
            bias_sum_ref[half] += grad_scores
            scaled = (grad_scores * scale).astype(BF16)
            attended = blocks(dot(soft_low, v_tall, ((0,), (0,))))
            grad_q = blocks(dot(scaled, k_tall, ((0,), (0,))))
            grad_v = collect(dot(soft_low, cot_diag))
            grad_k = collect(dot(scaled, q_diag))
            for n in range(2):
                att_ref[at[n], lanes(0)] = attended[n].astype(BF16)
                for part, value in enumerate((grad_q, grad_k, grad_v)):
                    packed_grad_ref[at[n], lanes(part)] = value[n].astype(BF16)
        return carry

    lax.fori_loop(0, cells // members // 2, pair_step, 0, unroll=2)
    grad = dot(packed_grad_ref[...], w_qkv_ref[...], ((1,), (1,)))
    for half in range(halves):
        lanes = slice(half * LANES, (half + 1) * LANES)
        for k, at in places():
            order_ref[half, at, :] = grad[k : k + GRID, lanes]
        grad_ref[:, lanes] = order_ref[half].astype(BF16)
    for half in range(halves):
        both = bias_sum_ref[half]
        bias_out_ref[half] = both[:, :members] + both[:, members:]


def run_attention(arrived, att_grad, w_qkv, bias_tall, heads, lines):
    cells, channels = att_grad.shape
    halves, tall, members2 = bias_tall.shape
    members = members2 // 2
    vmem = pl.BlockSpec(memory_space=pltpu.VMEM)
    return pl.pallas_call(
        functools.partial(attention_kernel, members, heads, lines),
        in_specs=[vmem] * 4,
        out_specs=[vmem] * 5,
        out_shape=[
            jax.ShapeDtypeStruct((cells, channels), BF16),
            jax.ShapeDtypeStruct((cells, channels), BF16),
            jax.ShapeDtypeStruct((cells, channels), BF16),
            jax.ShapeDtypeStruct((cells, 3 * channels), BF16),
            jax.ShapeDtypeStruct((halves, tall, members), F32),
        ],
        scratch_shapes=[
            pltpu.VMEM((channels // LANES, cells, LANES), F32),
            pltpu.VMEM((cells, 3 * channels), BF16),
            pltpu.VMEM(bias_tall.shape, F32),
        ],
        compiler_params=PARAMS,
        cost_estimate=estimate(14),
        name="attention",
    )(arrived.reshape(cells, channels), att_grad, w_qkv, bias_tall)


def attention_weights_kernel(x_ref, packed_grad_ref, att_ref, cot_ref, bias_ref, out_ref):
    channels = x_ref.shape[1]
    wide = 3 * channels
    out_ref[:, :wide] = dot(x_ref[...], packed_grad_ref[...], ((0,), (0,))).astype(BF16)
    out_ref[:, wide : wide + channels] = dot(att_ref[...], cot_ref[...], ((0,), (0,))).astype(BF16)
    halves, tall, members = bias_ref.shape
    for h in range(tall // members):
        rows = slice(h * members, (h + 1) * members)
        turned = jnp.concatenate([bias_ref[half, rows, :].T for half in range(halves)], axis=1)
        out_ref[rows, wide + channels :] = turned.astype(BF16)


def run_attention_weights(x, packed_grad, att, cot, bias):
    channels = x.shape[1]
    vmem = pl.BlockSpec(memory_space=pltpu.VMEM)
    width = 4 * channels + bias.shape[0] * bias.shape[2]
    return pl.pallas_call(
        attention_weights_kernel,
        in_specs=[vmem] * 5,
        out_specs=vmem,
        out_shape=jax.ShapeDtypeStruct((channels, width), BF16),
        compiler_params=PARAMS,
        cost_estimate=estimate(5),
        name="attention_weights",
    )(x, packed_grad, att, cot, bias)


def mixed_back_kernel(
    stride, bands,
    recv_ref, mixed_ref, cot_ref, gain_ref, act_ref, gate_ref, w_projt_ref,
    low_ref, norm_ref, project_ref, gate_grad_ref,
    turned_ref, total_ref,
):
    rows, cols, channels = mixed_ref.shape

    @pl.when(pl.program_id(0) == 0)
    def _():
        gain = gain_ref[...].astype(F32)
        lines = 4

        def some_rows(c, total):
            pieces = []
            for k in range(lines):
                i = c * lines + k
                a, p = lax.rem(i, stride), i // stride
                pieces += [recv_ref[a * bands + band, p] for band in range(bands)]
            grad = jnp.concatenate(pieces, axis=0).astype(F32)
            at = pl.ds(c * lines, lines)
            flat = lambda ref: ref[at].reshape(lines * cols, channels).astype(F32)
            unit, rstd = norm_rows(flat(mixed_ref))
            back = flat(cot_ref) + norm_rows_back(unit, rstd, gain, grad)
            low_ref[at] = back.astype(BF16).reshape(lines, cols, channels)
            return total + fold_rows(grad * unit)

        total = lax.fori_loop(
            0, rows // lines, some_rows, jnp.zeros((8, channels), F32), unroll=2
        )
        norm_ref[...] = jnp.sum(total, axis=0, keepdims=True)
        turned_ref[...] = low_ref[...].reshape(rows * cols, channels).T

    flat = act_ref[...].reshape(rows * cols, BLOCK)
    product = dot(turned_ref[...], flat)
    total = jnp.sum(product * w_projt_ref[...].astype(F32), axis=0, keepdims=True)
    step, steps = pl.program_id(0), pl.num_programs(0)
    total_ref[step] = total
    project_ref[...] = (product * gate_ref[...]).T.astype(BF16)

    @pl.when(step == steps - 1)
    def _():
        sums = [total_ref[e] for e in range(total_ref.shape[0])]
        high = [v.astype(BF16).astype(F32) for v in sums]
        terms = jnp.concatenate(high + [v - w for v, w in zip(sums, high)], axis=0)
        gate_grad_ref[...] = jnp.broadcast_to(terms.astype(BF16)[None], gate_grad_ref.shape)


def run_mixed_back(count, stride, recv, mixed, cot, gain, act, gate, w_project_t):
    rows, cols, channels = mixed.shape
    expanded = act.shape[2]
    return pl.pallas_call(
        functools.partial(mixed_back_kernel, stride, cols // SIDE),
        grid=(expanded // BLOCK,),
        in_specs=[
            whole(recv.shape), whole(mixed.shape), whole(cot.shape), whole(gain.shape),
            last_block(act.shape), last_block(gate.shape), last_block(w_project_t.shape),
        ],
        out_specs=[
            whole(mixed.shape), whole((1, channels)),
            last_block((BLOCK, expanded)), whole((count, 2 * expanded // BLOCK, BLOCK)),
        ],
        out_shape=[
            jax.ShapeDtypeStruct(mixed.shape, BF16),
            jax.ShapeDtypeStruct((1, channels), F32),
            jax.ShapeDtypeStruct((BLOCK, expanded), BF16),
            jax.ShapeDtypeStruct((count, 2 * expanded // BLOCK, BLOCK), BF16),
        ],
        scratch_shapes=[
            pltpu.VMEM((channels, rows * cols), BF16),
            pltpu.VMEM((expanded // BLOCK, 1, BLOCK), F32),
        ],
        compiler_params=PARAMS,
        cost_estimate=estimate(7),
        name="mixed_back",
    )(recv, mixed, cot, gain, act, gate, w_project_t)


def core_place():
    return (lax.axis_index("col") % 2).astype(jnp.int32).reshape(1)


def unpack_kernel(
    place_ref, near_ref, far_ref, expand_ref, depth_ref, norm0_ref, norm1_ref, tail_ref
):
    expanded = expand_ref.shape[2]
    for pair, source in enumerate((near_ref, far_ref)):
        at = lax.rem(place_ref[0] + pair, 2)
        expand_ref[at] = source[:, :expanded].astype(F32)
        tail_ref[at] = source[:, expanded:].astype(F32)
    tail = tail_ref[0]
    pieces = expanded // LANES
    for t in range(9):
        for k in range(pieces):
            row = t * pieces + k
            lanes = slice(k * LANES, (k + 1) * LANES)
            depth_ref[t // 3, t % 3 : t % 3 + 1, lanes] = tail[row : row + 1]
    start = 9 * pieces
    half = norm0_ref.shape[1] // LANES
    for k in range(half):
        lanes = slice(k * LANES, (k + 1) * LANES)
        norm0_ref[:, lanes] = tail[start + k : start + k + 1]
        norm1_ref[:, lanes] = tail[start + half + k : start + half + k + 1]


def run_unpack(near, far, expanded):
    rows = near.shape[0]
    channels = 2 * rows
    vmem = pl.BlockSpec(memory_space=pltpu.VMEM)
    return pl.pallas_call(
        unpack_kernel,
        in_specs=[pl.BlockSpec(memory_space=pltpu.SMEM), vmem, vmem],
        out_specs=[vmem] * 4,
        out_shape=[
            jax.ShapeDtypeStruct((2, rows, expanded), F32),
            jax.ShapeDtypeStruct((3, 3, expanded), F32),
            jax.ShapeDtypeStruct((1, channels), F32),
            jax.ShapeDtypeStruct((1, channels), F32),
        ],
        scratch_shapes=[pltpu.VMEM((2, rows, near.shape[1] - expanded), F32)],
        compiler_params=SMALL,
        cost_estimate=estimate(2),
        name="unpack",
    )(core_place(), near, far)


def expand_back_kernel(
    cells_total,
    place_ref, parts_ref, hidden_ref, gate_all_ref, w_sq_ref, w_ex_ref,
    low_ref, up_ref, down_ref, side_ref, w_projt_ref, gate_ref, slope_ref, side_slope_ref,
    spread_slope_ref, spread_ref, w_dep_ref, turned_ref, w_exp_ref, gain_ref, norm1_ref,
    mine_ref, other_ref, first_ref, logit_ref, pre_ref,
    main_ref, side_grad_ref, window_ref, expanded_ref, pool_ref, tail_ref, norm_ref,
):
    rows, cols, channels = low_ref.shape
    side = 8
    wide = cols + side
    step = pl.program_id(0)
    steps = pl.num_programs(0)

    @pl.when(step == 0)
    def _():
        gate = gate_all_ref[...]
        blocks = pool_ref.shape[0]
        terms = jnp.sum(parts_ref[...].astype(F32), axis=0)
        gate_grad = jnp.concatenate(
            [terms[e : e + 1] + terms[blocks + e : blocks + e + 1] for e in range(blocks)], axis=1
        )
        logit = gate_grad * gate * (1.0 - gate)
        hidden = hidden_ref[...]
        sig = jax.nn.sigmoid(hidden)
        pre = dot_exact(logit, w_ex_ref[...].astype(F32), ((1,), (1,))) * (
            sig + hidden * sig * (1.0 - sig)
        )
        logit_ref[...] = logit
        pre_ref[...] = pre
        pooled = dot_exact(pre, w_sq_ref[...].astype(F32), ((1,), (1,))) / cells_total
        for e in range(blocks):
            pool_ref[e] = pooled[:, e * BLOCK : (e + 1) * BLOCK]
        first_ref[...] = jnp.zeros(first_ref.shape, F32)
        tail_ref[...] = jnp.zeros(tail_ref.shape, F32)
        norm_ref[...] = jnp.zeros(norm_ref.shape, F32)

    w_projt = w_projt_ref[...]
    main_ref[pl.ds(0, cols), :] = dot(up_ref[0], w_projt)
    main_ref[pl.ds(cols, rows * cols), :] = dot(
        low_ref[...].reshape(rows * cols, channels), w_projt
    )
    main_ref[pl.ds((rows + 1) * cols, cols), :] = dot(down_ref[0], w_projt)
    side_grad_ref[...] = dot(side_ref[...], w_projt)

    @pl.loop(0, rows + 2, unroll=3)
    def _(i):
        for h in range(BLOCK // LANES):
            lanes = slice(h * LANES, (h + 1) * LANES)
            gate = gate_ref[:, lanes]
            pooled = pool_ref[step][:, lanes]
            gated = main_ref[pl.ds(pl.multiple_of(i * cols, 16), cols), lanes]
            main = (gated * gate + pooled) * slope_ref[i, :, lanes].astype(F32)
            gated = side_grad_ref[pl.ds(pl.multiple_of(i * side, side), side), lanes]
            edge = (gated * gate + pooled) * side_slope_ref[i, :, lanes]
            grad = jnp.concatenate([main, edge], axis=0)
            window_ref[0, i, :, lanes] = pltpu.roll(grad, wide - 1, 0)[:cols]
            window_ref[1, i, :, lanes] = grad[:cols]
            window_ref[2, i, :, lanes] = pltpu.roll(grad, 1, 0)[:cols]

    for h in range(BLOCK // LANES):
        lanes = slice(h * LANES, (h + 1) * LANES)
        taps = w_dep_ref[:, :, lanes].astype(F32)

        def back_row(i, sums):
            spread = spread_ref[i, :, lanes].astype(F32)
            total = jnp.zeros((cols, LANES), F32)
            new_sums = []
            for a in range(3):
                for b in range(3):
                    window = window_ref[b, i + 2 - a, :, lanes]
                    total = total + window * taps[a, b : b + 1]
                    new_sums.append(sums[a * 3 + b] + fold_rows(window * spread))
            grad = total * spread_slope_ref[i, :, lanes].astype(F32)
            expanded_ref[pl.ds(pl.multiple_of(i * cols, 16), cols), lanes] = grad.astype(BF16)
            return tuple(new_sums)

        sums = lax.fori_loop(0, rows, back_row, (jnp.zeros((8, LANES), F32),) * 9, unroll=2)
        for t in range(9):
            row = t * (steps * BLOCK // LANES) + step * (BLOCK // LANES) + h
            tail_ref[pl.ds(row, 1), :] = jnp.sum(sums[t], axis=0, keepdims=True)

    grad_expanded = expanded_ref[...]
    w_exp = w_exp_ref[...]
    weights = dot(turned_ref[...], grad_expanded)


    def keep(at, values):
        half = channels // 2
        upper, lower = values[:half], values[half:]
        first_core = place_ref[0] == 0
        mine_ref[:, at] = jnp.where(first_core, upper, lower).astype(BF16)
        other_ref[:, at] = jnp.where(first_core, lower, upper).astype(BF16)

    keep(pl.ds(pl.multiple_of(step * BLOCK, BLOCK), BLOCK), weights)
    norm_ref[...] += jnp.sum(weights * w_exp.astype(F32), axis=1, keepdims=True)
    first_ref[...] += dot(grad_expanded, w_exp, ((1,), (1,)))

    @pl.when(step == steps - 1)
    def _():
        norm = norm_ref[...].T[0:1] / gain_ref[...].astype(F32)
        start = 9 * steps * (BLOCK // LANES)
        for k in range(channels // LANES):
            piece = slice(k * LANES, (k + 1) * LANES)
            tail_ref[start + k : start + k + 1, :] = norm[:, piece]
            at = start + channels // LANES + k
            tail_ref[at : at + 1, :] = norm1_ref[:, piece]
        keep(slice(mine_ref.shape[1] - LANES, mine_ref.shape[1]), tail_ref[...])


def run_expand_back(
    cells_total, parts, hidden, gate, w_squeeze, w_excite, low, up, down, side,
    w_project_t, slope, side_slope, spread_slope, spread, w_depth, turned, w_expand, gain, norm1,
):
    rows, cols, channels = low.shape
    expanded = w_expand.shape[1]
    steps = expanded // BLOCK
    return pl.pallas_call(
        functools.partial(expand_back_kernel, cells_total),
        grid=(steps,),
        in_specs=[
            pl.BlockSpec(memory_space=pltpu.SMEM),
            pl.BlockSpec(
                (parts.shape[0], 2 * steps, BLOCK), lambda e: (0, parts.shape[1] // (2 * steps) - 1, 0)
            ),
            whole(hidden.shape), whole(gate.shape),
            whole(w_squeeze.shape), whole(w_excite.shape),
            whole(low.shape), whole(up.shape), whole(down.shape), whole(side.shape),
            last_block(w_project_t.shape), last_block(gate.shape), last_block(slope.shape),
            last_block(side_slope.shape), last_block(spread_slope.shape), last_block(spread.shape),
            last_block(w_depth.shape), whole(turned.shape), last_block(w_expand.shape),
            whole(gain.shape), whole(norm1.shape),
        ],
        out_specs=[
            whole((channels // 2, expanded + LANES)), whole((channels // 2, expanded + LANES)),
            whole((rows * cols, channels)),
            whole((1, expanded)), whole(hidden.shape),
        ],
        out_shape=[
            jax.ShapeDtypeStruct((channels // 2, expanded + LANES), BF16),
            jax.ShapeDtypeStruct((channels // 2, expanded + LANES), BF16),
            jax.ShapeDtypeStruct((rows * cols, channels), F32),
            jax.ShapeDtypeStruct((1, expanded), F32),
            jax.ShapeDtypeStruct(hidden.shape, F32),
        ],
        scratch_shapes=[
            pltpu.VMEM(((rows + 2) * cols, BLOCK), F32),
            pltpu.VMEM(((rows + 2) * 8, BLOCK), F32),
            pltpu.VMEM((3, rows + 2, cols, BLOCK), F32),
            pltpu.VMEM((rows * cols, BLOCK), BF16),
            pltpu.VMEM((steps, 1, BLOCK), F32),
            pltpu.VMEM((channels, LANES), F32),
            pltpu.VMEM((channels, LANES), F32),
        ],
        compiler_params=PARAMS,
        cost_estimate=estimate(14),
        name="expand_back",
    )(
        core_place(), parts, hidden, gate, w_squeeze, w_excite, low, up, down, side, w_project_t, gate,
        slope, side_slope, spread_slope, spread, w_depth, turned, w_expand, gain, norm1,
    )


def image_back_kernel(image_ref, gain_ref, first_ref, mixed_ref, out_ref):
    unit, rstd = norm_rows(image_ref[...].astype(F32))
    grad = first_ref[...]
    back = mixed_ref[...].astype(F32) + norm_rows_back(unit, rstd, gain_ref[...].astype(F32), grad)
    out_ref[...] = back.astype(BF16)


def run_image_back(image, gain, first, mixed):
    cells, channels = image.shape
    block = pl.BlockSpec((cells // 4, channels), lambda r: (r, 0))
    return pl.pallas_call(
        image_back_kernel,
        grid=(4,),
        in_specs=[block, whole(gain.shape), block, block],
        out_specs=block,
        out_shape=jax.ShapeDtypeStruct((cells, channels), BF16),
        compiler_params=SMALL,
        cost_estimate=estimate(4),
        name="image_back",
    )(image, gain, first, mixed)


def shift(cells, axis, step):
    count = lax.axis_size(axis)
    pairs = [(i, i + step) for i in range(count) if 0 <= i + step < count]
    return lax.ppermute(cells, axis, pairs)


def halo_rows(cells, width):
    up = shift(cells[cells.shape[0] - width :], "row", 1)
    down = shift(cells[:width], "row", -1)
    return up, down


def halo_sides(cells, up, down, width):
    rows, cols, channels = cells.shape
    first = jnp.concatenate([up[:, :width], cells[:, :width], down[:, :width]], axis=0)
    last = jnp.concatenate(
        [up[:, cols - width :], cells[:, cols - width :], down[:, cols - width :]], axis=0
    )
    left = shift(last, "col", 1)
    right = shift(first, "col", -1)
    gap = jnp.zeros((rows + 2 * width, 8 - 2 * width, channels), cells.dtype)
    side = jnp.concatenate([right, gap, left], axis=1)
    return side.reshape(-1, channels)


def hand_around(blocks):
    return lax.all_to_all(blocks, AXES, split_axis=0, concat_axis=0, tiled=True)


def sum_steps():
    return [("col", 1, 2), ("row", 1, lax.axis_size("row")), ("col", 2, lax.axis_size("col") // 2)]


def send_on(v, axis, stride, size, k):
    pairs = []
    for i in range(lax.axis_size(axis)):
        place = i // stride % size
        pairs.append((i, i + ((place + k) % size - place) * stride))
    return lax.ppermute(v, axis, pairs)


def sum_parts(matrix, axis, stride, size):
    place = lax.axis_index(axis) // stride % size
    parts = matrix.reshape(size, matrix.shape[0] // size, matrix.shape[1])
    part = lambda i: lax.dynamic_index_in_dim(parts, i % size, 0, False)
    total = part(place).astype(F32)
    for k in range(1, size):
        total = total + send_on(part(place + k), axis, stride, size, k).astype(F32)
    return total.astype(BF16)


def sum_shares(mine, other):
    rows, columns = 2 * mine.shape[0], mine.shape[1]
    count = lax.axis_size("row") * lax.axis_size("col")
    pair = ("col", 1, 2)
    half = (mine.astype(F32) + send_on(other, *pair, 1).astype(F32)).astype(BF16)
    same_core = [list(range(k, count, 2)) for k in range(2)]

    def around(blocks):
        return lax.all_to_all(
            blocks, AXES, split_axis=0, concat_axis=0, tiled=True, axis_index_groups=same_core
        )

    arrived = around(half.reshape(count // 2, rows // count, columns))
    total = jnp.sum(arrived.astype(F32), axis=0).astype(BF16)
    sent = jnp.broadcast_to(total[None], (count // 2,) + total.shape)
    gathered = around(sent).reshape(rows // 2, columns)
    return gathered, send_on(gathered, *pair, 1)


def stack_kernel(*refs):
    for k, ref in enumerate(refs[:-1]):
        refs[-1][k] = ref[...]


def join_parts(blocks, axis, stride, size):
    arrived = [blocks] + [send_on(blocks, axis, stride, size, k) for k in range(1, size)]
    vmem = pl.BlockSpec(memory_space=pltpu.VMEM)
    stacked = pl.pallas_call(
        stack_kernel,
        in_specs=[vmem] * size,
        out_specs=vmem,
        out_shape=jax.ShapeDtypeStruct((size,) + blocks.shape, blocks.dtype),
        compiler_params=SMALL,
        cost_estimate=estimate(1),
        name="stack",
    )(*arrived)
    return stacked.reshape((size * blocks.shape[0],) + blocks.shape[1:])


def unpack_weights_kernel(
    sizes, places_ref, near_ref, far_ref, qkv_ref, out_ref, bias_ref, project_ref
):
    channels = out_ref.shape[2]
    halves, members = bias_ref.shape[0], bias_ref.shape[3]
    cuts = (0, 3 * channels, 4 * channels, 4 * channels + halves * members)
    pairs, over_row, rest = sizes
    for pair, source in enumerate((near_ref, far_ref)):
        for r in range(over_row):
            for c in range(rest):
                block = source[r * rest + c].astype(F32)
                at = lax.rem(places_ref[0] + pairs - pair, pairs)
                at = at * over_row + lax.rem(places_ref[1] + over_row - r, over_row)
                at = at * rest + lax.rem(places_ref[2] + rest - c, rest)
                qkv_ref[at] = block[:, : cuts[1]]
                out_ref[at] = block[:, cuts[1] : cuts[2]]
                for half in range(halves):
                    start = cuts[2] + half * members
                    bias_ref[half, at] = block[:, start : start + members]
                for e in range(project_ref.shape[0]):
                    start = cuts[3] + e * channels
                    project_ref[e, at] = block[:, start : start + channels]


def run_unpack_weights(steps, near, far, channels, expanded, halves, members):
    count, rows, _ = near.shape
    count *= 2
    places = jnp.stack([lax.axis_index(axis) // stride % size for axis, stride, size in steps])
    vmem = pl.BlockSpec(memory_space=pltpu.VMEM)
    blocks = lambda width: jax.ShapeDtypeStruct((count, rows, width), F32)
    return pl.pallas_call(
        functools.partial(unpack_weights_kernel, tuple(size for _, _, size in steps)),
        in_specs=[pl.BlockSpec(memory_space=pltpu.SMEM), vmem, vmem],
        out_specs=[vmem] * 4,
        out_shape=[
            blocks(3 * channels), blocks(channels),
            jax.ShapeDtypeStruct((halves, count, rows, members), F32),
            jax.ShapeDtypeStruct((expanded // BLOCK, count, rows, channels), F32),
        ],
        compiler_params=SMALL,
        cost_estimate=estimate(2),
        name="unpack_weights",
    )(places.astype(jnp.int32), near, far)


def swap_groups(blocks, parity):
    groups = None
    if parity > 1:
        over_row = lax.axis_size("row")
        over_col = lax.axis_size("col")
        groups = [
            [r * over_col + c for r in range(over_row) for c in range(k, over_col, parity)]
            for k in range(parity)
        ]
    return lax.all_to_all(
        blocks, AXES, split_axis=0, concat_axis=0, tiled=True, axis_index_groups=groups
    )


def on_device(
    image, out_cotangent, norm0_gain, w_expand, w_depth, w_squeeze, w_excite, w_project,
    norm1_gain, w_qkv, w_out, attn_bias,
):
    rows, cols, channels = image.shape
    over_row = lax.axis_size("row")
    over_col = lax.axis_size("col")
    count = over_row * over_col
    cells_total = rows * cols * count
    stride = rows * over_row // GRID
    parity = over_col // GRID
    lines = rows // stride
    bands = cols // SIDE
    members = GRID * GRID
    expanded = w_expand.shape[1]

    def into_members(arrived):
        parted = arrived.reshape(over_row, GRID, lines, SIDE, channels)
        return parted.transpose(3, 0, 2, 1, 4).reshape(SIDE * members, channels)

    def out_of_members(values):
        parted = values.reshape(SIDE, over_row, lines, GRID, channels)
        return parted.transpose(1, 3, 2, 0, 4).reshape(-1, lines, SIDE, channels)

    row, col = lax.axis_index("row"), lax.axis_index("col")
    flags = jnp.stack([row > 0, row < over_row - 1, col > 0, col < over_col - 1]).astype(F32)
    gain_first = norm0_gain.reshape(1, channels)
    gain_second = norm1_gain.reshape(1, channels)
    w_project_t = w_project.T
    heads = attn_bias.shape[0]
    halves = channels // LANES
    bias_tall = attn_bias.transpose(0, 2, 1).reshape(halves, heads // halves * members, members)
    bias_tall = jnp.concatenate([bias_tall, bias_tall], axis=2)

    up, down = halo_rows(image, 2)
    normed_first, spread, pre_spread = run_expand(image, gain_first, w_expand)
    up, down, spread = lax.optimization_barrier((up, down, spread))
    side = halo_sides(image, up, down, 2)
    cot_sent = (
        out_cotangent.reshape(lines, stride, bands, SIDE, channels)
        .transpose(1, 2, 0, 3, 4)
        .reshape(stride * bands, lines, SIDE, channels)
    )
    cot_members = into_members(swap_groups(cot_sent, parity))
    ring, act, pool = run_depthwise(count, up, down, side, gain_first, w_expand, w_depth, spread)
    pooled, hidden, gate, mixed, normed_sent = run_mix(
        cells_total, stride, hand_around(pool), w_squeeze, w_excite, act, image, w_project,
        gain_second, cot_members,
    )
    slope, side_slope, spread_slope, turned_first = run_slope(
        flags, ring, w_depth, spread, pre_spread, normed_first
    )
    normed_arrived = swap_groups(normed_sent, parity)
    att_grad = dot(cot_members, w_out, ((1,), (1,))).astype(BF16)
    normed_arrived, slope, att_grad = lax.optimization_barrier((normed_arrived, slope, att_grad))
    normed_members, attended, grad_normed, packed_grad, grad_bias = run_attention(
        normed_arrived, att_grad, w_qkv, bias_tall, heads, lines
    )
    grad_normed_home = swap_groups(grad_normed.reshape(normed_sent.shape), parity)
    weights = run_attention_weights(normed_members, packed_grad, attended, cot_members, grad_bias)
    grad_normed_home, weights = lax.optimization_barrier((grad_normed_home, weights))
    grad_low, grad_norm1, grad_project, gate_grad = run_mixed_back(
        count, stride, grad_normed_home, mixed, out_cotangent, gain_second, act, gate, w_project_t
    )
    attended_sent = out_of_members(attended)
    if parity == 1:
        both = hand_around(
            jnp.concatenate([attended_sent.reshape(count, -1, channels), gate_grad], axis=1)
        )
        parts = both
        attended_home = both[:, : lines * SIDE].reshape(attended_sent.shape)
    else:
        parts = hand_around(gate_grad)
        attended_home = swap_groups(attended_sent, parity)
    up, down = halo_rows(grad_low, 1)
    side = halo_sides(grad_low, up, down, 1)
    weights = jnp.concatenate([weights, grad_project], axis=1)
    weights, _ = lax.optimization_barrier((weights, up))
    steps = sum_steps()
    for step in steps:
        weights = sum_parts(weights, *step)
    late, late_other, grad_first, logit, pre = run_expand_back(
        cells_total, parts, hidden, gate, w_squeeze, w_excite, grad_low, up, down, side,
        w_project_t, slope, side_slope, spread_slope, spread, w_depth, turned_first, w_expand,
        gain_first, grad_norm1,
    )
    weights, _ = lax.optimization_barrier((weights, late))
    weights = weights[None]
    for step in steps[:0:-1]:
        weights = join_parts(weights, *step)
    other = send_on(weights, *steps[0], 1)
    grad_qkv, grad_out_proj, grad_bias, grad_project = run_unpack_weights(
        steps, weights, other, channels, expanded, halves, members
    )
    grad_expand, grad_depth, grad_norm0, grad_norm1 = run_unpack(*sum_shares(late, late_other), expanded)
    grad_image = run_image_back(
        image.reshape(-1, channels), gain_first, grad_first, grad_low.reshape(-1, channels)
    )
    attended_map = (
        attended_home.reshape(stride, bands, lines, SIDE, channels)
        .transpose(2, 0, 1, 3, 4)
        .reshape(rows * cols, channels)
    )
    block_out = (mixed.reshape(-1, channels).astype(F32) + dot(attended_map, w_out)).astype(BF16)

    silu = jax.nn.silu(hidden)
    grad_squeeze = pooled.reshape(expanded, 1) * pre
    grad_excite = silu.reshape(-1, 1) * logit

    return (
        block_out.reshape(image.shape),
        grad_image.reshape(image.shape),
        grad_norm0[0],
        grad_expand.reshape(w_expand.shape),
        grad_depth,
        grad_squeeze,
        grad_excite,
        grad_project.reshape(w_project.shape),
        grad_norm1[0],
        grad_qkv.reshape(w_qkv.shape),
        grad_out_proj.reshape(w_out.shape),
        grad_bias.reshape(attn_bias.shape),
    )


def solution(mesh):
    cells = P("row", "col", None)
    return jax.shard_map(
        on_device,
        mesh=mesh,
        in_specs=(cells, cells) + (P(),) * 10,
        out_specs=(cells, cells) + (P(),) * 10,
        check_vma=False,
    )
```
